128 devices in a mesh: row: 8 (over z_hi, y), col: 16 (over x, z_lo, core).
Axes of the slice: x: 4, y: 4, z: 4 (z_hi: 2, z_lo: 2; z = z_hi * 2 + z_lo), core: 2. Of those that a mesh axis runs over, the one named last changes fastest.
Arguments:
- object_tile: float32 [2, 2048, 4096], P(None, 'row', 'col'), may hold values from -6 to 6
- probe: float32 [2, 2, 256, 256], replicated, may hold values from -6 to 6
- amplitudes: float32 [8, 16, 4, 256, 256], P('row', 'col'), may hold values from 0 to 15
- offsets: int32 [8, 16, 4, 2], P('row', 'col'), may hold values from 0 to 256
Outputs:
- object_update: float32 [2, 2048, 4096], P(None, 'row', 'col')
- probe_update: float32 [2, 2, 256, 256], replicated
- position_step: float32 [8, 16, 4, 2], P('row', 'col')
- relative_error: float32 [1], replicated
The draws below stay inside these ranges and needn't reach their ends.
All inputs are finite; a program needn't handle non-finite values.
Results may differ from the reference program's by a relative error of at most 0.00021.
Values sent between devices are 32-bit elements; how exact they have to be, the bound alone decides.
No kernel may reach another device: no remote copies, remote signals or barrier semaphores. Data moves between devices by JAX's collectives and lax.ppermute only.
A program may use at most 128 MiB of HBM per device.

```python
import jax
import jax.numpy as jnp
from jax import lax

TILE = 256
POS_DEV = 4
PATCH = 256
MODES = 2
NY = 2048
NX = 4096
N_ROW = 8
N_COL = 16


def draw_amplitudes(key, part):
    key = jax.random.fold_in(key, 7)
    shape = (N_ROW, N_COL, POS_DEV, PATCH, PATCH)
    count = N_ROW * N_COL
    order = jnp.arange(count, dtype=jnp.float32).reshape(N_ROW, N_COL, 1, 1, 1)
    rising = 1.0 + 2.0 * order / max(count - 1, 1)
    base = jnp.minimum(jnp.abs(jax.random.normal(key, shape, jnp.float32)) * 1.5, 5.0)
    return base * rising


def set_ends(drawn, own_key, least, largest):
    place = [jax.random.randint(jax.random.fold_in(own_key, axis), (), 0, length) for axis, length in enumerate(drawn.shape)]
    main_axis = drawn.shape.index(max(drawn.shape))
    neighbour = place[:main_axis] + [(place[main_axis] + 1) % drawn.shape[main_axis]] + place[main_axis + 1:]
    return drawn.at[tuple(place)].set(least).at[tuple(neighbour)].set(largest)


def steps_of(own_key, dims, pieces, low, high):
    def one(position, parts):
        steps = jax.random.uniform(jax.random.fold_in(jax.random.fold_in(own_key, 6), position), (parts,), jnp.float32, low / len(pieces), high / len(pieces))
        return jnp.repeat(jnp.exp(steps), dims[position] // parts).reshape((-1,) + (1,) * (len(dims) - position - 1))

    level = one(*pieces[0])
    for cut in pieces[1:]:
        level = level * one(*cut)
    return level


def bell_draw(key, extent, deviation, most, pieces=(), kind=jnp.bfloat16):
    values = deviation * jax.random.normal(key, extent, jnp.float32)
    if pieces:
        values = values * steps_of(key, extent, pieces, -0.22, 0.18)
    return jnp.clip(values, -most, most).astype(kind)


def setup_inputs(seed: int = 0) -> dict:
    arg_keys = jax.random.split(jax.random.key(seed), 5)
    object_tile = bell_draw(arg_keys[0], (2, NY, NX), 1.0, 6.0, ((1, 8), (2, 16)), jnp.float32)
    probe = bell_draw(arg_keys[1], (MODES, 2, PATCH, PATCH), 1.0, 6.0, (), jnp.float32)
    amplitudes = draw_amplitudes(jax.random.fold_in(arg_keys[4], 71), 0)
    offsets = set_ends(jax.random.randint(arg_keys[3], (N_ROW, N_COL, POS_DEV, 2), 0, TILE + 1), jax.random.fold_in(arg_keys[3], 1), 0, TILE).astype(jnp.int32)
    return dict(object_tile=object_tile, probe=probe, amplitudes=amplitudes, offsets=offsets)


intensity_floor = 0.1
object_damping = 1.0
small_value = 1e-06

def derivative(field, axis):
    widths = [(1, 1) if dimension == axis else (0, 0) for dimension in range(field.ndim)]
    padded = jnp.pad(field, widths)
    length = padded.shape[axis]
    upper = lax.slice_in_dim(padded, 2, length, axis=axis)
    lower = lax.slice_in_dim(padded, 0, length - 2, axis=axis)
    return 0.5 * (upper - lower)

def reference(object_tile, probe, amplitudes, offsets):
    halo_width = PATCH // 2
    padded = jnp.pad(object_tile, ((0, 0), (halo_width, halo_width), (halo_width, halo_width)))
    grid_rows = jnp.arange(N_ROW, dtype=jnp.int32)[:, None, None] * TILE
    grid_cols = jnp.arange(N_COL, dtype=jnp.int32)[None, :, None] * TILE
    start_rows = (grid_rows + offsets[..., 0]).reshape(-1).astype(jnp.int32)
    start_cols = (grid_cols + offsets[..., 1]).reshape(-1).astype(jnp.int32)
    measured_all = amplitudes.reshape(-1, PATCH, PATCH)
    probe_field = probe[:, 0] + 1j * probe[:, 1]
    probe_power = lax.optimization_barrier(jnp.sum(probe[:, 0] ** 2 + probe[:, 1] ** 2, axis=0))
    zero_scalar = jnp.zeros((), jnp.float32)
    initial = (jnp.zeros((3,) + padded.shape[1:], jnp.float32), jnp.zeros((2, MODES, PATCH, PATCH), jnp.float32), jnp.zeros((PATCH, PATCH), jnp.float32), zero_scalar, zero_scalar)

    def advance(carry, inputs):
        accum, probe_grad, power_sum, error_sum, energy_sum = carry
        row_start, col_start, measured = inputs
        where = (jnp.int32(0), row_start, col_start)
        window = lax.dynamic_slice(padded, where, (2, PATCH, PATCH))
        patch_field = window[0] + 1j * window[1]
        farfield = jnp.fft.fft2(probe_field * patch_field, norm='ortho')
        intensity = lax.optimization_barrier(jnp.sum(jnp.real(farfield) ** 2 + jnp.imag(farfield) ** 2, axis=0))
        modulus = jnp.sqrt(jnp.maximum(intensity, intensity_floor))
        back = jnp.fft.ifft2(farfield * (1.0 - measured / modulus), norm='ortho')
        object_grad = lax.optimization_barrier(jnp.sum(jnp.conj(probe_field) * back, axis=0))
        contribution = jnp.stack([jnp.real(object_grad), jnp.imag(object_grad), probe_power])
        current = lax.dynamic_slice(accum, where, (3, PATCH, PATCH))
        accum = lax.dynamic_update_slice(accum, current + contribution, where)
        probe_term = jnp.conj(patch_field)[None] * back
        probe_grad = probe_grad + jnp.stack([jnp.real(probe_term), jnp.imag(probe_term)])
        power_sum = power_sum + window[0] ** 2 + window[1] ** 2
        results = []
        for dimension in (0, 1):
            slope = probe_field * derivative(patch_field, dimension)
            numerator = jnp.sum(jnp.real(back) * jnp.real(slope) + jnp.imag(back) * jnp.imag(slope))
            denominator = jnp.sum(jnp.real(slope) ** 2 + jnp.imag(slope) ** 2) + small_value
            results.append(-numerator / denominator)
        error_sum = error_sum + jnp.sum((modulus - measured) ** 2)
        energy_sum = energy_sum + jnp.sum(measured ** 2)
        return ((accum, probe_grad, power_sum, error_sum, energy_sum), jnp.stack(results))
    final, position_flat = lax.scan(advance, initial, (start_rows, start_cols, measured_all))
    accum, probe_grad, power_sum, error_sum, energy_sum = final
    inner = accum[:, halo_width:halo_width + NY, halo_width:halo_width + NX]
    object_update = inner[:2] / (inner[2] + object_damping)
    probe_update = jnp.transpose(probe_grad / power_sum, (1, 0, 2, 3))
    position_step = position_flat.reshape(N_ROW, N_COL, POS_DEV, 2)
    relative_error = (error_sum / energy_sum).reshape(1)
    return (object_update, probe_update, position_step, relative_error)
```

```python
import jax
import jax.numpy as jnp
import ml_dtypes
import numpy as np
from jax import lax
from jax.experimental import pallas as pl
from jax.experimental.pallas import tpu as pltpu
from jax.sharding import PartitionSpec as P

intensity_floor = 0.1
object_damping = 1.0
small_value = 1e-06

SIZE = 256
HALF = 128
CHUNK = 32
BF = jnp.bfloat16
F32 = jnp.float32
AXES = ("row", "col")
VMEM_LIMIT = 56 * 2**20


def transform_matrices():
    n = np.arange(HALF)[:, None]
    q = np.arange(HALF)[None, :]
    out = []
    for odd in (0, 1):
        angle = -2.0 * np.pi * ((n * (2 * q + odd)) % SIZE) / SIZE
        re, im = np.cos(angle) / 16.0, np.sin(angle) / 16.0
        out.append(np.block([[re, im], [-im, re]]))
    return out


def split_np(matrix):
    high = matrix.astype(ml_dtypes.bfloat16)
    low = (matrix - high.astype(np.float64)).astype(ml_dtypes.bfloat16)
    return high, low


def constants():
    right_f, left_f, right_i, left_i = [], [], [], []
    for matrix in transform_matrices():
        high, low = split_np(matrix)
        right_f.append(np.concatenate([high, high, low], 0))
        left_f.append(np.concatenate([high.T, low.T, high.T], 1))
        right_i.append(np.concatenate([high.T, high.T, low.T], 0))
        left_i.append(np.concatenate([high, low, high], 1))
    return [np.stack(x) for x in (right_f, left_f, right_i, left_i)]


def permutation():
    order = np.concatenate([np.arange(0, SIZE, 2), np.arange(1, SIZE, 2)])
    onehot = np.zeros((SIZE, SIZE), np.float32)
    onehot[order, np.arange(SIZE)] = 1.0
    columns = np.concatenate([onehot] * 3, 0).astype(ml_dtypes.bfloat16)
    rows = np.concatenate([onehot.T] * 3, 1).astype(ml_dtypes.bfloat16)
    return columns, rows


def split2(value):
    high = value.astype(BF)
    return high, (value - high.astype(F32)).astype(BF)


def split3(value):
    high = value.astype(BF)
    rest = value - high.astype(F32)
    middle = rest.astype(BF)
    return high, middle, (rest - middle.astype(F32)).astype(BF)


def dot(a, b):
    return jnp.dot(a, b, preferred_element_type=F32)


def lane_index(rows):
    return lax.broadcasted_iota(jnp.int32, (rows, HALF), 1)


def spread(first, second, shift, lanes):
    a = pltpu.roll(first, shift, 1)
    b = pltpu.roll(second, shift, 1)
    wrapped = lanes < shift
    return jnp.where(wrapped, 0.0, a), jnp.where(wrapped, a, b), jnp.where(wrapped, b, 0.0)


def gather_lanes(blocks, shift, lanes):
    back = jnp.where(shift == 0, 0, HALF - shift)
    a, b, c = [pltpu.roll(x, back, 1) for x in blocks]
    inside = lanes < HALF - shift
    return jnp.where(inside, a, b), jnp.where(inside, b, c)


def fold8(value):
    return jnp.sum(value.reshape(-1, 8, HALF), axis=0)


def prepare_kernel(starts, probe, measured, cols, rows, center, left, right, permuted, power, accum):
    accum[...] = jnp.zeros_like(accum)
    for i in range(0, SIZE, CHUNK):
        part = pl.ds(i, CHUNK)
        total = probe[0, 0, part] ** 2 + probe[0, 1, part] ** 2
        power[part] = total + probe[1, 0, part] ** 2 + probe[1, 1, part] ** 2
    lanes = lane_index(CHUNK)
    for j in range(measured.shape[0]):
        row, col = starts[j, 0], starts[j, 1]
        base, shift = col // HALF, lax.rem(col, HALF)
        for i in range(0, SIZE, CHUNK):
            part = pl.ds(i, CHUNK)
            moved = spread(power[part, :HALF], power[part, HALF:], shift, lanes)
            where = pl.ds(row + i, CHUNK)
            for b in range(3):
                accum[base + b, where, :] += moved[b]
    center[:, :HALF] = accum[1]
    center[:, HALF:] = accum[2]
    left[...] = accum[0]
    right[...] = accum[3]
    for j in range(measured.shape[0]):
        moved = dot(jnp.concatenate(split3(measured[j]), 1), cols[...])
        permuted[j] = dot(rows[...], jnp.concatenate(split3(moved), 0))


def main_kernel(
    starts, core, own, up, down, left, right, left_corner, right_corner, probe, power, measured,
    right_f, left_f, right_i, left_i,
    grad_center, grad_left, grad_right, keep, send, steps,
    tile, patch, grad, totals, xs, zs, gs, ys, back, sums,
):
    step = pl.program_id(0)
    modes = probe.shape[0]
    lanes = lane_index(CHUNK)

    @pl.when(step == 0)
    def _():
        for p in range(2):
            tile[p, 0, 0:128] = left_corner[0, p]
            tile[p, 0, 128:384] = left[p]
            tile[p, 0, 384:512] = left_corner[1, p]
            tile[p, 3, 0:128] = right_corner[0, p]
            tile[p, 3, 128:384] = right[p]
            tile[p, 3, 384:512] = right_corner[1, p]
            for b in range(2):
                span = slice(b * HALF, (b + 1) * HALF)
                tile[p, 1 + b, 0:128] = up[p, :, span]
                tile[p, 1 + b, 128:384] = own[p, :, span]
                tile[p, 1 + b, 384:512] = down[p, :, span]
            tile[p, 4] = jnp.zeros((2 * SIZE, HALF), F32)
        grad[...] = jnp.zeros_like(grad)
        totals[...] = jnp.zeros_like(totals)
        sums[...] = jnp.zeros_like(sums)
        patch[:, :, 0:8, :] = jnp.zeros((2, 2, 8, HALF), F32)
        patch[:, :, 264:272, :] = jnp.zeros((2, 2, 8, HALF), F32)

    row, col = starts[step, 0], starts[step, 1]
    base, shift = col // HALF, lax.rem(col, HALF)

    for i in range(0, SIZE, CHUNK):
        part = pl.ds(i, CHUNK)
        where = pl.ds(row + i, CHUNK)
        obj = []
        for p in range(2):
            blocks = [tile[p, base + b, where, :] for b in range(3)]
            obj.append(gather_lanes(blocks, shift, lanes))
            for b in range(2):
                patch[p, b, pl.ds(8 + i, CHUNK), :] = obj[p][b]
        for m in range(modes):
            wave = []
            for b in range(2):
                span = slice(b * HALF, (b + 1) * HALF)
                pr, pi = probe[m, 0, part, span], probe[m, 1, part, span]
                wave.append((pr * obj[0][b] - pi * obj[1][b], pr * obj[1][b] + pi * obj[0][b]))
            for odd in range(2):
                sign = 1.0 - 2.0 * odd
                for p in range(2):
                    high, low = split2(wave[0][p] + sign * wave[1][p])
                    at = pl.ds(m * SIZE + i, CHUNK)
                    xs[odd, at, p * HALF : (p + 1) * HALF] = high
                    xs[odd, at, SIZE + p * HALF : SIZE + (p + 1) * HALF] = low
                    xs[odd, at, 2 * SIZE + p * HALF : 2 * SIZE + (p + 1) * HALF] = high

    for odd in range(2):
        ys[odd] = dot(xs[odd], right_f[odd])

    for m in range(modes):
        for odd in range(2):
            lane_span = slice(odd * HALF, (odd + 1) * HALF)
            for i in range(0, HALF, CHUNK):
                top = ys[odd, pl.ds(m * SIZE + i, CHUNK), :]
                bottom = ys[odd, pl.ds(m * SIZE + HALF + i, CHUNK), :]
                for odd_row in range(2):
                    high, low = split2(top + bottom if odd_row == 0 else top - bottom)
                    for p in range(2):
                        span = slice(p * HALF, (p + 1) * HALF)
                        at = p * HALF + i
                        zs[m, odd_row, pl.ds(at, CHUNK), lane_span] = high[:, span]
                        zs[m, odd_row, pl.ds(SIZE + at, CHUNK), lane_span] = high[:, span]
                        zs[m, odd_row, pl.ds(2 * SIZE + at, CHUNK), lane_span] = low[:, span]

    error = jnp.zeros((8, HALF), F32)
    energy = jnp.zeros((8, HALF), F32)
    for odd_row in range(2):
        far = [dot(left_f[odd_row], zs[m, odd_row]) for m in range(modes)]
        for i in range(0, HALF, CHUNK):
            parts = [(f[i : i + CHUNK], f[HALF + i : HALF + i + CHUNK]) for f in far]
            intensity = parts[0][0] ** 2 + parts[0][1] ** 2 + (parts[1][0] ** 2 + parts[1][1] ** 2)
            intensity = jnp.maximum(intensity, intensity_floor)
            inverse = lax.rsqrt(intensity)
            modulus = intensity * inverse
            amplitude = measured[0, pl.ds(odd_row * HALF + i, CHUNK), :]
            factor = 1.0 - amplitude * inverse
            misfit = (modulus - amplitude) ** 2
            strength = amplitude**2
            error = error + fold8(misfit[:, :HALF]) + fold8(misfit[:, HALF:])
            energy = energy + fold8(strength[:, :HALF]) + fold8(strength[:, HALF:])
            for m in range(modes):
                for p in range(2):
                    high, low = split2(parts[m][p] * factor)
                    at = p * HALF + i
                    gs[m, odd_row, pl.ds(at, CHUNK), :] = high
                    gs[m, odd_row, pl.ds(SIZE + at, CHUNK), :] = high
                    gs[m, odd_row, pl.ds(2 * SIZE + at, CHUNK), :] = low
    sums[0] += error
    sums[1] += energy

    for m in range(modes):
        even = dot(left_i[0], gs[m, 0])
        odds = dot(left_i[1], gs[m, 1])
        for i in range(0, HALF, CHUNK):
            for p in range(2):
                a, b = even[p * HALF + i : p * HALF + i + CHUNK], odds[p * HALF + i : p * HALF + i + CHUNK]
                for bottom in range(2):
                    high, low = split2(a - b if bottom else a + b)
                    at = pl.ds(m * SIZE + bottom * HALF + i, CHUNK)
                    for odd in range(2):
                        span = slice(odd * HALF, (odd + 1) * HALF)
                        xs[odd, at, p * HALF : (p + 1) * HALF] = high[:, span]
                        xs[odd, at, SIZE + p * HALF : SIZE + (p + 1) * HALF] = low[:, span]
                        xs[odd, at, 2 * SIZE + p * HALF : 2 * SIZE + (p + 1) * HALF] = high[:, span]

    for odd in range(2):
        back[odd] = dot(xs[odd], right_i[odd])

    parts = [jnp.zeros((8, HALF), F32) for _ in range(4)]
    for i in range(0, SIZE, CHUNK):
        part = pl.ds(i, CHUNK)
        obj = [[patch[p, b, pl.ds(8 + i, CHUNK), :] for b in range(2)] for p in range(2)]
        grads = [[0.0, 0.0], [0.0, 0.0]]
        for m in range(modes):
            at = pl.ds(m * SIZE + i, CHUNK)
            for b in range(2):
                span = slice(b * HALF, (b + 1) * HALF)
                br, bi = [
                    back[0, at, p * HALF : (p + 1) * HALF] + (1.0 - 2.0 * b) * back[1, at, p * HALF : (p + 1) * HALF]
                    for p in range(2)
                ]
                pr, pi = probe[m, 0, part, span], probe[m, 1, part, span]
                grads[0][b] = grads[0][b] + (pr * br + pi * bi)
                grads[1][b] = grads[1][b] + (pr * bi - pi * br)
                totals[b, 2 * m, part, :] += obj[0][b] * br + obj[1][b] * bi
                totals[b, 2 * m + 1, part, :] += obj[0][b] * bi - obj[1][b] * br
        for b in range(2):
            totals[b, 4, part, :] += obj[0][b] ** 2 + obj[1][b] ** 2
        where = pl.ds(row + i, CHUNK)
        for p in range(2):
            moved = spread(grads[p][0], grads[p][1], shift, lanes)
            for b in range(3):
                grad[p, base + b, where, :] += moved[b]
        first, last = lanes == 0, lanes == HALF - 1
        slopes = [[None, None], [None, None]]
        for p in range(2):
            before = [pltpu.roll(obj[p][b], 1, 1) for b in range(2)]
            after = [pltpu.roll(obj[p][b], HALF - 1, 1) for b in range(2)]
            slopes[p][0] = jnp.where(last, after[1], after[0]) - jnp.where(first, 0.0, before[0])
            slopes[p][1] = jnp.where(last, 0.0, after[1]) - jnp.where(first, before[0], before[1])
        for b in range(2):
            strength = power[part, b * HALF : (b + 1) * HALF]
            rows = [
                patch[p, b, pl.ds(9 + i, CHUNK), :] - patch[p, b, pl.ds(7 + i, CHUNK), :] for p in range(2)
            ]
            for d, slope in enumerate((rows, [slopes[0][b], slopes[1][b]])):
                parts[2 * d] = parts[2 * d] + fold8(grads[0][b] * slope[0] + grads[1][b] * slope[1])
                parts[2 * d + 1] = parts[2 * d + 1] + fold8(strength * (slope[0] ** 2 + slope[1] ** 2))

    for d in range(2):
        numerator = 0.5 * jnp.sum(parts[2 * d], keepdims=True)
        denominator = 0.25 * jnp.sum(parts[2 * d + 1], keepdims=True) + small_value
        steps[pl.ds(2 * step + d, 1), :] = jnp.broadcast_to(-numerator / denominator, (1, HALF))

    @pl.when(step == pl.num_programs(0) - 1)
    def _():
        for p in range(2):
            grad_left[p] = grad[p, 0]
            grad_right[p] = grad[p, 3]
            grad_center[p, :, :HALF] = grad[p, 1]
            grad_center[p, :, HALF:] = grad[p, 2]
        k = core[0]
        scalar = jnp.where(
            lax.broadcasted_iota(jnp.int32, (1, 4, HALF), 2) == 0,
            jnp.sum(sums[0]),
            jnp.sum(sums[1]),
        )
        for out, block in ((keep, k), (send, 1 - k)):
            for c in range(5):
                out[:, 4 * c : 4 * c + 4, :] = totals[block, c].reshape(64, 4, HALF)
            out[:, 20:24, :] = jnp.broadcast_to(scalar, (64, 4, HALF))


def whole(*shape):
    return pl.BlockSpec(shape, lambda *_: (0,) * len(shape))


def prepare(starts, probe, measured):
    count = measured.shape[0]
    cols, rows = permutation()
    shapes = [(2 * SIZE, SIZE), (2 * SIZE, HALF), (2 * SIZE, HALF), (count, SIZE, SIZE), (SIZE, SIZE)]
    return pl.pallas_call(
        prepare_kernel,
        out_shape=[jax.ShapeDtypeStruct(s, F32) for s in shapes],
        grid_spec=pltpu.PrefetchScalarGridSpec(
            num_scalar_prefetch=1,
            grid=(),
            in_specs=[whole(*x.shape) for x in (probe, measured, cols, rows)],
            out_specs=[whole(*s) for s in shapes],
            scratch_shapes=[pltpu.VMEM((5, 2 * SIZE, HALF), F32)],
        ),
        compiler_params=pltpu.CompilerParams(vmem_limit_bytes=VMEM_LIMIT),
        cost_estimate=pl.CostEstimate(flops=1 << 30, bytes_accessed=5 << 20, transcendentals=0),
    )(starts, probe, measured, jnp.asarray(cols), jnp.asarray(rows))


def compute(starts, core, own, halo, probe, power, measured):
    mats = [jnp.asarray(x) for x in constants()]
    arrays = [own, *halo, probe, power]
    count = measured.shape[0]
    shapes = [
        (2, 2 * SIZE, SIZE), (2, 2 * SIZE, HALF), (2, 2 * SIZE, HALF), (64, 24, HALF), (64, 24, HALF), (2 * count, HALF),
    ]
    return pl.pallas_call(
        main_kernel,
        out_shape=[jax.ShapeDtypeStruct(s, F32) for s in shapes],
        grid_spec=pltpu.PrefetchScalarGridSpec(
            num_scalar_prefetch=2,
            grid=(count,),
            in_specs=[whole(*x.shape) for x in arrays]
            + [pl.BlockSpec((1, SIZE, SIZE), lambda i, *_: (i, 0, 0))]
            + [whole(*x.shape) for x in mats],
            out_specs=[whole(*s) for s in shapes],
            scratch_shapes=[
                pltpu.VMEM((2, 5, 2 * SIZE, HALF), F32),
                pltpu.VMEM((2, 2, SIZE + 16, HALF), F32),
                pltpu.VMEM((2, 5, 2 * SIZE, HALF), F32),
                pltpu.VMEM((2, 5, SIZE, HALF), F32),
                pltpu.VMEM((2, 2 * SIZE, 3 * SIZE), BF),
                pltpu.VMEM((2, 2, 3 * SIZE, SIZE), BF),
                pltpu.VMEM((2, 2, 3 * SIZE, SIZE), BF),
                pltpu.VMEM((2, 2 * SIZE, SIZE), F32),
                pltpu.VMEM((2, 2 * SIZE, SIZE), F32),
                pltpu.VMEM((2, 8, HALF), F32),
            ],
        ),
        compiler_params=pltpu.CompilerParams(vmem_limit_bytes=VMEM_LIMIT),
        cost_estimate=pl.CostEstimate(flops=13 << 30, bytes_accessed=8 << 20, transcendentals=1 << 18),
    )(starts, core, *arrays, measured, *mats)


def neighbours(axis):
    up = [(i, i + 1) for i in range(lax.axis_size(axis) - 1)]
    return up, [(j, i) for i, j in up]


def local(object_tile, probe, amplitudes, offsets):
    starts = offsets[0, 0]
    measured = amplitudes[0, 0]
    row_up, row_down = neighbours("row")
    col_up, col_down = neighbours("col")
    col_index = lax.axis_index("col")
    core = lax.rem(col_index, 2)

    with jax.named_scope("object_halo"):
        up = lax.ppermute(object_tile[:, HALF:], "row", row_up)
        down = lax.ppermute(object_tile[:, :HALF], "row", row_down)
        left = lax.ppermute(object_tile[:, :, HALF:], "col", col_up)
        right = lax.ppermute(object_tile[:, :, :HALF], "col", col_down)
    center, light_left, light_right, permuted, power = prepare(starts, probe, measured)
    with jax.named_scope("object_corners"):
        left_corner = lax.ppermute(jnp.stack([up[:, :, HALF:], down[:, :, HALF:]]), "col", col_up)
        right_corner = lax.ppermute(jnp.stack([up[:, :, :HALF], down[:, :, :HALF]]), "col", col_down)

    halo = [up, down, left, right, left_corner, right_corner]
    grad_center, grad_left, grad_right, keep, send, steps = compute(
        starts, core.reshape(1), object_tile, halo, probe, power, permuted
    )

    with jax.named_scope("gradient_columns"):
        strip_left = jnp.concatenate([grad_left, light_left[None]], 0)
        strip_right = jnp.concatenate([grad_right, light_right[None]], 0)
        from_left = lax.ppermute(strip_right, "col", col_up)
        from_right = lax.ppermute(strip_left, "col", col_down)

    with jax.named_scope("probe_reduce"):
        devices = lax.axis_size("row") * lax.axis_size("col")
        partners = [(i, i ^ 1) for i in range(devices)]
        groups = [[i for i in range(devices) if i % 2 == k] for k in range(2)]
        chunk = keep + lax.ppermute(send, AXES, partners)
        chunk = lax.all_to_all(chunk, AXES, 0, 0, axis_index_groups=groups, tiled=True)
        total = jnp.sum(chunk, axis=0)
        quotient = total[:16].reshape(4, 4, HALF) / total[16:20]
        relative_error = (total[20, 0] / total[20, 1]).reshape(1)

    with jax.named_scope("gradient_rows"):
        fields = jnp.concatenate([grad_center, center[None]], 0)
        fields = fields + jnp.concatenate([from_left, from_right], 2)
        from_above = lax.ppermute(fields[:, SIZE + HALF :], "row", row_up)
        from_below = lax.ppermute(fields[:, :HALF], "row", row_down)

    with jax.named_scope("probe_gather"):
        spread_out = jnp.broadcast_to(quotient.reshape(1, 16, HALF), (devices // 2, 16, HALF))
        gathered = lax.all_to_all(spread_out, AXES, 0, 0, axis_index_groups=groups, tiled=True)
        other = lax.ppermute(gathered, AXES, partners)
        first = jnp.where(core == 0, gathered, other)
        second = jnp.where(core == 0, other, gathered)
        both = jnp.stack([first, second], 0).reshape(2, 64, 4, 4, HALF)
        probe_update = both.transpose(2, 1, 3, 0, 4).reshape(2, 2, SIZE, SIZE)

    with jax.named_scope("object_update"):
        combined = fields[:, HALF : HALF + SIZE] + jnp.concatenate([from_above, from_below], 1)
        object_update = combined[:2] / (combined[2:] + object_damping)

    position_step = steps[:, 0].reshape(1, 1, -1, 2)
    return (object_update, probe_update, position_step, relative_error)


def solution(mesh):
    in_specs = (
        P(None, "row", "col"),
        P(),
        P("row", "col", None, None, None),
        P("row", "col", None, None),
    )
    out_specs = (P(None, "row", "col"), P(), P("row", "col", None, None), P())
    return jax.shard_map(local, mesh=mesh, in_specs=in_specs, out_specs=out_specs, check_vma=False)
```

```python
import jax
import jax.numpy as jnp
import ml_dtypes
import numpy as np
from jax import lax
from jax.experimental import pallas as pl
from jax.experimental.pallas import tpu as pltpu
from jax.sharding import PartitionSpec as P

intensity_floor = 0.1
object_damping = 1.0
small_value = 1e-06

SIZE = 256
HALF = 128
CHUNK = 32
UNIT = 88
BF = jnp.bfloat16
F32 = jnp.float32
AXES = ("row", "col")
VMEM_LIMIT = 56 * 2**20


def transform_matrices():
    n = np.arange(HALF)[:, None]
    q = np.arange(HALF)[None, :]
    out = []
    for odd in (0, 1):
        angle = -2.0 * np.pi * ((n * (2 * q + odd)) % SIZE) / SIZE
        re, im = np.cos(angle) / 16.0, np.sin(angle) / 16.0
        out.append(np.block([[re, im], [-im, re]]))
    return out


def split_np(matrix):
    high = matrix.astype(ml_dtypes.bfloat16)
    low = (matrix - high.astype(np.float64)).astype(ml_dtypes.bfloat16)
    return high, low


def constants():
    right_f, left_f, right_i, left_i = [], [], [], []
    for matrix in transform_matrices():
        high, low = split_np(matrix)
        right_f.append(np.concatenate([high, high, low], 0))
        left_f.append(np.concatenate([high.T, low.T, high.T], 1))
        right_i.append(np.concatenate([high.T, high.T, low.T], 0))
        left_i.append(np.concatenate([high, low, high], 1))
    return [np.stack(x) for x in (right_f, left_f, right_i, left_i)]


def permutation():
    order = np.concatenate([np.arange(0, SIZE, 2), np.arange(1, SIZE, 2)])
    onehot = np.zeros((SIZE, SIZE), np.float32)
    onehot[order, np.arange(SIZE)] = 1.0
    columns = np.concatenate([onehot] * 3, 0).astype(ml_dtypes.bfloat16)
    rows = np.concatenate([onehot.T] * 3, 1).astype(ml_dtypes.bfloat16)
    return columns, rows


def split2(value):
    high = value.astype(BF)
    return high, (value - high.astype(F32)).astype(BF)


def split3(value):
    high = value.astype(BF)
    rest = value - high.astype(F32)
    middle = rest.astype(BF)
    return high, middle, (rest - middle.astype(F32)).astype(BF)


def dot(a, b):
    return jnp.dot(a, b, preferred_element_type=F32)


def lane_index(rows):
    return lax.broadcasted_iota(jnp.int32, (rows, HALF), 1)


def spread(first, second, shift, lanes):
    a = pltpu.roll(first, shift, 1)
    b = pltpu.roll(second, shift, 1)
    wrapped = lanes < shift
    return jnp.where(wrapped, 0.0, a), jnp.where(wrapped, a, b), jnp.where(wrapped, b, 0.0)


def gather_lanes(blocks, shift, lanes):
    back = jnp.where(shift == 0, 0, HALF - shift)
    a, b, c = [pltpu.roll(x, back, 1) for x in blocks]
    inside = lanes < HALF - shift
    return jnp.where(inside, a, b), jnp.where(inside, b, c)


def fold8(value):
    return jnp.sum(value.reshape(-1, 8, HALF), axis=0)


def prepare_kernel(measured, cols, rows, permuted):
    for j in range(measured.shape[0]):
        moved = dot(jnp.concatenate(split3(measured[j]), 1), cols[...])
        permuted[j] = dot(rows[...], jnp.concatenate(split3(moved), 0))


def transform_kernel(
    starts, place, own, up, down, left, right, up_corner, down_corner, probe, measured,
    right_f, left_f, right_i, left_i,
    keep, send, object_part, patch,
    tile, totals, xs, zs, gs, ys, back, sums,
):
    step = pl.program_id(0)
    modes = probe.shape[0]
    lanes = lane_index(CHUNK)

    @pl.when(step == 0)
    def _():
        for p in range(2):
            for side, (strip, at) in enumerate(((left, 0), (right, 3))):
                tile[p, at, 0:128] = up_corner[side, p]
                tile[p, at, 128:384] = strip[p]
                tile[p, at, 384:512] = down_corner[side, p]
            for b in range(2):
                span = slice(b * HALF, (b + 1) * HALF)
                tile[p, 1 + b, 0:128] = up[p, :, span]
                tile[p, 1 + b, 128:384] = own[p, :, span]
                tile[p, 1 + b, 384:512] = down[p, :, span]
            tile[p, 4] = jnp.zeros((2 * SIZE, HALF), F32)
        totals[...] = jnp.zeros_like(totals)
        sums[...] = jnp.zeros_like(sums)

    row, col = starts[step, 0], starts[step, 1]
    base, shift = col // HALF, lax.rem(col, HALF)

    for i in range(0, SIZE, CHUNK):
        part = pl.ds(i, CHUNK)
        where = pl.ds(row + i, CHUNK)
        obj = []
        for p in range(2):
            blocks = [tile[p, base + b, where, :] for b in range(3)]
            obj.append(gather_lanes(blocks, shift, lanes))
            for b in range(2):
                patch[0, p, b, part, :] = obj[p][b]
        for m in range(modes):
            wave = []
            for b in range(2):
                span = slice(b * HALF, (b + 1) * HALF)
                pr, pi = probe[m, 0, part, span], probe[m, 1, part, span]
                wave.append((pr * obj[0][b] - pi * obj[1][b], pr * obj[1][b] + pi * obj[0][b]))
            for odd in range(2):
                for p in range(2):
                    high, low = split2(wave[0][p] - wave[1][p] if odd else wave[0][p] + wave[1][p])
                    at = pl.ds(m * SIZE + i, CHUNK)
                    xs[odd, at, p * HALF : (p + 1) * HALF] = high
                    xs[odd, at, SIZE + p * HALF : SIZE + (p + 1) * HALF] = low
                    xs[odd, at, 2 * SIZE + p * HALF : 2 * SIZE + (p + 1) * HALF] = high

    for odd in range(2):
        ys[odd] = dot(xs[odd], right_f[odd])

    for m in range(modes):
        for odd in range(2):
            lane_span = slice(odd * HALF, (odd + 1) * HALF)
            for i in range(0, HALF, CHUNK):
                top = ys[odd, pl.ds(m * SIZE + i, CHUNK), :]
                bottom = ys[odd, pl.ds(m * SIZE + HALF + i, CHUNK), :]
                for odd_row in range(2):
                    high, low = split2(top - bottom if odd_row else top + bottom)
                    for p in range(2):
                        span = slice(p * HALF, (p + 1) * HALF)
                        at = p * HALF + i
                        zs[m, odd_row, pl.ds(at, CHUNK), lane_span] = high[:, span]
                        zs[m, odd_row, pl.ds(SIZE + at, CHUNK), lane_span] = high[:, span]
                        zs[m, odd_row, pl.ds(2 * SIZE + at, CHUNK), lane_span] = low[:, span]

    error = jnp.zeros((8, HALF), F32)
    energy = jnp.zeros((8, HALF), F32)
    for odd_row in range(2):
        far = [dot(left_f[odd_row], zs[m, odd_row]) for m in range(modes)]
        for i in range(0, HALF, CHUNK):
            parts = [(f[i : i + CHUNK], f[HALF + i : HALF + i + CHUNK]) for f in far]
            intensity = parts[0][0] ** 2 + parts[0][1] ** 2 + (parts[1][0] ** 2 + parts[1][1] ** 2)
            intensity = jnp.maximum(intensity, intensity_floor)
            inverse = lax.rsqrt(intensity)
            modulus = intensity * inverse
            amplitude = measured[0, pl.ds(odd_row * HALF + i, CHUNK), :]
            factor = 1.0 - amplitude * inverse
            misfit = (modulus - amplitude) ** 2
            strength = amplitude**2
            error = error + fold8(misfit[:, :HALF]) + fold8(misfit[:, HALF:])
            energy = energy + fold8(strength[:, :HALF]) + fold8(strength[:, HALF:])
            for m in range(modes):
                for p in range(2):
                    high, low = split2(parts[m][p] * factor)
                    at = p * HALF + i
                    gs[m, odd_row, pl.ds(at, CHUNK), :] = high
                    gs[m, odd_row, pl.ds(SIZE + at, CHUNK), :] = high
                    gs[m, odd_row, pl.ds(2 * SIZE + at, CHUNK), :] = low
    sums[0] += error
    sums[1] += energy

    for m in range(modes):
        even = dot(left_i[0], gs[m, 0])
        odds = dot(left_i[1], gs[m, 1])
        for i in range(0, HALF, CHUNK):
            for p in range(2):
                a, b = even[p * HALF + i : p * HALF + i + CHUNK], odds[p * HALF + i : p * HALF + i + CHUNK]
                for bottom in range(2):
                    high, low = split2(a - b if bottom else a + b)
                    at = pl.ds(m * SIZE + bottom * HALF + i, CHUNK)
                    for odd in range(2):
                        span = slice(odd * HALF, (odd + 1) * HALF)
                        xs[odd, at, p * HALF : (p + 1) * HALF] = high[:, span]
                        xs[odd, at, SIZE + p * HALF : SIZE + (p + 1) * HALF] = low[:, span]
                        xs[odd, at, 2 * SIZE + p * HALF : 2 * SIZE + (p + 1) * HALF] = high[:, span]

    for odd in range(2):
        back[odd] = dot(xs[odd], right_i[odd])

    for i in range(0, SIZE, CHUNK):
        part = pl.ds(i, CHUNK)
        for b in range(2):
            re, im = patch[0, 0, b, part, :], patch[0, 1, b, part, :]
            span = slice(b * HALF, (b + 1) * HALF)
            grad_re, grad_im = 0.0, 0.0
            for m in range(modes):
                at = pl.ds(m * SIZE + i, CHUNK)
                even = [back[0, at, p * HALF : (p + 1) * HALF] for p in range(2)]
                odds = [back[1, at, p * HALF : (p + 1) * HALF] for p in range(2)]
                br, bi = [x - y if b else x + y for x, y in zip(even, odds)]
                pr, pi = probe[m, 0, part, span], probe[m, 1, part, span]
                grad_re = grad_re + (pr * br + pi * bi)
                grad_im = grad_im + (pr * bi - pi * br)
                totals[b, 2 * m, part, :] += re * br + im * bi
                totals[b, 2 * m + 1, part, :] += re * bi - im * br
            object_part[0, 0, b, part, :] = grad_re
            object_part[0, 1, b, part, :] = grad_im
            totals[b, 4, part, :] += re**2 + im**2

    @pl.when(step == pl.num_programs(0) - 1)
    def _():
        core, x, y = place[0], place[1], place[2]
        scalar = jnp.where(lax.broadcasted_iota(jnp.int32, (8, HALF), 1) == 0, jnp.sum(sums[0]), jnp.sum(sums[1]))
        for out, block in ((keep, core), (send, 1 - core)):
            for ry in range(4):
                for rx in range(4):
                    unit = 4 * lax.rem(y + ry, 4) + lax.rem(x + rx, 4)
                    at = UNIT * (4 * ry + rx)
                    for c in range(5):
                        source = pl.ds(pl.multiple_of(16 * unit, 16), 16)
                        out[at + 16 * c : at + 16 * c + 16, :] = totals[block, c, source, :]
                    out[at + 80 : at + 88, :] = scalar


def place_kernel(starts, object_part, patch, probe, center, left, right, steps, padded, power, accum):
    step = pl.program_id(0)
    lanes = lane_index(CHUNK)

    @pl.when(step == 0)
    def _():
        accum[...] = jnp.zeros_like(accum)
        padded[:, :, 0:8, :] = jnp.zeros((2, 2, 8, HALF), F32)
        padded[:, :, 264:272, :] = jnp.zeros((2, 2, 8, HALF), F32)
        for i in range(0, SIZE, CHUNK):
            part = pl.ds(i, CHUNK)
            total = probe[0, 0, part] ** 2 + probe[0, 1, part] ** 2
            power[part] = total + probe[1, 0, part] ** 2 + probe[1, 1, part] ** 2

    row, col = starts[step, 0], starts[step, 1]
    base, shift = col // HALF, lax.rem(col, HALF)
    for p in range(2):
        for b in range(2):
            padded[p, b, 8:264] = patch[0, p, b]

    first, last = lanes == 0, lanes == HALF - 1
    parts = [jnp.zeros((8, HALF), F32) for _ in range(4)]
    for i in range(0, SIZE, CHUNK):
        part = pl.ds(i, CHUNK)
        where = pl.ds(row + i, CHUNK)
        grads = [[object_part[0, p, b, part, :] for b in range(2)] for p in range(2)]
        strength = [power[part, :HALF], power[part, HALF:]]
        for p, pair in enumerate(grads + [strength]):
            moved = spread(pair[0], pair[1], shift, lanes)
            for b in range(3):
                accum[p, base + b, where, :] += moved[b]
        columns = []
        for p in range(2):
            obj = [patch[0, p, b, part, :] for b in range(2)]
            before = [pltpu.roll(x, 1, 1) for x in obj]
            after = [pltpu.roll(x, HALF - 1, 1) for x in obj]
            columns.append(
                (
                    jnp.where(last, after[1], after[0]) - jnp.where(first, 0.0, before[0]),
                    jnp.where(last, 0.0, after[1]) - jnp.where(first, before[0], before[1]),
                )
            )
        for b in range(2):
            rows = [padded[p, b, pl.ds(9 + i, CHUNK), :] - padded[p, b, pl.ds(7 + i, CHUNK), :] for p in range(2)]
            for d, slope in enumerate((rows, [columns[0][b], columns[1][b]])):
                parts[2 * d] = parts[2 * d] + fold8(grads[0][b] * slope[0] + grads[1][b] * slope[1])
                parts[2 * d + 1] = parts[2 * d + 1] + fold8(strength[b] * (slope[0] ** 2 + slope[1] ** 2))

    for d in range(2):
        numerator = 0.5 * jnp.sum(parts[2 * d], keepdims=True)
        denominator = 0.25 * jnp.sum(parts[2 * d + 1], keepdims=True) + small_value
        steps[pl.ds(2 * step + d, 1), :] = jnp.broadcast_to(-numerator / denominator, (1, HALF))

    @pl.when(step == pl.num_programs(0) - 1)
    def _():
        for p in range(3):
            left[p] = accum[p, 0]
            right[p] = accum[p, 3]
            center[p, :, :HALF] = accum[p, 1]
            center[p, :, HALF:] = accum[p, 2]


def assemble_kernel(place, mine, other, out):
    core, x, y = place[0], place[1], place[2]

    def write(source, block):
        for sy in range(4):
            for sx in range(4):
                unit = 4 * lax.rem(y + 4 - sy, 4) + lax.rem(x + 4 - sx, 4)
                target = pl.ds(pl.multiple_of(16 * unit, 16), 16)
                for c in range(4):
                    at = 64 * (4 * sy + sx) + 16 * c
                    out[c, target, block * HALF : (block + 1) * HALF] = source[at : at + 16, :]

    @pl.when(core == 0)
    def _():
        write(mine, 0)
        write(other, 1)

    @pl.when(core == 1)
    def _():
        write(mine, 1)
        write(other, 0)


def whole(*shape):
    return pl.BlockSpec(shape, lambda *_: (0,) * len(shape))


def stepped(*shape):
    return pl.BlockSpec((1, *shape), lambda i, *_: (i,) + (0,) * len(shape))


def shaped(shapes):
    return [jax.ShapeDtypeStruct(s, F32) for s in shapes]


def params():
    return pltpu.CompilerParams(vmem_limit_bytes=VMEM_LIMIT)


def cost(flops, size):
    return pl.CostEstimate(flops=flops, bytes_accessed=size, transcendentals=0)


def prepare(measured):
    cols, rows = permutation()
    return pl.pallas_call(
        prepare_kernel,
        out_shape=jax.ShapeDtypeStruct(measured.shape, F32),
        compiler_params=params(),
        cost_estimate=cost(1 << 30, 3 << 20),
    )(measured, jnp.asarray(cols), jnp.asarray(rows))


def transforms(starts, place, own, halo, probe, measured):
    mats = [jnp.asarray(x) for x in constants()]
    arrays = [own, *halo, probe]
    count = measured.shape[0]
    halves = (16 * UNIT, HALF)
    fields = (2, 2, SIZE, HALF)
    return pl.pallas_call(
        transform_kernel,
        out_shape=shaped([halves, halves, (count, *fields), (count, *fields)]),
        grid_spec=pltpu.PrefetchScalarGridSpec(
            num_scalar_prefetch=2,
            grid=(count,),
            in_specs=[whole(*x.shape) for x in arrays] + [stepped(SIZE, SIZE)] + [whole(*x.shape) for x in mats],
            out_specs=[whole(*halves), whole(*halves), stepped(*fields), stepped(*fields)],
            scratch_shapes=[
                pltpu.VMEM((2, 5, 2 * SIZE, HALF), F32),
                pltpu.VMEM((2, 5, SIZE, HALF), F32),
                pltpu.VMEM((2, 2 * SIZE, 3 * SIZE), BF),
                pltpu.VMEM((2, 2, 3 * SIZE, SIZE), BF),
                pltpu.VMEM((2, 2, 3 * SIZE, SIZE), BF),
                pltpu.VMEM((2, 2 * SIZE, SIZE), F32),
                pltpu.VMEM((2, 2 * SIZE, SIZE), F32),
                pltpu.VMEM((2, 8, HALF), F32),
            ],
        ),
        compiler_params=params(),
        cost_estimate=cost(13 << 30, 12 << 20),
    )(starts, place, *arrays, measured, *mats)


def place_parts(starts, object_part, patch, probe):
    count = patch.shape[0]
    fields = (2, 2, SIZE, HALF)
    shapes = [(3, 2 * SIZE, SIZE), (3, 2 * SIZE, HALF), (3, 2 * SIZE, HALF), (2 * count, HALF)]
    return pl.pallas_call(
        place_kernel,
        out_shape=shaped(shapes),
        grid_spec=pltpu.PrefetchScalarGridSpec(
            num_scalar_prefetch=1,
            grid=(count,),
            in_specs=[stepped(*fields), stepped(*fields), whole(*probe.shape)],
            out_specs=[whole(*s) for s in shapes],
            scratch_shapes=[
                pltpu.VMEM((2, 2, SIZE + 16, HALF), F32),
                pltpu.VMEM((SIZE, SIZE), F32),
                pltpu.VMEM((3, 5, 2 * SIZE, HALF), F32),
            ],
        ),
        compiler_params=params(),
        cost_estimate=cost(5 << 30, 8 << 20),
    )(starts, object_part, patch, probe)


def assemble(place, mine, other):
    shape = (4, SIZE, SIZE)
    return pl.pallas_call(
        assemble_kernel,
        out_shape=jax.ShapeDtypeStruct(shape, F32),
        grid_spec=pltpu.PrefetchScalarGridSpec(
            num_scalar_prefetch=1,
            grid=(),
            in_specs=[whole(*mine.shape), whole(*other.shape)],
            out_specs=whole(*shape),
        ),
        compiler_params=params(),
        cost_estimate=cost(1 << 20, 2 << 20),
    )(place, mine, other)


def neighbours(axis):
    up = [(i, i + 1) for i in range(lax.axis_size(axis) - 1)]
    return up, [(j, i) for i, j in up]


def chips(index):
    row, col = divmod(index, 16)
    return [col // 4, row % 4, 2 * (row // 4) + col // 2 % 2, col % 2]


def device(x, y, z, core):
    return (4 * (z // 2) + y) * 16 + 4 * x + 2 * (z % 2) + core


def along(value, dim, distance):
    pairs = []
    for source in range(lax.axis_size("row") * lax.axis_size("col")):
        target = chips(source)
        target[dim] = (target[dim] + distance) % (2 if dim == 3 else 4)
        pairs.append((source, device(*target)))
    return lax.ppermute(value, AXES, pairs)


def others(pieces, dim):
    return [pieces[0]] + [along(pieces[d], dim, d) for d in (1, 2, 3)]


def total_of(values):
    return (values[0] + values[1]) + (values[2] + values[3])


def local(object_tile, probe, amplitudes, offsets):
    starts = offsets[0, 0]
    measured = amplitudes[0, 0]
    row_up, row_down = neighbours("row")
    col_up, col_down = neighbours("col")
    row_index, col_index = lax.axis_index("row"), lax.axis_index("col")
    place = jnp.stack([lax.rem(col_index, 2), lax.div(col_index, 4), lax.rem(row_index, 4)])

    with jax.named_scope("object_halo"):
        left = lax.ppermute(object_tile[:, :, HALF:], "col", col_up)
        right = lax.ppermute(object_tile[:, :, :HALF], "col", col_down)
        up = lax.ppermute(object_tile[:, HALF:], "row", row_up)
        down = lax.ppermute(object_tile[:, :HALF], "row", row_down)
    permuted = prepare(measured)
    with jax.named_scope("object_corners"):
        left, right, permuted = lax.optimization_barrier((left, right, permuted))
        up_corner = lax.ppermute(jnp.stack([left[:, HALF:], right[:, HALF:]]), "row", row_up)
        down_corner = lax.ppermute(jnp.stack([left[:, :HALF], right[:, :HALF]]), "row", row_down)

    halo = [up, down, left, right, up_corner, down_corner]
    keep, send, object_part, patch = transforms(starts, place, object_tile, halo, probe, permuted)

    with jax.named_scope("probe_reduce"):
        chunk = keep + along(send, 3, 1)
        chunk, object_part = lax.optimization_barrier((chunk, object_part))
        chunk = total_of(others(jnp.split(chunk, 4), 1))

    parts = place_parts(starts, object_part, patch, probe)
    chunk, (center, grad_left, grad_right, steps) = lax.optimization_barrier((chunk, parts))

    with jax.named_scope("gradient_columns"):
        from_left = lax.ppermute(grad_right, "col", col_up)
        from_right = lax.ppermute(grad_left, "col", col_down)

    with jax.named_scope("probe_sum"):
        chunk = total_of(others(jnp.split(chunk, 4), 0))
        chunk = total_of([chunk] + [along(chunk, 2, d) for d in (1, 2, 3)])
        quotient = (chunk[:64].reshape(4, 16, HALF) / chunk[64:80]).reshape(64, HALF)
        relative_error = (chunk[80, 0] / chunk[80, 1]).reshape(1)

    with jax.named_scope("gradient_rows"):
        fields = center + jnp.concatenate([from_left, from_right], 2)
        quotient, fields = lax.optimization_barrier((quotient, fields))
        from_above = lax.ppermute(fields[:, SIZE + HALF :], "row", row_up)
        from_below = lax.ppermute(fields[:, :HALF], "row", row_down)

    with jax.named_scope("probe_gather"):
        quotient = jnp.concatenate(others([quotient] * 4, 0))
        quotient = jnp.concatenate(others([quotient] * 4, 1))

    with jax.named_scope("object_update"):
        combined = fields[:, HALF : HALF + SIZE] + jnp.concatenate([from_above, from_below], 1)
        object_update = combined[:2] / (combined[2:] + object_damping)
        quotient, object_update = lax.optimization_barrier((quotient, object_update))

    probe_update = assemble(place, quotient, along(quotient, 3, 1)).reshape(probe.shape)
    position_step = steps[:, 0].reshape(1, 1, -1, 2)
    return (object_update, probe_update, position_step, relative_error)


def solution(mesh):
    in_specs = (
        P(None, "row", "col"),
        P(),
        P("row", "col", None, None, None),
        P("row", "col", None, None),
    )
    out_specs = (P(None, "row", "col"), P(), P("row", "col", None, None), P())
    return jax.shard_map(local, mesh=mesh, in_specs=in_specs, out_specs=out_specs, check_vma=False)
```

```python
import jax
import jax.numpy as jnp
import ml_dtypes
import numpy as np
from jax import lax
from jax.experimental import pallas as pl
from jax.experimental.pallas import tpu as pltpu
from jax.sharding import PartitionSpec as P

intensity_floor = 0.1
object_damping = 1.0
small_value = 1e-06

SIZE = 256
HALF = 128
CHUNK = 32
BF = jnp.bfloat16
F32 = jnp.float32
AXES = ("row", "col")
VMEM_LIMIT = 56 * 2**20


def transform_matrices():
    n = np.arange(HALF)[:, None]
    q = np.arange(HALF)[None, :]
    out = []
    for odd in (0, 1):
        angle = -2.0 * np.pi * ((n * (2 * q + odd)) % SIZE) / SIZE
        re, im = np.cos(angle) / 16.0, np.sin(angle) / 16.0
        out.append(np.block([[re, im], [-im, re]]))
    return out


def split_np(matrix):
    high = matrix.astype(ml_dtypes.bfloat16)
    low = (matrix - high.astype(np.float64)).astype(ml_dtypes.bfloat16)
    return high, low


def constants():
    right_f, left_f, right_i, left_i = [], [], [], []
    for matrix in transform_matrices():
        high, low = split_np(matrix)
        right_f.append(np.concatenate([high, high, low], 0))
        left_f.append(np.concatenate([high.T, low.T, high.T], 1))
        right_i.append(np.concatenate([high.T, high.T, low.T], 0))
        left_i.append(np.concatenate([high, low, high], 1))
    return [np.stack(x) for x in (right_f, left_f, right_i, left_i)]


def permutation():
    order = np.concatenate([np.arange(0, SIZE, 2), np.arange(1, SIZE, 2)])
    onehot = np.zeros((SIZE, SIZE), np.float32)
    onehot[order, np.arange(SIZE)] = 1.0
    columns = np.concatenate([onehot] * 3, 0).astype(ml_dtypes.bfloat16)
    rows = np.concatenate([onehot.T] * 3, 1).astype(ml_dtypes.bfloat16)
    return columns, rows


def split2(value):
    high = value.astype(BF)
    return high, (value - high.astype(F32)).astype(BF)


def split3(value):
    high = value.astype(BF)
    rest = value - high.astype(F32)
    middle = rest.astype(BF)
    return high, middle, (rest - middle.astype(F32)).astype(BF)


def dot(a, b):
    return jnp.dot(a, b, preferred_element_type=F32)


def lane_index(rows):
    return lax.broadcasted_iota(jnp.int32, (rows, HALF), 1)


def spread(first, second, shift, lanes):
    a = pltpu.roll(first, shift, 1)
    b = pltpu.roll(second, shift, 1)
    wrapped = lanes < shift
    return jnp.where(wrapped, 0.0, a), jnp.where(wrapped, a, b), jnp.where(wrapped, b, 0.0)


def gather_lanes(blocks, shift, lanes):
    back = jnp.where(shift == 0, 0, HALF - shift)
    a, b, c = [pltpu.roll(x, back, 1) for x in blocks]
    inside = lanes < HALF - shift
    return jnp.where(inside, a, b), jnp.where(inside, b, c)


def fold8(value):
    return jnp.sum(value.reshape(-1, 8, HALF), axis=0)


def prepare_kernel(measured, cols, rows, permuted):
    for j in range(measured.shape[0]):
        moved = dot(jnp.concatenate(split3(measured[j]), 1), cols[...])
        permuted[j] = dot(rows[...], jnp.concatenate(split3(moved), 0))


def pack_kernel(starts, place, own, even, odd, cross, same):
    row_odd, core = place[0], place[1]
    lanes = lane_index(8)
    offsets = jnp.zeros((8, HALF), F32)
    for j in range(starts.shape[0]):
        for d in range(2):
            offsets = jnp.where(lanes == 2 * j + d, (starts[j, d] + 1).astype(F32), offsets)
    at = pl.multiple_of(HALF * row_odd, HALF)
    for p in range(2):
        even[p, :HALF] = own[p, pl.ds(HALF - at, HALF), :]
        odd[p, :HALF] = own[p, pl.ds(at, HALF), :]
        for b in range(2):
            for out in (even, odd):
                out[p, HALF:, b * HALF : (b + 1) * HALF] = offsets
        for out in (cross, same):
            out[p, SIZE:] = offsets

    for k in range(2):

        @pl.when(core == k)
        def _(k=k):
            for p in range(2):
                cross[p, :SIZE] = own[p, :, k * HALF : (k + 1) * HALF]
                same[p, :SIZE] = own[p, :, (1 - k) * HALF : (2 - k) * HALF]


def sides(place):
    even_row = pl.multiple_of(3 * HALF * (1 - place[0]), HALF)
    odd_row = pl.multiple_of(3 * HALF * place[0], HALF)
    return even_row, odd_row, 3 * place[1], 3 - 3 * place[1]


def transform_kernel(
    starts, place, own, even_strip, odd_strip, cross, same, cross_corner, same_corner, probe, measured,
    right_f, left_f, right_i, left_i,
    keep, send, object_part, patch,
    tile, totals, xs, zs, gs, ys, back, sums,
):
    step = pl.program_id(0)
    modes = probe.shape[0]
    lanes = lane_index(CHUNK)

    @pl.when(step == 0)
    def _():
        even_row, odd_row, cross_block, same_block = sides(place)
        for p in range(2):
            for block, strip, corner in ((cross_block, cross, cross_corner), (same_block, same, same_corner)):
                tile[p, block, 128:384] = strip[p, :SIZE]
                tile[p, block, pl.ds(even_row, HALF)] = corner[0, p, :HALF]
                tile[p, block, pl.ds(odd_row, HALF)] = corner[1, p, :HALF]
            for b in range(2):
                span = slice(b * HALF, (b + 1) * HALF)
                tile[p, 1 + b, 128:384] = own[p, :, span]
                tile[p, 1 + b, pl.ds(even_row, HALF)] = even_strip[p, :HALF, span]
                tile[p, 1 + b, pl.ds(odd_row, HALF)] = odd_strip[p, :HALF, span]
            tile[p, 4] = jnp.zeros((2 * SIZE, HALF), F32)
        totals[...] = jnp.zeros_like(totals)
        sums[...] = jnp.zeros_like(sums)

    row, col = starts[step, 0], starts[step, 1]
    base, shift = col // HALF, lax.rem(col, HALF)

    for i in range(0, SIZE, CHUNK):
        part = pl.ds(i, CHUNK)
        where = pl.ds(row + i, CHUNK)
        obj = []
        for p in range(2):
            blocks = [tile[p, base + b, where, :] for b in range(3)]
            obj.append(gather_lanes(blocks, shift, lanes))
            for b in range(2):
                patch[0, p, b, part, :] = obj[p][b]
        for m in range(modes):
            wave = []
            for b in range(2):
                span = slice(b * HALF, (b + 1) * HALF)
                pr, pi = probe[m, 0, part, span], probe[m, 1, part, span]
                wave.append((pr * obj[0][b] - pi * obj[1][b], pr * obj[1][b] + pi * obj[0][b]))
            for odd in range(2):
                for p in range(2):
                    high, low = split2(wave[0][p] - wave[1][p] if odd else wave[0][p] + wave[1][p])
                    at = pl.ds(m * SIZE + i, CHUNK)
                    xs[odd, at, p * HALF : (p + 1) * HALF] = high
                    xs[odd, at, SIZE + p * HALF : SIZE + (p + 1) * HALF] = low
                    xs[odd, at, 2 * SIZE + p * HALF : 2 * SIZE + (p + 1) * HALF] = high

    for odd in range(2):
        ys[odd] = dot(xs[odd], right_f[odd])

    for m in range(modes):
        for odd in range(2):
            lane_span = slice(odd * HALF, (odd + 1) * HALF)
            for i in range(0, HALF, CHUNK):
                top = ys[odd, pl.ds(m * SIZE + i, CHUNK), :]
                bottom = ys[odd, pl.ds(m * SIZE + HALF + i, CHUNK), :]
                for odd_row in range(2):
                    high, low = split2(top - bottom if odd_row else top + bottom)
                    for p in range(2):
                        span = slice(p * HALF, (p + 1) * HALF)
                        at = p * HALF + i
                        zs[m, odd_row, pl.ds(at, CHUNK), lane_span] = high[:, span]
                        zs[m, odd_row, pl.ds(SIZE + at, CHUNK), lane_span] = high[:, span]
                        zs[m, odd_row, pl.ds(2 * SIZE + at, CHUNK), lane_span] = low[:, span]

    error = jnp.zeros((8, HALF), F32)
    energy = jnp.zeros((8, HALF), F32)
    for odd_row in range(2):
        far = [dot(left_f[odd_row], zs[m, odd_row]) for m in range(modes)]
        for i in range(0, HALF, CHUNK):
            parts = [(f[i : i + CHUNK], f[HALF + i : HALF + i + CHUNK]) for f in far]
            intensity = parts[0][0] ** 2 + parts[0][1] ** 2 + (parts[1][0] ** 2 + parts[1][1] ** 2)
            intensity = jnp.maximum(intensity, intensity_floor)
            inverse = lax.rsqrt(intensity)
            modulus = intensity * inverse
            amplitude = measured[0, pl.ds(odd_row * HALF + i, CHUNK), :]
            factor = 1.0 - amplitude * inverse
            misfit = (modulus - amplitude) ** 2
            strength = amplitude**2
            error = error + fold8(misfit[:, :HALF]) + fold8(misfit[:, HALF:])
            energy = energy + fold8(strength[:, :HALF]) + fold8(strength[:, HALF:])
            for m in range(modes):
                for p in range(2):
                    high, low = split2(parts[m][p] * factor)
                    at = p * HALF + i
                    gs[m, odd_row, pl.ds(at, CHUNK), :] = high
                    gs[m, odd_row, pl.ds(SIZE + at, CHUNK), :] = high
                    gs[m, odd_row, pl.ds(2 * SIZE + at, CHUNK), :] = low
    sums[0] += error
    sums[1] += energy

    for m in range(modes):
        even = dot(left_i[0], gs[m, 0])
        odds = dot(left_i[1], gs[m, 1])
        for i in range(0, HALF, CHUNK):
            for p in range(2):
                a, b = even[p * HALF + i : p * HALF + i + CHUNK], odds[p * HALF + i : p * HALF + i + CHUNK]
                for bottom in range(2):
                    high, low = split2(a - b if bottom else a + b)
                    at = pl.ds(m * SIZE + bottom * HALF + i, CHUNK)
                    for odd in range(2):
                        span = slice(odd * HALF, (odd + 1) * HALF)
                        xs[odd, at, p * HALF : (p + 1) * HALF] = high[:, span]
                        xs[odd, at, SIZE + p * HALF : SIZE + (p + 1) * HALF] = low[:, span]
                        xs[odd, at, 2 * SIZE + p * HALF : 2 * SIZE + (p + 1) * HALF] = high[:, span]

    for odd in range(2):
        back[odd] = dot(xs[odd], right_i[odd])

    for i in range(0, SIZE, CHUNK):
        part = pl.ds(i, CHUNK)
        for b in range(2):
            re, im = patch[0, 0, b, part, :], patch[0, 1, b, part, :]
            span = slice(b * HALF, (b + 1) * HALF)
            grad_re, grad_im = 0.0, 0.0
            for m in range(modes):
                at = pl.ds(m * SIZE + i, CHUNK)
                even = [back[0, at, p * HALF : (p + 1) * HALF] for p in range(2)]
                odds = [back[1, at, p * HALF : (p + 1) * HALF] for p in range(2)]
                br, bi = [x - y if b else x + y for x, y in zip(even, odds)]
                pr, pi = probe[m, 0, part, span], probe[m, 1, part, span]
                grad_re = grad_re + (pr * br + pi * bi)
                grad_im = grad_im + (pr * bi - pi * br)
                totals[b, 2 * m, part, :] += re * br + im * bi
                totals[b, 2 * m + 1, part, :] += re * bi - im * br
            object_part[0, 0, b, part, :] = grad_re
            object_part[0, 1, b, part, :] = grad_im
            totals[b, 4, part, :] += re**2 + im**2

    @pl.when(step == pl.num_programs(0) - 1)
    def _():
        core = place[1]
        scalar = jnp.where(lax.broadcasted_iota(jnp.int32, (1, 4, HALF), 2) == 0, jnp.sum(sums[0]), jnp.sum(sums[1]))
        for out, block in ((keep, core), (send, 1 - core)):
            for c in range(5):
                out[:, 4 * c : 4 * c + 4, :] = totals[block, c].reshape(64, 4, HALF)
            out[:, 20:24, :] = jnp.broadcast_to(scalar, (64, 4, HALF))


def place_kernel(
    starts, place, object_part, patch, probe,
    center, even, odd, cross, same, cross_corner, same_corner, steps,
    padded, power, accum,
):
    step = pl.program_id(0)
    lanes = lane_index(CHUNK)

    @pl.when(step == 0)
    def _():
        accum[...] = jnp.zeros_like(accum)
        padded[:, :, 0:8, :] = jnp.zeros((2, 2, 8, HALF), F32)
        padded[:, :, 264:272, :] = jnp.zeros((2, 2, 8, HALF), F32)
        for i in range(0, SIZE, CHUNK):
            part = pl.ds(i, CHUNK)
            power[part] = probe_power(probe, part)

    row, col = starts[step, 0], starts[step, 1]
    base, shift = col // HALF, lax.rem(col, HALF)
    for p in range(2):
        for b in range(2):
            padded[p, b, 8:264] = patch[0, p, b]

    first, last = lanes == 0, lanes == HALF - 1
    parts = [jnp.zeros((8, HALF), F32) for _ in range(4)]
    for i in range(0, SIZE, CHUNK):
        part = pl.ds(i, CHUNK)
        where = pl.ds(row + i, CHUNK)
        grads = [[object_part[0, p, b, part, :] for b in range(2)] for p in range(2)]
        strength = [power[part, :HALF], power[part, HALF:]]
        for p, pair in enumerate(grads):
            moved = spread(pair[0], pair[1], shift, lanes)
            for b in range(3):
                accum[p, base + b, where, :] += moved[b]
        columns = []
        for p in range(2):
            obj = [patch[0, p, b, part, :] for b in range(2)]
            before = [pltpu.roll(x, 1, 1) for x in obj]
            after = [pltpu.roll(x, HALF - 1, 1) for x in obj]
            columns.append(
                (
                    jnp.where(last, after[1], after[0]) - jnp.where(first, 0.0, before[0]),
                    jnp.where(last, 0.0, after[1]) - jnp.where(first, before[0], before[1]),
                )
            )
        for b in range(2):
            rows = [padded[p, b, pl.ds(9 + i, CHUNK), :] - padded[p, b, pl.ds(7 + i, CHUNK), :] for p in range(2)]
            for d, slope in enumerate((rows, [columns[0][b], columns[1][b]])):
                parts[2 * d] = parts[2 * d] + fold8(grads[0][b] * slope[0] + grads[1][b] * slope[1])
                parts[2 * d + 1] = parts[2 * d + 1] + fold8(strength[b] * (slope[0] ** 2 + slope[1] ** 2))

    for d in range(2):
        numerator = 0.5 * jnp.sum(parts[2 * d], keepdims=True)
        denominator = 0.25 * jnp.sum(parts[2 * d + 1], keepdims=True) + small_value
        steps[pl.ds(2 * step + d, 1), :] = jnp.broadcast_to(-numerator / denominator, (1, HALF))

    @pl.when(step == pl.num_programs(0) - 1)
    def _():
        even_row, odd_row, cross_block, same_block = sides(place)
        for p in range(2):
            for b in range(2):
                span = slice(b * HALF, (b + 1) * HALF)
                center[p, :, span] = accum[p, 1 + b, 128:384]
                even[p, :, span] = accum[p, 1 + b, pl.ds(even_row, HALF)]
                odd[p, :, span] = accum[p, 1 + b, pl.ds(odd_row, HALF)]
            for block, strip, corner in ((cross_block, cross, cross_corner), (same_block, same, same_corner)):
                strip[p] = accum[p, block, 128:384]
                corner[0, p] = accum[p, block, pl.ds(even_row, HALF)]
                corner[1, p] = accum[p, block, pl.ds(odd_row, HALF)]


def probe_power(probe, part):
    return (probe[0, 0, part] ** 2 + probe[0, 1, part] ** 2) + (probe[1, 0, part] ** 2 + probe[1, 1, part] ** 2)


def light_kernel(starts, around, place, probe, light, power, accum):
    accum[...] = jnp.zeros_like(accum)
    for i in range(0, SIZE, CHUNK):
        part = pl.ds(i, CHUNK)
        total = probe_power(probe, part)
        power[0, part] = total[:, :HALF]
        power[1, part] = total[:, HALF:]
    lanes = lane_index(CHUNK)
    even, cross = 1 - 2 * place[0], 2 * place[1] - 1
    neighbours = [(even, None), (-even, None), (None, cross), (None, -cross)]
    neighbours += [(even, cross), (-even, cross), (even, -cross), (-even, -cross)]

    def add(row, col, down, right):
        rows, source_row, row = (SIZE, 0, row + HALF) if down is None else (
            HALF, pl.multiple_of(jnp.where(down < 0, HALF, 0), HALF), row + jnp.where(down < 0, 0, 3 * HALF)
        )
        if right is None:
            col = col + HALF
        else:
            source = jnp.where(right < 0, 1, 0)
            col = col + jnp.where(right < 0, 0, 3 * HALF)
        base, shift = col // HALF, lax.rem(col, HALF)
        for i in range(0, rows, CHUNK):
            part = pl.ds(source_row + i, CHUNK)
            where = pl.ds(row + i, CHUNK)
            if right is None:
                moved = spread(power[0, part], power[1, part], shift, lanes)
            else:
                rolled = pltpu.roll(power[source, part], shift, 1)
                moved = jnp.where(lanes < shift, 0.0, rolled), jnp.where(lanes < shift, rolled, 0.0)
            for b, value in enumerate(moved):
                accum[base + b, where, :] += value

    for j in range(starts.shape[0]):
        add(starts[j, 0], starts[j, 1], None, None)
    for n, (down, right) in enumerate(neighbours):
        for j in range(starts.shape[0]):
            row, col = around[n, 2 * j] - 1, around[n, 2 * j + 1] - 1
            near = row >= 0
            if down is not None:
                near = near & jnp.where(down < 0, row > HALF, row < HALF)
            if right is not None:
                near = near & jnp.where(right < 0, col > HALF, col < HALF)

            @pl.when(near)
            def _(row=row, col=col, down=down, right=right):
                add(row, col, down, right)

    light[:, :HALF] = accum[2, 256:512]
    light[:, HALF:] = accum[3, 256:512]


def update_kernel(place, center, even, odd, cross, same, light, out, total):
    for p in range(2):
        total[p] = center[p]
    even_half = pl.ds(pl.multiple_of(HALF * (1 - place[0]), HALF), HALF)
    odd_half = pl.ds(pl.multiple_of(HALF * place[0], HALF), HALF)
    for p in range(2):
        total[p, even_half, :] += even[p]
        total[p, odd_half, :] += odd[p]
    swapped = place[1] == 1
    for i in range(0, SIZE, CHUNK):
        part = pl.ds(i, CHUNK)
        scale = 1.0 / (light[part] + object_damping)
        for p in range(2):
            a, b = cross[p, part], same[p, part]
            out[p, part, :HALF] = (total[p, part, :HALF] + jnp.where(swapped, b, a)) * scale[:, :HALF]
            out[p, part, HALF:] = (total[p, part, HALF:] + jnp.where(swapped, a, b)) * scale[:, HALF:]


def assemble_kernel(place, mine, other, out):
    def write(source, block):
        for c in range(4):
            out[c, :, block * HALF : (block + 1) * HALF] = source[:, 4 * c : 4 * c + 4, :].reshape(SIZE, HALF)

    @pl.when(place[1] == 0)
    def _():
        write(mine, 0)
        write(other, 1)

    @pl.when(place[1] == 1)
    def _():
        write(mine, 1)
        write(other, 0)


def whole(*shape):
    return pl.BlockSpec(shape, lambda *_: (0,) * len(shape))


def stepped(*shape):
    return pl.BlockSpec((1, *shape), lambda i, *_: (i,) + (0,) * len(shape))


def shaped(shapes):
    return [jax.ShapeDtypeStruct(s, F32) for s in shapes]


def params():
    return pltpu.CompilerParams(vmem_limit_bytes=VMEM_LIMIT)


def cost(flops, size):
    return pl.CostEstimate(flops=flops, bytes_accessed=size, transcendentals=0)


def simple(kernel, scalars, arrays, shapes, scratch, flops, size):
    single = not isinstance(shapes, list)
    outs = [shapes] if single else shapes
    call = pl.pallas_call(
        kernel,
        out_shape=shaped(outs)[0] if single else shaped(outs),
        grid_spec=pltpu.PrefetchScalarGridSpec(
            num_scalar_prefetch=len(scalars),
            grid=(),
            in_specs=[whole(*x.shape) for x in arrays],
            out_specs=whole(*shapes) if single else [whole(*s) for s in outs],
            scratch_shapes=[pltpu.VMEM(s, F32) for s in scratch],
        ),
        compiler_params=params(),
        cost_estimate=cost(flops, size),
    )
    return call(*scalars, *arrays)


def pack(starts, place, own):
    rows, columns = (2, HALF + 8, SIZE), (2, SIZE + 8, HALF)
    return simple(pack_kernel, [starts, place], [own], [rows, rows, columns, columns], [], 1 << 10, 2 << 20)


def prepare(measured):
    cols, rows = permutation()
    arrays = [measured, jnp.asarray(cols), jnp.asarray(rows)]
    return simple(prepare_kernel, [], arrays, measured.shape, [], 1 << 30, 3 << 20)


def transforms(starts, place, own, halo, probe, measured):
    mats = [jnp.asarray(x) for x in constants()]
    arrays = [own, *halo, probe]
    count = measured.shape[0]
    halves = (64, 24, HALF)
    fields = (2, 2, SIZE, HALF)
    return pl.pallas_call(
        transform_kernel,
        out_shape=shaped([halves, halves, (count, *fields), (count, *fields)]),
        grid_spec=pltpu.PrefetchScalarGridSpec(
            num_scalar_prefetch=2,
            grid=(count,),
            in_specs=[whole(*x.shape) for x in arrays] + [stepped(SIZE, SIZE)] + [whole(*x.shape) for x in mats],
            out_specs=[whole(*halves), whole(*halves), stepped(*fields), stepped(*fields)],
            scratch_shapes=[
                pltpu.VMEM((2, 5, 2 * SIZE, HALF), F32),
                pltpu.VMEM((2, 5, SIZE, HALF), F32),
                pltpu.VMEM((2, 2 * SIZE, 3 * SIZE), BF),
                pltpu.VMEM((2, 2, 3 * SIZE, SIZE), BF),
                pltpu.VMEM((2, 2, 3 * SIZE, SIZE), BF),
                pltpu.VMEM((2, 2 * SIZE, SIZE), F32),
                pltpu.VMEM((2, 2 * SIZE, SIZE), F32),
                pltpu.VMEM((2, 8, HALF), F32),
            ],
        ),
        compiler_params=params(),
        cost_estimate=cost(13 << 30, 12 << 20),
    )(starts, place, *arrays, measured, *mats)


def place_parts(starts, place, object_part, patch, probe):
    count = patch.shape[0]
    fields = (2, 2, SIZE, HALF)
    rows, columns, corners = (2, HALF, SIZE), (2, SIZE, HALF), (2, 2, HALF, HALF)
    shapes = [(2, SIZE, SIZE), rows, rows, columns, columns, corners, corners, (2 * count, HALF)]
    return pl.pallas_call(
        place_kernel,
        out_shape=shaped(shapes),
        grid_spec=pltpu.PrefetchScalarGridSpec(
            num_scalar_prefetch=2,
            grid=(count,),
            in_specs=[stepped(*fields), stepped(*fields), whole(*probe.shape)],
            out_specs=[whole(*s) for s in shapes],
            scratch_shapes=[
                pltpu.VMEM((2, 2, SIZE + 16, HALF), F32),
                pltpu.VMEM((SIZE, SIZE), F32),
                pltpu.VMEM((2, 5, 2 * SIZE, HALF), F32),
            ],
        ),
        compiler_params=params(),
        cost_estimate=cost(5 << 30, 8 << 20),
    )(starts, place, object_part, patch, probe)


def illuminate(starts, around, place, probe):
    scratch = [(2, SIZE, HALF), (7, 3 * SIZE, HALF)]
    return simple(light_kernel, [starts, around, place], [probe], (SIZE, SIZE), scratch, 2 << 30, 4 << 20)


def update(place, arrays):
    shape = arrays[0].shape
    return simple(update_kernel, [place], arrays, shape, [shape], 1 << 20, 3 << 20)


def assemble(place, mine, other):
    return simple(assemble_kernel, [place], [mine, other], (4, SIZE, SIZE), [], 1 << 20, 2 << 20)


def pairs_from(first, count):
    pairs = []
    for i in range(first, count - 1, 2):
        pairs += [(i, i + 1), (i + 1, i)]
    return pairs


def swap_rows(value, first):
    return lax.ppermute(value, "row", pairs_from(first, lax.axis_size("row")))


def swap_columns(value, first):
    return lax.ppermute(value, "col", pairs_from(first, lax.axis_size("col")))


def half_lanes(value, first):
    return jnp.where(first, value[..., :HALF], value[..., HALF:])


def local(object_tile, probe, amplitudes, offsets):
    starts = offsets[0, 0]
    measured = amplitudes[0, 0]
    core = lax.rem(lax.axis_index("col"), 2)
    place = jnp.stack([lax.rem(lax.axis_index("row"), 2), core])
    devices = lax.axis_size("row") * lax.axis_size("col")
    groups = [[i for i in range(devices) if i % 2 == k] for k in range(2)]

    with jax.named_scope("object_halo"):
        even, odd, cross, same = pack(starts, place, object_tile)
        even = swap_rows(even, 0)
        odd = swap_rows(odd, 1)
        cross = swap_columns(cross, 1)
        same = swap_columns(same, 0)
    permuted = prepare(measured)
    with jax.named_scope("object_corners"):
        rows, permuted = lax.optimization_barrier((jnp.stack([even, odd]), permuted))
        cross_corner = swap_columns(half_lanes(rows, core == 0), 1)
        same_corner = swap_columns(half_lanes(rows, core == 1), 0)

    halo = [even, odd, cross, same, cross_corner, same_corner]
    keep, send, object_part, patch = transforms(starts, place, object_tile, halo, probe, permuted)

    with jax.named_scope("probe_reduce"):
        chunk = keep + swap_columns(send, 0)
        around = [x[0, -8:-7, :8] for x in halo[:4]]
        around += [x[n, 0, -8:-7, :8] for x in halo[4:] for n in range(2)]
        around = jnp.concatenate(around, 0).astype(jnp.int32)
        chunk, object_part, around = lax.optimization_barrier((chunk, object_part, around))
        chunk = lax.all_to_all(chunk, AXES, 0, 0, axis_index_groups=groups, tiled=True)

    parts = place_parts(starts, place, object_part, patch, probe)
    light = illuminate(starts, around, place, probe)
    chunk, parts, light = lax.optimization_barrier((chunk, parts, light))
    center, even, odd, cross, same, cross_corner, same_corner, steps = parts

    with jax.named_scope("gradient_corners"):
        cross_corner = swap_columns(cross_corner, 1)
        same_corner = swap_columns(same_corner, 0)

    with jax.named_scope("probe_sum"):
        total = jnp.sum(chunk, axis=0)
        quotient = total[:16].reshape(4, 4, HALF) / total[16:20]
        relative_error = (total[20, 0] / total[20, 1]).reshape(1)

    with jax.named_scope("gradient_rows"):
        first = jnp.where(core == 0, cross_corner, same_corner)
        second = jnp.where(core == 0, same_corner, cross_corner)
        added = jnp.concatenate([first, second], -1)
        even = swap_rows(even + added[0], 0)
        odd = swap_rows(odd + added[1], 1)
        cross = swap_columns(cross, 1)
        same = swap_columns(same, 0)

    with jax.named_scope("probe_gather"):
        spread_out = jnp.broadcast_to(quotient.reshape(1, 16, HALF), (devices // 2, 16, HALF))
        gathered = lax.all_to_all(spread_out, AXES, 0, 0, axis_index_groups=groups, tiled=True)
        probe_update = assemble(place, gathered, swap_columns(gathered, 0)).reshape(probe.shape)

    object_update = update(place, [center, even, odd, cross, same, light])
    position_step = steps[:, 0].reshape(1, 1, -1, 2)
    return (object_update, probe_update, position_step, relative_error)


def solution(mesh):
    in_specs = (
        P(None, "row", "col"),
        P(),
        P("row", "col", None, None, None),
        P("row", "col", None, None),
    )
    out_specs = (P(None, "row", "col"), P(), P("row", "col", None, None), P())
    return jax.shard_map(local, mesh=mesh, in_specs=in_specs, out_specs=out_specs, check_vma=False)
```

```python
import jax
import jax.numpy as jnp
import ml_dtypes
import numpy as np
from jax import lax
from jax.experimental import pallas as pl
from jax.experimental.pallas import tpu as pltpu
from jax.sharding import PartitionSpec as P

intensity_floor = 0.1
object_damping = 1.0
small_value = 1e-06

SIZE = 256
HALF = 128
CHUNK = 32
BF = jnp.bfloat16
F32 = jnp.float32
AXES = ("row", "col")
VMEM_LIMIT = 32 * 2**20


def transform_matrices():
    n = np.arange(HALF)[:, None]
    q = np.arange(HALF)[None, :]
    out = []
    for odd in (0, 1):
        angle = -2.0 * np.pi * ((n * (2 * q + odd)) % SIZE) / SIZE
        re, im = np.cos(angle) / 16.0, np.sin(angle) / 16.0
        out.append(np.block([[re, im], [-im, re]]))
    return out


def split_np(matrix):
    high = matrix.astype(ml_dtypes.bfloat16)
    low = (matrix - high.astype(np.float64)).astype(ml_dtypes.bfloat16)
    return high, low


def constants():
    return np.stack([np.stack([np.stack(split_np(x)) for x in (m, m.T)]) for m in transform_matrices()])


def permutation():
    order = np.concatenate([np.arange(0, SIZE, 2), np.arange(1, SIZE, 2)])
    onehot = np.zeros((SIZE, SIZE), np.float32)
    onehot[order, np.arange(SIZE)] = 1.0
    columns = np.concatenate([onehot] * 3, 0).astype(ml_dtypes.bfloat16)
    rows = np.concatenate([onehot.T] * 3, 1).astype(ml_dtypes.bfloat16)
    return columns, rows


def split2(value):
    high = value.astype(BF)
    return high, (value - high.astype(F32)).astype(BF)


def split3(value):
    high = value.astype(BF)
    rest = value - high.astype(F32)
    middle = rest.astype(BF)
    return high, middle, (rest - middle.astype(F32)).astype(BF)


def dot(a, b):
    return jnp.dot(a, b, preferred_element_type=F32)


def lane_index(rows):
    return lax.broadcasted_iota(jnp.int32, (rows, HALF), 1)


def spread(first, second, shift, lanes):
    a = pltpu.roll(first, shift, 1)
    b = pltpu.roll(second, shift, 1)
    wrapped = lanes < shift
    return jnp.where(wrapped, 0.0, a), jnp.where(wrapped, a, b), jnp.where(wrapped, b, 0.0)


def gather_lanes(blocks, shift, lanes):
    back = jnp.where(shift == 0, 0, HALF - shift)
    a, b, c = [pltpu.roll(x, back, 1) for x in blocks]
    inside = lanes < HALF - shift
    return jnp.where(inside, a, b), jnp.where(inside, b, c)


def fold8(value):
    return jnp.sum(value.reshape(-1, 8, HALF), axis=0)


def prepare_kernel(measured, cols, rows, permuted):
    for j in range(measured.shape[0]):
        moved = dot(jnp.concatenate(split3(measured[j]), 1), cols[...])
        permuted[j] = dot(rows[...], jnp.concatenate(split3(moved), 0))


def place_of():
    return lax.rem(lax.axis_index("row"), 2), lax.rem(lax.axis_index("col"), 2)


def run_all(copies):
    for copy in copies:
        copy.start()
    for copy in copies:
        copy.wait()


def pack_kernel(starts, own, even, odd, cross, same, offsets, sems):
    row_odd, core = place_of()
    lanes = lane_index(8)
    value = jnp.zeros((8, HALF), F32)
    for j in range(starts.shape[1]):
        for d in range(2):
            value = jnp.where(lanes == 2 * j + d, (starts[d, j] + 1).astype(F32), value)
    for p in range(2):
        offsets[p, :, :HALF] = value
        offsets[p, :, HALF:] = value
    top = pl.ds(pl.multiple_of(HALF * row_odd, HALF), HALF)
    bottom = pl.ds(pl.multiple_of(HALF * (1 - row_odd), HALF), HALF)
    near = pl.ds(pl.multiple_of(HALF * core, HALF), HALF)
    far = pl.ds(pl.multiple_of(HALF * (1 - core), HALF), HALF)
    moves = [
        (own.at[:, top, :], odd.at[:, :HALF, :]),
        (own.at[:, bottom, :], even.at[:, :HALF, :]),
        (own.at[:, :, near], cross.at[:, :SIZE, :]),
        (own.at[:, :, far], same.at[:, :SIZE, :]),
        (offsets, odd.at[:, HALF:, :]),
        (offsets, even.at[:, HALF:, :]),
        (offsets.at[:, :, :HALF], cross.at[:, SIZE:, :]),
        (offsets.at[:, :, :HALF], same.at[:, SIZE:, :]),
    ]
    run_all([pltpu.make_async_copy(x, y, sems.at[n]) for n, (x, y) in enumerate(moves)])


def sides():
    row_odd, core = place_of()
    even_rows = pl.ds(pl.multiple_of(3 * HALF * (1 - row_odd), HALF), HALF)
    odd_rows = pl.ds(pl.multiple_of(3 * HALF * row_odd, HALF), HALF)
    return even_rows, odd_rows, 3 * core, 3 - 3 * core


def transform_kernel(
    starts, own, even_strip, odd_strip, cross, same, cross_corner, same_corner, probe_in, matrices, measured,
    keep, send, object_part, patch, around,
    tile, probe, mats, offsets, totals, xs, zs, gs, ys, back, sums, sems,
):
    step = pl.program_id(0)
    modes = probe.shape[0]
    lanes = lane_index(CHUNK)
    late = pltpu.make_async_copy(matrices, mats, sems.at[0])

    @pl.when(step == 0)
    def _():
        late.start()
        even_rows, odd_rows, cross_block, same_block = sides()
        center = pl.ds(HALF, SIZE)
        moves = [(probe_in, probe)]
        for block, strip, corner in ((cross_block, cross, cross_corner), (same_block, same, same_corner)):
            moves.append((strip.at[:, :SIZE, :], tile.at[:, block, center, :]))
            moves.append((corner.at[0, :, :HALF, :], tile.at[:, block, even_rows, :]))
            moves.append((corner.at[1, :, :HALF, :], tile.at[:, block, odd_rows, :]))
        for b in range(2):
            span = pl.ds(b * HALF, HALF)
            moves.append((own.at[:, :, span], tile.at[:, 1 + b, center, :]))
            moves.append((even_strip.at[:, :HALF, span], tile.at[:, 1 + b, even_rows, :]))
            moves.append((odd_strip.at[:, :HALF, span], tile.at[:, 1 + b, odd_rows, :]))
        strips = [x.at[0] for x in (even_strip, odd_strip, cross, same)]
        strips += [x.at[n, 0] for x in (cross_corner, same_corner) for n in range(2)]
        for n, strip in enumerate(strips):
            moves.append((strip.at[pl.ds(strip.shape[0] - 8, 8), pl.ds(0, HALF)], offsets.at[n]))
        copies = [pltpu.make_async_copy(x, y, sems.at[1 + n]) for n, (x, y) in enumerate(moves)]
        for copy in copies:
            copy.start()
        tile[:, 4] = jnp.zeros((2, 2 * SIZE, HALF), F32)
        totals[...] = jnp.zeros_like(totals)
        sums[...] = jnp.zeros_like(sums)
        for copy in copies:
            copy.wait()
        for n in range(8):
            around[pl.ds(n, 1), :] = offsets[n, :1, :].astype(jnp.int32)

    row, col = starts[0, step], starts[1, step]
    base, shift = col // HALF, lax.rem(col, HALF)

    for i in range(0, SIZE, CHUNK):
        part = pl.ds(i, CHUNK)
        where = pl.ds(row + i, CHUNK)
        obj = []
        for p in range(2):
            blocks = [tile[p, base + b, where, :] for b in range(3)]
            obj.append(gather_lanes(blocks, shift, lanes))
            for b in range(2):
                patch[0, p, b, part, :] = obj[p][b]
        for m in range(modes):
            wave = []
            for b in range(2):
                span = slice(b * HALF, (b + 1) * HALF)
                pr, pi = probe[m, 0, part, span], probe[m, 1, part, span]
                wave.append((pr * obj[0][b] - pi * obj[1][b], pr * obj[1][b] + pi * obj[0][b]))
            for odd in range(2):
                for p in range(2):
                    high, low = split2(wave[0][p] - wave[1][p] if odd else wave[0][p] + wave[1][p])
                    at = pl.ds(m * SIZE + i, CHUNK)
                    xs[odd, at, p * HALF : (p + 1) * HALF] = high
                    xs[odd, at, SIZE + p * HALF : SIZE + (p + 1) * HALF] = low
                    xs[odd, at, 2 * SIZE + p * HALF : 2 * SIZE + (p + 1) * HALF] = high

    @pl.when(step == 0)
    def _():
        late.wait()

    def right(odd, transposed):
        high, low = mats[odd, transposed, 0], mats[odd, transposed, 1]
        return jnp.concatenate([high, high, low], 0)

    def left(odd, transposed):
        high, low = mats[odd, transposed, 0], mats[odd, transposed, 1]
        return jnp.concatenate([high, low, high], 1)

    for odd in range(2):
        ys[odd] = dot(xs[odd], right(odd, 0))

    for m in range(modes):
        for odd in range(2):
            lane_span = slice(odd * HALF, (odd + 1) * HALF)
            for i in range(0, HALF, CHUNK):
                top = ys[odd, pl.ds(m * SIZE + i, CHUNK), :]
                bottom = ys[odd, pl.ds(m * SIZE + HALF + i, CHUNK), :]
                for odd_row in range(2):
                    high, low = split2(top - bottom if odd_row else top + bottom)
                    for p in range(2):
                        span = slice(p * HALF, (p + 1) * HALF)
                        at = p * HALF + i
                        zs[m, odd_row, pl.ds(at, CHUNK), lane_span] = high[:, span]
                        zs[m, odd_row, pl.ds(SIZE + at, CHUNK), lane_span] = high[:, span]
                        zs[m, odd_row, pl.ds(2 * SIZE + at, CHUNK), lane_span] = low[:, span]

    error = jnp.zeros((8, HALF), F32)
    energy = jnp.zeros((8, HALF), F32)
    for odd_row in range(2):
        far = [dot(left(odd_row, 1), zs[m, odd_row]) for m in range(modes)]
        for i in range(0, HALF, CHUNK):
            parts = [(f[i : i + CHUNK], f[HALF + i : HALF + i + CHUNK]) for f in far]
            intensity = parts[0][0] ** 2 + parts[0][1] ** 2 + (parts[1][0] ** 2 + parts[1][1] ** 2)
            intensity = jnp.maximum(intensity, intensity_floor)
            inverse = lax.rsqrt(intensity)
            modulus = intensity * inverse
            amplitude = measured[0, pl.ds(odd_row * HALF + i, CHUNK), :]
            factor = 1.0 - amplitude * inverse
            misfit = (modulus - amplitude) ** 2
            strength = amplitude**2
            error = error + fold8(misfit[:, :HALF]) + fold8(misfit[:, HALF:])
            energy = energy + fold8(strength[:, :HALF]) + fold8(strength[:, HALF:])
            for m in range(modes):
                for p in range(2):
                    high, low = split2(parts[m][p] * factor)
                    at = p * HALF + i
                    gs[m, odd_row, pl.ds(at, CHUNK), :] = high
                    gs[m, odd_row, pl.ds(SIZE + at, CHUNK), :] = high
                    gs[m, odd_row, pl.ds(2 * SIZE + at, CHUNK), :] = low
    sums[0] += error
    sums[1] += energy

    for m in range(modes):
        even = dot(left(0, 0), gs[m, 0])
        odds = dot(left(1, 0), gs[m, 1])
        for i in range(0, HALF, CHUNK):
            for p in range(2):
                a, b = even[p * HALF + i : p * HALF + i + CHUNK], odds[p * HALF + i : p * HALF + i + CHUNK]
                for bottom in range(2):
                    high, low = split2(a - b if bottom else a + b)
                    at = pl.ds(m * SIZE + bottom * HALF + i, CHUNK)
                    for odd in range(2):
                        span = slice(odd * HALF, (odd + 1) * HALF)
                        xs[odd, at, p * HALF : (p + 1) * HALF] = high[:, span]
                        xs[odd, at, SIZE + p * HALF : SIZE + (p + 1) * HALF] = low[:, span]
                        xs[odd, at, 2 * SIZE + p * HALF : 2 * SIZE + (p + 1) * HALF] = high[:, span]

    for odd in range(2):
        back[odd] = dot(xs[odd], right(odd, 1))

    for i in range(0, SIZE, CHUNK):
        part = pl.ds(i, CHUNK)
        for b in range(2):
            re, im = patch[0, 0, b, part, :], patch[0, 1, b, part, :]
            span = slice(b * HALF, (b + 1) * HALF)
            grad_re, grad_im = 0.0, 0.0
            for m in range(modes):
                at = pl.ds(m * SIZE + i, CHUNK)
                even = [back[0, at, p * HALF : (p + 1) * HALF] for p in range(2)]
                odds = [back[1, at, p * HALF : (p + 1) * HALF] for p in range(2)]
                br, bi = [x - y if b else x + y for x, y in zip(even, odds)]
                pr, pi = probe[m, 0, part, span], probe[m, 1, part, span]
                grad_re = grad_re + (pr * br + pi * bi)
                grad_im = grad_im + (pr * bi - pi * br)
                totals[b, 2 * m, part, :] += re * br + im * bi
                totals[b, 2 * m + 1, part, :] += re * bi - im * br
            object_part[0, 0, b, part, :] = grad_re
            object_part[0, 1, b, part, :] = grad_im
            totals[b, 4, part, :] += re**2 + im**2

    @pl.when(step == pl.num_programs(0) - 1)
    def _():
        core = place_of()[1]
        scalar = jnp.where(lax.broadcasted_iota(jnp.int32, (1, 4, HALF), 2) == 0, jnp.sum(sums[0]), jnp.sum(sums[1]))
        for out, block in ((keep, core), (send, 1 - core)):
            for c in range(5):
                out[:, 4 * c : 4 * c + 4, :] = totals[block, c].reshape(64, 4, HALF)
            out[:, 20:24, :] = jnp.broadcast_to(scalar, (64, 4, HALF))


def place_kernel(
    starts, object_part, patch, probe,
    center, even, odd, cross, same, cross_corner, same_corner, steps,
    padded, power, accum,
):
    step = pl.program_id(0)
    lanes = lane_index(CHUNK)

    @pl.when(step == 0)
    def _():
        accum[...] = jnp.zeros_like(accum)
        padded[:, :, 0:8, :] = jnp.zeros((2, 2, 8, HALF), F32)
        padded[:, :, 264:272, :] = jnp.zeros((2, 2, 8, HALF), F32)
        for i in range(0, SIZE, CHUNK):
            part = pl.ds(i, CHUNK)
            power[part] = probe_power(probe, part)

    row, col = starts[0, step], starts[1, step]
    base, shift = col // HALF, lax.rem(col, HALF)
    for p in range(2):
        for b in range(2):
            padded[p, b, 8:264] = patch[0, p, b]

    first, last = lanes == 0, lanes == HALF - 1
    parts = [jnp.zeros((8, HALF), F32) for _ in range(4)]
    for i in range(0, SIZE, CHUNK):
        part = pl.ds(i, CHUNK)
        where = pl.ds(row + i, CHUNK)
        grads = [[object_part[0, p, b, part, :] for b in range(2)] for p in range(2)]
        strength = [power[part, :HALF], power[part, HALF:]]
        for p, pair in enumerate(grads):
            moved = spread(pair[0], pair[1], shift, lanes)
            for b in range(3):
                accum[p, base + b, where, :] += moved[b]
        columns = []
        for p in range(2):
            obj = [patch[0, p, b, part, :] for b in range(2)]
            before = [pltpu.roll(x, 1, 1) for x in obj]
            after = [pltpu.roll(x, HALF - 1, 1) for x in obj]
            columns.append(
                (
                    jnp.where(last, after[1], after[0]) - jnp.where(first, 0.0, before[0]),
                    jnp.where(last, 0.0, after[1]) - jnp.where(first, before[0], before[1]),
                )
            )
        for b in range(2):
            rows = [padded[p, b, pl.ds(9 + i, CHUNK), :] - padded[p, b, pl.ds(7 + i, CHUNK), :] for p in range(2)]
            for d, slope in enumerate((rows, [columns[0][b], columns[1][b]])):
                parts[2 * d] = parts[2 * d] + fold8(grads[0][b] * slope[0] + grads[1][b] * slope[1])
                parts[2 * d + 1] = parts[2 * d + 1] + fold8(strength[b] * (slope[0] ** 2 + slope[1] ** 2))

    for d in range(2):
        numerator = 0.5 * jnp.sum(parts[2 * d], keepdims=True)
        denominator = 0.25 * jnp.sum(parts[2 * d + 1], keepdims=True) + small_value
        steps[pl.ds(2 * step + d, 1), :] = jnp.broadcast_to(-numerator / denominator, (1, HALF))

    @pl.when(step == pl.num_programs(0) - 1)
    def _():
        even_rows, odd_rows, cross_block, same_block = sides()
        for p in range(2):
            for b in range(2):
                span = slice(b * HALF, (b + 1) * HALF)
                center[p, :, span] = accum[p, 1 + b, 128:384]
                even[p, :, span] = accum[p, 1 + b, even_rows]
                odd[p, :, span] = accum[p, 1 + b, odd_rows]
            for block, strip, corner in ((cross_block, cross, cross_corner), (same_block, same, same_corner)):
                strip[p] = accum[p, block, 128:384]
                corner[0, p] = accum[p, block, even_rows]
                corner[1, p] = accum[p, block, odd_rows]


def probe_power(probe, part):
    return (probe[0, 0, part] ** 2 + probe[0, 1, part] ** 2) + (probe[1, 0, part] ** 2 + probe[1, 1, part] ** 2)


def light_kernel(starts, around, probe, light, power, accum):
    accum[...] = jnp.zeros_like(accum)
    for i in range(0, SIZE, CHUNK):
        part = pl.ds(i, CHUNK)
        total = probe_power(probe, part)
        power[0, part] = total[:, :HALF]
        power[1, part] = total[:, HALF:]
    lanes = lane_index(CHUNK)
    row_odd, core = place_of()
    even, cross = 1 - 2 * row_odd, 2 * core - 1
    neighbours = [(even, None), (-even, None), (None, cross), (None, -cross)]
    neighbours += [(even, cross), (-even, cross), (even, -cross), (-even, -cross)]

    def add(row, col, down, right):
        rows, source_row, row = (SIZE, 0, row + HALF) if down is None else (
            HALF, pl.multiple_of(jnp.where(down < 0, HALF, 0), HALF), row + jnp.where(down < 0, 0, 3 * HALF)
        )
        if right is None:
            col = col + HALF
        else:
            source = jnp.where(right < 0, 1, 0)
            col = col + jnp.where(right < 0, 0, 3 * HALF)
        base, shift = col // HALF, lax.rem(col, HALF)
        for i in range(0, rows, CHUNK):
            part = pl.ds(source_row + i, CHUNK)
            where = pl.ds(row + i, CHUNK)
            if right is None:
                moved = spread(power[0, part], power[1, part], shift, lanes)
            else:
                rolled = pltpu.roll(power[source, part], shift, 1)
                moved = jnp.where(lanes < shift, 0.0, rolled), jnp.where(lanes < shift, rolled, 0.0)
            for b, value in enumerate(moved):
                accum[base + b, where, :] += value

    count = starts.shape[1]
    for j in range(count):
        add(starts[0, j], starts[1, j], None, None)
    for n, (down, right) in enumerate(neighbours):
        for j in range(count):
            row, col = around[n, 2 * j] - 1, around[n, 2 * j + 1] - 1
            near = row >= 0
            if down is not None:
                near = near & jnp.where(down < 0, row > HALF, row < HALF)
            if right is not None:
                near = near & jnp.where(right < 0, col > HALF, col < HALF)

            @pl.when(near)
            def _(row=row, col=col, down=down, right=right):
                add(row, col, down, right)

    light[:, :HALF] = accum[2, 256:512]
    light[:, HALF:] = accum[3, 256:512]


def update_kernel(center, even, odd, cross, same, light, out, total):
    for p in range(2):
        total[p] = center[p]
    row_odd, core = place_of()
    even_half = pl.ds(pl.multiple_of(HALF * (1 - row_odd), HALF), HALF)
    odd_half = pl.ds(pl.multiple_of(HALF * row_odd, HALF), HALF)
    for p in range(2):
        total[p, even_half, :] += even[p]
        total[p, odd_half, :] += odd[p]
    swapped = core == 1
    for i in range(0, SIZE, CHUNK):
        part = pl.ds(i, CHUNK)
        scale = 1.0 / (light[part] + object_damping)
        for p in range(2):
            a, b = cross[p, part], same[p, part]
            out[p, part, :HALF] = (total[p, part, :HALF] + jnp.where(swapped, b, a)) * scale[:, :HALF]
            out[p, part, HALF:] = (total[p, part, HALF:] + jnp.where(swapped, a, b)) * scale[:, HALF:]


def assemble_kernel(mine, other, out):
    core = place_of()[1]

    def write(source, block):
        for c in range(4):
            out[c, :, block * HALF : (block + 1) * HALF] = source[:, 4 * c : 4 * c + 4, :].reshape(SIZE, HALF)

    @pl.when(core == 0)
    def _():
        write(mine, 0)
        write(other, 1)

    @pl.when(core == 1)
    def _():
        write(mine, 1)
        write(other, 0)


def whole(*shape):
    return pl.BlockSpec(shape, lambda *_: (0,) * len(shape))


ANY = pl.BlockSpec(memory_space=pl.ANY)


def stepped(*shape):
    return pl.BlockSpec((1, *shape), lambda i, *_: (i,) + (0,) * len(shape))


def shaped(shapes):
    return [jax.ShapeDtypeStruct(s, F32) for s in shapes]


def params():
    return pltpu.CompilerParams(vmem_limit_bytes=VMEM_LIMIT)


def cost(flops, size):
    return pl.CostEstimate(flops=flops, bytes_accessed=size, transcendentals=0)


def simple(kernel, scalars, arrays, shapes, scratch, flops, size):
    single = not isinstance(shapes, list)
    outs = [shapes] if single else shapes
    call = pl.pallas_call(
        kernel,
        out_shape=shaped(outs)[0] if single else shaped(outs),
        grid_spec=pltpu.PrefetchScalarGridSpec(
            num_scalar_prefetch=len(scalars),
            grid=(),
            in_specs=[whole(*x.shape) for x in arrays],
            out_specs=whole(*shapes) if single else [whole(*s) for s in outs],
            scratch_shapes=[pltpu.VMEM(s, F32) for s in scratch],
        ),
        compiler_params=params(),
        cost_estimate=cost(flops, size),
    )
    return call(*scalars, *arrays)


def pack(starts, own):
    rows, columns = (2, HALF + 8, SIZE), (2, SIZE + 8, HALF)
    return pl.pallas_call(
        pack_kernel,
        out_shape=shaped([rows, rows, columns, columns]),
        grid_spec=pltpu.PrefetchScalarGridSpec(
            num_scalar_prefetch=1,
            grid=(),
            in_specs=[ANY],
            out_specs=[ANY] * 4,
            scratch_shapes=[pltpu.VMEM((2, 8, SIZE), F32), pltpu.SemaphoreType.DMA((8,))],
        ),
        compiler_params=params(),
        cost_estimate=cost(1 << 10, 2 << 20),
    )(starts, own)


def prepare(measured):
    cols, rows = permutation()
    arrays = [measured, jnp.asarray(cols), jnp.asarray(rows)]
    return simple(prepare_kernel, [], arrays, measured.shape, [], 1 << 30, 3 << 20)


def transforms(starts, own, halo, probe, measured):
    mats = jnp.asarray(constants())
    arrays = [own, *halo, probe, mats]
    count = measured.shape[0]
    halves = (64, 24, HALF)
    fields = (2, 2, SIZE, HALF)
    return pl.pallas_call(
        transform_kernel,
        out_shape=shaped([halves, halves, (count, *fields), (count, *fields)])
        + [jax.ShapeDtypeStruct((8, HALF), jnp.int32)],
        grid_spec=pltpu.PrefetchScalarGridSpec(
            num_scalar_prefetch=1,
            grid=(count,),
            in_specs=[ANY] * len(arrays) + [stepped(SIZE, SIZE)],
            out_specs=[whole(*halves), whole(*halves), stepped(*fields), stepped(*fields), whole(8, HALF)],
            scratch_shapes=[
                pltpu.VMEM((2, 5, 2 * SIZE, HALF), F32),
                pltpu.VMEM(probe.shape, F32),
                pltpu.VMEM(mats.shape, BF),
                pltpu.VMEM((8, 8, HALF), F32),
                pltpu.VMEM((2, 5, SIZE, HALF), F32),
                pltpu.VMEM((2, 2 * SIZE, 3 * SIZE), BF),
                pltpu.VMEM((2, 2, 3 * SIZE, SIZE), BF),
                pltpu.VMEM((2, 2, 3 * SIZE, SIZE), BF),
                pltpu.VMEM((2, 2 * SIZE, SIZE), F32),
                pltpu.VMEM((2, 2 * SIZE, SIZE), F32),
                pltpu.VMEM((2, 8, HALF), F32),
                pltpu.SemaphoreType.DMA((24,)),
            ],
        ),
        compiler_params=params(),
        cost_estimate=cost(13 << 30, 12 << 20),
    )(starts, *arrays, measured)


def place_parts(starts, object_part, patch, probe):
    count = patch.shape[0]
    fields = (2, 2, SIZE, HALF)
    rows, columns, corners = (2, HALF, SIZE), (2, SIZE, HALF), (2, 2, HALF, HALF)
    shapes = [(2, SIZE, SIZE), rows, rows, columns, columns, corners, corners, (2 * count, HALF)]
    return pl.pallas_call(
        place_kernel,
        out_shape=shaped(shapes),
        grid_spec=pltpu.PrefetchScalarGridSpec(
            num_scalar_prefetch=1,
            grid=(count,),
            in_specs=[stepped(*fields), stepped(*fields), whole(*probe.shape)],
            out_specs=[whole(*s) for s in shapes],
            scratch_shapes=[
                pltpu.VMEM((2, 2, SIZE + 16, HALF), F32),
                pltpu.VMEM((SIZE, SIZE), F32),
                pltpu.VMEM((2, 5, 2 * SIZE, HALF), F32),
            ],
        ),
        compiler_params=params(),
        cost_estimate=cost(5 << 30, 8 << 20),
    )(starts, object_part, patch, probe)


def illuminate(starts, around, probe):
    scratch = [(2, SIZE, HALF), (7, 3 * SIZE, HALF)]
    return simple(light_kernel, [starts, around], [probe], (SIZE, SIZE), scratch, 2 << 30, 4 << 20)


def update(arrays):
    shape = arrays[0].shape
    return simple(update_kernel, [], arrays, shape, [shape], 1 << 20, 3 << 20)


def assemble(mine, other):
    return simple(assemble_kernel, [], [mine, other], (4, SIZE, SIZE), [], 1 << 20, 2 << 20)


def pairs_from(first, count):
    pairs = []
    for i in range(first, count - 1, 2):
        pairs += [(i, i + 1), (i + 1, i)]
    return pairs


def swap_rows(value, first):
    return lax.ppermute(value, "row", pairs_from(first, lax.axis_size("row")))


def swap_columns(value, first):
    return lax.ppermute(value, "col", pairs_from(first, lax.axis_size("col")))


def half_lanes(value, first):
    return jnp.where(first, value[..., :HALF], value[..., HALF:])


def local(object_tile, probe, amplitudes, offsets):
    starts = offsets[0, 0].T
    measured = amplitudes[0, 0]
    core = lax.rem(lax.axis_index("col"), 2)
    devices = lax.axis_size("row") * lax.axis_size("col")
    groups = [[i for i in range(devices) if i % 2 == k] for k in range(2)]

    with jax.named_scope("object_halo"):
        even, odd, cross, same = pack(starts, object_tile)
        odd = swap_rows(odd, 1)
        even = swap_rows(even, 0)
        cross = swap_columns(cross, 1)
        same = swap_columns(same, 0)
    permuted = prepare(measured)
    with jax.named_scope("object_corners"):
        rows, permuted = lax.optimization_barrier((jnp.stack([even, odd]), permuted))
        cross_corner = swap_columns(half_lanes(rows, core == 0), 1)
        same_corner = swap_columns(half_lanes(rows, core == 1), 0)

    halo = [even, odd, cross, same, cross_corner, same_corner]
    keep, send, object_part, patch, around = transforms(starts, object_tile, halo, probe, permuted)

    with jax.named_scope("probe_reduce"):
        chunk = keep + swap_columns(send, 0)
        chunk, object_part, around = lax.optimization_barrier((chunk, object_part, around))
        chunk = lax.all_to_all(chunk, AXES, 0, 0, axis_index_groups=groups, tiled=True)

    parts = place_parts(starts, object_part, patch, probe)
    center, even, odd, cross, same, cross_corner, same_corner, steps = parts

    with jax.named_scope("gradient_corners"):
        cross_corner = swap_columns(cross_corner, 1)
        same_corner = swap_columns(same_corner, 0)
        cross = swap_columns(cross, 1)
        same = swap_columns(same, 0)
    around, steps = lax.optimization_barrier((around, steps))
    light = illuminate(starts, around, probe)
    chunk, light, center = lax.optimization_barrier((chunk, light, center))

    with jax.named_scope("probe_sum"):
        total = jnp.sum(chunk, axis=0)
        quotient = total[:16].reshape(4, 4, HALF) / total[16:20]
        relative_error = (total[20, 0] / total[20, 1]).reshape(1)

    with jax.named_scope("gradient_rows"):
        first = jnp.where(core == 0, cross_corner, same_corner)
        second = jnp.where(core == 0, same_corner, cross_corner)
        added = jnp.concatenate([first, second], -1)
        odd = swap_rows(odd + added[1], 1)
        even = swap_rows(even + added[0], 0)

    with jax.named_scope("probe_gather"):
        spread_out = jnp.broadcast_to(quotient.reshape(1, 16, HALF), (devices // 2, 16, HALF))
        gathered = lax.all_to_all(spread_out, AXES, 0, 0, axis_index_groups=groups, tiled=True)
        probe_update = assemble(gathered, swap_columns(gathered, 0)).reshape(probe.shape)

    probe_update, even, odd = lax.optimization_barrier((probe_update, even, odd))
    object_update = update([center, even, odd, cross, same, light])
    position_step = steps[:, 0].reshape(1, 1, -1, 2)
    return (object_update, probe_update, position_step, relative_error)


def solution(mesh):
    in_specs = (
        P(None, "row", "col"),
        P(),
        P("row", "col", None, None, None),
        P("row", "col", None, None),
    )
    out_specs = (P(None, "row", "col"), P(), P("row", "col", None, None), P())
    return jax.shard_map(local, mesh=mesh, in_specs=in_specs, out_specs=out_specs, check_vma=False)
```

```python
import jax
import jax.numpy as jnp
import ml_dtypes
import numpy as np
from jax import lax
from jax.experimental import pallas as pl
from jax.experimental.pallas import tpu as pltpu
from jax.sharding import PartitionSpec as P

intensity_floor = 0.1
object_damping = 1.0
small_value = 1e-06

SIZE = 256
HALF = 128
CHUNK = 32
BF = jnp.bfloat16
F32 = jnp.float32
AXES = ("row", "col")
VMEM_LIMIT = 32 * 2**20


def transform_matrices():
    n = np.arange(HALF)[:, None]
    q = np.arange(HALF)[None, :]
    out = []
    for odd in (0, 1):
        angle = -2.0 * np.pi * ((n * (2 * q + odd)) % SIZE) / SIZE
        re, im = np.cos(angle) / 16.0, np.sin(angle) / 16.0
        out.append(np.block([[re, im], [-im, re]]))
    return out


def split_np(matrix):
    high = matrix.astype(ml_dtypes.bfloat16)
    low = (matrix - high.astype(np.float64)).astype(ml_dtypes.bfloat16)
    return high, low


def constants():
    return np.stack([np.stack([np.stack(split_np(x)) for x in (m, m.T)]) for m in transform_matrices()])


def permutation():
    order = np.concatenate([np.arange(0, SIZE, 2), np.arange(1, SIZE, 2)])
    onehot = np.zeros((SIZE, SIZE), np.float32)
    onehot[order, np.arange(SIZE)] = 1.0
    columns = np.concatenate([onehot] * 3, 0).astype(ml_dtypes.bfloat16)
    rows = np.concatenate([onehot.T] * 3, 1).astype(ml_dtypes.bfloat16)
    return columns, rows


def split2(value):
    high = value.astype(BF)
    return high, (value - high.astype(F32)).astype(BF)


def split3(value):
    high = value.astype(BF)
    rest = value - high.astype(F32)
    middle = rest.astype(BF)
    return high, middle, (rest - middle.astype(F32)).astype(BF)


def dot(a, b):
    return jnp.dot(a, b, preferred_element_type=F32)


def lane_index(rows):
    return lax.broadcasted_iota(jnp.int32, (rows, HALF), 1)


def spread(first, second, shift, lanes):
    a = pltpu.roll(first, shift, 1)
    b = pltpu.roll(second, shift, 1)
    wrapped = lanes < shift
    return jnp.where(wrapped, 0.0, a), jnp.where(wrapped, a, b), jnp.where(wrapped, b, 0.0)


def gather_lanes(blocks, shift, lanes):
    back = jnp.where(shift == 0, 0, HALF - shift)
    a, b, c = [pltpu.roll(x, back, 1) for x in blocks]
    inside = lanes < HALF - shift
    return jnp.where(inside, a, b), jnp.where(inside, b, c)


def fold8(value):
    return jnp.sum(value.reshape(-1, 8, HALF), axis=0)


def prepare_kernel(measured, cols, rows, permuted):
    for j in range(measured.shape[0]):
        moved = dot(jnp.concatenate(split3(measured[j]), 1), cols[...])
        permuted[j] = dot(rows[...], jnp.concatenate(split3(moved), 0))


def place_of():
    return lax.rem(lax.axis_index("row"), 2), lax.rem(lax.axis_index("col"), 2)


def run_all(copies):
    for copy in copies:
        copy.start()
    for copy in copies:
        copy.wait()


def pack_kernel(starts, own, even, odd, cross, same, offsets, sems):
    row_odd, core = place_of()
    lanes = lane_index(8)
    value = jnp.zeros((8, HALF), F32)
    for j in range(starts.shape[1]):
        for d in range(2):
            value = jnp.where(lanes == 2 * j + d, (starts[d, j] + 1).astype(F32), value)
    for p in range(2):
        offsets[p, :, :HALF] = value
        offsets[p, :, HALF:] = value
    top = pl.ds(pl.multiple_of(HALF * row_odd, HALF), HALF)
    bottom = pl.ds(pl.multiple_of(HALF * (1 - row_odd), HALF), HALF)
    near = pl.ds(pl.multiple_of(HALF * core, HALF), HALF)
    far = pl.ds(pl.multiple_of(HALF * (1 - core), HALF), HALF)
    moves = [
        (own.at[:, top, :], odd.at[:, :HALF, :]),
        (own.at[:, bottom, :], even.at[:, :HALF, :]),
        (own.at[:, :, near], cross.at[:, :SIZE, :]),
        (own.at[:, :, far], same.at[:, :SIZE, :]),
        (offsets, odd.at[:, HALF:, :]),
        (offsets, even.at[:, HALF:, :]),
        (offsets.at[:, :, :HALF], cross.at[:, SIZE:, :]),
        (offsets.at[:, :, :HALF], same.at[:, SIZE:, :]),
    ]
    run_all([pltpu.make_async_copy(x, y, sems.at[n]) for n, (x, y) in enumerate(moves)])


def sides():
    row_odd, core = place_of()
    even_rows = pl.ds(pl.multiple_of(3 * HALF * (1 - row_odd), HALF), HALF)
    odd_rows = pl.ds(pl.multiple_of(3 * HALF * row_odd, HALF), HALF)
    return even_rows, odd_rows, 3 * core, 3 - 3 * core


def transform_kernel(
    starts, own, even_strip, odd_strip, cross, same, cross_corner, same_corner, probe_in, matrices, measured,
    keep, send, object_part, patch, around,
    tile, probe, mats, offsets, totals, xs, zs, gs, ys, back, sums, sems,
):
    step = pl.program_id(0)
    modes = probe.shape[0]
    lanes = lane_index(CHUNK)
    late = pltpu.make_async_copy(matrices, mats, sems.at[0])

    @pl.when(step == 0)
    def _():
        late.start()
        even_rows, odd_rows, cross_block, same_block = sides()
        center = pl.ds(HALF, SIZE)
        moves = [(probe_in, probe)]
        for block, strip, corner in ((cross_block, cross, cross_corner), (same_block, same, same_corner)):
            moves.append((strip.at[:, :SIZE, :], tile.at[:, block, center, :]))
            moves.append((corner.at[0, :, :HALF, :], tile.at[:, block, even_rows, :]))
            moves.append((corner.at[1, :, :HALF, :], tile.at[:, block, odd_rows, :]))
        for b in range(2):
            span = pl.ds(b * HALF, HALF)
            moves.append((own.at[:, :, span], tile.at[:, 1 + b, center, :]))
            moves.append((even_strip.at[:, :HALF, span], tile.at[:, 1 + b, even_rows, :]))
            moves.append((odd_strip.at[:, :HALF, span], tile.at[:, 1 + b, odd_rows, :]))
        strips = [x.at[0] for x in (even_strip, odd_strip, cross, same)]
        strips += [x.at[n, 0] for x in (cross_corner, same_corner) for n in range(2)]
        for n, strip in enumerate(strips):
            moves.append((strip.at[pl.ds(strip.shape[0] - 8, 8), pl.ds(0, HALF)], offsets.at[n]))
        copies = [pltpu.make_async_copy(x, y, sems.at[1 + n]) for n, (x, y) in enumerate(moves)]
        for copy in copies:
            copy.start()
        tile[:, 4] = jnp.zeros((2, 2 * SIZE, HALF), F32)
        totals[...] = jnp.zeros_like(totals)
        sums[...] = jnp.zeros_like(sums)
        for copy in copies:
            copy.wait()
        for n in range(8):
            around[pl.ds(n, 1), :] = offsets[n, :1, :].astype(jnp.int32)

    row, col = starts[0, step], starts[1, step]
    base, shift = col // HALF, lax.rem(col, HALF)

    for i in range(0, SIZE, CHUNK):
        part = pl.ds(i, CHUNK)
        where = pl.ds(row + i, CHUNK)
        obj = []
        for p in range(2):
            blocks = [tile[p, base + b, where, :] for b in range(3)]
            obj.append(gather_lanes(blocks, shift, lanes))
            for b in range(2):
                patch[0, p, b, part, :] = obj[p][b]
        for m in range(modes):
            wave = []
            for b in range(2):
                span = slice(b * HALF, (b + 1) * HALF)
                pr, pi = probe[m, 0, part, span], probe[m, 1, part, span]
                wave.append((pr * obj[0][b] - pi * obj[1][b], pr * obj[1][b] + pi * obj[0][b]))
            for odd in range(2):
                for p in range(2):
                    high, low = split2(wave[0][p] - wave[1][p] if odd else wave[0][p] + wave[1][p])
                    at = pl.ds(m * SIZE + i, CHUNK)
                    xs[odd, at, p * HALF : (p + 1) * HALF] = high
                    xs[odd, at, SIZE + p * HALF : SIZE + (p + 1) * HALF] = low
                    xs[odd, at, 2 * SIZE + p * HALF : 2 * SIZE + (p + 1) * HALF] = high

    @pl.when(step == 0)
    def _():
        late.wait()

    def right(odd, transposed):
        high, low = mats[odd, transposed, 0], mats[odd, transposed, 1]
        return jnp.concatenate([high, high, low], 0)

    def left(odd, transposed):
        high, low = mats[odd, transposed, 0], mats[odd, transposed, 1]
        return jnp.concatenate([high, low, high], 1)

    for odd in range(2):
        ys[odd] = dot(xs[odd], right(odd, 0))

    for m in range(modes):
        for odd in range(2):
            lane_span = slice(odd * HALF, (odd + 1) * HALF)
            for i in range(0, HALF, CHUNK):
                top = ys[odd, pl.ds(m * SIZE + i, CHUNK), :]
                bottom = ys[odd, pl.ds(m * SIZE + HALF + i, CHUNK), :]
                for odd_row in range(2):
                    high, low = split2(top - bottom if odd_row else top + bottom)
                    for p in range(2):
                        span = slice(p * HALF, (p + 1) * HALF)
                        at = p * HALF + i
                        zs[m, odd_row, pl.ds(at, CHUNK), lane_span] = high[:, span]
                        zs[m, odd_row, pl.ds(SIZE + at, CHUNK), lane_span] = high[:, span]
                        zs[m, odd_row, pl.ds(2 * SIZE + at, CHUNK), lane_span] = low[:, span]

    error = jnp.zeros((8, HALF), F32)
    energy = jnp.zeros((8, HALF), F32)
    for odd_row in range(2):
        far = [dot(left(odd_row, 1), zs[m, odd_row]) for m in range(modes)]
        for i in range(0, HALF, CHUNK):
            parts = [(f[i : i + CHUNK], f[HALF + i : HALF + i + CHUNK]) for f in far]
            intensity = parts[0][0] ** 2 + parts[0][1] ** 2 + (parts[1][0] ** 2 + parts[1][1] ** 2)
            intensity = jnp.maximum(intensity, intensity_floor)
            inverse = lax.rsqrt(intensity)
            modulus = intensity * inverse
            amplitude = measured[0, pl.ds(odd_row * HALF + i, CHUNK), :]
            factor = 1.0 - amplitude * inverse
            misfit = (modulus - amplitude) ** 2
            strength = amplitude**2
            error = error + fold8(misfit[:, :HALF]) + fold8(misfit[:, HALF:])
            energy = energy + fold8(strength[:, :HALF]) + fold8(strength[:, HALF:])
            for m in range(modes):
                for p in range(2):
                    high, low = split2(parts[m][p] * factor)
                    at = p * HALF + i
                    gs[m, odd_row, pl.ds(at, CHUNK), :] = high
                    gs[m, odd_row, pl.ds(SIZE + at, CHUNK), :] = high
                    gs[m, odd_row, pl.ds(2 * SIZE + at, CHUNK), :] = low
    sums[0] += error
    sums[1] += energy

    for m in range(modes):
        even = dot(left(0, 0), gs[m, 0])
        odds = dot(left(1, 0), gs[m, 1])
        for i in range(0, HALF, CHUNK):
            for p in range(2):
                a, b = even[p * HALF + i : p * HALF + i + CHUNK], odds[p * HALF + i : p * HALF + i + CHUNK]
                for bottom in range(2):
                    high, low = split2(a - b if bottom else a + b)
                    at = pl.ds(m * SIZE + bottom * HALF + i, CHUNK)
                    for odd in range(2):
                        span = slice(odd * HALF, (odd + 1) * HALF)
                        xs[odd, at, p * HALF : (p + 1) * HALF] = high[:, span]
                        xs[odd, at, SIZE + p * HALF : SIZE + (p + 1) * HALF] = low[:, span]
                        xs[odd, at, 2 * SIZE + p * HALF : 2 * SIZE + (p + 1) * HALF] = high[:, span]

    for odd in range(2):
        back[odd] = dot(xs[odd], right(odd, 1))

    for i in range(0, SIZE, CHUNK):
        part = pl.ds(i, CHUNK)
        for b in range(2):
            re, im = patch[0, 0, b, part, :], patch[0, 1, b, part, :]
            span = slice(b * HALF, (b + 1) * HALF)
            grad_re, grad_im = 0.0, 0.0
            for m in range(modes):
                at = pl.ds(m * SIZE + i, CHUNK)
                even = [back[0, at, p * HALF : (p + 1) * HALF] for p in range(2)]
                odds = [back[1, at, p * HALF : (p + 1) * HALF] for p in range(2)]
                br, bi = [x - y if b else x + y for x, y in zip(even, odds)]
                pr, pi = probe[m, 0, part, span], probe[m, 1, part, span]
                grad_re = grad_re + (pr * br + pi * bi)
                grad_im = grad_im + (pr * bi - pi * br)
                totals[b, 2 * m, part, :] += re * br + im * bi
                totals[b, 2 * m + 1, part, :] += re * bi - im * br
            object_part[0, 0, b, part, :] = grad_re
            object_part[0, 1, b, part, :] = grad_im
            totals[b, 4, part, :] += re**2 + im**2

    @pl.when(step == pl.num_programs(0) - 1)
    def _():
        core = place_of()[1]
        scalar = jnp.where(lax.broadcasted_iota(jnp.int32, (1, 4, HALF), 2) == 0, jnp.sum(sums[0]), jnp.sum(sums[1]))
        for out, block in ((keep, core), (send, 1 - core)):
            for c in range(5):
                out[:, 4 * c : 4 * c + 4, :] = totals[block, c].reshape(64, 4, HALF)
            out[:, 20:24, :] = jnp.broadcast_to(scalar, (64, 4, HALF))


def place_kernel(
    starts, object_part, patch, probe,
    center, even, odd, cross, same, cross_corner, same_corner, steps,
    padded, power, accum,
):
    step = pl.program_id(0)
    lanes = lane_index(CHUNK)

    @pl.when(step == 0)
    def _():
        accum[...] = jnp.zeros_like(accum)
        padded[:, :, 0:8, :] = jnp.zeros((2, 2, 8, HALF), F32)
        padded[:, :, 264:272, :] = jnp.zeros((2, 2, 8, HALF), F32)
        for i in range(0, SIZE, CHUNK):
            part = pl.ds(i, CHUNK)
            power[part] = probe_power(probe, part)

    row, col = starts[0, step], starts[1, step]
    base, shift = col // HALF, lax.rem(col, HALF)
    for p in range(2):
        for b in range(2):
            padded[p, b, 8:264] = patch[0, p, b]

    first, last = lanes == 0, lanes == HALF - 1
    parts = [jnp.zeros((8, HALF), F32) for _ in range(4)]
    for i in range(0, SIZE, CHUNK):
        part = pl.ds(i, CHUNK)
        where = pl.ds(row + i, CHUNK)
        grads = [[object_part[0, p, b, part, :] for b in range(2)] for p in range(2)]
        strength = [power[part, :HALF], power[part, HALF:]]
        for p, pair in enumerate(grads):
            moved = spread(pair[0], pair[1], shift, lanes)
            for b in range(3):
                accum[p, base + b, where, :] += moved[b]
        columns = []
        for p in range(2):
            obj = [patch[0, p, b, part, :] for b in range(2)]
            before = [pltpu.roll(x, 1, 1) for x in obj]
            after = [pltpu.roll(x, HALF - 1, 1) for x in obj]
            columns.append(
                (
                    jnp.where(last, after[1], after[0]) - jnp.where(first, 0.0, before[0]),
                    jnp.where(last, 0.0, after[1]) - jnp.where(first, before[0], before[1]),
                )
            )
        for b in range(2):
            rows = [padded[p, b, pl.ds(9 + i, CHUNK), :] - padded[p, b, pl.ds(7 + i, CHUNK), :] for p in range(2)]
            for d, slope in enumerate((rows, [columns[0][b], columns[1][b]])):
                parts[2 * d] = parts[2 * d] + fold8(grads[0][b] * slope[0] + grads[1][b] * slope[1])
                parts[2 * d + 1] = parts[2 * d + 1] + fold8(strength[b] * (slope[0] ** 2 + slope[1] ** 2))

    for d in range(2):
        numerator = 0.5 * jnp.sum(parts[2 * d], keepdims=True)
        denominator = 0.25 * jnp.sum(parts[2 * d + 1], keepdims=True) + small_value
        steps[pl.ds(2 * step + d, 1), :] = jnp.broadcast_to(-numerator / denominator, (1, HALF))

    @pl.when(step == pl.num_programs(0) - 1)
    def _():
        even_rows, odd_rows, cross_block, same_block = sides()
        for p in range(2):
            for b in range(2):
                span = slice(b * HALF, (b + 1) * HALF)
                center[p, :, span] = accum[p, 1 + b, 128:384]
                even[p, :, span] = accum[p, 1 + b, even_rows]
                odd[p, :, span] = accum[p, 1 + b, odd_rows]
            for block, strip, corner in ((cross_block, cross, cross_corner), (same_block, same, same_corner)):
                strip[p] = accum[p, block, 128:384]
                corner[0, p] = accum[p, block, even_rows]
                corner[1, p] = accum[p, block, odd_rows]


def probe_power(probe, part):
    return (probe[0, 0, part] ** 2 + probe[0, 1, part] ** 2) + (probe[1, 0, part] ** 2 + probe[1, 1, part] ** 2)


def light_kernel(starts, around, probe, light, power, accum):
    accum[...] = jnp.zeros_like(accum)
    for i in range(0, SIZE, CHUNK):
        part = pl.ds(i, CHUNK)
        total = probe_power(probe, part)
        power[0, part] = total[:, :HALF]
        power[1, part] = total[:, HALF:]
    lanes = lane_index(CHUNK)
    row_odd, core = place_of()
    even, cross = 1 - 2 * row_odd, 2 * core - 1
    neighbours = [(even, None), (-even, None), (None, cross), (None, -cross)]
    neighbours += [(even, cross), (-even, cross), (even, -cross), (-even, -cross)]

    def add(row, col, down, right):
        rows, source_row, row = (SIZE, 0, row + HALF) if down is None else (
            HALF, pl.multiple_of(jnp.where(down < 0, HALF, 0), HALF), row + jnp.where(down < 0, 0, 3 * HALF)
        )
        if right is None:
            col = col + HALF
        else:
            source = jnp.where(right < 0, 1, 0)
            col = col + jnp.where(right < 0, 0, 3 * HALF)
        base, shift = col // HALF, lax.rem(col, HALF)
        for i in range(0, rows, CHUNK):
            part = pl.ds(source_row + i, CHUNK)
            where = pl.ds(row + i, CHUNK)
            if right is None:
                moved = spread(power[0, part], power[1, part], shift, lanes)
            else:
                rolled = pltpu.roll(power[source, part], shift, 1)
                moved = jnp.where(lanes < shift, 0.0, rolled), jnp.where(lanes < shift, rolled, 0.0)
            for b, value in enumerate(moved):
                accum[base + b, where, :] += value

    count = starts.shape[1]
    for j in range(count):
        add(starts[0, j], starts[1, j], None, None)
    for n, (down, right) in enumerate(neighbours):
        for j in range(count):
            row, col = around[n, 2 * j] - 1, around[n, 2 * j + 1] - 1
            near = row >= 0
            if down is not None:
                near = near & jnp.where(down < 0, row > HALF, row < HALF)
            if right is not None:
                near = near & jnp.where(right < 0, col > HALF, col < HALF)

            @pl.when(near)
            def _(row=row, col=col, down=down, right=right):
                add(row, col, down, right)

    light[:, :HALF] = accum[2, 256:512]
    light[:, HALF:] = accum[3, 256:512]


def update_kernel(center, even, odd, cross, same, light, out, total):
    for p in range(2):
        total[p] = center[p]
    row_odd, core = place_of()
    even_half = pl.ds(pl.multiple_of(HALF * (1 - row_odd), HALF), HALF)
    odd_half = pl.ds(pl.multiple_of(HALF * row_odd, HALF), HALF)
    for p in range(2):
        total[p, even_half, :] += even[p]
        total[p, odd_half, :] += odd[p]
    swapped = core == 1
    for i in range(0, SIZE, CHUNK):
        part = pl.ds(i, CHUNK)
        scale = 1.0 / (light[part] + object_damping)
        for p in range(2):
            a, b = cross[p, part], same[p, part]
            out[p, part, :HALF] = (total[p, part, :HALF] + jnp.where(swapped, b, a)) * scale[:, :HALF]
            out[p, part, HALF:] = (total[p, part, HALF:] + jnp.where(swapped, a, b)) * scale[:, HALF:]


def assemble_kernel(mine, other, out):
    core = place_of()[1]

    def write(source, block):
        for c in range(4):
            out[c, :, block * HALF : (block + 1) * HALF] = source[:, 4 * c : 4 * c + 4, :].reshape(SIZE, HALF)

    @pl.when(core == 0)
    def _():
        write(mine, 0)
        write(other, 1)

    @pl.when(core == 1)
    def _():
        write(mine, 1)
        write(other, 0)


def whole(*shape):
    return pl.BlockSpec(shape, lambda *_: (0,) * len(shape))


ANY = pl.BlockSpec(memory_space=pl.ANY)


def stepped(*shape):
    return pl.BlockSpec((1, *shape), lambda i, *_: (i,) + (0,) * len(shape))


def shaped(shapes):
    return [jax.ShapeDtypeStruct(s, F32) for s in shapes]


def params():
    return pltpu.CompilerParams(vmem_limit_bytes=VMEM_LIMIT)


def cost(flops, size):
    return pl.CostEstimate(flops=flops, bytes_accessed=size, transcendentals=0)


def simple(kernel, scalars, arrays, shapes, scratch, flops, size):
    single = not isinstance(shapes, list)
    outs = [shapes] if single else shapes
    call = pl.pallas_call(
        kernel,
        out_shape=shaped(outs)[0] if single else shaped(outs),
        grid_spec=pltpu.PrefetchScalarGridSpec(
            num_scalar_prefetch=len(scalars),
            grid=(),
            in_specs=[whole(*x.shape) for x in arrays],
            out_specs=whole(*shapes) if single else [whole(*s) for s in outs],
            scratch_shapes=[pltpu.VMEM(s, F32) for s in scratch],
        ),
        compiler_params=params(),
        cost_estimate=cost(flops, size),
    )
    return call(*scalars, *arrays)


def pack(starts, own):
    rows, columns = (2, HALF + 8, SIZE), (2, SIZE + 8, HALF)
    return pl.pallas_call(
        pack_kernel,
        out_shape=shaped([rows, rows, columns, columns]),
        grid_spec=pltpu.PrefetchScalarGridSpec(
            num_scalar_prefetch=1,
            grid=(),
            in_specs=[pl.BlockSpec(memory_space=pltpu.HBM)],
            out_specs=[ANY] * 4,
            scratch_shapes=[pltpu.VMEM((2, 8, SIZE), F32), pltpu.SemaphoreType.DMA((8,))],
        ),
        compiler_params=params(),
        cost_estimate=cost(1 << 10, 2 << 20),
    )(starts, own)


def prepare(measured):
    cols, rows = permutation()
    arrays = [measured, jnp.asarray(cols), jnp.asarray(rows)]
    return simple(prepare_kernel, [], arrays, measured.shape, [], 1 << 30, 3 << 20)


def transforms(starts, own, halo, probe, measured):
    mats = jnp.asarray(constants())
    arrays = [own, *halo, probe, mats]
    count = measured.shape[0]
    halves = (64, 24, HALF)
    fields = (2, 2, SIZE, HALF)
    return pl.pallas_call(
        transform_kernel,
        out_shape=shaped([halves, halves, (count, *fields), (count, *fields)])
        + [jax.ShapeDtypeStruct((8, HALF), jnp.int32)],
        grid_spec=pltpu.PrefetchScalarGridSpec(
            num_scalar_prefetch=1,
            grid=(count,),
            in_specs=[ANY] * len(arrays) + [stepped(SIZE, SIZE)],
            out_specs=[whole(*halves), whole(*halves), stepped(*fields), stepped(*fields), whole(8, HALF)],
            scratch_shapes=[
                pltpu.VMEM((2, 5, 2 * SIZE, HALF), F32),
                pltpu.VMEM(probe.shape, F32),
                pltpu.VMEM(mats.shape, BF),
                pltpu.VMEM((8, 8, HALF), F32),
                pltpu.VMEM((2, 5, SIZE, HALF), F32),
                pltpu.VMEM((2, 2 * SIZE, 3 * SIZE), BF),
                pltpu.VMEM((2, 2, 3 * SIZE, SIZE), BF),
                pltpu.VMEM((2, 2, 3 * SIZE, SIZE), BF),
                pltpu.VMEM((2, 2 * SIZE, SIZE), F32),
                pltpu.VMEM((2, 2 * SIZE, SIZE), F32),
                pltpu.VMEM((2, 8, HALF), F32),
                pltpu.SemaphoreType.DMA((24,)),
            ],
        ),
        compiler_params=params(),
        cost_estimate=cost(13 << 30, 12 << 20),
    )(starts, *arrays, measured)


def place_parts(starts, object_part, patch, probe):
    count = patch.shape[0]
    fields = (2, 2, SIZE, HALF)
    rows, columns, corners = (2, HALF, SIZE), (2, SIZE, HALF), (2, 2, HALF, HALF)
    shapes = [(2, SIZE, SIZE), rows, rows, columns, columns, corners, corners, (2 * count, HALF)]
    return pl.pallas_call(
        place_kernel,
        out_shape=shaped(shapes),
        grid_spec=pltpu.PrefetchScalarGridSpec(
            num_scalar_prefetch=1,
            grid=(count,),
            in_specs=[stepped(*fields), stepped(*fields), whole(*probe.shape)],
            out_specs=[whole(*s) for s in shapes],
            scratch_shapes=[
                pltpu.VMEM((2, 2, SIZE + 16, HALF), F32),
                pltpu.VMEM((SIZE, SIZE), F32),
                pltpu.VMEM((2, 5, 2 * SIZE, HALF), F32),
            ],
        ),
        compiler_params=params(),
        cost_estimate=cost(5 << 30, 8 << 20),
    )(starts, object_part, patch, probe)


def illuminate(starts, around, probe):
    scratch = [(2, SIZE, HALF), (7, 3 * SIZE, HALF)]
    return simple(light_kernel, [starts, around], [probe], (SIZE, SIZE), scratch, 2 << 30, 4 << 20)


def update(arrays):
    shape = arrays[0].shape
    return simple(update_kernel, [], arrays, shape, [shape], 1 << 20, 3 << 20)


def assemble(mine, other):
    return simple(assemble_kernel, [], [mine, other], (4, SIZE, SIZE), [], 1 << 20, 2 << 20)


def pairs_from(first, count):
    pairs = []
    for i in range(first, count - 1, 2):
        pairs += [(i, i + 1), (i + 1, i)]
    return pairs


def swap_rows(value, first):
    return lax.ppermute(value, "row", pairs_from(first, lax.axis_size("row")))


def swap_columns(value, first):
    return lax.ppermute(value, "col", pairs_from(first, lax.axis_size("col")))


def half_lanes(value, first):
    return jnp.where(first, value[..., :HALF], value[..., HALF:])


def local(object_tile, probe, amplitudes, offsets):
    starts = offsets[0, 0].T
    measured = amplitudes[0, 0]
    core = lax.rem(lax.axis_index("col"), 2)
    devices = lax.axis_size("row") * lax.axis_size("col")
    groups = [[i for i in range(devices) if i % 2 == k] for k in range(2)]

    with jax.named_scope("object_halo"):
        even, odd, cross, same = pack(starts, object_tile)
        odd = swap_rows(odd, 1)
        even = swap_rows(even, 0)
        cross = swap_columns(cross, 1)
        same = swap_columns(same, 0)
    permuted = prepare(measured)
    with jax.named_scope("object_corners"):
        even, odd, cross, same, permuted = lax.optimization_barrier((even, odd, cross, same, permuted))
        rows = jnp.stack([even, odd])
        cross_corner = swap_columns(half_lanes(rows, core == 0), 1)
        same_corner = swap_columns(half_lanes(rows, core == 1), 0)

    halo = [even, odd, cross, same, cross_corner, same_corner]
    keep, send, object_part, patch, around = transforms(starts, object_tile, halo, probe, permuted)

    parts = place_parts(starts, object_part, patch, probe)
    with jax.named_scope("probe_reduce"):
        chunk, parts, around = lax.optimization_barrier((keep + swap_columns(send, 0), parts, around))
        chunk = lax.all_to_all(chunk, AXES, 0, 0, axis_index_groups=groups, tiled=True)
    center, even, odd, cross, same, cross_corner, same_corner, steps = parts

    with jax.named_scope("gradient_corners"):
        cross_corner = swap_columns(cross_corner, 1)
        same_corner = swap_columns(same_corner, 0)
        cross = swap_columns(cross, 1)
        same = swap_columns(same, 0)
    light = illuminate(starts, around, probe)
    chunk, light, cross_corner, same_corner, cross, same = lax.optimization_barrier(
        (chunk, light, cross_corner, same_corner, cross, same)
    )

    with jax.named_scope("probe_sum"):
        total = jnp.sum(chunk, axis=0)
        quotient = total[:16].reshape(4, 4, HALF) / total[16:20]
        relative_error = (total[20, 0] / total[20, 1]).reshape(1)

    with jax.named_scope("gradient_rows"):
        first = jnp.where(core == 0, cross_corner, same_corner)
        second = jnp.where(core == 0, same_corner, cross_corner)
        added = jnp.concatenate([first, second], -1)
        odd = swap_rows(odd + added[1], 1)
        even = swap_rows(even + added[0], 0)

    with jax.named_scope("probe_gather"):
        spread_out = jnp.broadcast_to(quotient.reshape(1, 16, HALF), (devices // 2, 16, HALF))
        gathered = lax.all_to_all(spread_out, AXES, 0, 0, axis_index_groups=groups, tiled=True)
        gathered, odd, even = lax.optimization_barrier((gathered, odd, even))
        probe_update = assemble(gathered, swap_columns(gathered, 0)).reshape(probe.shape)

    object_update = update([center, even, odd, cross, same, light])
    position_step = steps[:, 0].reshape(1, 1, -1, 2)
    return (object_update, probe_update, position_step, relative_error)


def solution(mesh):
    in_specs = (
        P(None, "row", "col"),
        P(),
        P("row", "col", None, None, None),
        P("row", "col", None, None),
    )
    out_specs = (P(None, "row", "col"), P(), P("row", "col", None, None), P())
    return jax.shard_map(local, mesh=mesh, in_specs=in_specs, out_specs=out_specs, check_vma=False)
```

```python
import jax
import jax.numpy as jnp
import ml_dtypes
import numpy as np
from jax import lax
from jax.experimental import pallas as pl
from jax.experimental.pallas import tpu as pltpu
from jax.sharding import PartitionSpec as P

intensity_floor = 0.1
object_damping = 1.0
small_value = 1e-06

SIZE = 256
HALF = 128
CHUNK = 32
BF = jnp.bfloat16
F32 = jnp.float32
AXES = ("row", "col")
VMEM_LIMIT = 32 * 2**20


def transform_matrices():
    n = np.arange(HALF)[:, None]
    q = np.arange(HALF)[None, :]
    out = []
    for odd in (0, 1):
        angle = -2.0 * np.pi * ((n * (2 * q + odd)) % SIZE) / SIZE
        re, im = np.cos(angle) / 16.0, np.sin(angle) / 16.0
        out.append(np.block([[re, im], [-im, re]]))
    return out


def split_np(matrix):
    high = matrix.astype(ml_dtypes.bfloat16)
    low = (matrix - high.astype(np.float64)).astype(ml_dtypes.bfloat16)
    return high, low


def constants():
    return np.stack([np.stack([np.stack(split_np(x)) for x in (m, m.T)]) for m in transform_matrices()])


def permutation():
    order = np.concatenate([np.arange(0, SIZE, 2), np.arange(1, SIZE, 2)])
    onehot = np.zeros((SIZE, SIZE), np.float32)
    onehot[order, np.arange(SIZE)] = 1.0
    columns = np.concatenate([onehot] * 3, 0).astype(ml_dtypes.bfloat16)
    rows = np.concatenate([onehot.T] * 3, 1).astype(ml_dtypes.bfloat16)
    return columns, rows


def split2(value):
    high = value.astype(BF)
    return high, (value - high.astype(F32)).astype(BF)


def split3(value):
    high = value.astype(BF)
    rest = value - high.astype(F32)
    middle = rest.astype(BF)
    return high, middle, (rest - middle.astype(F32)).astype(BF)


def dot(a, b):
    return jnp.dot(a, b, preferred_element_type=F32)


def lane_index(rows):
    return lax.broadcasted_iota(jnp.int32, (rows, HALF), 1)


def spread(first, second, shift, lanes):
    a = pltpu.roll(first, shift, 1)
    b = pltpu.roll(second, shift, 1)
    wrapped = lanes < shift
    return jnp.where(wrapped, 0.0, a), jnp.where(wrapped, a, b), jnp.where(wrapped, b, 0.0)


def gather_lanes(blocks, shift, lanes):
    back = jnp.where(shift == 0, 0, HALF - shift)
    a, b, c = [pltpu.roll(x, back, 1) for x in blocks]
    inside = lanes < HALF - shift
    return jnp.where(inside, a, b), jnp.where(inside, b, c)


def fold8(value):
    return jnp.sum(value.reshape(-1, 8, HALF), axis=0)


def prepare_kernel(measured, cols, rows, permuted):
    for j in range(measured.shape[0]):
        moved = dot(jnp.concatenate(split3(measured[j]), 1), cols[...])
        permuted[j] = dot(rows[...], jnp.concatenate(split3(moved), 0))


def place_of():
    return lax.rem(lax.axis_index("row"), 2), lax.rem(lax.axis_index("col"), 2)


def run_all(copies):
    for copy in copies:
        copy.start()
    for copy in copies:
        copy.wait()


def pack_kernel(starts, own, even, odd, cross, same, offsets, sems):
    row_odd, core = place_of()
    lanes = lane_index(8)
    value = jnp.zeros((8, HALF), F32)
    for j in range(starts.shape[1]):
        for d in range(2):
            value = jnp.where(lanes == 2 * j + d, (starts[d, j] + 1).astype(F32), value)
    for p in range(2):
        offsets[p, :, :HALF] = value
        offsets[p, :, HALF:] = value
    top = pl.ds(pl.multiple_of(HALF * row_odd, HALF), HALF)
    bottom = pl.ds(pl.multiple_of(HALF * (1 - row_odd), HALF), HALF)
    near = pl.ds(pl.multiple_of(HALF * core, HALF), HALF)
    far = pl.ds(pl.multiple_of(HALF * (1 - core), HALF), HALF)
    moves = [
        (own.at[:, top, :], odd.at[:, :HALF, :]),
        (own.at[:, bottom, :], even.at[:, :HALF, :]),
        (own.at[:, :, near], cross.at[:, :SIZE, :]),
        (own.at[:, :, far], same.at[:, :SIZE, :]),
        (offsets, odd.at[:, HALF:, :]),
        (offsets, even.at[:, HALF:, :]),
        (offsets.at[:, :, :HALF], cross.at[:, SIZE:, :]),
        (offsets.at[:, :, :HALF], same.at[:, SIZE:, :]),
    ]
    run_all([pltpu.make_async_copy(x, y, sems.at[n]) for n, (x, y) in enumerate(moves)])


def sides():
    row_odd, core = place_of()
    even_rows = pl.ds(pl.multiple_of(3 * HALF * (1 - row_odd), HALF), HALF)
    odd_rows = pl.ds(pl.multiple_of(3 * HALF * row_odd, HALF), HALF)
    return even_rows, odd_rows, 3 * core, 3 - 3 * core


def transform_kernel(
    starts, own, even_strip, odd_strip, cross, same, cross_corner, same_corner, probe_in, matrices, measured,
    keep, send, object_part, patch, around,
    tile, probe, mats, offsets, totals, xs, zs, gs, ys, back, sums, sems,
):
    step = pl.program_id(0)
    modes = probe.shape[0]
    lanes = lane_index(CHUNK)
    late = pltpu.make_async_copy(matrices, mats, sems.at[0])

    @pl.when(step == 0)
    def _():
        late.start()
        even_rows, odd_rows, cross_block, same_block = sides()
        center = pl.ds(HALF, SIZE)
        moves = [(probe_in, probe)]
        for block, strip, corner in ((cross_block, cross, cross_corner), (same_block, same, same_corner)):
            moves.append((strip.at[:, :SIZE, :], tile.at[:, block, center, :]))
            moves.append((corner.at[0, :, :HALF, :], tile.at[:, block, even_rows, :]))
            moves.append((corner.at[1, :, :HALF, :], tile.at[:, block, odd_rows, :]))
        for b in range(2):
            span = pl.ds(b * HALF, HALF)
            moves.append((own.at[:, :, span], tile.at[:, 1 + b, center, :]))
            moves.append((even_strip.at[:, :HALF, span], tile.at[:, 1 + b, even_rows, :]))
            moves.append((odd_strip.at[:, :HALF, span], tile.at[:, 1 + b, odd_rows, :]))
        strips = [x.at[0] for x in (even_strip, odd_strip, cross, same)]
        strips += [x.at[n, 0] for x in (cross_corner, same_corner) for n in range(2)]
        for n, strip in enumerate(strips):
            moves.append((strip.at[pl.ds(strip.shape[0] - 8, 8), pl.ds(0, HALF)], offsets.at[n]))
        copies = [pltpu.make_async_copy(x, y, sems.at[1 + n]) for n, (x, y) in enumerate(moves)]
        for copy in copies:
            copy.start()
        tile[:, 4] = jnp.zeros((2, 2 * SIZE, HALF), F32)
        totals[...] = jnp.zeros_like(totals)
        sums[...] = jnp.zeros_like(sums)
        for copy in copies:
            copy.wait()
        for n in range(8):
            around[pl.ds(n, 1), :] = offsets[n, :1, :].astype(jnp.int32)

    row, col = starts[0, step], starts[1, step]
    base, shift = col // HALF, lax.rem(col, HALF)

    for i in range(0, SIZE, CHUNK):
        part = pl.ds(i, CHUNK)
        where = pl.ds(row + i, CHUNK)
        obj = []
        for p in range(2):
            blocks = [tile[p, base + b, where, :] for b in range(3)]
            obj.append(gather_lanes(blocks, shift, lanes))
            for b in range(2):
                patch[0, p, b, part, :] = obj[p][b]
        for m in range(modes):
            wave = []
            for b in range(2):
                span = slice(b * HALF, (b + 1) * HALF)
                pr, pi = probe[m, 0, part, span], probe[m, 1, part, span]
                wave.append((pr * obj[0][b] - pi * obj[1][b], pr * obj[1][b] + pi * obj[0][b]))
            for odd in range(2):
                for p in range(2):
                    high, low = split2(wave[0][p] - wave[1][p] if odd else wave[0][p] + wave[1][p])
                    at = pl.ds(m * SIZE + i, CHUNK)
                    xs[odd, at, p * HALF : (p + 1) * HALF] = high
                    xs[odd, at, SIZE + p * HALF : SIZE + (p + 1) * HALF] = low
                    xs[odd, at, 2 * SIZE + p * HALF : 2 * SIZE + (p + 1) * HALF] = high

    @pl.when(step == 0)
    def _():
        late.wait()

    def right(odd, transposed):
        high, low = mats[odd, transposed, 0], mats[odd, transposed, 1]
        return jnp.concatenate([high, high, low], 0)

    def left(odd, transposed):
        high, low = mats[odd, transposed, 0], mats[odd, transposed, 1]
        return jnp.concatenate([high, low, high], 1)

    for odd in range(2):
        ys[odd] = dot(xs[odd], right(odd, 0))

    for m in range(modes):
        for odd in range(2):
            lane_span = slice(odd * HALF, (odd + 1) * HALF)
            for i in range(0, HALF, CHUNK):
                top = ys[odd, pl.ds(m * SIZE + i, CHUNK), :]
                bottom = ys[odd, pl.ds(m * SIZE + HALF + i, CHUNK), :]
                for odd_row in range(2):
                    high, low = split2(top - bottom if odd_row else top + bottom)
                    for p in range(2):
                        span = slice(p * HALF, (p + 1) * HALF)
                        at = p * HALF + i
                        zs[m, odd_row, pl.ds(at, CHUNK), lane_span] = high[:, span]
                        zs[m, odd_row, pl.ds(SIZE + at, CHUNK), lane_span] = high[:, span]
                        zs[m, odd_row, pl.ds(2 * SIZE + at, CHUNK), lane_span] = low[:, span]

    error = jnp.zeros((8, HALF), F32)
    energy = jnp.zeros((8, HALF), F32)
    for odd_row in range(2):
        far = [dot(left(odd_row, 1), zs[m, odd_row]) for m in range(modes)]
        for i in range(0, HALF, CHUNK):
            parts = [(f[i : i + CHUNK], f[HALF + i : HALF + i + CHUNK]) for f in far]
            intensity = parts[0][0] ** 2 + parts[0][1] ** 2 + (parts[1][0] ** 2 + parts[1][1] ** 2)
            intensity = jnp.maximum(intensity, intensity_floor)
            inverse = lax.rsqrt(intensity)
            modulus = intensity * inverse
            amplitude = measured[0, pl.ds(odd_row * HALF + i, CHUNK), :]
            factor = 1.0 - amplitude * inverse
            misfit = (modulus - amplitude) ** 2
            strength = amplitude**2
            error = error + fold8(misfit[:, :HALF]) + fold8(misfit[:, HALF:])
            energy = energy + fold8(strength[:, :HALF]) + fold8(strength[:, HALF:])
            for m in range(modes):
                for p in range(2):
                    high, low = split2(parts[m][p] * factor)
                    at = p * HALF + i
                    gs[m, odd_row, pl.ds(at, CHUNK), :] = high
                    gs[m, odd_row, pl.ds(SIZE + at, CHUNK), :] = high
                    gs[m, odd_row, pl.ds(2 * SIZE + at, CHUNK), :] = low
    sums[0] += error
    sums[1] += energy

    for m in range(modes):
        even = dot(left(0, 0), gs[m, 0])
        odds = dot(left(1, 0), gs[m, 1])
        for i in range(0, HALF, CHUNK):
            for p in range(2):
                a, b = even[p * HALF + i : p * HALF + i + CHUNK], odds[p * HALF + i : p * HALF + i + CHUNK]
                for bottom in range(2):
                    high, low = split2(a - b if bottom else a + b)
                    at = pl.ds(m * SIZE + bottom * HALF + i, CHUNK)
                    for odd in range(2):
                        span = slice(odd * HALF, (odd + 1) * HALF)
                        xs[odd, at, p * HALF : (p + 1) * HALF] = high[:, span]
                        xs[odd, at, SIZE + p * HALF : SIZE + (p + 1) * HALF] = low[:, span]
                        xs[odd, at, 2 * SIZE + p * HALF : 2 * SIZE + (p + 1) * HALF] = high[:, span]

    for odd in range(2):
        back[odd] = dot(xs[odd], right(odd, 1))

    for i in range(0, SIZE, CHUNK):
        part = pl.ds(i, CHUNK)
        for b in range(2):
            re, im = patch[0, 0, b, part, :], patch[0, 1, b, part, :]
            span = slice(b * HALF, (b + 1) * HALF)
            grad_re, grad_im = 0.0, 0.0
            for m in range(modes):
                at = pl.ds(m * SIZE + i, CHUNK)
                even = [back[0, at, p * HALF : (p + 1) * HALF] for p in range(2)]
                odds = [back[1, at, p * HALF : (p + 1) * HALF] for p in range(2)]
                br, bi = [x - y if b else x + y for x, y in zip(even, odds)]
                pr, pi = probe[m, 0, part, span], probe[m, 1, part, span]
                grad_re = grad_re + (pr * br + pi * bi)
                grad_im = grad_im + (pr * bi - pi * br)
                totals[b, 2 * m, part, :] += re * br + im * bi
                totals[b, 2 * m + 1, part, :] += re * bi - im * br
            object_part[0, 0, b, part, :] = grad_re
            object_part[0, 1, b, part, :] = grad_im
            totals[b, 4, part, :] += re**2 + im**2

    @pl.when(step == pl.num_programs(0) - 1)
    def _():
        core = place_of()[1]
        scalar = jnp.where(lax.broadcasted_iota(jnp.int32, (1, 4, HALF), 2) == 0, jnp.sum(sums[0]), jnp.sum(sums[1]))
        for out, block in ((keep, core), (send, 1 - core)):
            for c in range(5):
                out[:, 4 * c : 4 * c + 4, :] = totals[block, c].reshape(64, 4, HALF)
            out[:, 20:24, :] = jnp.broadcast_to(scalar, (64, 4, HALF))


def place_kernel(
    starts, object_part, patch, probe,
    center, even, odd, cross, same, cross_corner, same_corner, steps,
    padded, power, accum,
):
    step = pl.program_id(0)
    lanes = lane_index(CHUNK)

    @pl.when(step == 0)
    def _():
        accum[...] = jnp.zeros_like(accum)
        padded[:, :, 0:8, :] = jnp.zeros((2, 2, 8, HALF), F32)
        padded[:, :, 264:272, :] = jnp.zeros((2, 2, 8, HALF), F32)
        for i in range(0, SIZE, CHUNK):
            part = pl.ds(i, CHUNK)
            power[part] = probe_power(probe, part)

    row, col = starts[0, step], starts[1, step]
    base, shift = col // HALF, lax.rem(col, HALF)
    for p in range(2):
        for b in range(2):
            padded[p, b, 8:264] = patch[0, p, b]

    first, last = lanes == 0, lanes == HALF - 1
    parts = [jnp.zeros((8, HALF), F32) for _ in range(4)]
    for i in range(0, SIZE, CHUNK):
        part = pl.ds(i, CHUNK)
        where = pl.ds(row + i, CHUNK)
        grads = [[object_part[0, p, b, part, :] for b in range(2)] for p in range(2)]
        strength = [power[part, :HALF], power[part, HALF:]]
        for p, pair in enumerate(grads):
            moved = spread(pair[0], pair[1], shift, lanes)
            for b in range(3):
                accum[p, base + b, where, :] += moved[b]
        columns = []
        for p in range(2):
            obj = [patch[0, p, b, part, :] for b in range(2)]
            before = [pltpu.roll(x, 1, 1) for x in obj]
            after = [pltpu.roll(x, HALF - 1, 1) for x in obj]
            columns.append(
                (
                    jnp.where(last, after[1], after[0]) - jnp.where(first, 0.0, before[0]),
                    jnp.where(last, 0.0, after[1]) - jnp.where(first, before[0], before[1]),
                )
            )
        for b in range(2):
            rows = [padded[p, b, pl.ds(9 + i, CHUNK), :] - padded[p, b, pl.ds(7 + i, CHUNK), :] for p in range(2)]
            for d, slope in enumerate((rows, [columns[0][b], columns[1][b]])):
                parts[2 * d] = parts[2 * d] + fold8(grads[0][b] * slope[0] + grads[1][b] * slope[1])
                parts[2 * d + 1] = parts[2 * d + 1] + fold8(strength[b] * (slope[0] ** 2 + slope[1] ** 2))

    for d in range(2):
        numerator = 0.5 * jnp.sum(parts[2 * d], keepdims=True)
        denominator = 0.25 * jnp.sum(parts[2 * d + 1], keepdims=True) + small_value
        steps[pl.ds(2 * step + d, 1), :] = jnp.broadcast_to(-numerator / denominator, (1, HALF))

    @pl.when(step == pl.num_programs(0) - 1)
    def _():
        even_rows, odd_rows, cross_block, same_block = sides()
        for p in range(2):
            for b in range(2):
                span = slice(b * HALF, (b + 1) * HALF)
                center[p, :, span] = accum[p, 1 + b, 128:384]
                even[p, :, span] = accum[p, 1 + b, even_rows]
                odd[p, :, span] = accum[p, 1 + b, odd_rows]
            for block, strip, corner in ((cross_block, cross, cross_corner), (same_block, same, same_corner)):
                strip[p] = accum[p, block, 128:384]
                corner[0, p] = accum[p, block, even_rows]
                corner[1, p] = accum[p, block, odd_rows]


def probe_power(probe, part):
    return (probe[0, 0, part] ** 2 + probe[0, 1, part] ** 2) + (probe[1, 0, part] ** 2 + probe[1, 1, part] ** 2)


def light_kernel(starts, around, probe, light, power, accum):
    accum[...] = jnp.zeros_like(accum)
    for i in range(0, SIZE, CHUNK):
        part = pl.ds(i, CHUNK)
        total = probe_power(probe, part)
        power[0, part] = total[:, :HALF]
        power[1, part] = total[:, HALF:]
    lanes = lane_index(CHUNK)
    row_odd, core = place_of()
    even, cross = 1 - 2 * row_odd, 2 * core - 1
    neighbours = [(even, None), (-even, None), (None, cross), (None, -cross)]
    neighbours += [(even, cross), (-even, cross), (even, -cross), (-even, -cross)]

    def add(row, col, down, right):
        rows, source_row, row = (SIZE, 0, row + HALF) if down is None else (
            HALF, pl.multiple_of(jnp.where(down < 0, HALF, 0), HALF), row + jnp.where(down < 0, 0, 3 * HALF)
        )
        if right is None:
            col = col + HALF
        else:
            source = jnp.where(right < 0, 1, 0)
            col = col + jnp.where(right < 0, 0, 3 * HALF)
        base, shift = col // HALF, lax.rem(col, HALF)
        for i in range(0, rows, CHUNK):
            part = pl.ds(source_row + i, CHUNK)
            where = pl.ds(row + i, CHUNK)
            if right is None:
                moved = spread(power[0, part], power[1, part], shift, lanes)
            else:
                rolled = pltpu.roll(power[source, part], shift, 1)
                moved = jnp.where(lanes < shift, 0.0, rolled), jnp.where(lanes < shift, rolled, 0.0)
            for b, value in enumerate(moved):
                accum[base + b, where, :] += value

    count = starts.shape[1]
    for j in range(count):
        add(starts[0, j], starts[1, j], None, None)
    for n, (down, right) in enumerate(neighbours):
        for j in range(count):
            row, col = around[n, 2 * j] - 1, around[n, 2 * j + 1] - 1
            near = row >= 0
            if down is not None:
                near = near & jnp.where(down < 0, row > HALF, row < HALF)
            if right is not None:
                near = near & jnp.where(right < 0, col > HALF, col < HALF)

            @pl.when(near)
            def _(row=row, col=col, down=down, right=right):
                add(row, col, down, right)

    light[:, :HALF] = accum[2, 256:512]
    light[:, HALF:] = accum[3, 256:512]


def update_kernel(center, even, odd, cross, same, light, out, total):
    for p in range(2):
        total[p] = center[p]
    row_odd, core = place_of()
    even_half = pl.ds(pl.multiple_of(HALF * (1 - row_odd), HALF), HALF)
    odd_half = pl.ds(pl.multiple_of(HALF * row_odd, HALF), HALF)
    for p in range(2):
        total[p, even_half, :] += even[p]
        total[p, odd_half, :] += odd[p]
    swapped = core == 1
    for i in range(0, SIZE, CHUNK):
        part = pl.ds(i, CHUNK)
        scale = 1.0 / (light[part] + object_damping)
        for p in range(2):
            a, b = cross[p, part], same[p, part]
            out[p, part, :HALF] = (total[p, part, :HALF] + jnp.where(swapped, b, a)) * scale[:, :HALF]
            out[p, part, HALF:] = (total[p, part, HALF:] + jnp.where(swapped, a, b)) * scale[:, HALF:]


def assemble_kernel(mine, other, out):
    core = place_of()[1]

    def write(source, block):
        for c in range(4):
            out[c, :, block * HALF : (block + 1) * HALF] = source[:, 4 * c : 4 * c + 4, :].reshape(SIZE, HALF)

    @pl.when(core == 0)
    def _():
        write(mine, 0)
        write(other, 1)

    @pl.when(core == 1)
    def _():
        write(mine, 1)
        write(other, 0)


def whole(*shape):
    return pl.BlockSpec(shape, lambda *_: (0,) * len(shape))


ANY = pl.BlockSpec(memory_space=pl.ANY)


def stepped(*shape):
    return pl.BlockSpec((1, *shape), lambda i, *_: (i,) + (0,) * len(shape))


def shaped(shapes):
    return [jax.ShapeDtypeStruct(s, F32) for s in shapes]


def params():
    return pltpu.CompilerParams(vmem_limit_bytes=VMEM_LIMIT)


def cost(flops, size):
    return pl.CostEstimate(flops=flops, bytes_accessed=size, transcendentals=0)


def simple(kernel, scalars, arrays, shapes, scratch, flops, size):
    single = not isinstance(shapes, list)
    outs = [shapes] if single else shapes
    call = pl.pallas_call(
        kernel,
        out_shape=shaped(outs)[0] if single else shaped(outs),
        grid_spec=pltpu.PrefetchScalarGridSpec(
            num_scalar_prefetch=len(scalars),
            grid=(),
            in_specs=[whole(*x.shape) for x in arrays],
            out_specs=whole(*shapes) if single else [whole(*s) for s in outs],
            scratch_shapes=[pltpu.VMEM(s, F32) for s in scratch],
        ),
        compiler_params=params(),
        cost_estimate=cost(flops, size),
    )
    return call(*scalars, *arrays)


def pack(starts, own):
    rows, columns = (2, HALF + 8, SIZE), (2, SIZE + 8, HALF)
    return pl.pallas_call(
        pack_kernel,
        out_shape=shaped([rows, rows, columns, columns]),
        grid_spec=pltpu.PrefetchScalarGridSpec(
            num_scalar_prefetch=1,
            grid=(),
            in_specs=[pl.BlockSpec(memory_space=pltpu.HBM)],
            out_specs=[ANY] * 4,
            scratch_shapes=[pltpu.VMEM((2, 8, SIZE), F32), pltpu.SemaphoreType.DMA((8,))],
        ),
        compiler_params=params(),
        cost_estimate=cost(1 << 10, 2 << 20),
    )(starts, own)


def prepare(measured):
    cols, rows = permutation()
    arrays = [measured, jnp.asarray(cols), jnp.asarray(rows)]
    return simple(prepare_kernel, [], arrays, measured.shape, [], 1 << 30, 3 << 20)


def transforms(starts, own, halo, probe, measured):
    mats = jnp.asarray(constants())
    arrays = [own, *halo, probe, mats]
    count = measured.shape[0]
    halves = (64, 24, HALF)
    fields = (2, 2, SIZE, HALF)
    return pl.pallas_call(
        transform_kernel,
        out_shape=shaped([halves, halves, (count, *fields), (count, *fields)])
        + [jax.ShapeDtypeStruct((8, HALF), jnp.int32)],
        grid_spec=pltpu.PrefetchScalarGridSpec(
            num_scalar_prefetch=1,
            grid=(count,),
            in_specs=[ANY] * len(arrays) + [stepped(SIZE, SIZE)],
            out_specs=[whole(*halves), whole(*halves), stepped(*fields), stepped(*fields), whole(8, HALF)],
            scratch_shapes=[
                pltpu.VMEM((2, 5, 2 * SIZE, HALF), F32),
                pltpu.VMEM(probe.shape, F32),
                pltpu.VMEM(mats.shape, BF),
                pltpu.VMEM((8, 8, HALF), F32),
                pltpu.VMEM((2, 5, SIZE, HALF), F32),
                pltpu.VMEM((2, 2 * SIZE, 3 * SIZE), BF),
                pltpu.VMEM((2, 2, 3 * SIZE, SIZE), BF),
                pltpu.VMEM((2, 2, 3 * SIZE, SIZE), BF),
                pltpu.VMEM((2, 2 * SIZE, SIZE), F32),
                pltpu.VMEM((2, 2 * SIZE, SIZE), F32),
                pltpu.VMEM((2, 8, HALF), F32),
                pltpu.SemaphoreType.DMA((24,)),
            ],
        ),
        compiler_params=params(),
        cost_estimate=cost(13 << 30, 12 << 20),
    )(starts, *arrays, measured)


def place_parts(starts, object_part, patch, probe):
    count = patch.shape[0]
    fields = (2, 2, SIZE, HALF)
    rows, columns, corners = (2, HALF, SIZE), (2, SIZE, HALF), (2, 2, HALF, HALF)
    shapes = [(2, SIZE, SIZE), rows, rows, columns, columns, corners, corners, (2 * count, HALF)]
    return pl.pallas_call(
        place_kernel,
        out_shape=shaped(shapes),
        grid_spec=pltpu.PrefetchScalarGridSpec(
            num_scalar_prefetch=1,
            grid=(count,),
            in_specs=[stepped(*fields), stepped(*fields), whole(*probe.shape)],
            out_specs=[whole(*s) for s in shapes],
            scratch_shapes=[
                pltpu.VMEM((2, 2, SIZE + 16, HALF), F32),
                pltpu.VMEM((SIZE, SIZE), F32),
                pltpu.VMEM((2, 5, 2 * SIZE, HALF), F32),
            ],
        ),
        compiler_params=params(),
        cost_estimate=cost(5 << 30, 8 << 20),
    )(starts, object_part, patch, probe)


def illuminate(starts, around, probe):
    scratch = [(2, SIZE, HALF), (7, 3 * SIZE, HALF)]
    return simple(light_kernel, [starts, around], [probe], (SIZE, SIZE), scratch, 2 << 30, 4 << 20)


def update(arrays):
    shape = arrays[0].shape
    return simple(update_kernel, [], arrays, shape, [shape], 1 << 20, 3 << 20)


def assemble(mine, other):
    return simple(assemble_kernel, [], [mine, other], (4, SIZE, SIZE), [], 1 << 20, 2 << 20)


def pairs_from(first, count):
    pairs = []
    for i in range(first, count - 1, 2):
        pairs += [(i, i + 1), (i + 1, i)]
    return pairs


def swap_rows(value, first):
    return lax.ppermute(value, "row", pairs_from(first, lax.axis_size("row")))


def swap_columns(value, first):
    return lax.ppermute(value, "col", pairs_from(first, lax.axis_size("col")))


def half_lanes(value, first):
    return jnp.where(first, value[..., :HALF], value[..., HALF:])


def local(object_tile, probe, amplitudes, offsets):
    starts = offsets[0, 0].T
    measured = amplitudes[0, 0]
    core = lax.rem(lax.axis_index("col"), 2)
    devices = lax.axis_size("row") * lax.axis_size("col")
    groups = [[i for i in range(devices) if i % 2 == k] for k in range(2)]

    with jax.named_scope("object_halo"):
        even, odd, cross, same = pack(starts, object_tile)
        odd = swap_rows(odd, 1)
        even = swap_rows(even, 0)
        cross = swap_columns(cross, 1)
        same = swap_columns(same, 0)
    permuted = prepare(measured)
    with jax.named_scope("object_corners"):
        even, odd, cross, same, permuted = lax.optimization_barrier((even, odd, cross, same, permuted))
        rows = jnp.stack([even, odd])
        cross_corner = swap_columns(half_lanes(rows, core == 0), 1)
        same_corner = swap_columns(half_lanes(rows, core == 1), 0)

    halo = [even, odd, cross, same, cross_corner, same_corner]
    keep, send, object_part, patch, around = transforms(starts, object_tile, halo, probe, permuted)

    parts = place_parts(starts, object_part, patch, probe)
    with jax.named_scope("probe_reduce"):
        chunk, parts, around = lax.optimization_barrier((keep + swap_columns(send, 0), parts, around))
        chunk = lax.all_to_all(chunk, AXES, 0, 0, axis_index_groups=groups, tiled=True)
    center, even, odd, cross, same, cross_corner, same_corner, steps = parts

    with jax.named_scope("gradient_corners"):
        cross_corner = swap_columns(cross_corner, 1)
        same_corner = swap_columns(same_corner, 0)
        cross = swap_columns(cross, 1)
        same = swap_columns(same, 0)
    with jax.named_scope("gradient_rows"):
        first = jnp.where(core == 0, cross_corner, same_corner)
        second = jnp.where(core == 0, same_corner, cross_corner)
        added = jnp.concatenate([first, second], -1)
        odd, even = odd + added[1], even + added[0]
        light = illuminate(starts, around, probe)
        chunk, light, odd, even = lax.optimization_barrier((chunk, light, odd, even))
        odd = swap_rows(odd, 1)
        even = swap_rows(even, 0)
        object_update = update([center, even, odd, cross, same, light])

    with jax.named_scope("probe_sum"):
        total = jnp.sum(chunk, axis=0)
        quotient = total[:16].reshape(4, 4, HALF) / total[16:20]
        relative_error = (total[20, 0] / total[20, 1]).reshape(1)

    with jax.named_scope("probe_gather"):
        spread_out = jnp.broadcast_to(quotient.reshape(1, 16, HALF), (devices // 2, 16, HALF))
        gathered = lax.all_to_all(spread_out, AXES, 0, 0, axis_index_groups=groups, tiled=True)
        gathered, object_update = lax.optimization_barrier((gathered, object_update))
        probe_update = assemble(gathered, swap_columns(gathered, 0)).reshape(probe.shape)

    position_step = steps[:, 0].reshape(1, 1, -1, 2)
    return (object_update, probe_update, position_step, relative_error)


def solution(mesh):
    in_specs = (
        P(None, "row", "col"),
        P(),
        P("row", "col", None, None, None),
        P("row", "col", None, None),
    )
    out_specs = (P(None, "row", "col"), P(), P("row", "col", None, None), P())
    return jax.shard_map(local, mesh=mesh, in_specs=in_specs, out_specs=out_specs, check_vma=False)
```

```python
import jax
import jax.numpy as jnp
import ml_dtypes
import numpy as np
from jax import lax
from jax.experimental import pallas as pl
from jax.experimental.pallas import tpu as pltpu
from jax.sharding import PartitionSpec as P

intensity_floor = 0.1
object_damping = 1.0
small_value = 1e-06

SIZE = 256
HALF = 128
CHUNK = 32
BF = jnp.bfloat16
F32 = jnp.float32
AXES = ("row", "col")
VMEM_LIMIT = 32 * 2**20


def transform_matrices():
    n = np.arange(HALF)[:, None]
    q = np.arange(HALF)[None, :]
    out = []
    for odd in (0, 1):
        angle = -2.0 * np.pi * ((n * (2 * q + odd)) % SIZE) / SIZE
        re, im = np.cos(angle) / 16.0, np.sin(angle) / 16.0
        out.append(np.block([[re, im], [-im, re]]))
    return out


def split_np(matrix):
    high = matrix.astype(ml_dtypes.bfloat16)
    low = (matrix - high.astype(np.float64)).astype(ml_dtypes.bfloat16)
    return high, low


def constants():
    return np.stack([np.stack([np.stack(split_np(x)) for x in (m, m.T)]) for m in transform_matrices()])


def permutation():
    order = np.concatenate([np.arange(0, SIZE, 2), np.arange(1, SIZE, 2)])
    onehot = np.zeros((SIZE, SIZE), np.float32)
    onehot[order, np.arange(SIZE)] = 1.0
    columns = np.concatenate([onehot] * 3, 0).astype(ml_dtypes.bfloat16)
    rows = np.concatenate([onehot.T] * 3, 1).astype(ml_dtypes.bfloat16)
    return columns, rows


def split2(value):
    high = value.astype(BF)
    return high, (value - high.astype(F32)).astype(BF)


def split3(value):
    high = value.astype(BF)
    rest = value - high.astype(F32)
    middle = rest.astype(BF)
    return high, middle, (rest - middle.astype(F32)).astype(BF)


def dot(a, b):
    return jnp.dot(a, b, preferred_element_type=F32)


def lane_index(rows):
    return lax.broadcasted_iota(jnp.int32, (rows, HALF), 1)


def spread(first, second, shift, lanes):
    a = pltpu.roll(first, shift, 1)
    b = pltpu.roll(second, shift, 1)
    wrapped = lanes < shift
    return jnp.where(wrapped, 0.0, a), jnp.where(wrapped, a, b), jnp.where(wrapped, b, 0.0)


def gather_lanes(blocks, shift, lanes):
    back = jnp.where(shift == 0, 0, HALF - shift)
    a, b, c = [pltpu.roll(x, back, 1) for x in blocks]
    inside = lanes < HALF - shift
    return jnp.where(inside, a, b), jnp.where(inside, b, c)


def fold8(value):
    return jnp.sum(value.reshape(-1, 8, HALF), axis=0)


def prepare_kernel(measured, cols, rows, permuted):
    for j in range(measured.shape[0]):
        moved = dot(jnp.concatenate(split3(measured[j]), 1), cols[...])
        permuted[j] = dot(rows[...], jnp.concatenate(split3(moved), 0))


def place_of():
    return lax.rem(lax.axis_index("row"), 2), lax.rem(lax.axis_index("col"), 2)


def run_all(copies):
    for copy in copies:
        copy.start()
    for copy in copies:
        copy.wait()


def pack_kernel(starts, own, even, odd, cross, same, offsets, sems):
    row_odd, core = place_of()
    lanes = lane_index(8)
    value = jnp.zeros((8, HALF), F32)
    for j in range(starts.shape[1]):
        for d in range(2):
            value = jnp.where(lanes == 2 * j + d, (starts[d, j] + 1).astype(F32), value)
    for p in range(2):
        offsets[p, :, :HALF] = value
        offsets[p, :, HALF:] = value
    top = pl.ds(pl.multiple_of(HALF * row_odd, HALF), HALF)
    bottom = pl.ds(pl.multiple_of(HALF * (1 - row_odd), HALF), HALF)
    near = pl.ds(pl.multiple_of(HALF * core, HALF), HALF)
    far = pl.ds(pl.multiple_of(HALF * (1 - core), HALF), HALF)
    moves = [
        (own.at[:, top, :], odd.at[:, :HALF, :]),
        (own.at[:, bottom, :], even.at[:, :HALF, :]),
        (own.at[:, :, near], cross.at[:, :SIZE, :]),
        (own.at[:, :, far], same.at[:, :SIZE, :]),
        (offsets, odd.at[:, HALF:, :]),
        (offsets, even.at[:, HALF:, :]),
        (offsets.at[:, :, :HALF], cross.at[:, SIZE:, :]),
        (offsets.at[:, :, :HALF], same.at[:, SIZE:, :]),
    ]
    run_all([pltpu.make_async_copy(x, y, sems.at[n]) for n, (x, y) in enumerate(moves)])


def sides():
    row_odd, core = place_of()
    even_rows = pl.ds(pl.multiple_of(3 * HALF * (1 - row_odd), HALF), HALF)
    odd_rows = pl.ds(pl.multiple_of(3 * HALF * row_odd, HALF), HALF)
    return even_rows, odd_rows, 3 * core, 3 - 3 * core


def transform_kernel(
    starts, own, odd_strip, even_strip, cross, same, cross_corner, same_corner, probe_in, matrices, measured,
    keep, send, object_part, patch, around,
    tile, probe, mats, offsets, totals, xs, zs, gs, ys, back, sums, sems,
):
    step = pl.program_id(0)
    modes = probe.shape[0]
    lanes = lane_index(CHUNK)
    late = pltpu.make_async_copy(matrices, mats, sems.at[0])

    @pl.when(step == 0)
    def _():
        late.start()
        even_rows, odd_rows, cross_block, same_block = sides()
        center = pl.ds(HALF, SIZE)
        moves = [(probe_in, probe)]
        for block, strip, corner in ((cross_block, cross, cross_corner), (same_block, same, same_corner)):
            moves.append((strip.at[:, :SIZE, :], tile.at[:, block, center, :]))
            moves.append((corner.at[1, :, :HALF, :], tile.at[:, block, even_rows, :]))
            moves.append((corner.at[0, :, :HALF, :], tile.at[:, block, odd_rows, :]))
        for b in range(2):
            span = pl.ds(b * HALF, HALF)
            moves.append((own.at[:, :, span], tile.at[:, 1 + b, center, :]))
            moves.append((even_strip.at[:, :HALF, span], tile.at[:, 1 + b, even_rows, :]))
            moves.append((odd_strip.at[:, :HALF, span], tile.at[:, 1 + b, odd_rows, :]))
        strips = [x.at[0] for x in (odd_strip, even_strip, cross, same)]
        strips += [x.at[n, 0] for x in (cross_corner, same_corner) for n in range(2)]
        for n, strip in enumerate(strips):
            moves.append((strip.at[pl.ds(strip.shape[0] - 8, 8), pl.ds(0, HALF)], offsets.at[n]))
        copies = [pltpu.make_async_copy(x, y, sems.at[1 + n]) for n, (x, y) in enumerate(moves)]
        for copy in copies:
            copy.start()
        tile[:, 4] = jnp.zeros((2, 2 * SIZE, HALF), F32)
        totals[...] = jnp.zeros_like(totals)
        sums[...] = jnp.zeros_like(sums)
        for copy in copies:
            copy.wait()
        for n in range(8):
            around[pl.ds(n, 1), :] = offsets[n, :1, :].astype(jnp.int32)

    row, col = starts[0, step], starts[1, step]
    base, shift = col // HALF, lax.rem(col, HALF)

    for i in range(0, SIZE, CHUNK):
        part = pl.ds(i, CHUNK)
        where = pl.ds(row + i, CHUNK)
        obj = []
        for p in range(2):
            blocks = [tile[p, base + b, where, :] for b in range(3)]
            obj.append(gather_lanes(blocks, shift, lanes))
            for b in range(2):
                patch[0, p, b, part, :] = obj[p][b]
        for m in range(modes):
            wave = []
            for b in range(2):
                span = slice(b * HALF, (b + 1) * HALF)
                pr, pi = probe[m, 0, part, span], probe[m, 1, part, span]
                wave.append((pr * obj[0][b] - pi * obj[1][b], pr * obj[1][b] + pi * obj[0][b]))
            for odd in range(2):
                for p in range(2):
                    high, low = split2(wave[0][p] - wave[1][p] if odd else wave[0][p] + wave[1][p])
                    at = pl.ds(m * SIZE + i, CHUNK)
                    xs[odd, at, p * HALF : (p + 1) * HALF] = high
                    xs[odd, at, SIZE + p * HALF : SIZE + (p + 1) * HALF] = low
                    xs[odd, at, 2 * SIZE + p * HALF : 2 * SIZE + (p + 1) * HALF] = high

    @pl.when(step == 0)
    def _():
        late.wait()

    def right(odd, transposed):
        high, low = mats[odd, transposed, 0], mats[odd, transposed, 1]
        return jnp.concatenate([high, high, low], 0)

    def left(odd, transposed):
        high, low = mats[odd, transposed, 0], mats[odd, transposed, 1]
        return jnp.concatenate([high, low, high], 1)

    for odd in range(2):
        ys[odd] = dot(xs[odd], right(odd, 0))

    for m in range(modes):
        for odd in range(2):
            lane_span = slice(odd * HALF, (odd + 1) * HALF)
            for i in range(0, HALF, CHUNK):
                top = ys[odd, pl.ds(m * SIZE + i, CHUNK), :]
                bottom = ys[odd, pl.ds(m * SIZE + HALF + i, CHUNK), :]
                for odd_row in range(2):
                    high, low = split2(top - bottom if odd_row else top + bottom)
                    for p in range(2):
                        span = slice(p * HALF, (p + 1) * HALF)
                        at = p * HALF + i
                        zs[m, odd_row, pl.ds(at, CHUNK), lane_span] = high[:, span]
                        zs[m, odd_row, pl.ds(SIZE + at, CHUNK), lane_span] = high[:, span]
                        zs[m, odd_row, pl.ds(2 * SIZE + at, CHUNK), lane_span] = low[:, span]

    error = jnp.zeros((8, HALF), F32)
    energy = jnp.zeros((8, HALF), F32)
    for odd_row in range(2):
        far = [dot(left(odd_row, 1), zs[m, odd_row]) for m in range(modes)]
        for i in range(0, HALF, CHUNK):
            parts = [(f[i : i + CHUNK], f[HALF + i : HALF + i + CHUNK]) for f in far]
            intensity = parts[0][0] ** 2 + parts[0][1] ** 2 + (parts[1][0] ** 2 + parts[1][1] ** 2)
            intensity = jnp.maximum(intensity, intensity_floor)
            inverse = lax.rsqrt(intensity)
            modulus = intensity * inverse
            amplitude = measured[0, pl.ds(odd_row * HALF + i, CHUNK), :]
            factor = 1.0 - amplitude * inverse
            misfit = (modulus - amplitude) ** 2
            strength = amplitude**2
            error = error + fold8(misfit[:, :HALF]) + fold8(misfit[:, HALF:])
            energy = energy + fold8(strength[:, :HALF]) + fold8(strength[:, HALF:])
            for m in range(modes):
                for p in range(2):
                    high, low = split2(parts[m][p] * factor)
                    at = p * HALF + i
                    gs[m, odd_row, pl.ds(at, CHUNK), :] = high
                    gs[m, odd_row, pl.ds(SIZE + at, CHUNK), :] = high
                    gs[m, odd_row, pl.ds(2 * SIZE + at, CHUNK), :] = low
    sums[0] += error
    sums[1] += energy

    for m in range(modes):
        even = dot(left(0, 0), gs[m, 0])
        odds = dot(left(1, 0), gs[m, 1])
        for i in range(0, HALF, CHUNK):
            for p in range(2):
                a, b = even[p * HALF + i : p * HALF + i + CHUNK], odds[p * HALF + i : p * HALF + i + CHUNK]
                for bottom in range(2):
                    high, low = split2(a - b if bottom else a + b)
                    at = pl.ds(m * SIZE + bottom * HALF + i, CHUNK)
                    for odd in range(2):
                        span = slice(odd * HALF, (odd + 1) * HALF)
                        xs[odd, at, p * HALF : (p + 1) * HALF] = high[:, span]
                        xs[odd, at, SIZE + p * HALF : SIZE + (p + 1) * HALF] = low[:, span]
                        xs[odd, at, 2 * SIZE + p * HALF : 2 * SIZE + (p + 1) * HALF] = high[:, span]

    for odd in range(2):
        back[odd] = dot(xs[odd], right(odd, 1))

    for i in range(0, SIZE, CHUNK):
        part = pl.ds(i, CHUNK)
        for b in range(2):
            re, im = patch[0, 0, b, part, :], patch[0, 1, b, part, :]
            span = slice(b * HALF, (b + 1) * HALF)
            grad_re, grad_im = 0.0, 0.0
            for m in range(modes):
                at = pl.ds(m * SIZE + i, CHUNK)
                even = [back[0, at, p * HALF : (p + 1) * HALF] for p in range(2)]
                odds = [back[1, at, p * HALF : (p + 1) * HALF] for p in range(2)]
                br, bi = [x - y if b else x + y for x, y in zip(even, odds)]
                pr, pi = probe[m, 0, part, span], probe[m, 1, part, span]
                grad_re = grad_re + (pr * br + pi * bi)
                grad_im = grad_im + (pr * bi - pi * br)
                totals[b, 2 * m, part, :] += re * br + im * bi
                totals[b, 2 * m + 1, part, :] += re * bi - im * br
            object_part[0, 0, b, part, :] = grad_re
            object_part[0, 1, b, part, :] = grad_im
            totals[b, 4, part, :] += re**2 + im**2

    @pl.when(step == pl.num_programs(0) - 1)
    def _():
        core = place_of()[1]
        scalar = jnp.where(lax.broadcasted_iota(jnp.int32, (1, 4, HALF), 2) == 0, jnp.sum(sums[0]), jnp.sum(sums[1]))
        for out, block in ((keep, core), (send, 1 - core)):
            for c in range(5):
                out[:, 4 * c : 4 * c + 4, :] = totals[block, c].reshape(64, 4, HALF)
            out[:, 20:24, :] = jnp.broadcast_to(scalar, (64, 4, HALF))


def place_kernel(
    starts, object_part, patch, probe,
    center, even, odd, cross, same, cross_corner, same_corner, steps,
    padded, power, accum,
):
    step = pl.program_id(0)
    lanes = lane_index(CHUNK)

    @pl.when(step == 0)
    def _():
        accum[...] = jnp.zeros_like(accum)
        padded[:, :, 0:8, :] = jnp.zeros((2, 2, 8, HALF), F32)
        padded[:, :, 264:272, :] = jnp.zeros((2, 2, 8, HALF), F32)
        for i in range(0, SIZE, CHUNK):
            part = pl.ds(i, CHUNK)
            power[part] = probe_power(probe, part)

    row, col = starts[0, step], starts[1, step]
    base, shift = col // HALF, lax.rem(col, HALF)
    for p in range(2):
        for b in range(2):
            padded[p, b, 8:264] = patch[0, p, b]

    first, last = lanes == 0, lanes == HALF - 1
    parts = [jnp.zeros((8, HALF), F32) for _ in range(4)]
    for i in range(0, SIZE, CHUNK):
        part = pl.ds(i, CHUNK)
        where = pl.ds(row + i, CHUNK)
        grads = [[object_part[0, p, b, part, :] for b in range(2)] for p in range(2)]
        strength = [power[part, :HALF], power[part, HALF:]]
        for p, pair in enumerate(grads):
            moved = spread(pair[0], pair[1], shift, lanes)
            for b in range(3):
                accum[p, base + b, where, :] += moved[b]
        columns = []
        for p in range(2):
            obj = [patch[0, p, b, part, :] for b in range(2)]
            before = [pltpu.roll(x, 1, 1) for x in obj]
            after = [pltpu.roll(x, HALF - 1, 1) for x in obj]
            columns.append(
                (
                    jnp.where(last, after[1], after[0]) - jnp.where(first, 0.0, before[0]),
                    jnp.where(last, 0.0, after[1]) - jnp.where(first, before[0], before[1]),
                )
            )
        for b in range(2):
            rows = [padded[p, b, pl.ds(9 + i, CHUNK), :] - padded[p, b, pl.ds(7 + i, CHUNK), :] for p in range(2)]
            for d, slope in enumerate((rows, [columns[0][b], columns[1][b]])):
                parts[2 * d] = parts[2 * d] + fold8(grads[0][b] * slope[0] + grads[1][b] * slope[1])
                parts[2 * d + 1] = parts[2 * d + 1] + fold8(strength[b] * (slope[0] ** 2 + slope[1] ** 2))

    for d in range(2):
        numerator = 0.5 * jnp.sum(parts[2 * d], keepdims=True)
        denominator = 0.25 * jnp.sum(parts[2 * d + 1], keepdims=True) + small_value
        steps[pl.ds(2 * step + d, 1), :] = jnp.broadcast_to(-numerator / denominator, (1, HALF))

    @pl.when(step == pl.num_programs(0) - 1)
    def _():
        even_rows, odd_rows, cross_block, same_block = sides()
        for p in range(2):
            for b in range(2):
                span = slice(b * HALF, (b + 1) * HALF)
                center[p, :, span] = accum[p, 1 + b, 128:384]
                even[p, :, span] = accum[p, 1 + b, even_rows]
                odd[p, :, span] = accum[p, 1 + b, odd_rows]
            for block, strip, corner in ((cross_block, cross, cross_corner), (same_block, same, same_corner)):
                strip[p] = accum[p, block, 128:384]
                corner[0, p] = accum[p, block, even_rows]
                corner[1, p] = accum[p, block, odd_rows]


def probe_power(probe, part):
    return (probe[0, 0, part] ** 2 + probe[0, 1, part] ** 2) + (probe[1, 0, part] ** 2 + probe[1, 1, part] ** 2)


def light_kernel(starts, around, probe, light, power, accum):
    accum[...] = jnp.zeros_like(accum)
    for i in range(0, SIZE, CHUNK):
        part = pl.ds(i, CHUNK)
        total = probe_power(probe, part)
        power[0, part] = total[:, :HALF]
        power[1, part] = total[:, HALF:]
    lanes = lane_index(CHUNK)
    row_odd, core = place_of()
    even, cross = 1 - 2 * row_odd, 2 * core - 1
    neighbours = [(-even, None), (even, None), (None, cross), (None, -cross)]
    neighbours += [(-even, cross), (even, cross), (-even, -cross), (even, -cross)]

    def add(row, col, down, right):
        rows, source_row, row = (SIZE, 0, row + HALF) if down is None else (
            HALF, pl.multiple_of(jnp.where(down < 0, HALF, 0), HALF), row + jnp.where(down < 0, 0, 3 * HALF)
        )
        if right is None:
            col = col + HALF
        else:
            source = jnp.where(right < 0, 1, 0)
            col = col + jnp.where(right < 0, 0, 3 * HALF)
        base, shift = col // HALF, lax.rem(col, HALF)
        for i in range(0, rows, CHUNK):
            part = pl.ds(source_row + i, CHUNK)
            where = pl.ds(row + i, CHUNK)
            if right is None:
                moved = spread(power[0, part], power[1, part], shift, lanes)
            else:
                rolled = pltpu.roll(power[source, part], shift, 1)
                moved = jnp.where(lanes < shift, 0.0, rolled), jnp.where(lanes < shift, rolled, 0.0)
            for b, value in enumerate(moved):
                accum[base + b, where, :] += value

    count = starts.shape[1]
    for j in range(count):
        add(starts[0, j], starts[1, j], None, None)
    for n, (down, right) in enumerate(neighbours):
        for j in range(count):
            row, col = around[n, 2 * j] - 1, around[n, 2 * j + 1] - 1
            near = row >= 0
            if down is not None:
                near = near & jnp.where(down < 0, row > HALF, row < HALF)
            if right is not None:
                near = near & jnp.where(right < 0, col > HALF, col < HALF)

            @pl.when(near)
            def _(row=row, col=col, down=down, right=right):
                add(row, col, down, right)

    light[:, :HALF] = accum[2, 256:512]
    light[:, HALF:] = accum[3, 256:512]


def quotient_kernel(chunk, spread_out, ratio):
    total = jnp.sum(chunk[...], axis=0)
    power = total[16:20]
    for c in range(4):
        quotient = total[4 * c : 4 * c + 4] / power
        spread_out[:, 4 * c : 4 * c + 4, :] = jnp.broadcast_to(quotient[None], (64, 4, HALF))
    ratio[...] = jnp.broadcast_to(total[20:21, 0:1] / total[20:21, 1:2], (8, HALF))


def update_kernel(center, even, odd, cross, same, light, out, total):
    for p in range(2):
        total[p] = center[p]
    row_odd, core = place_of()
    even_half = pl.ds(pl.multiple_of(HALF * (1 - row_odd), HALF), HALF)
    odd_half = pl.ds(pl.multiple_of(HALF * row_odd, HALF), HALF)
    for p in range(2):
        total[p, even_half, :] += even[p]
        total[p, odd_half, :] += odd[p]
    swapped = core == 1
    for i in range(0, SIZE, CHUNK):
        part = pl.ds(i, CHUNK)
        scale = 1.0 / (light[part] + object_damping)
        for p in range(2):
            a, b = cross[p, part], same[p, part]
            out[p, part, :HALF] = (total[p, part, :HALF] + jnp.where(swapped, b, a)) * scale[:, :HALF]
            out[p, part, HALF:] = (total[p, part, HALF:] + jnp.where(swapped, a, b)) * scale[:, HALF:]


def assemble_kernel(mine, other, out):
    core = place_of()[1]

    def write(source, block):
        for c in range(4):
            out[c, :, block * HALF : (block + 1) * HALF] = source[:, 4 * c : 4 * c + 4, :].reshape(SIZE, HALF)

    @pl.when(core == 0)
    def _():
        write(mine, 0)
        write(other, 1)

    @pl.when(core == 1)
    def _():
        write(mine, 1)
        write(other, 0)


def whole(*shape):
    return pl.BlockSpec(shape, lambda *_: (0,) * len(shape))


ANY = pl.BlockSpec(memory_space=pl.ANY)


def stepped(*shape):
    return pl.BlockSpec((1, *shape), lambda i, *_: (i,) + (0,) * len(shape))


def shaped(shapes):
    return [jax.ShapeDtypeStruct(s, F32) for s in shapes]


def params():
    return pltpu.CompilerParams(vmem_limit_bytes=VMEM_LIMIT)


def cost(flops, size):
    return pl.CostEstimate(flops=flops, bytes_accessed=size, transcendentals=0)


def simple(kernel, scalars, arrays, shapes, scratch, flops, size):
    single = not isinstance(shapes, list)
    outs = [shapes] if single else shapes
    call = pl.pallas_call(
        kernel,
        out_shape=shaped(outs)[0] if single else shaped(outs),
        grid_spec=pltpu.PrefetchScalarGridSpec(
            num_scalar_prefetch=len(scalars),
            grid=(),
            in_specs=[whole(*x.shape) for x in arrays],
            out_specs=whole(*shapes) if single else [whole(*s) for s in outs],
            scratch_shapes=[pltpu.VMEM(s, F32) for s in scratch],
        ),
        compiler_params=params(),
        cost_estimate=cost(flops, size),
    )
    return call(*scalars, *arrays)


def pack(starts, own):
    rows, columns = (2, HALF + 8, SIZE), (2, SIZE + 8, HALF)
    return pl.pallas_call(
        pack_kernel,
        out_shape=shaped([rows, rows, columns, columns]),
        grid_spec=pltpu.PrefetchScalarGridSpec(
            num_scalar_prefetch=1,
            grid=(),
            in_specs=[pl.BlockSpec(memory_space=pltpu.HBM)],
            out_specs=[ANY] * 4,
            scratch_shapes=[pltpu.VMEM((2, 8, SIZE), F32), pltpu.SemaphoreType.DMA((8,))],
        ),
        compiler_params=params(),
        cost_estimate=cost(1 << 10, 2 << 20),
    )(starts, own)


def prepare(measured):
    cols, rows = permutation()
    arrays = [measured, jnp.asarray(cols), jnp.asarray(rows)]
    return simple(prepare_kernel, [], arrays, measured.shape, [], 1 << 30, 3 << 20)


def transforms(starts, own, halo, probe, measured):
    mats = jnp.asarray(constants())
    arrays = [own, *halo, probe, mats]
    count = measured.shape[0]
    halves = (64, 24, HALF)
    fields = (2, 2, SIZE, HALF)
    return pl.pallas_call(
        transform_kernel,
        out_shape=shaped([halves, halves, (count, *fields), (count, *fields)])
        + [jax.ShapeDtypeStruct((8, HALF), jnp.int32)],
        grid_spec=pltpu.PrefetchScalarGridSpec(
            num_scalar_prefetch=1,
            grid=(count,),
            in_specs=[ANY] * len(arrays) + [stepped(SIZE, SIZE)],
            out_specs=[whole(*halves), whole(*halves), stepped(*fields), stepped(*fields), whole(8, HALF)],
            scratch_shapes=[
                pltpu.VMEM((2, 5, 2 * SIZE, HALF), F32),
                pltpu.VMEM(probe.shape, F32),
                pltpu.VMEM(mats.shape, BF),
                pltpu.VMEM((8, 8, HALF), F32),
                pltpu.VMEM((2, 5, SIZE, HALF), F32),
                pltpu.VMEM((2, 2 * SIZE, 3 * SIZE), BF),
                pltpu.VMEM((2, 2, 3 * SIZE, SIZE), BF),
                pltpu.VMEM((2, 2, 3 * SIZE, SIZE), BF),
                pltpu.VMEM((2, 2 * SIZE, SIZE), F32),
                pltpu.VMEM((2, 2 * SIZE, SIZE), F32),
                pltpu.VMEM((2, 8, HALF), F32),
                pltpu.SemaphoreType.DMA((24,)),
            ],
        ),
        compiler_params=params(),
        cost_estimate=cost(13 << 30, 12 << 20),
    )(starts, *arrays, measured)


def place_parts(starts, object_part, patch, probe):
    count = patch.shape[0]
    fields = (2, 2, SIZE, HALF)
    rows, columns, corners = (2, HALF, SIZE), (2, SIZE, HALF), (2, 2, HALF, HALF)
    shapes = [(2, SIZE, SIZE), rows, rows, columns, columns, corners, corners, (2 * count, HALF)]
    return pl.pallas_call(
        place_kernel,
        out_shape=shaped(shapes),
        grid_spec=pltpu.PrefetchScalarGridSpec(
            num_scalar_prefetch=1,
            grid=(count,),
            in_specs=[stepped(*fields), stepped(*fields), whole(*probe.shape)],
            out_specs=[whole(*s) for s in shapes],
            scratch_shapes=[
                pltpu.VMEM((2, 2, SIZE + 16, HALF), F32),
                pltpu.VMEM((SIZE, SIZE), F32),
                pltpu.VMEM((2, 5, 2 * SIZE, HALF), F32),
            ],
        ),
        compiler_params=params(),
        cost_estimate=cost(5 << 30, 8 << 20),
    )(starts, object_part, patch, probe)


def illuminate(starts, around, probe):
    scratch = [(2, SIZE, HALF), (7, 3 * SIZE, HALF)]
    return simple(light_kernel, [starts, around], [probe], (SIZE, SIZE), scratch, 2 << 30, 4 << 20)


def update(arrays):
    shape = arrays[0].shape
    return simple(update_kernel, [], arrays, shape, [shape], 1 << 20, 3 << 20)


def assemble(mine, other):
    return simple(assemble_kernel, [], [mine, other], (4, SIZE, SIZE), [], 1 << 20, 2 << 20)


def pairs_from(first, count):
    pairs = []
    for i in range(first, count - 1, 2):
        pairs += [(i, i + 1), (i + 1, i)]
    return pairs


def swap_rows(value, first):
    return lax.ppermute(value, "row", pairs_from(first, lax.axis_size("row")))


def swap_columns(value, first):
    return lax.ppermute(value, "col", pairs_from(first, lax.axis_size("col")))


def half_lanes(value, first):
    return jnp.where(first, value[..., :HALF], value[..., HALF:])


def local(object_tile, probe, amplitudes, offsets):
    starts = offsets[0, 0].T
    measured = amplitudes[0, 0]
    core = lax.rem(lax.axis_index("col"), 2)
    devices = lax.axis_size("row") * lax.axis_size("col")
    groups = [[i for i in range(devices) if i % 2 == k] for k in range(2)]

    with jax.named_scope("object_halo"):
        even, odd, cross, same = pack(starts, object_tile)
        odd = swap_rows(odd, 1)
        even = swap_rows(even, 0)
        cross = swap_columns(cross, 1)
        same = swap_columns(same, 0)
    permuted = prepare(measured)
    with jax.named_scope("object_corners"):
        odd, even, cross, same, permuted = lax.optimization_barrier((odd, even, cross, same, permuted))
        rows = jnp.stack([odd, even])
        cross_corner = swap_columns(half_lanes(rows, core == 0), 1)
        same_corner = swap_columns(half_lanes(rows, core == 1), 0)

    halo = [odd, even, cross, same, cross_corner, same_corner]
    keep, send, object_part, patch, around = transforms(starts, object_tile, halo, probe, permuted)

    parts = place_parts(starts, object_part, patch, probe)
    with jax.named_scope("probe_reduce"):
        chunk, parts, around = lax.optimization_barrier((keep + swap_columns(send, 0), parts, around))
        chunk = lax.all_to_all(chunk, AXES, 0, 0, axis_index_groups=groups, tiled=True)
    center, even, odd, cross, same, cross_corner, same_corner, steps = parts

    with jax.named_scope("gradient_corners"):
        cross_corner = swap_columns(cross_corner, 1)
        same_corner = swap_columns(same_corner, 0)
        cross = swap_columns(cross, 1)
        same = swap_columns(same, 0)
    with jax.named_scope("gradient_rows"):
        first = jnp.where(core == 0, cross_corner, same_corner)
        second = jnp.where(core == 0, same_corner, cross_corner)
        added = jnp.concatenate([first, second], -1)
        odd, even = odd + added[1], even + added[0]
        light = illuminate(starts, around, probe)
        chunk, light, odd, even = lax.optimization_barrier((chunk, light, odd, even))
        odd = swap_rows(odd, 1)
        even = swap_rows(even, 0)
        object_update = update([center, even, odd, cross, same, light])

    with jax.named_scope("probe_gather"):
        spread_out, ratio = simple(quotient_kernel, [], [chunk], [(64, 16, HALF), (8, HALF)], [], 1 << 20, 2 << 20)
        gathered = lax.all_to_all(spread_out, AXES, 0, 0, axis_index_groups=groups, tiled=True)
        probe_update = assemble(gathered, swap_columns(gathered, 0)).reshape(probe.shape)

    relative_error = ratio[0, :1]
    position_step = steps[:, 0].reshape(1, 1, -1, 2)
    return (object_update, probe_update, position_step, relative_error)


def solution(mesh):
    in_specs = (
        P(None, "row", "col"),
        P(),
        P("row", "col", None, None, None),
        P("row", "col", None, None),
    )
    out_specs = (P(None, "row", "col"), P(), P("row", "col", None, None), P())
    return jax.shard_map(local, mesh=mesh, in_specs=in_specs, out_specs=out_specs, check_vma=False)
```

```python
import jax
import jax.numpy as jnp
import ml_dtypes
import numpy as np
from jax import lax
from jax.experimental import pallas as pl
from jax.experimental.pallas import tpu as pltpu
from jax.sharding import PartitionSpec as P

intensity_floor = 0.1
object_damping = 1.0
small_value = 1e-06

SIZE = 256
HALF = 128
CHUNK = 32
BF = jnp.bfloat16
F32 = jnp.float32
AXES = ("row", "col")
VMEM_LIMIT = 32 * 2**20


def transform_matrices():
    n = np.arange(HALF)[:, None]
    q = np.arange(HALF)[None, :]
    out = []
    for odd in (0, 1):
        angle = -2.0 * np.pi * ((n * (2 * q + odd)) % SIZE) / SIZE
        re, im = np.cos(angle) / 16.0, np.sin(angle) / 16.0
        out.append(np.block([[re, im], [-im, re]]))
    return out


def split_np(matrix):
    high = matrix.astype(ml_dtypes.bfloat16)
    low = (matrix - high.astype(np.float64)).astype(ml_dtypes.bfloat16)
    return high, low


def constants():
    return np.stack([np.stack([np.stack(split_np(x)) for x in (m, m.T)]) for m in transform_matrices()])


def permutation():
    order = np.concatenate([np.arange(0, SIZE, 2), np.arange(1, SIZE, 2)])
    onehot = np.zeros((SIZE, SIZE), np.float32)
    onehot[order, np.arange(SIZE)] = 1.0
    columns = np.concatenate([onehot] * 3, 0).astype(ml_dtypes.bfloat16)
    rows = np.concatenate([onehot.T] * 3, 1).astype(ml_dtypes.bfloat16)
    return columns, rows


def split2(value):
    high = value.astype(BF)
    return high, (value - high.astype(F32)).astype(BF)


def split3(value):
    high = value.astype(BF)
    rest = value - high.astype(F32)
    middle = rest.astype(BF)
    return high, middle, (rest - middle.astype(F32)).astype(BF)


def dot(a, b):
    return jnp.dot(a, b, preferred_element_type=F32)


def lane_index(rows):
    return lax.broadcasted_iota(jnp.int32, (rows, HALF), 1)


def spread(first, second, shift, lanes):
    a = pltpu.roll(first, shift, 1)
    b = pltpu.roll(second, shift, 1)
    wrapped = lanes < shift
    return jnp.where(wrapped, 0.0, a), jnp.where(wrapped, a, b), jnp.where(wrapped, b, 0.0)


def gather_lanes(blocks, shift, lanes):
    back = jnp.where(shift == 0, 0, HALF - shift)
    a, b, c = [pltpu.roll(x, back, 1) for x in blocks]
    inside = lanes < HALF - shift
    return jnp.where(inside, a, b), jnp.where(inside, b, c)


def fold8(value):
    return jnp.sum(value.reshape(-1, 8, HALF), axis=0)


def prepare_kernel(measured, cols, rows, permuted):
    for j in range(measured.shape[0]):
        moved = dot(jnp.concatenate(split3(measured[j]), 1), cols[...])
        permuted[j] = dot(rows[...], jnp.concatenate(split3(moved), 0))


def place_of():
    return lax.rem(lax.axis_index("row"), 2), lax.rem(lax.axis_index("col"), 2)


def run_all(copies):
    for copy in copies:
        copy.start()
    for copy in copies:
        copy.wait()


def pack_kernel(starts, own, even, odd, cross, same, offsets, sems):
    row_odd, core = place_of()
    lanes = lane_index(8)
    value = jnp.zeros((8, HALF), F32)
    for j in range(starts.shape[1]):
        for d in range(2):
            value = jnp.where(lanes == 2 * j + d, (starts[d, j] + 1).astype(F32), value)
    for p in range(2):
        offsets[p, :, :HALF] = value
        offsets[p, :, HALF:] = value
    top = pl.ds(pl.multiple_of(HALF * row_odd, HALF), HALF)
    bottom = pl.ds(pl.multiple_of(HALF * (1 - row_odd), HALF), HALF)
    near = pl.ds(pl.multiple_of(HALF * core, HALF), HALF)
    far = pl.ds(pl.multiple_of(HALF * (1 - core), HALF), HALF)
    moves = [
        (own.at[:, top, :], odd.at[:, :HALF, :]),
        (own.at[:, bottom, :], even.at[:, :HALF, :]),
        (own.at[:, :, near], cross.at[:, :SIZE, :]),
        (own.at[:, :, far], same.at[:, :SIZE, :]),
        (offsets, odd.at[:, HALF:, :]),
        (offsets, even.at[:, HALF:, :]),
        (offsets.at[:, :, :HALF], cross.at[:, SIZE:, :]),
        (offsets.at[:, :, :HALF], same.at[:, SIZE:, :]),
    ]
    run_all([pltpu.make_async_copy(x, y, sems.at[n]) for n, (x, y) in enumerate(moves)])


def sides():
    row_odd, core = place_of()
    even_rows = pl.ds(pl.multiple_of(3 * HALF * (1 - row_odd), HALF), HALF)
    odd_rows = pl.ds(pl.multiple_of(3 * HALF * row_odd, HALF), HALF)
    return even_rows, odd_rows, 3 * core, 3 - 3 * core


def transform_kernel(
    starts, own, odd_strip, even_strip, cross, same, cross_corner, same_corner, probe_in, matrices, measured,
    keep, send, object_part, patch, around,
    tile, probe, mats, offsets, totals, xs, zs, gs, ys, back, sums, sems,
):
    step = pl.program_id(0)
    modes = probe.shape[0]
    lanes = lane_index(CHUNK)
    late = pltpu.make_async_copy(matrices, mats, sems.at[0])

    @pl.when(step == 0)
    def _():
        late.start()
        even_rows, odd_rows, cross_block, same_block = sides()
        center = pl.ds(HALF, SIZE)
        moves = [(probe_in, probe)]
        for block, strip, corner in ((cross_block, cross, cross_corner), (same_block, same, same_corner)):
            moves.append((strip.at[:, :SIZE, :], tile.at[:, block, center, :]))
            moves.append((corner.at[1, :, :HALF, :], tile.at[:, block, even_rows, :]))
            moves.append((corner.at[0, :, :HALF, :], tile.at[:, block, odd_rows, :]))
        for b in range(2):
            span = pl.ds(b * HALF, HALF)
            moves.append((own.at[:, :, span], tile.at[:, 1 + b, center, :]))
            moves.append((even_strip.at[:, :HALF, span], tile.at[:, 1 + b, even_rows, :]))
            moves.append((odd_strip.at[:, :HALF, span], tile.at[:, 1 + b, odd_rows, :]))
        strips = [x.at[0] for x in (odd_strip, even_strip, cross, same)]
        strips += [x.at[n, 0] for x in (cross_corner, same_corner) for n in range(2)]
        for n, strip in enumerate(strips):
            moves.append((strip.at[pl.ds(strip.shape[0] - 8, 8), pl.ds(0, HALF)], offsets.at[n]))
        copies = [pltpu.make_async_copy(x, y, sems.at[1 + n]) for n, (x, y) in enumerate(moves)]
        for copy in copies:
            copy.start()
        tile[:, 4] = jnp.zeros((2, 2 * SIZE, HALF), F32)
        totals[...] = jnp.zeros_like(totals)
        sums[...] = jnp.zeros_like(sums)
        for copy in copies:
            copy.wait()
        for n in range(8):
            around[pl.ds(n, 1), :] = offsets[n, :1, :].astype(jnp.int32)

    row, col = starts[0, step], starts[1, step]
    base, shift = col // HALF, lax.rem(col, HALF)

    for i in range(0, SIZE, CHUNK):
        part = pl.ds(i, CHUNK)
        where = pl.ds(row + i, CHUNK)
        obj = []
        for p in range(2):
            blocks = [tile[p, base + b, where, :] for b in range(3)]
            obj.append(gather_lanes(blocks, shift, lanes))
            for b in range(2):
                patch[0, p, b, part, :] = obj[p][b]
        for m in range(modes):
            wave = []
            for b in range(2):
                span = slice(b * HALF, (b + 1) * HALF)
                pr, pi = probe[m, 0, part, span], probe[m, 1, part, span]
                wave.append((pr * obj[0][b] - pi * obj[1][b], pr * obj[1][b] + pi * obj[0][b]))
            for odd in range(2):
                for p in range(2):
                    high, low = split2(wave[0][p] - wave[1][p] if odd else wave[0][p] + wave[1][p])
                    at = pl.ds(m * SIZE + i, CHUNK)
                    xs[odd, at, p * HALF : (p + 1) * HALF] = high
                    xs[odd, at, SIZE + p * HALF : SIZE + (p + 1) * HALF] = low
                    xs[odd, at, 2 * SIZE + p * HALF : 2 * SIZE + (p + 1) * HALF] = high

    @pl.when(step == 0)
    def _():
        late.wait()

    def right(odd, transposed):
        high, low = mats[odd, transposed, 0], mats[odd, transposed, 1]
        return jnp.concatenate([high, high, low], 0)

    def left(odd, transposed):
        high, low = mats[odd, transposed, 0], mats[odd, transposed, 1]
        return jnp.concatenate([high, low, high], 1)

    for odd in range(2):
        ys[odd] = dot(xs[odd], right(odd, 0))

    for m in range(modes):
        for odd in range(2):
            lane_span = slice(odd * HALF, (odd + 1) * HALF)
            for i in range(0, HALF, CHUNK):
                top = ys[odd, pl.ds(m * SIZE + i, CHUNK), :]
                bottom = ys[odd, pl.ds(m * SIZE + HALF + i, CHUNK), :]
                for odd_row in range(2):
                    high, low = split2(top - bottom if odd_row else top + bottom)
                    for p in range(2):
                        span = slice(p * HALF, (p + 1) * HALF)
                        at = p * HALF + i
                        zs[m, odd_row, pl.ds(at, CHUNK), lane_span] = high[:, span]
                        zs[m, odd_row, pl.ds(SIZE + at, CHUNK), lane_span] = high[:, span]
                        zs[m, odd_row, pl.ds(2 * SIZE + at, CHUNK), lane_span] = low[:, span]

    error = jnp.zeros((8, HALF), F32)
    energy = jnp.zeros((8, HALF), F32)
    for odd_row in range(2):
        far = [dot(left(odd_row, 1), zs[m, odd_row]) for m in range(modes)]
        for i in range(0, HALF, CHUNK):
            parts = [(f[i : i + CHUNK], f[HALF + i : HALF + i + CHUNK]) for f in far]
            intensity = parts[0][0] ** 2 + parts[0][1] ** 2 + (parts[1][0] ** 2 + parts[1][1] ** 2)
            intensity = jnp.maximum(intensity, intensity_floor)
            inverse = lax.rsqrt(intensity)
            modulus = intensity * inverse
            amplitude = measured[0, pl.ds(odd_row * HALF + i, CHUNK), :]
            factor = 1.0 - amplitude * inverse
            misfit = (modulus - amplitude) ** 2
            strength = amplitude**2
            error = error + fold8(misfit[:, :HALF]) + fold8(misfit[:, HALF:])
            energy = energy + fold8(strength[:, :HALF]) + fold8(strength[:, HALF:])
            for m in range(modes):
                for p in range(2):
                    high, low = split2(parts[m][p] * factor)
                    at = p * HALF + i
                    gs[m, odd_row, pl.ds(at, CHUNK), :] = high
                    gs[m, odd_row, pl.ds(SIZE + at, CHUNK), :] = high
                    gs[m, odd_row, pl.ds(2 * SIZE + at, CHUNK), :] = low
    sums[0] += error
    sums[1] += energy

    for m in range(modes):
        even = dot(left(0, 0), gs[m, 0])
        odds = dot(left(1, 0), gs[m, 1])
        for i in range(0, HALF, CHUNK):
            for p in range(2):
                a, b = even[p * HALF + i : p * HALF + i + CHUNK], odds[p * HALF + i : p * HALF + i + CHUNK]
                for bottom in range(2):
                    high, low = split2(a - b if bottom else a + b)
                    at = pl.ds(m * SIZE + bottom * HALF + i, CHUNK)
                    for odd in range(2):
                        span = slice(odd * HALF, (odd + 1) * HALF)
                        xs[odd, at, p * HALF : (p + 1) * HALF] = high[:, span]
                        xs[odd, at, SIZE + p * HALF : SIZE + (p + 1) * HALF] = low[:, span]
                        xs[odd, at, 2 * SIZE + p * HALF : 2 * SIZE + (p + 1) * HALF] = high[:, span]

    for odd in range(2):
        back[odd] = dot(xs[odd], right(odd, 1))

    for i in range(0, SIZE, CHUNK):
        part = pl.ds(i, CHUNK)
        for b in range(2):
            re, im = patch[0, 0, b, part, :], patch[0, 1, b, part, :]
            span = slice(b * HALF, (b + 1) * HALF)
            grad_re, grad_im = 0.0, 0.0
            for m in range(modes):
                at = pl.ds(m * SIZE + i, CHUNK)
                even = [back[0, at, p * HALF : (p + 1) * HALF] for p in range(2)]
                odds = [back[1, at, p * HALF : (p + 1) * HALF] for p in range(2)]
                br, bi = [x - y if b else x + y for x, y in zip(even, odds)]
                pr, pi = probe[m, 0, part, span], probe[m, 1, part, span]
                grad_re = grad_re + (pr * br + pi * bi)
                grad_im = grad_im + (pr * bi - pi * br)
                totals[b, 2 * m, part, :] += re * br + im * bi
                totals[b, 2 * m + 1, part, :] += re * bi - im * br
            object_part[0, 0, b, part, :] = grad_re
            object_part[0, 1, b, part, :] = grad_im
            totals[b, 4, part, :] += re**2 + im**2

    @pl.when(step == pl.num_programs(0) - 1)
    def _():
        core = place_of()[1]
        scalar = jnp.where(lax.broadcasted_iota(jnp.int32, (1, 8, HALF), 2) == 0, jnp.sum(sums[0]), jnp.sum(sums[1]))
        for out, block in ((keep, core), (send, 1 - core)):
            for c in range(5):
                out[:, 16 * c : 16 * c + 16, :] = totals[block, c].reshape(16, 16, HALF)
            out[:, 80:88, :] = jnp.broadcast_to(scalar, (16, 8, HALF))


def place_kernel(
    starts, object_part, patch, probe,
    center, even, odd, cross, same, cross_corner, same_corner, steps,
    padded, power, accum,
):
    step = pl.program_id(0)
    lanes = lane_index(CHUNK)

    @pl.when(step == 0)
    def _():
        accum[...] = jnp.zeros_like(accum)
        padded[:, :, 0:8, :] = jnp.zeros((2, 2, 8, HALF), F32)
        padded[:, :, 264:272, :] = jnp.zeros((2, 2, 8, HALF), F32)
        for i in range(0, SIZE, CHUNK):
            part = pl.ds(i, CHUNK)
            power[part] = probe_power(probe, part)

    row, col = starts[0, step], starts[1, step]
    base, shift = col // HALF, lax.rem(col, HALF)
    for p in range(2):
        for b in range(2):
            padded[p, b, 8:264] = patch[0, p, b]

    first, last = lanes == 0, lanes == HALF - 1
    parts = [jnp.zeros((8, HALF), F32) for _ in range(4)]
    for i in range(0, SIZE, CHUNK):
        part = pl.ds(i, CHUNK)
        where = pl.ds(row + i, CHUNK)
        grads = [[object_part[0, p, b, part, :] for b in range(2)] for p in range(2)]
        strength = [power[part, :HALF], power[part, HALF:]]
        for p, pair in enumerate(grads):
            moved = spread(pair[0], pair[1], shift, lanes)
            for b in range(3):
                accum[p, base + b, where, :] += moved[b]
        columns = []
        for p in range(2):
            obj = [patch[0, p, b, part, :] for b in range(2)]
            before = [pltpu.roll(x, 1, 1) for x in obj]
            after = [pltpu.roll(x, HALF - 1, 1) for x in obj]
            columns.append(
                (
                    jnp.where(last, after[1], after[0]) - jnp.where(first, 0.0, before[0]),
                    jnp.where(last, 0.0, after[1]) - jnp.where(first, before[0], before[1]),
                )
            )
        for b in range(2):
            rows = [padded[p, b, pl.ds(9 + i, CHUNK), :] - padded[p, b, pl.ds(7 + i, CHUNK), :] for p in range(2)]
            for d, slope in enumerate((rows, [columns[0][b], columns[1][b]])):
                parts[2 * d] = parts[2 * d] + fold8(grads[0][b] * slope[0] + grads[1][b] * slope[1])
                parts[2 * d + 1] = parts[2 * d + 1] + fold8(strength[b] * (slope[0] ** 2 + slope[1] ** 2))

    for d in range(2):
        numerator = 0.5 * jnp.sum(parts[2 * d], keepdims=True)
        denominator = 0.25 * jnp.sum(parts[2 * d + 1], keepdims=True) + small_value
        steps[pl.ds(2 * step + d, 1), :] = jnp.broadcast_to(-numerator / denominator, (1, HALF))

    @pl.when(step == pl.num_programs(0) - 1)
    def _():
        even_rows, odd_rows, cross_block, same_block = sides()
        for p in range(2):
            for b in range(2):
                span = slice(b * HALF, (b + 1) * HALF)
                center[p, :, span] = accum[p, 1 + b, 128:384]
                even[p, :, span] = accum[p, 1 + b, even_rows]
                odd[p, :, span] = accum[p, 1 + b, odd_rows]
            for block, strip, corner in ((cross_block, cross, cross_corner), (same_block, same, same_corner)):
                strip[p] = accum[p, block, 128:384]
                corner[0, p] = accum[p, block, even_rows]
                corner[1, p] = accum[p, block, odd_rows]


def probe_power(probe, part):
    return (probe[0, 0, part] ** 2 + probe[0, 1, part] ** 2) + (probe[1, 0, part] ** 2 + probe[1, 1, part] ** 2)


def light_kernel(starts, around, probe, light, power, accum):
    accum[...] = jnp.zeros_like(accum)
    for i in range(0, SIZE, CHUNK):
        part = pl.ds(i, CHUNK)
        total = probe_power(probe, part)
        power[0, part] = total[:, :HALF]
        power[1, part] = total[:, HALF:]
    lanes = lane_index(CHUNK)
    row_odd, core = place_of()
    even, cross = 1 - 2 * row_odd, 2 * core - 1
    neighbours = [(-even, None), (even, None), (None, cross), (None, -cross)]
    neighbours += [(-even, cross), (even, cross), (-even, -cross), (even, -cross)]

    def add(row, col, down, right):
        rows, source_row, row = (SIZE, 0, row + HALF) if down is None else (
            HALF, pl.multiple_of(jnp.where(down < 0, HALF, 0), HALF), row + jnp.where(down < 0, 0, 3 * HALF)
        )
        if right is None:
            col = col + HALF
        else:
            source = jnp.where(right < 0, 1, 0)
            col = col + jnp.where(right < 0, 0, 3 * HALF)
        base, shift = col // HALF, lax.rem(col, HALF)
        for i in range(0, rows, CHUNK):
            part = pl.ds(source_row + i, CHUNK)
            where = pl.ds(row + i, CHUNK)
            if right is None:
                moved = spread(power[0, part], power[1, part], shift, lanes)
            else:
                rolled = pltpu.roll(power[source, part], shift, 1)
                moved = jnp.where(lanes < shift, 0.0, rolled), jnp.where(lanes < shift, rolled, 0.0)
            for b, value in enumerate(moved):
                accum[base + b, where, :] += value

    count = starts.shape[1]
    for j in range(count):
        add(starts[0, j], starts[1, j], None, None)
    for n, (down, right) in enumerate(neighbours):
        for j in range(count):
            row, col = around[n, 2 * j] - 1, around[n, 2 * j + 1] - 1
            near = row >= 0
            if down is not None:
                near = near & jnp.where(down < 0, row > HALF, row < HALF)
            if right is not None:
                near = near & jnp.where(right < 0, col > HALF, col < HALF)

            @pl.when(near)
            def _(row=row, col=col, down=down, right=right):
                add(row, col, down, right)

    light[:, :HALF] = accum[2, 256:512]
    light[:, HALF:] = accum[3, 256:512]


def sum_kernel(chunk, total):
    total[...] = jnp.sum(chunk[...], axis=0)


def quotient_kernel(own, first, second, third, spread_out, ratio, held):
    z = 2 * lax.div(lax.axis_index("row"), 4) + lax.rem(lax.div(lax.axis_index("col"), 2), 2)
    for distance, part in enumerate((own, first, second, third)):
        held[lax.rem(z + 4 - distance, 4)] = part[...]
    total = (held[0] + held[1]) + (held[2] + held[3])
    for c in range(4):
        quotient = total[16 * c : 16 * c + 16] / total[64:80]
        spread_out[:, 16 * c : 16 * c + 16, :] = jnp.broadcast_to(quotient[None], (16, 16, HALF))
    ratio[...] = jnp.broadcast_to(total[80:81, 0:1] / total[80:81, 1:2], (8, HALF))


def update_kernel(center, even, odd, cross, same, light, out, total):
    for p in range(2):
        total[p] = center[p]
    row_odd, core = place_of()
    even_half = pl.ds(pl.multiple_of(HALF * (1 - row_odd), HALF), HALF)
    odd_half = pl.ds(pl.multiple_of(HALF * row_odd, HALF), HALF)
    for p in range(2):
        total[p, even_half, :] += even[p]
        total[p, odd_half, :] += odd[p]
    swapped = core == 1
    for i in range(0, SIZE, CHUNK):
        part = pl.ds(i, CHUNK)
        scale = 1.0 / (light[part] + object_damping)
        for p in range(2):
            a, b = cross[p, part], same[p, part]
            out[p, part, :HALF] = (total[p, part, :HALF] + jnp.where(swapped, b, a)) * scale[:, :HALF]
            out[p, part, HALF:] = (total[p, part, HALF:] + jnp.where(swapped, a, b)) * scale[:, HALF:]


def assemble_kernel(mine, other, out):
    core = place_of()[1]

    def write(source, block):
        for c in range(4):
            out[c, :, block * HALF : (block + 1) * HALF] = source[:, 16 * c : 16 * c + 16, :].reshape(SIZE, HALF)

    @pl.when(core == 0)
    def _():
        write(mine, 0)
        write(other, 1)

    @pl.when(core == 1)
    def _():
        write(mine, 1)
        write(other, 0)


def whole(*shape):
    return pl.BlockSpec(shape, lambda *_: (0,) * len(shape))


ANY = pl.BlockSpec(memory_space=pl.ANY)


def stepped(*shape):
    return pl.BlockSpec((1, *shape), lambda i, *_: (i,) + (0,) * len(shape))


def shaped(shapes):
    return [jax.ShapeDtypeStruct(s, F32) for s in shapes]


def params():
    return pltpu.CompilerParams(vmem_limit_bytes=VMEM_LIMIT)


def cost(flops, size):
    return pl.CostEstimate(flops=flops, bytes_accessed=size, transcendentals=0)


def simple(kernel, scalars, arrays, shapes, scratch, flops, size):
    single = not isinstance(shapes, list)
    outs = [shapes] if single else shapes
    call = pl.pallas_call(
        kernel,
        out_shape=shaped(outs)[0] if single else shaped(outs),
        grid_spec=pltpu.PrefetchScalarGridSpec(
            num_scalar_prefetch=len(scalars),
            grid=(),
            in_specs=[whole(*x.shape) for x in arrays],
            out_specs=whole(*shapes) if single else [whole(*s) for s in outs],
            scratch_shapes=[pltpu.VMEM(s, F32) for s in scratch],
        ),
        compiler_params=params(),
        cost_estimate=cost(flops, size),
    )
    return call(*scalars, *arrays)


def pack(starts, own):
    rows, columns = (2, HALF + 8, SIZE), (2, SIZE + 8, HALF)
    return pl.pallas_call(
        pack_kernel,
        out_shape=shaped([rows, rows, columns, columns]),
        grid_spec=pltpu.PrefetchScalarGridSpec(
            num_scalar_prefetch=1,
            grid=(),
            in_specs=[pl.BlockSpec(memory_space=pltpu.HBM)],
            out_specs=[ANY] * 4,
            scratch_shapes=[pltpu.VMEM((2, 8, SIZE), F32), pltpu.SemaphoreType.DMA((8,))],
        ),
        compiler_params=params(),
        cost_estimate=cost(1 << 10, 2 << 20),
    )(starts, own)


def prepare(measured):
    cols, rows = permutation()
    arrays = [measured, jnp.asarray(cols), jnp.asarray(rows)]
    return simple(prepare_kernel, [], arrays, measured.shape, [], 1 << 30, 3 << 20)


def transforms(starts, own, halo, probe, measured):
    mats = jnp.asarray(constants())
    arrays = [own, *halo, probe, mats]
    count = measured.shape[0]
    halves = (16, 88, HALF)
    fields = (2, 2, SIZE, HALF)
    return pl.pallas_call(
        transform_kernel,
        out_shape=shaped([halves, halves, (count, *fields), (count, *fields)])
        + [jax.ShapeDtypeStruct((8, HALF), jnp.int32)],
        grid_spec=pltpu.PrefetchScalarGridSpec(
            num_scalar_prefetch=1,
            grid=(count,),
            in_specs=[ANY] * len(arrays) + [stepped(SIZE, SIZE)],
            out_specs=[whole(*halves), whole(*halves), stepped(*fields), stepped(*fields), whole(8, HALF)],
            scratch_shapes=[
                pltpu.VMEM((2, 5, 2 * SIZE, HALF), F32),
                pltpu.VMEM(probe.shape, F32),
                pltpu.VMEM(mats.shape, BF),
                pltpu.VMEM((8, 8, HALF), F32),
                pltpu.VMEM((2, 5, SIZE, HALF), F32),
                pltpu.VMEM((2, 2 * SIZE, 3 * SIZE), BF),
                pltpu.VMEM((2, 2, 3 * SIZE, SIZE), BF),
                pltpu.VMEM((2, 2, 3 * SIZE, SIZE), BF),
                pltpu.VMEM((2, 2 * SIZE, SIZE), F32),
                pltpu.VMEM((2, 2 * SIZE, SIZE), F32),
                pltpu.VMEM((2, 8, HALF), F32),
                pltpu.SemaphoreType.DMA((24,)),
            ],
        ),
        compiler_params=params(),
        cost_estimate=cost(13 << 30, 12 << 20),
    )(starts, *arrays, measured)


def place_parts(starts, object_part, patch, probe):
    count = patch.shape[0]
    fields = (2, 2, SIZE, HALF)
    rows, columns, corners = (2, HALF, SIZE), (2, SIZE, HALF), (2, 2, HALF, HALF)
    shapes = [(2, SIZE, SIZE), rows, rows, columns, columns, corners, corners, (2 * count, HALF)]
    return pl.pallas_call(
        place_kernel,
        out_shape=shaped(shapes),
        grid_spec=pltpu.PrefetchScalarGridSpec(
            num_scalar_prefetch=1,
            grid=(count,),
            in_specs=[stepped(*fields), stepped(*fields), whole(*probe.shape)],
            out_specs=[whole(*s) for s in shapes],
            scratch_shapes=[
                pltpu.VMEM((2, 2, SIZE + 16, HALF), F32),
                pltpu.VMEM((SIZE, SIZE), F32),
                pltpu.VMEM((2, 5, 2 * SIZE, HALF), F32),
            ],
        ),
        compiler_params=params(),
        cost_estimate=cost(5 << 30, 8 << 20),
    )(starts, object_part, patch, probe)


def illuminate(starts, around, probe):
    scratch = [(2, SIZE, HALF), (7, 3 * SIZE, HALF)]
    return simple(light_kernel, [starts, around], [probe], (SIZE, SIZE), scratch, 2 << 30, 4 << 20)


def update(arrays):
    shape = arrays[0].shape
    return simple(update_kernel, [], arrays, shape, [shape], 1 << 20, 3 << 20)


def assemble(mine, other):
    return simple(assemble_kernel, [], [mine, other], (4, SIZE, SIZE), [], 1 << 20, 2 << 20)


def pairs_from(first, count):
    pairs = []
    for i in range(first, count - 1, 2):
        pairs += [(i, i + 1), (i + 1, i)]
    return pairs


def swap_rows(value, first):
    return lax.ppermute(value, "row", pairs_from(first, lax.axis_size("row")))


def swap_columns(value, first):
    return lax.ppermute(value, "col", pairs_from(first, lax.axis_size("col")))


def along_z(value, distance):
    pairs = []
    for row in range(lax.axis_size("row")):
        for col in range(lax.axis_size("col")):
            z = (2 * (row // 4) + col // 2 % 2 + distance) % 4
            target = (4 * (z // 2) + row % 4) * 16 + col // 4 * 4 + 2 * (z % 2) + col % 2
            pairs.append((row * 16 + col, target))
    return lax.ppermute(value, AXES, pairs)


def planes():
    groups = {}
    for row in range(lax.axis_size("row")):
        for col in range(lax.axis_size("col")):
            groups.setdefault((row // 4, col % 4), []).append(row * 16 + col)
    return list(groups.values())


def half_lanes(value, first):
    return jnp.where(first, value[..., :HALF], value[..., HALF:])


def local(object_tile, probe, amplitudes, offsets):
    starts = offsets[0, 0].T
    measured = amplitudes[0, 0]
    core = lax.rem(lax.axis_index("col"), 2)
    groups = planes()

    with jax.named_scope("object_halo"):
        even, odd, cross, same = pack(starts, object_tile)
        odd = swap_rows(odd, 1)
        even = swap_rows(even, 0)
        cross = swap_columns(cross, 1)
        same = swap_columns(same, 0)
    permuted = prepare(measured)
    with jax.named_scope("object_corners"):
        odd, even, cross, same, permuted = lax.optimization_barrier((odd, even, cross, same, permuted))
        rows = jnp.stack([odd, even])
        cross_corner = swap_columns(half_lanes(rows, core == 0), 1)
        same_corner = swap_columns(half_lanes(rows, core == 1), 0)

    halo = [odd, even, cross, same, cross_corner, same_corner]
    keep, send, object_part, patch, around = transforms(starts, object_tile, halo, probe, permuted)

    parts = place_parts(starts, object_part, patch, probe)
    with jax.named_scope("probe_reduce"):
        chunk, parts, around = lax.optimization_barrier((keep + swap_columns(send, 0), parts, around))
        chunk = lax.all_to_all(chunk, AXES, 0, 0, axis_index_groups=groups, tiled=True)
    center, even, odd, cross, same, cross_corner, same_corner, steps = parts

    with jax.named_scope("gradient_corners"):
        cross_corner = swap_columns(cross_corner, 1)
        same_corner = swap_columns(same_corner, 0)
        cross = swap_columns(cross, 1)
        same = swap_columns(same, 0)
    with jax.named_scope("gradient_rows"):
        first = jnp.where(core == 0, cross_corner, same_corner)
        second = jnp.where(core == 0, same_corner, cross_corner)
        added = jnp.concatenate([first, second], -1)
        odd, even = odd + added[1], even + added[0]
        light = illuminate(starts, around, probe)
        chunk, light, odd, even = lax.optimization_barrier((chunk, light, odd, even))
        odd = swap_rows(odd, 1)
        even = swap_rows(even, 0)

    with jax.named_scope("probe_sum"):
        total = simple(sum_kernel, [], [chunk], (88, HALF), [], 1 << 20, 1 << 20)
        parts = [total] + [along_z(total, d) for d in (1, 2, 3)]
        shapes = [(16, 64, HALF), (8, HALF)]
        spread_out, ratio = simple(quotient_kernel, [], parts, shapes, [(4, 88, HALF)], 1 << 20, 2 << 20)

    with jax.named_scope("probe_gather"):
        gathered = lax.all_to_all(spread_out, AXES, 0, 0, axis_index_groups=groups, tiled=True)
        gathered, odd, even, cross, same = lax.optimization_barrier((gathered, odd, even, cross, same))
        probe_update = assemble(gathered, swap_columns(gathered, 0)).reshape(probe.shape)

    object_update = update([center, even, odd, cross, same, light])
    relative_error = ratio[0, :1]
    position_step = steps[:, 0].reshape(1, 1, -1, 2)
    return (object_update, probe_update, position_step, relative_error)


def solution(mesh):
    in_specs = (
        P(None, "row", "col"),
        P(),
        P("row", "col", None, None, None),
        P("row", "col", None, None),
    )
    out_specs = (P(None, "row", "col"), P(), P("row", "col", None, None), P())
    return jax.shard_map(local, mesh=mesh, in_specs=in_specs, out_specs=out_specs, check_vma=False)
```

```python
import jax
import jax.numpy as jnp
import ml_dtypes
import numpy as np
from jax import lax
from jax.experimental import pallas as pl
from jax.experimental.pallas import tpu as pltpu
from jax.sharding import PartitionSpec as P

intensity_floor = 0.1
object_damping = 1.0
small_value = 1e-06

SIZE = 256
HALF = 128
CHUNK = 32
BF = jnp.bfloat16
F32 = jnp.float32
AXES = ("row", "col")
VMEM_LIMIT = 32 * 2**20


def transform_matrices():
    n = np.arange(HALF)[:, None]
    q = np.arange(HALF)[None, :]
    out = []
    for odd in (0, 1):
        angle = -2.0 * np.pi * ((n * (2 * q + odd)) % SIZE) / SIZE
        re, im = np.cos(angle) / 16.0, np.sin(angle) / 16.0
        out.append(np.block([[re, im], [-im, re]]))
    return out


def split_np(matrix):
    high = matrix.astype(ml_dtypes.bfloat16)
    low = (matrix - high.astype(np.float64)).astype(ml_dtypes.bfloat16)
    return high, low


def constants():
    return np.stack([np.stack([np.stack(split_np(x)) for x in (m, m.T)]) for m in transform_matrices()])


def permutation():
    order = np.concatenate([np.arange(0, SIZE, 2), np.arange(1, SIZE, 2)])
    onehot = np.zeros((SIZE, SIZE), np.float32)
    onehot[order, np.arange(SIZE)] = 1.0
    columns = np.concatenate([onehot] * 3, 0).astype(ml_dtypes.bfloat16)
    rows = np.concatenate([onehot.T] * 3, 1).astype(ml_dtypes.bfloat16)
    return columns, rows


def split2(value):
    high = value.astype(BF)
    return high, (value - high.astype(F32)).astype(BF)


def split3(value):
    high = value.astype(BF)
    rest = value - high.astype(F32)
    middle = rest.astype(BF)
    return high, middle, (rest - middle.astype(F32)).astype(BF)


def dot(a, b):
    return jnp.dot(a, b, preferred_element_type=F32)


def lane_index(rows):
    return lax.broadcasted_iota(jnp.int32, (rows, HALF), 1)


def spread(first, second, shift, lanes):
    a = pltpu.roll(first, shift, 1)
    b = pltpu.roll(second, shift, 1)
    wrapped = lanes < shift
    return jnp.where(wrapped, 0.0, a), jnp.where(wrapped, a, b), jnp.where(wrapped, b, 0.0)


def gather_lanes(blocks, shift, lanes):
    back = jnp.where(shift == 0, 0, HALF - shift)
    a, b, c = [pltpu.roll(x, back, 1) for x in blocks]
    inside = lanes < HALF - shift
    return jnp.where(inside, a, b), jnp.where(inside, b, c)


def fold8(value):
    return jnp.sum(value.reshape(-1, 8, HALF), axis=0)


def prepare_kernel(measured, cols, rows, permuted):
    for j in range(measured.shape[0]):
        moved = dot(jnp.concatenate(split3(measured[j]), 1), cols[...])
        permuted[j] = dot(rows[...], jnp.concatenate(split3(moved), 0))


def place_of():
    return lax.rem(lax.axis_index("row"), 2), lax.rem(lax.axis_index("col"), 2)


def run_all(copies):
    for copy in copies:
        copy.start()
    for copy in copies:
        copy.wait()


def pack_kernel(starts, own, even, odd, cross, same, offsets, sems):
    row_odd, core = place_of()
    lanes = lane_index(8)
    value = jnp.zeros((8, HALF), F32)
    for j in range(starts.shape[1]):
        for d in range(2):
            value = jnp.where(lanes == 2 * j + d, (starts[d, j] + 1).astype(F32), value)
    for p in range(2):
        offsets[p, :, :HALF] = value
        offsets[p, :, HALF:] = value
    top = pl.ds(pl.multiple_of(HALF * row_odd, HALF), HALF)
    bottom = pl.ds(pl.multiple_of(HALF * (1 - row_odd), HALF), HALF)
    near = pl.ds(pl.multiple_of(HALF * core, HALF), HALF)
    far = pl.ds(pl.multiple_of(HALF * (1 - core), HALF), HALF)
    moves = [
        (own.at[:, top, :], odd.at[:, :HALF, :]),
        (own.at[:, bottom, :], even.at[:, :HALF, :]),
        (own.at[:, :, near], cross.at[:, :SIZE, :]),
        (own.at[:, :, far], same.at[:, :SIZE, :]),
        (offsets, odd.at[:, HALF:, :]),
        (offsets, even.at[:, HALF:, :]),
        (offsets.at[:, :, :HALF], cross.at[:, SIZE:, :]),
        (offsets.at[:, :, :HALF], same.at[:, SIZE:, :]),
    ]
    run_all([pltpu.make_async_copy(x, y, sems.at[n]) for n, (x, y) in enumerate(moves)])


def sides():
    row_odd, core = place_of()
    even_rows = pl.ds(pl.multiple_of(3 * HALF * (1 - row_odd), HALF), HALF)
    odd_rows = pl.ds(pl.multiple_of(3 * HALF * row_odd, HALF), HALF)
    return even_rows, odd_rows, 3 * core, 3 - 3 * core


def transform_kernel(
    starts, own, odd_strip, even_strip, cross, same, cross_corner, same_corner, probe_in, matrices, measured,
    keep, send, object_part, patch, around,
    tile, probe, mats, offsets, totals, xs, zs, gs, ys, back, sums, sems,
):
    step = pl.program_id(0)
    modes = probe.shape[0]
    lanes = lane_index(CHUNK)
    late = pltpu.make_async_copy(matrices, mats, sems.at[0])

    @pl.when(step == 0)
    def _():
        late.start()
        even_rows, odd_rows, cross_block, same_block = sides()
        center = pl.ds(HALF, SIZE)
        moves = [(probe_in, probe)]
        for block, strip, corner in ((cross_block, cross, cross_corner), (same_block, same, same_corner)):
            moves.append((strip.at[:, :SIZE, :], tile.at[:, block, center, :]))
            moves.append((corner.at[1, :, :HALF, :], tile.at[:, block, even_rows, :]))
            moves.append((corner.at[0, :, :HALF, :], tile.at[:, block, odd_rows, :]))
        for b in range(2):
            span = pl.ds(b * HALF, HALF)
            moves.append((own.at[:, :, span], tile.at[:, 1 + b, center, :]))
            moves.append((even_strip.at[:, :HALF, span], tile.at[:, 1 + b, even_rows, :]))
            moves.append((odd_strip.at[:, :HALF, span], tile.at[:, 1 + b, odd_rows, :]))
        strips = [x.at[0] for x in (odd_strip, even_strip, cross, same)]
        strips += [x.at[n, 0] for x in (cross_corner, same_corner) for n in range(2)]
        for n, strip in enumerate(strips):
            moves.append((strip.at[pl.ds(strip.shape[0] - 8, 8), pl.ds(0, HALF)], offsets.at[n]))
        copies = [pltpu.make_async_copy(x, y, sems.at[1 + n]) for n, (x, y) in enumerate(moves)]
        for copy in copies:
            copy.start()
        tile[:, 4] = jnp.zeros((2, 2 * SIZE, HALF), F32)
        totals[...] = jnp.zeros_like(totals)
        sums[...] = jnp.zeros_like(sums)
        for copy in copies:
            copy.wait()
        for n in range(8):
            around[pl.ds(n, 1), :] = offsets[n, :1, :].astype(jnp.int32)

    row, col = starts[0, step], starts[1, step]
    base, shift = col // HALF, lax.rem(col, HALF)

    for i in range(0, SIZE, CHUNK):
        part = pl.ds(i, CHUNK)
        where = pl.ds(row + i, CHUNK)
        obj = []
        for p in range(2):
            blocks = [tile[p, base + b, where, :] for b in range(3)]
            obj.append(gather_lanes(blocks, shift, lanes))
            for b in range(2):
                patch[0, p, b, part, :] = obj[p][b]
        for m in range(modes):
            wave = []
            for b in range(2):
                span = slice(b * HALF, (b + 1) * HALF)
                pr, pi = probe[m, 0, part, span], probe[m, 1, part, span]
                wave.append((pr * obj[0][b] - pi * obj[1][b], pr * obj[1][b] + pi * obj[0][b]))
            for odd in range(2):
                for p in range(2):
                    high, low = split2(wave[0][p] - wave[1][p] if odd else wave[0][p] + wave[1][p])
                    at = pl.ds(m * SIZE + i, CHUNK)
                    xs[odd, at, p * HALF : (p + 1) * HALF] = high
                    xs[odd, at, SIZE + p * HALF : SIZE + (p + 1) * HALF] = low
                    xs[odd, at, 2 * SIZE + p * HALF : 2 * SIZE + (p + 1) * HALF] = high

    @pl.when(step == 0)
    def _():
        late.wait()

    def right(odd, transposed):
        high, low = mats[odd, transposed, 0], mats[odd, transposed, 1]
        return jnp.concatenate([high, high, low], 0)

    def left(odd, transposed):
        high, low = mats[odd, transposed, 0], mats[odd, transposed, 1]
        return jnp.concatenate([high, low, high], 1)

    for odd in range(2):
        ys[odd] = dot(xs[odd], right(odd, 0))

    for m in range(modes):
        for odd in range(2):
            lane_span = slice(odd * HALF, (odd + 1) * HALF)
            for i in range(0, HALF, CHUNK):
                top = ys[odd, pl.ds(m * SIZE + i, CHUNK), :]
                bottom = ys[odd, pl.ds(m * SIZE + HALF + i, CHUNK), :]
                for odd_row in range(2):
                    high, low = split2(top - bottom if odd_row else top + bottom)
                    for p in range(2):
                        span = slice(p * HALF, (p + 1) * HALF)
                        at = p * HALF + i
                        zs[m, odd_row, pl.ds(at, CHUNK), lane_span] = high[:, span]
                        zs[m, odd_row, pl.ds(SIZE + at, CHUNK), lane_span] = high[:, span]
                        zs[m, odd_row, pl.ds(2 * SIZE + at, CHUNK), lane_span] = low[:, span]

    error = jnp.zeros((8, HALF), F32)
    energy = jnp.zeros((8, HALF), F32)
    for odd_row in range(2):
        far = [dot(left(odd_row, 1), zs[m, odd_row]) for m in range(modes)]
        for i in range(0, HALF, CHUNK):
            parts = [(f[i : i + CHUNK], f[HALF + i : HALF + i + CHUNK]) for f in far]
            intensity = parts[0][0] ** 2 + parts[0][1] ** 2 + (parts[1][0] ** 2 + parts[1][1] ** 2)
            intensity = jnp.maximum(intensity, intensity_floor)
            inverse = lax.rsqrt(intensity)
            modulus = intensity * inverse
            amplitude = measured[0, pl.ds(odd_row * HALF + i, CHUNK), :]
            factor = 1.0 - amplitude * inverse
            misfit = (modulus - amplitude) ** 2
            strength = amplitude**2
            error = error + fold8(misfit[:, :HALF]) + fold8(misfit[:, HALF:])
            energy = energy + fold8(strength[:, :HALF]) + fold8(strength[:, HALF:])
            for m in range(modes):
                for p in range(2):
                    high, low = split2(parts[m][p] * factor)
                    at = p * HALF + i
                    gs[m, odd_row, pl.ds(at, CHUNK), :] = high
                    gs[m, odd_row, pl.ds(SIZE + at, CHUNK), :] = high
                    gs[m, odd_row, pl.ds(2 * SIZE + at, CHUNK), :] = low
    sums[0] += error
    sums[1] += energy

    for m in range(modes):
        even = dot(left(0, 0), gs[m, 0])
        odds = dot(left(1, 0), gs[m, 1])
        for i in range(0, HALF, CHUNK):
            for p in range(2):
                a, b = even[p * HALF + i : p * HALF + i + CHUNK], odds[p * HALF + i : p * HALF + i + CHUNK]
                for bottom in range(2):
                    high, low = split2(a - b if bottom else a + b)
                    at = pl.ds(m * SIZE + bottom * HALF + i, CHUNK)
                    for odd in range(2):
                        span = slice(odd * HALF, (odd + 1) * HALF)
                        xs[odd, at, p * HALF : (p + 1) * HALF] = high[:, span]
                        xs[odd, at, SIZE + p * HALF : SIZE + (p + 1) * HALF] = low[:, span]
                        xs[odd, at, 2 * SIZE + p * HALF : 2 * SIZE + (p + 1) * HALF] = high[:, span]

    for odd in range(2):
        back[odd] = dot(xs[odd], right(odd, 1))

    for i in range(0, SIZE, CHUNK):
        part = pl.ds(i, CHUNK)
        for b in range(2):
            re, im = patch[0, 0, b, part, :], patch[0, 1, b, part, :]
            span = slice(b * HALF, (b + 1) * HALF)
            grad_re, grad_im = 0.0, 0.0
            for m in range(modes):
                at = pl.ds(m * SIZE + i, CHUNK)
                even = [back[0, at, p * HALF : (p + 1) * HALF] for p in range(2)]
                odds = [back[1, at, p * HALF : (p + 1) * HALF] for p in range(2)]
                br, bi = [x - y if b else x + y for x, y in zip(even, odds)]
                pr, pi = probe[m, 0, part, span], probe[m, 1, part, span]
                grad_re = grad_re + (pr * br + pi * bi)
                grad_im = grad_im + (pr * bi - pi * br)
                totals[b, 2 * m, part, :] += re * br + im * bi
                totals[b, 2 * m + 1, part, :] += re * bi - im * br
            object_part[0, 0, b, part, :] = grad_re
            object_part[0, 1, b, part, :] = grad_im
            totals[b, 4, part, :] += re**2 + im**2

    @pl.when(step == pl.num_programs(0) - 1)
    def _():
        core = place_of()[1]
        scalar = jnp.where(lax.broadcasted_iota(jnp.int32, (1, 8, HALF), 2) == 0, jnp.sum(sums[0]), jnp.sum(sums[1]))
        for out, block in ((keep, core), (send, 1 - core)):
            for c in range(5):
                out[:, 16 * c : 16 * c + 16, :] = totals[block, c].reshape(16, 16, HALF)
            out[:, 80:88, :] = jnp.broadcast_to(scalar, (16, 8, HALF))


def place_kernel(
    starts, object_part, patch, probe,
    center, even, odd, cross, same, cross_corner, same_corner, steps,
    padded, power, accum,
):
    step = pl.program_id(0)
    lanes = lane_index(CHUNK)

    @pl.when(step == 0)
    def _():
        accum[...] = jnp.zeros_like(accum)
        padded[:, :, 0:8, :] = jnp.zeros((2, 2, 8, HALF), F32)
        padded[:, :, 264:272, :] = jnp.zeros((2, 2, 8, HALF), F32)
        for i in range(0, SIZE, CHUNK):
            part = pl.ds(i, CHUNK)
            power[part] = probe_power(probe, part)

    row, col = starts[0, step], starts[1, step]
    base, shift = col // HALF, lax.rem(col, HALF)
    for p in range(2):
        for b in range(2):
            padded[p, b, 8:264] = patch[0, p, b]

    first, last = lanes == 0, lanes == HALF - 1
    parts = [jnp.zeros((8, HALF), F32) for _ in range(4)]
    for i in range(0, SIZE, CHUNK):
        part = pl.ds(i, CHUNK)
        where = pl.ds(row + i, CHUNK)
        grads = [[object_part[0, p, b, part, :] for b in range(2)] for p in range(2)]
        strength = [power[part, :HALF], power[part, HALF:]]
        for p, pair in enumerate(grads):
            moved = spread(pair[0], pair[1], shift, lanes)
            for b in range(3):
                accum[p, base + b, where, :] += moved[b]
        columns = []
        for p in range(2):
            obj = [patch[0, p, b, part, :] for b in range(2)]
            before = [pltpu.roll(x, 1, 1) for x in obj]
            after = [pltpu.roll(x, HALF - 1, 1) for x in obj]
            columns.append(
                (
                    jnp.where(last, after[1], after[0]) - jnp.where(first, 0.0, before[0]),
                    jnp.where(last, 0.0, after[1]) - jnp.where(first, before[0], before[1]),
                )
            )
        for b in range(2):
            rows = [padded[p, b, pl.ds(9 + i, CHUNK), :] - padded[p, b, pl.ds(7 + i, CHUNK), :] for p in range(2)]
            for d, slope in enumerate((rows, [columns[0][b], columns[1][b]])):
                parts[2 * d] = parts[2 * d] + fold8(grads[0][b] * slope[0] + grads[1][b] * slope[1])
                parts[2 * d + 1] = parts[2 * d + 1] + fold8(strength[b] * (slope[0] ** 2 + slope[1] ** 2))

    for d in range(2):
        numerator = 0.5 * jnp.sum(parts[2 * d], keepdims=True)
        denominator = 0.25 * jnp.sum(parts[2 * d + 1], keepdims=True) + small_value
        steps[pl.ds(2 * step + d, 1), :] = jnp.broadcast_to(-numerator / denominator, (1, HALF))

    @pl.when(step == pl.num_programs(0) - 1)
    def _():
        even_rows, odd_rows, cross_block, same_block = sides()
        for p in range(2):
            for b in range(2):
                span = slice(b * HALF, (b + 1) * HALF)
                center[p, :, span] = accum[p, 1 + b, 128:384]
                even[p, :, span] = accum[p, 1 + b, even_rows]
                odd[p, :, span] = accum[p, 1 + b, odd_rows]
            for block, strip, corner in ((cross_block, cross, cross_corner), (same_block, same, same_corner)):
                strip[p] = accum[p, block, 128:384]
                corner[0, p] = accum[p, block, even_rows]
                corner[1, p] = accum[p, block, odd_rows]


def probe_power(probe, part):
    return (probe[0, 0, part] ** 2 + probe[0, 1, part] ** 2) + (probe[1, 0, part] ** 2 + probe[1, 1, part] ** 2)


def light_kernel(starts, around, probe, light, power, accum):
    accum[...] = jnp.zeros_like(accum)
    for i in range(0, SIZE, CHUNK):
        part = pl.ds(i, CHUNK)
        total = probe_power(probe, part)
        power[0, part] = total[:, :HALF]
        power[1, part] = total[:, HALF:]
    lanes = lane_index(CHUNK)
    row_odd, core = place_of()
    even, cross = 1 - 2 * row_odd, 2 * core - 1
    neighbours = [(-even, None), (even, None), (None, cross), (None, -cross)]
    neighbours += [(-even, cross), (even, cross), (-even, -cross), (even, -cross)]

    def add(row, col, down, right):
        rows, source_row, row = (SIZE, 0, row + HALF) if down is None else (
            HALF, pl.multiple_of(jnp.where(down < 0, HALF, 0), HALF), row + jnp.where(down < 0, 0, 3 * HALF)
        )
        if right is None:
            col = col + HALF
        else:
            source = jnp.where(right < 0, 1, 0)
            col = col + jnp.where(right < 0, 0, 3 * HALF)
        base, shift = col // HALF, lax.rem(col, HALF)
        for i in range(0, rows, CHUNK):
            part = pl.ds(source_row + i, CHUNK)
            where = pl.ds(row + i, CHUNK)
            if right is None:
                moved = spread(power[0, part], power[1, part], shift, lanes)
            else:
                rolled = pltpu.roll(power[source, part], shift, 1)
                moved = jnp.where(lanes < shift, 0.0, rolled), jnp.where(lanes < shift, rolled, 0.0)
            for b, value in enumerate(moved):
                accum[base + b, where, :] += value

    count = starts.shape[1]
    for j in range(count):
        add(starts[0, j], starts[1, j], None, None)
    for n, (down, right) in enumerate(neighbours):
        for j in range(count):
            row, col = around[n, 2 * j] - 1, around[n, 2 * j + 1] - 1
            near = row >= 0
            if down is not None:
                near = near & jnp.where(down < 0, row > HALF, row < HALF)
            if right is not None:
                near = near & jnp.where(right < 0, col > HALF, col < HALF)

            @pl.when(near)
            def _(row=row, col=col, down=down, right=right):
                add(row, col, down, right)

    light[:, :HALF] = accum[2, 256:512]
    light[:, HALF:] = accum[3, 256:512]


def sum_kernel(chunk, total):
    total[...] = jnp.sum(chunk[...], axis=0)


def quotient_kernel(own, first, second, third, spread_out, ratio, held):
    z = 2 * lax.div(lax.axis_index("row"), 4) + lax.rem(lax.div(lax.axis_index("col"), 2), 2)
    for distance, part in enumerate((own, first, second, third)):
        held[lax.rem(z + 4 - distance, 4)] = part[...]
    total = (held[0] + held[1]) + (held[2] + held[3])
    for c in range(4):
        quotient = total[16 * c : 16 * c + 16] / total[64:80]
        spread_out[:, 16 * c : 16 * c + 16, :] = jnp.broadcast_to(quotient[None], (16, 16, HALF))
    ratio[...] = jnp.broadcast_to(total[80:81, 0:1] / total[80:81, 1:2], (8, HALF))


def update_kernel(center, even, odd, cross, same, light, out, total):
    for p in range(2):
        total[p] = center[p]
    row_odd, core = place_of()
    even_half = pl.ds(pl.multiple_of(HALF * (1 - row_odd), HALF), HALF)
    odd_half = pl.ds(pl.multiple_of(HALF * row_odd, HALF), HALF)
    for p in range(2):
        total[p, even_half, :] += even[p]
        total[p, odd_half, :] += odd[p]
    swapped = core == 1
    for i in range(0, SIZE, CHUNK):
        part = pl.ds(i, CHUNK)
        scale = 1.0 / (light[part] + object_damping)
        for p in range(2):
            a, b = cross[p, part], same[p, part]
            out[p, part, :HALF] = (total[p, part, :HALF] + jnp.where(swapped, b, a)) * scale[:, :HALF]
            out[p, part, HALF:] = (total[p, part, HALF:] + jnp.where(swapped, a, b)) * scale[:, HALF:]


def assemble_kernel(mine, other, out):
    core = place_of()[1]

    def write(source, block):
        for c in range(4):
            out[c, :, block * HALF : (block + 1) * HALF] = source[:, 16 * c : 16 * c + 16, :].reshape(SIZE, HALF)

    @pl.when(core == 0)
    def _():
        write(mine, 0)
        write(other, 1)

    @pl.when(core == 1)
    def _():
        write(mine, 1)
        write(other, 0)


def whole(*shape):
    return pl.BlockSpec(shape, lambda *_: (0,) * len(shape))


ANY = pl.BlockSpec(memory_space=pl.ANY)


def stepped(*shape):
    return pl.BlockSpec((1, *shape), lambda i, *_: (i,) + (0,) * len(shape))


def shaped(shapes):
    return [jax.ShapeDtypeStruct(s, F32) for s in shapes]


def params():
    return pltpu.CompilerParams(vmem_limit_bytes=VMEM_LIMIT)


def cost(flops, size):
    return pl.CostEstimate(flops=flops, bytes_accessed=size, transcendentals=0)


def simple(kernel, scalars, arrays, shapes, scratch, flops, size):
    single = not isinstance(shapes, list)
    outs = [shapes] if single else shapes
    call = pl.pallas_call(
        kernel,
        out_shape=shaped(outs)[0] if single else shaped(outs),
        grid_spec=pltpu.PrefetchScalarGridSpec(
            num_scalar_prefetch=len(scalars),
            grid=(),
            in_specs=[whole(*x.shape) for x in arrays],
            out_specs=whole(*shapes) if single else [whole(*s) for s in outs],
            scratch_shapes=[pltpu.VMEM(s, F32) for s in scratch],
        ),
        compiler_params=params(),
        cost_estimate=cost(flops, size),
    )
    return call(*scalars, *arrays)


def pack(starts, own):
    rows, columns = (2, HALF + 8, SIZE), (2, SIZE + 8, HALF)
    return pl.pallas_call(
        pack_kernel,
        out_shape=shaped([rows, rows, columns, columns]),
        grid_spec=pltpu.PrefetchScalarGridSpec(
            num_scalar_prefetch=1,
            grid=(),
            in_specs=[pl.BlockSpec(memory_space=pltpu.HBM)],
            out_specs=[ANY] * 4,
            scratch_shapes=[pltpu.VMEM((2, 8, SIZE), F32), pltpu.SemaphoreType.DMA((8,))],
        ),
        compiler_params=params(),
        cost_estimate=cost(1 << 10, 2 << 20),
    )(starts, own)


def prepare(measured):
    cols, rows = permutation()
    arrays = [measured, jnp.asarray(cols), jnp.asarray(rows)]
    return simple(prepare_kernel, [], arrays, measured.shape, [], 1 << 30, 3 << 20)


def transforms(starts, own, halo, probe, measured):
    mats = jnp.asarray(constants())
    arrays = [own, *halo, probe, mats]
    count = measured.shape[0]
    halves = (16, 88, HALF)
    fields = (2, 2, SIZE, HALF)
    return pl.pallas_call(
        transform_kernel,
        out_shape=shaped([halves, halves, (count, *fields), (count, *fields)])
        + [jax.ShapeDtypeStruct((8, HALF), jnp.int32)],
        grid_spec=pltpu.PrefetchScalarGridSpec(
            num_scalar_prefetch=1,
            grid=(count,),
            in_specs=[ANY] * len(arrays) + [stepped(SIZE, SIZE)],
            out_specs=[whole(*halves), whole(*halves), stepped(*fields), stepped(*fields), whole(8, HALF)],
            scratch_shapes=[
                pltpu.VMEM((2, 5, 2 * SIZE, HALF), F32),
                pltpu.VMEM(probe.shape, F32),
                pltpu.VMEM(mats.shape, BF),
                pltpu.VMEM((8, 8, HALF), F32),
                pltpu.VMEM((2, 5, SIZE, HALF), F32),
                pltpu.VMEM((2, 2 * SIZE, 3 * SIZE), BF),
                pltpu.VMEM((2, 2, 3 * SIZE, SIZE), BF),
                pltpu.VMEM((2, 2, 3 * SIZE, SIZE), BF),
                pltpu.VMEM((2, 2 * SIZE, SIZE), F32),
                pltpu.VMEM((2, 2 * SIZE, SIZE), F32),
                pltpu.VMEM((2, 8, HALF), F32),
                pltpu.SemaphoreType.DMA((24,)),
            ],
        ),
        compiler_params=params(),
        cost_estimate=cost(13 << 30, 12 << 20),
    )(starts, *arrays, measured)


def place_parts(starts, object_part, patch, probe):
    count = patch.shape[0]
    fields = (2, 2, SIZE, HALF)
    rows, columns, corners = (2, HALF, SIZE), (2, SIZE, HALF), (2, 2, HALF, HALF)
    shapes = [(2, SIZE, SIZE), rows, rows, columns, columns, corners, corners, (2 * count, HALF)]
    return pl.pallas_call(
        place_kernel,
        out_shape=shaped(shapes),
        grid_spec=pltpu.PrefetchScalarGridSpec(
            num_scalar_prefetch=1,
            grid=(count,),
            in_specs=[stepped(*fields), stepped(*fields), whole(*probe.shape)],
            out_specs=[whole(*s) for s in shapes],
            scratch_shapes=[
                pltpu.VMEM((2, 2, SIZE + 16, HALF), F32),
                pltpu.VMEM((SIZE, SIZE), F32),
                pltpu.VMEM((2, 5, 2 * SIZE, HALF), F32),
            ],
        ),
        compiler_params=params(),
        cost_estimate=cost(5 << 30, 8 << 20),
    )(starts, object_part, patch, probe)


def illuminate(starts, around, probe):
    scratch = [(2, SIZE, HALF), (7, 3 * SIZE, HALF)]
    return simple(light_kernel, [starts, around], [probe], (SIZE, SIZE), scratch, 2 << 30, 4 << 20)


def update(arrays):
    shape = arrays[0].shape
    return simple(update_kernel, [], arrays, shape, [shape], 1 << 20, 3 << 20)


def assemble(mine, other):
    return simple(assemble_kernel, [], [mine, other], (4, SIZE, SIZE), [], 1 << 20, 2 << 20)


def pairs_from(first, count):
    pairs = []
    for i in range(first, count - 1, 2):
        pairs += [(i, i + 1), (i + 1, i)]
    return pairs


def swap_rows(value, first):
    return lax.ppermute(value, "row", pairs_from(first, lax.axis_size("row")))


def swap_columns(value, first):
    return lax.ppermute(value, "col", pairs_from(first, lax.axis_size("col")))


def along_z(value, distance):
    pairs = []
    for row in range(lax.axis_size("row")):
        for col in range(lax.axis_size("col")):
            z = (2 * (row // 4) + col // 2 % 2 + distance) % 4
            target = (4 * (z // 2) + row % 4) * 16 + col // 4 * 4 + 2 * (z % 2) + col % 2
            pairs.append((row * 16 + col, target))
    return lax.ppermute(value, AXES, pairs)


def planes():
    groups = {}
    for row in range(lax.axis_size("row")):
        for col in range(lax.axis_size("col")):
            groups.setdefault((row // 4, col % 4), []).append(row * 16 + col)
    return list(groups.values())


def half_lanes(value, first):
    return jnp.where(first, value[..., :HALF], value[..., HALF:])


def local(object_tile, probe, amplitudes, offsets):
    starts = offsets[0, 0].T
    measured = amplitudes[0, 0]
    core = lax.rem(lax.axis_index("col"), 2)
    groups = planes()

    with jax.named_scope("object_halo"):
        even, odd, cross, same = pack(starts, object_tile)
        odd = swap_rows(odd, 1)
        even = swap_rows(even, 0)
        cross = swap_columns(cross, 1)
        same = swap_columns(same, 0)
    permuted = prepare(measured)
    with jax.named_scope("object_corners"):
        odd, even, cross, same, permuted = lax.optimization_barrier((odd, even, cross, same, permuted))
        rows = jnp.stack([odd, even])
        cross_corner = swap_columns(half_lanes(rows, core == 0), 1)
        same_corner = swap_columns(half_lanes(rows, core == 1), 0)

    halo = [odd, even, cross, same, cross_corner, same_corner]
    keep, send, object_part, patch, around = transforms(starts, object_tile, halo, probe, permuted)

    parts = place_parts(starts, object_part, patch, probe)
    with jax.named_scope("probe_reduce"):
        chunk, parts, around = lax.optimization_barrier((keep + swap_columns(send, 0), parts, around))
        chunk = lax.all_to_all(chunk, AXES, 0, 0, axis_index_groups=groups, tiled=True)
    center, even, odd, cross, same, cross_corner, same_corner, steps = parts

    with jax.named_scope("gradient_corners"):
        cross_corner = swap_columns(cross_corner, 1)
        same_corner = swap_columns(same_corner, 0)
        cross = swap_columns(cross, 1)
        same = swap_columns(same, 0)
    with jax.named_scope("gradient_rows"):
        first = jnp.where(core == 0, cross_corner, same_corner)
        second = jnp.where(core == 0, same_corner, cross_corner)
        added = jnp.concatenate([first, second], -1)
        odd, even = odd + added[1], even + added[0]
        light = illuminate(starts, around, probe)
        tied = (chunk, light, odd, even, cross, same)
        chunk, light, odd, even, cross, same = lax.optimization_barrier(tied)
        odd = swap_rows(odd, 1)
        even = swap_rows(even, 0)
        object_update = update([center, even, odd, cross, same, light])

    with jax.named_scope("probe_sum"):
        total = simple(sum_kernel, [], [chunk], (88, HALF), [], 1 << 20, 1 << 20)
        parts = [total] + [along_z(total, d) for d in (1, 2, 3)]
        shapes = [(16, 64, HALF), (8, HALF)]
        spread_out, ratio = simple(quotient_kernel, [], parts, shapes, [(4, 88, HALF)], 1 << 20, 2 << 20)
        spread_out, object_update = lax.optimization_barrier((spread_out, object_update))

    with jax.named_scope("probe_gather"):
        gathered = lax.all_to_all(spread_out, AXES, 0, 0, axis_index_groups=groups, tiled=True)
        probe_update = assemble(gathered, swap_columns(gathered, 0)).reshape(probe.shape)

    relative_error = ratio[0, :1]
    position_step = steps[:, 0].reshape(1, 1, -1, 2)
    return (object_update, probe_update, position_step, relative_error)


def solution(mesh):
    in_specs = (
        P(None, "row", "col"),
        P(),
        P("row", "col", None, None, None),
        P("row", "col", None, None),
    )
    out_specs = (P(None, "row", "col"), P(), P("row", "col", None, None), P())
    return jax.shard_map(local, mesh=mesh, in_specs=in_specs, out_specs=out_specs, check_vma=False)
```

```python
import jax
import jax.numpy as jnp
import ml_dtypes
import numpy as np
from jax import lax
from jax.experimental import pallas as pl
from jax.experimental.pallas import tpu as pltpu
from jax.sharding import PartitionSpec as P

intensity_floor = 0.1
object_damping = 1.0
small_value = 1e-06

SIZE = 256
HALF = 128
CHUNK = 32
WIDTH = 2
BF = jnp.bfloat16
F32 = jnp.float32
AXES = ("row", "col")
VMEM_LIMIT = 32 * 2**20


def transform_matrices():
    n = np.arange(HALF)[:, None]
    q = np.arange(HALF)[None, :]
    out = []
    for odd in (0, 1):
        angle = -2.0 * np.pi * ((n * (2 * q + odd)) % SIZE) / SIZE
        re, im = np.cos(angle) / 16.0, np.sin(angle) / 16.0
        out.append(np.block([[re, im], [-im, re]]))
    return out


def split_np(matrix):
    high = matrix.astype(ml_dtypes.bfloat16)
    low = (matrix - high.astype(np.float64)).astype(ml_dtypes.bfloat16)
    return high, low


def constants():
    return np.stack([np.stack([np.stack(split_np(x)) for x in (m, m.T)]) for m in transform_matrices()])


def permutation():
    order = np.concatenate([np.arange(0, SIZE, 2), np.arange(1, SIZE, 2)])
    onehot = np.zeros((SIZE, SIZE), np.float32)
    onehot[order, np.arange(SIZE)] = 1.0
    columns = np.concatenate([onehot] * 3, 0).astype(ml_dtypes.bfloat16)
    rows = np.concatenate([onehot.T] * 3, 1).astype(ml_dtypes.bfloat16)
    return columns, rows


def split2(value):
    high = value.astype(BF)
    return high, (value - high.astype(F32)).astype(BF)


def split3(value):
    high = value.astype(BF)
    rest = value - high.astype(F32)
    middle = rest.astype(BF)
    return high, middle, (rest - middle.astype(F32)).astype(BF)


def dot(a, b):
    return jnp.dot(a, b, preferred_element_type=F32)


def lane_index(rows):
    return lax.broadcasted_iota(jnp.int32, (rows, HALF), 1)


def spread(first, second, shift, lanes):
    a = pltpu.roll(first, shift, 1)
    b = pltpu.roll(second, shift, 1)
    wrapped = lanes < shift
    return jnp.where(wrapped, 0.0, a), jnp.where(wrapped, a, b), jnp.where(wrapped, b, 0.0)


def gather_lanes(blocks, shift, lanes):
    back = jnp.where(shift == 0, 0, HALF - shift)
    a, b, c = [pltpu.roll(x, back, 1) for x in blocks]
    inside = lanes < HALF - shift
    return jnp.where(inside, a, b), jnp.where(inside, b, c)


def fold8(value):
    return jnp.sum(value.reshape(-1, 8, HALF), axis=0)


def prepare_kernel(measured, cols, rows, permuted):
    for j in range(measured.shape[0]):
        moved = dot(jnp.concatenate(split3(measured[j]), 1), cols[...])
        permuted[j] = dot(rows[...], jnp.concatenate(split3(moved), 0))


def place_of():
    return lax.rem(lax.axis_index("row"), 2), lax.rem(lax.axis_index("col"), 2)


def run_all(copies):
    for copy in copies:
        copy.start()
    for copy in copies:
        copy.wait()


def pack_kernel(starts, own, even, odd, cross, same, offsets, sems):
    row_odd, core = place_of()
    lanes = lane_index(8)
    value = jnp.zeros((8, HALF), F32)
    for j in range(starts.shape[1]):
        for d in range(2):
            value = jnp.where(lanes == 2 * j + d, (starts[d, j] + 1).astype(F32), value)
    for p in range(2):
        offsets[p, :, :HALF] = value
        offsets[p, :, HALF:] = value
    top = pl.ds(pl.multiple_of(HALF * row_odd, HALF), HALF)
    bottom = pl.ds(pl.multiple_of(HALF * (1 - row_odd), HALF), HALF)
    near = pl.ds(pl.multiple_of(HALF * core, HALF), HALF)
    far = pl.ds(pl.multiple_of(HALF * (1 - core), HALF), HALF)
    moves = [
        (own.at[:, top, :], odd.at[:, :HALF, :]),
        (own.at[:, bottom, :], even.at[:, :HALF, :]),
        (own.at[:, :, near], cross.at[:, :SIZE, :]),
        (own.at[:, :, far], same.at[:, :SIZE, :]),
        (offsets, odd.at[:, HALF:, :]),
        (offsets, even.at[:, HALF:, :]),
        (offsets.at[:, :, :HALF], cross.at[:, SIZE:, :]),
        (offsets.at[:, :, :HALF], same.at[:, SIZE:, :]),
    ]
    run_all([pltpu.make_async_copy(x, y, sems.at[n]) for n, (x, y) in enumerate(moves)])


def sides():
    row_odd, core = place_of()
    even_rows = pl.ds(pl.multiple_of(3 * HALF * (1 - row_odd), HALF), HALF)
    odd_rows = pl.ds(pl.multiple_of(3 * HALF * row_odd, HALF), HALF)
    return even_rows, odd_rows, 3 * core, 3 - 3 * core


def transform_kernel(
    starts, own, odd_strip, even_strip, cross, same, cross_corner, same_corner, probe_in, matrices, measured,
    keep, send, around, center, even, odd, cross_out, same_out, steps,
    tile, probe, mats, offsets, totals, sums, accum, power, sems, *slots,
):
    step = pl.program_id(0)
    modes = probe.shape[0]
    lanes = lane_index(CHUNK)
    width = measured.shape[0]
    per_slot = len(slots) // width
    slots = [slots[n * per_slot : (n + 1) * per_slot] for n in range(width)]

    @pl.when(step == 0)
    def _():
        even_rows, odd_rows, cross_block, same_block = sides()
        middle = pl.ds(HALF, SIZE)
        moves = [(probe_in, probe), (matrices, mats)]
        for block, strip, corner in ((cross_block, cross, cross_corner), (same_block, same, same_corner)):
            moves.append((strip.at[:, :SIZE, :], tile.at[:, block, middle, :]))
            moves.append((corner.at[1, :, :HALF, :], tile.at[:, block, even_rows, :]))
            moves.append((corner.at[0, :, :HALF, :], tile.at[:, block, odd_rows, :]))
        for b in range(2):
            span = pl.ds(b * HALF, HALF)
            moves.append((own.at[:, :, span], tile.at[:, 1 + b, middle, :]))
            moves.append((even_strip.at[:, :HALF, span], tile.at[:, 1 + b, even_rows, :]))
            moves.append((odd_strip.at[:, :HALF, span], tile.at[:, 1 + b, odd_rows, :]))
        strips = [x.at[0] for x in (odd_strip, even_strip, cross, same)]
        strips += [x.at[n, 0] for x in (cross_corner, same_corner) for n in range(2)]
        for n, strip in enumerate(strips):
            moves.append((strip.at[pl.ds(strip.shape[0] - 8, 8), pl.ds(0, HALF)], offsets.at[n]))
        copies = [pltpu.make_async_copy(x, y, sems.at[n]) for n, (x, y) in enumerate(moves)]
        for copy in copies:
            copy.start()
        tile[:, 4] = jnp.zeros((2, 2 * SIZE, HALF), F32)
        totals[...] = jnp.zeros_like(totals)
        sums[...] = jnp.zeros_like(sums)
        accum[...] = jnp.zeros_like(accum)
        for slot in slots:
            slot[4][:, :, 0:8, :] = jnp.zeros((2, 2, 8, HALF), F32)
            slot[4][:, :, 264:272, :] = jnp.zeros((2, 2, 8, HALF), F32)
        for copy in copies:
            copy.wait()
        for i in range(0, SIZE, CHUNK):
            part = pl.ds(i, CHUNK)
            power[part] = probe_power(probe, part)
        for n in range(8):
            around[pl.ds(n, 1), :] = offsets[n, :1, :].astype(jnp.int32)

    def right(odd, transposed):
        high, low = mats[odd, transposed, 0], mats[odd, transposed, 1]
        return jnp.concatenate([high, high, low], 0)

    def left(odd, transposed):
        high, low = mats[odd, transposed, 0], mats[odd, transposed, 1]
        return jnp.concatenate([high, low, high], 1)

    def position(n):
        col = starts[1, width * step + n]
        return starts[0, width * step + n], col // HALF, lax.rem(col, HALF)

    def enter(n):
        xs, patch = slots[n][0], slots[n][4]
        row, base, shift = position(n)
        for i in range(0, SIZE, CHUNK):
            part = pl.ds(i, CHUNK)
            where = pl.ds(row + i, CHUNK)
            obj = []
            for p in range(2):
                blocks = [tile[p, base + b, where, :] for b in range(3)]
                obj.append(gather_lanes(blocks, shift, lanes))
                for b in range(2):
                    patch[p, b, pl.ds(8 + i, CHUNK), :] = obj[p][b]
            for m in range(modes):
                wave = []
                for b in range(2):
                    span = slice(b * HALF, (b + 1) * HALF)
                    pr, pi = probe[m, 0, part, span], probe[m, 1, part, span]
                    wave.append((pr * obj[0][b] - pi * obj[1][b], pr * obj[1][b] + pi * obj[0][b]))
                for odd in range(2):
                    for p in range(2):
                        high, low = split2(wave[0][p] - wave[1][p] if odd else wave[0][p] + wave[1][p])
                        at = pl.ds(m * SIZE + i, CHUNK)
                        xs[odd, at, p * HALF : (p + 1) * HALF] = high
                        xs[odd, at, SIZE + p * HALF : SIZE + (p + 1) * HALF] = low
                        xs[odd, at, 2 * SIZE + p * HALF : 2 * SIZE + (p + 1) * HALF] = high

    def lanes_forward(n):
        xs, ys = slots[n][0], slots[n][2]
        for odd in range(2):
            ys[odd] = dot(xs[odd], right(odd, 0))

    def rows_split(n):
        zs, ys = slots[n][1], slots[n][2]
        for m in range(modes):
            for odd in range(2):
                lane_span = slice(odd * HALF, (odd + 1) * HALF)
                for i in range(0, HALF, CHUNK):
                    top = ys[odd, pl.ds(m * SIZE + i, CHUNK), :]
                    bottom = ys[odd, pl.ds(m * SIZE + HALF + i, CHUNK), :]
                    for odd_row in range(2):
                        high, low = split2(top - bottom if odd_row else top + bottom)
                        for p in range(2):
                            span = slice(p * HALF, (p + 1) * HALF)
                            at = p * HALF + i
                            zs[m, odd_row, pl.ds(at, CHUNK), lane_span] = high[:, span]
                            zs[m, odd_row, pl.ds(SIZE + at, CHUNK), lane_span] = high[:, span]
                            zs[m, odd_row, pl.ds(2 * SIZE + at, CHUNK), lane_span] = low[:, span]

    def rows_forward(n):
        zs, fs = slots[n][1], slots[n][3]
        for odd_row in range(2):
            for m in range(modes):
                fs[m, odd_row] = dot(left(odd_row, 1), zs[m, odd_row])

    def scale(n):
        zs, fs = slots[n][1], slots[n][3]
        error = jnp.zeros((8, HALF), F32)
        energy = jnp.zeros((8, HALF), F32)
        for odd_row in range(2):
            for i in range(0, HALF, CHUNK):
                parts = [[fs[m, odd_row, pl.ds(p * HALF + i, CHUNK), :] for p in range(2)] for m in range(modes)]
                intensity = parts[0][0] ** 2 + parts[0][1] ** 2 + (parts[1][0] ** 2 + parts[1][1] ** 2)
                intensity = jnp.maximum(intensity, intensity_floor)
                inverse = lax.rsqrt(intensity)
                modulus = intensity * inverse
                amplitude = measured[n, pl.ds(odd_row * HALF + i, CHUNK), :]
                factor = 1.0 - amplitude * inverse
                misfit = (modulus - amplitude) ** 2
                strength = amplitude**2
                error = error + fold8(misfit[:, :HALF]) + fold8(misfit[:, HALF:])
                energy = energy + fold8(strength[:, :HALF]) + fold8(strength[:, HALF:])
                for m in range(modes):
                    for p in range(2):
                        high, low = split2(parts[m][p] * factor)
                        at = p * HALF + i
                        zs[m, odd_row, pl.ds(at, CHUNK), :] = high
                        zs[m, odd_row, pl.ds(SIZE + at, CHUNK), :] = high
                        zs[m, odd_row, pl.ds(2 * SIZE + at, CHUNK), :] = low
        sums[0] += error
        sums[1] += energy

    def rows_back(n):
        zs, fs = slots[n][1], slots[n][3]
        for odd_row in range(2):
            for m in range(modes):
                fs[m, odd_row] = dot(left(odd_row, 0), zs[m, odd_row])

    def rows_join(n):
        xs, fs = slots[n][0], slots[n][3]
        for m in range(modes):
            for i in range(0, HALF, CHUNK):
                for p in range(2):
                    a, b = [fs[m, odd_row, pl.ds(p * HALF + i, CHUNK), :] for odd_row in range(2)]
                    for bottom in range(2):
                        high, low = split2(a - b if bottom else a + b)
                        at = pl.ds(m * SIZE + bottom * HALF + i, CHUNK)
                        for odd in range(2):
                            span = slice(odd * HALF, (odd + 1) * HALF)
                            xs[odd, at, p * HALF : (p + 1) * HALF] = high[:, span]
                            xs[odd, at, SIZE + p * HALF : SIZE + (p + 1) * HALF] = low[:, span]
                            xs[odd, at, 2 * SIZE + p * HALF : 2 * SIZE + (p + 1) * HALF] = high[:, span]

    def lanes_back(n):
        xs, ys = slots[n][0], slots[n][2]
        for odd in range(2):
            ys[odd] = dot(xs[odd], right(odd, 1))

    def leave(n):
        ys, patch = slots[n][2], slots[n][4]
        row, base, shift = position(n)
        first, last = lanes == 0, lanes == HALF - 1
        sums_of = [jnp.zeros((8, HALF), F32) for _ in range(4)]
        for i in range(0, SIZE, CHUNK):
            part = pl.ds(i, CHUNK)
            where = pl.ds(row + i, CHUNK)
            obj = [[patch[p, b, pl.ds(8 + i, CHUNK), :] for b in range(2)] for p in range(2)]
            grads = [[0.0, 0.0], [0.0, 0.0]]
            for b in range(2):
                re, im = obj[0][b], obj[1][b]
                span = slice(b * HALF, (b + 1) * HALF)
                for m in range(modes):
                    at = pl.ds(m * SIZE + i, CHUNK)
                    evens = [ys[0, at, p * HALF : (p + 1) * HALF] for p in range(2)]
                    odds = [ys[1, at, p * HALF : (p + 1) * HALF] for p in range(2)]
                    br, bi = [x - y if b else x + y for x, y in zip(evens, odds)]
                    pr, pi = probe[m, 0, part, span], probe[m, 1, part, span]
                    grads[0][b] = grads[0][b] + (pr * br + pi * bi)
                    grads[1][b] = grads[1][b] + (pr * bi - pi * br)
                    totals[b, 2 * m, part, :] += re * br + im * bi
                    totals[b, 2 * m + 1, part, :] += re * bi - im * br
                totals[b, 4, part, :] += re**2 + im**2
            for p in range(2):
                moved = spread(grads[p][0], grads[p][1], shift, lanes)
                for b in range(3):
                    accum[p, base + b, where, :] += moved[b]
            columns = []
            for p in range(2):
                before = [pltpu.roll(x, 1, 1) for x in obj[p]]
                after = [pltpu.roll(x, HALF - 1, 1) for x in obj[p]]
                columns.append(
                    (
                        jnp.where(last, after[1], after[0]) - jnp.where(first, 0.0, before[0]),
                        jnp.where(last, 0.0, after[1]) - jnp.where(first, before[0], before[1]),
                    )
                )
            for b in range(2):
                strength = power[part, b * HALF : (b + 1) * HALF]
                rows = [patch[p, b, pl.ds(9 + i, CHUNK), :] - patch[p, b, pl.ds(7 + i, CHUNK), :] for p in range(2)]
                for d, slope in enumerate((rows, [columns[0][b], columns[1][b]])):
                    sums_of[2 * d] = sums_of[2 * d] + fold8(grads[0][b] * slope[0] + grads[1][b] * slope[1])
                    sums_of[2 * d + 1] = sums_of[2 * d + 1] + fold8(strength * (slope[0] ** 2 + slope[1] ** 2))
        for d in range(2):
            numerator = 0.5 * jnp.sum(sums_of[2 * d], keepdims=True)
            denominator = 0.25 * jnp.sum(sums_of[2 * d + 1], keepdims=True) + small_value
            at = pl.ds(2 * (width * step + n) + d, 1)
            steps[at, :] = jnp.broadcast_to(-numerator / denominator, (1, HALF))

    stages = [enter, lanes_forward, rows_split, rows_forward, scale, rows_back, rows_join, lanes_back, leave]
    for at in range(len(stages) + width - 1):
        for n in range(width):
            if 0 <= at - n < len(stages):
                stages[at - n](n)

    @pl.when(step == pl.num_programs(0) - 1)
    def _():
        core = place_of()[1]
        scalar = jnp.where(lax.broadcasted_iota(jnp.int32, (1, 8, HALF), 2) == 0, jnp.sum(sums[0]), jnp.sum(sums[1]))
        for out, block in ((keep, core), (send, 1 - core)):
            for c in range(5):
                out[:, 16 * c : 16 * c + 16, :] = totals[block, c].reshape(16, 16, HALF)
            out[:, 80:88, :] = jnp.broadcast_to(scalar, (16, 8, HALF))
        even_rows, odd_rows, cross_block, same_block = sides()
        for p in range(2):
            for b in range(2):
                span = slice(b * HALF, (b + 1) * HALF)
                center[p, :, span] = accum[p, 1 + b, 128:384]
                even[p, :, span] = accum[p, 1 + b, even_rows]
                odd[p, :, span] = accum[p, 1 + b, odd_rows]
            cross_out[p] = accum[p, cross_block]
            same_out[p] = accum[p, same_block]


def probe_power(probe, part):
    return (probe[0, 0, part] ** 2 + probe[0, 1, part] ** 2) + (probe[1, 0, part] ** 2 + probe[1, 1, part] ** 2)


def light_kernel(starts, around, probe, light, power, accum):
    accum[...] = jnp.zeros_like(accum)
    for i in range(0, SIZE, CHUNK):
        part = pl.ds(i, CHUNK)
        total = probe_power(probe, part)
        power[0, part] = total[:, :HALF]
        power[1, part] = total[:, HALF:]
    lanes = lane_index(CHUNK)
    row_odd, core = place_of()
    even, cross = 1 - 2 * row_odd, 2 * core - 1
    neighbours = [(-even, None), (even, None), (None, cross), (None, -cross)]
    neighbours += [(-even, cross), (even, cross), (-even, -cross), (even, -cross)]

    def add(row, col, down, right):
        rows, source_row, row = (SIZE, 0, row + HALF) if down is None else (
            HALF, pl.multiple_of(jnp.where(down < 0, HALF, 0), HALF), row + jnp.where(down < 0, 0, 3 * HALF)
        )
        if right is None:
            col = col + HALF
        else:
            source = jnp.where(right < 0, 1, 0)
            col = col + jnp.where(right < 0, 0, 3 * HALF)
        base, shift = col // HALF, lax.rem(col, HALF)
        for i in range(0, rows, CHUNK):
            part = pl.ds(source_row + i, CHUNK)
            where = pl.ds(row + i, CHUNK)
            if right is None:
                moved = spread(power[0, part], power[1, part], shift, lanes)
            else:
                rolled = pltpu.roll(power[source, part], shift, 1)
                moved = jnp.where(lanes < shift, 0.0, rolled), jnp.where(lanes < shift, rolled, 0.0)
            for b, value in enumerate(moved):
                accum[base + b, where, :] += value

    count = starts.shape[1]
    for j in range(count):
        add(starts[0, j], starts[1, j], None, None)
    for n, (down, right) in enumerate(neighbours):
        for j in range(count):
            row, col = around[n, 2 * j] - 1, around[n, 2 * j + 1] - 1
            near = row >= 0
            if down is not None:
                near = near & jnp.where(down < 0, row > HALF, row < HALF)
            if right is not None:
                near = near & jnp.where(right < 0, col > HALF, col < HALF)

            @pl.when(near)
            def _(row=row, col=col, down=down, right=right):
                add(row, col, down, right)

    light[:, :HALF] = accum[2, 256:512]
    light[:, HALF:] = accum[3, 256:512]


def sum_kernel(chunk, total):
    total[...] = jnp.sum(chunk[...], axis=0)


def quotient_kernel(own, first, second, third, spread_out, ratio, held):
    z = 2 * lax.div(lax.axis_index("row"), 4) + lax.rem(lax.div(lax.axis_index("col"), 2), 2)
    for distance, part in enumerate((own, first, second, third)):
        held[lax.rem(z + 4 - distance, 4)] = part[...]
    total = (held[0] + held[1]) + (held[2] + held[3])
    for c in range(4):
        quotient = total[16 * c : 16 * c + 16] / total[64:80]
        spread_out[:, 16 * c : 16 * c + 16, :] = jnp.broadcast_to(quotient[None], (16, 16, HALF))
    ratio[...] = jnp.broadcast_to(total[80:81, 0:1] / total[80:81, 1:2], (8, HALF))


def fold_kernel(even, odd, cross, same, even_out, odd_out):
    even_rows, odd_rows, _, _ = sides()
    swapped = place_of()[1] == 1
    for p in range(2):
        for strip, rows, out in ((even, even_rows, even_out), (odd, odd_rows, odd_out)):
            a, b = cross[p, rows], same[p, rows]
            out[p, :, :HALF] = strip[p, :, :HALF] + jnp.where(swapped, b, a)
            out[p, :, HALF:] = strip[p, :, HALF:] + jnp.where(swapped, a, b)


def update_kernel(center, even, odd, cross, same, light, out, total):
    for p in range(2):
        total[p] = center[p]
    row_odd, core = place_of()
    even_half = pl.ds(pl.multiple_of(HALF * (1 - row_odd), HALF), HALF)
    odd_half = pl.ds(pl.multiple_of(HALF * row_odd, HALF), HALF)
    for p in range(2):
        total[p, even_half, :] += even[p]
        total[p, odd_half, :] += odd[p]
    swapped = core == 1
    for i in range(0, SIZE, CHUNK):
        part = pl.ds(i, CHUNK)
        scale = 1.0 / (light[part] + object_damping)
        for p in range(2):
            a, b = cross[p, pl.ds(HALF + i, CHUNK)], same[p, pl.ds(HALF + i, CHUNK)]
            out[p, part, :HALF] = (total[p, part, :HALF] + jnp.where(swapped, b, a)) * scale[:, :HALF]
            out[p, part, HALF:] = (total[p, part, HALF:] + jnp.where(swapped, a, b)) * scale[:, HALF:]


def assemble_kernel(mine, other, out):
    core = place_of()[1]

    def write(source, block):
        for c in range(4):
            out[c, :, block * HALF : (block + 1) * HALF] = source[:, 16 * c : 16 * c + 16, :].reshape(SIZE, HALF)

    @pl.when(core == 0)
    def _():
        write(mine, 0)
        write(other, 1)

    @pl.when(core == 1)
    def _():
        write(mine, 1)
        write(other, 0)


def whole(*shape):
    return pl.BlockSpec(shape, lambda *_: (0,) * len(shape))


ANY = pl.BlockSpec(memory_space=pl.ANY)


def shaped(shapes):
    return [jax.ShapeDtypeStruct(s, F32) for s in shapes]


def params():
    return pltpu.CompilerParams(vmem_limit_bytes=VMEM_LIMIT)


def cost(flops, size):
    return pl.CostEstimate(flops=flops, bytes_accessed=size, transcendentals=0)


def simple(kernel, scalars, arrays, shapes, scratch, flops, size):
    single = not isinstance(shapes, list)
    outs = [shapes] if single else shapes
    call = pl.pallas_call(
        kernel,
        out_shape=shaped(outs)[0] if single else shaped(outs),
        grid_spec=pltpu.PrefetchScalarGridSpec(
            num_scalar_prefetch=len(scalars),
            grid=(),
            in_specs=[whole(*x.shape) for x in arrays],
            out_specs=whole(*shapes) if single else [whole(*s) for s in outs],
            scratch_shapes=[pltpu.VMEM(s, F32) for s in scratch],
        ),
        compiler_params=params(),
        cost_estimate=cost(flops, size),
    )
    return call(*scalars, *arrays)


def pack(starts, own):
    rows, columns = (2, HALF + 8, SIZE), (2, SIZE + 8, HALF)
    return pl.pallas_call(
        pack_kernel,
        out_shape=shaped([rows, rows, columns, columns]),
        grid_spec=pltpu.PrefetchScalarGridSpec(
            num_scalar_prefetch=1,
            grid=(),
            in_specs=[pl.BlockSpec(memory_space=pltpu.HBM)],
            out_specs=[ANY] * 4,
            scratch_shapes=[pltpu.VMEM((2, 8, SIZE), F32), pltpu.SemaphoreType.DMA((8,))],
        ),
        compiler_params=params(),
        cost_estimate=cost(1 << 10, 2 << 20),
    )(starts, own)


def prepare(measured):
    cols, rows = permutation()
    arrays = [measured, jnp.asarray(cols), jnp.asarray(rows)]
    return simple(prepare_kernel, [], arrays, measured.shape, [], 1 << 30, 3 << 20)


def stepped(width, *shape):
    return pl.BlockSpec((width, *shape), lambda i, *_: (i,) + (0,) * len(shape))


def transforms(starts, own, halo, probe, measured):
    mats = jnp.asarray(constants())
    arrays = [own, *halo, probe, mats]
    count = measured.shape[0]
    width = WIDTH
    halves = (16, 88, HALF)
    rows, columns = (2, HALF, SIZE), (2, 2 * SIZE, HALF)
    shapes = [(2, SIZE, SIZE), rows, rows, columns, columns, (2 * count, HALF)]
    slot = [
        pltpu.VMEM((2, 2 * SIZE, 3 * SIZE), BF),
        pltpu.VMEM((2, 2, 3 * SIZE, SIZE), BF),
        pltpu.VMEM((2, 2 * SIZE, SIZE), F32),
        pltpu.VMEM((2, 2, SIZE, SIZE), F32),
        pltpu.VMEM((2, 2, SIZE + 16, HALF), F32),
    ]
    return pl.pallas_call(
        transform_kernel,
        out_shape=shaped([halves, halves]) + [jax.ShapeDtypeStruct((8, HALF), jnp.int32)] + shaped(shapes),
        grid_spec=pltpu.PrefetchScalarGridSpec(
            num_scalar_prefetch=1,
            grid=(count // width,),
            in_specs=[ANY] * len(arrays) + [stepped(width, SIZE, SIZE)],
            out_specs=[whole(*x) for x in [halves, halves, (8, HALF), *shapes]],
            scratch_shapes=[
                pltpu.VMEM((2, 5, 2 * SIZE, HALF), F32),
                pltpu.VMEM(probe.shape, F32),
                pltpu.VMEM(mats.shape, BF),
                pltpu.VMEM((8, 8, HALF), F32),
                pltpu.VMEM((2, 5, SIZE, HALF), F32),
                pltpu.VMEM((2, 8, HALF), F32),
                pltpu.VMEM((2, 5, 2 * SIZE, HALF), F32),
                pltpu.VMEM((SIZE, SIZE), F32),
                pltpu.SemaphoreType.DMA((24,)),
            ]
            + slot * width,
        ),
        compiler_params=params(),
        cost_estimate=cost(13 << 30, 12 << 20),
    )(starts, *arrays, measured)


def illuminate(starts, around, probe):
    scratch = [(2, SIZE, HALF), (7, 3 * SIZE, HALF)]
    return simple(light_kernel, [starts, around], [probe], (SIZE, SIZE), scratch, 2 << 30, 4 << 20)


def update(arrays):
    shape = arrays[0].shape
    return simple(update_kernel, [], arrays, shape, [shape], 1 << 20, 3 << 20)


def assemble(mine, other):
    return simple(assemble_kernel, [], [mine, other], (4, SIZE, SIZE), [], 1 << 20, 2 << 20)


def pairs_from(first, count):
    pairs = []
    for i in range(first, count - 1, 2):
        pairs += [(i, i + 1), (i + 1, i)]
    return pairs


def swap_rows(value, first):
    return lax.ppermute(value, "row", pairs_from(first, lax.axis_size("row")))


def swap_columns(value, first):
    return lax.ppermute(value, "col", pairs_from(first, lax.axis_size("col")))


def along_z(value, distance):
    pairs = []
    for row in range(lax.axis_size("row")):
        for col in range(lax.axis_size("col")):
            z = (2 * (row // 4) + col // 2 % 2 + distance) % 4
            target = (4 * (z // 2) + row % 4) * 16 + col // 4 * 4 + 2 * (z % 2) + col % 2
            pairs.append((row * 16 + col, target))
    return lax.ppermute(value, AXES, pairs)


def planes():
    groups = {}
    for row in range(lax.axis_size("row")):
        for col in range(lax.axis_size("col")):
            groups.setdefault((row // 4, col % 4), []).append(row * 16 + col)
    return list(groups.values())


def half_lanes(value, first):
    return jnp.where(first, value[..., :HALF], value[..., HALF:])


def local(object_tile, probe, amplitudes, offsets):
    starts = offsets[0, 0].T
    measured = amplitudes[0, 0]
    core = lax.rem(lax.axis_index("col"), 2)
    groups = planes()

    with jax.named_scope("object_halo"):
        even, odd, cross, same = pack(starts, object_tile)
        odd = swap_rows(odd, 1)
        even = swap_rows(even, 0)
        cross = swap_columns(cross, 1)
        same = swap_columns(same, 0)
    permuted = prepare(measured)
    with jax.named_scope("object_corners"):
        odd, even, cross, same, permuted = lax.optimization_barrier((odd, even, cross, same, permuted))
        rows = jnp.stack([odd, even])
        cross_corner = swap_columns(half_lanes(rows, core == 0), 1)
        same_corner = swap_columns(half_lanes(rows, core == 1), 0)

    halo = [odd, even, cross, same, cross_corner, same_corner]
    keep, send, around, *parts = transforms(starts, object_tile, halo, probe, permuted)

    center, even, odd, cross, same, steps = parts
    with jax.named_scope("gradient_columns"):
        cross = swap_columns(cross, 1)
        same = swap_columns(same, 0)

    with jax.named_scope("probe_reduce"):
        chunk, around = lax.optimization_barrier((keep + swap_columns(send, 0), around))
        chunk = lax.all_to_all(chunk, AXES, 0, 0, axis_index_groups=groups, tiled=True)

    with jax.named_scope("gradient_rows"):
        light = illuminate(starts, around, probe)
        even, odd = simple(fold_kernel, [], [even, odd, cross, same], [even.shape] * 2, [], 1 << 20, 1 << 20)
        chunk, light, odd, even = lax.optimization_barrier((chunk, light, odd, even))
        odd = swap_rows(odd, 1)
        even = swap_rows(even, 0)

    with jax.named_scope("probe_sum"):
        total = simple(sum_kernel, [], [chunk], (88, HALF), [], 1 << 20, 1 << 20)
        parts = [total] + [along_z(total, d) for d in (1, 2, 3)]
        shapes = [(16, 64, HALF), (8, HALF)]
        spread_out, ratio = simple(quotient_kernel, [], parts, shapes, [(4, 88, HALF)], 1 << 20, 2 << 20)

    with jax.named_scope("probe_gather"):
        gathered = lax.all_to_all(spread_out, AXES, 0, 0, axis_index_groups=groups, tiled=True)
        gathered, odd, even = lax.optimization_barrier((gathered, odd, even))
        probe_update = assemble(gathered, swap_columns(gathered, 0)).reshape(probe.shape)

    object_update = update([center, even, odd, cross, same, light])
    relative_error = ratio[0, :1]
    position_step = steps[:, 0].reshape(1, 1, -1, 2)
    return (object_update, probe_update, position_step, relative_error)


def solution(mesh):
    in_specs = (
        P(None, "row", "col"),
        P(),
        P("row", "col", None, None, None),
        P("row", "col", None, None),
    )
    out_specs = (P(None, "row", "col"), P(), P("row", "col", None, None), P())
    return jax.shard_map(local, mesh=mesh, in_specs=in_specs, out_specs=out_specs, check_vma=False)
```

```python
import jax
import jax.numpy as jnp
import ml_dtypes
import numpy as np
from jax import lax
from jax.experimental import pallas as pl
from jax.experimental.pallas import tpu as pltpu
from jax.sharding import PartitionSpec as P

intensity_floor = 0.1
object_damping = 1.0
small_value = 1e-06

SIZE = 256
HALF = 128
CHUNK = 32
WIDTH = 2
BF = jnp.bfloat16
F32 = jnp.float32
AXES = ("row", "col")
VMEM_LIMIT = 32 * 2**20


def transform_matrices():
    n = np.arange(HALF)[:, None]
    q = np.arange(HALF)[None, :]
    out = []
    for odd in (0, 1):
        angle = -2.0 * np.pi * ((n * (2 * q + odd)) % SIZE) / SIZE
        re, im = np.cos(angle) / 16.0, np.sin(angle) / 16.0
        out.append(np.block([[re, im], [-im, re]]))
    return out


def split_np(matrix):
    high = matrix.astype(ml_dtypes.bfloat16)
    low = (matrix - high.astype(np.float64)).astype(ml_dtypes.bfloat16)
    return high, low


def constants():
    return np.stack([np.stack([np.stack(split_np(x)) for x in (m, m.T)]) for m in transform_matrices()])


def permutation():
    order = np.concatenate([np.arange(0, SIZE, 2), np.arange(1, SIZE, 2)])
    onehot = np.zeros((SIZE, SIZE), np.float32)
    onehot[order, np.arange(SIZE)] = 1.0
    columns = np.concatenate([onehot] * 3, 0).astype(ml_dtypes.bfloat16)
    rows = np.concatenate([onehot.T] * 3, 1).astype(ml_dtypes.bfloat16)
    return columns, rows


def split2(value):
    high = value.astype(BF)
    return high, (value - high.astype(F32)).astype(BF)


def split3(value):
    high = value.astype(BF)
    rest = value - high.astype(F32)
    middle = rest.astype(BF)
    return high, middle, (rest - middle.astype(F32)).astype(BF)


def dot(a, b):
    return jnp.dot(a, b, preferred_element_type=F32)


def lane_index(rows):
    return lax.broadcasted_iota(jnp.int32, (rows, HALF), 1)


def spread(first, second, shift, lanes):
    a = pltpu.roll(first, shift, 1)
    b = pltpu.roll(second, shift, 1)
    wrapped = lanes < shift
    return jnp.where(wrapped, 0.0, a), jnp.where(wrapped, a, b), jnp.where(wrapped, b, 0.0)


def gather_lanes(blocks, shift, lanes):
    back = jnp.where(shift == 0, 0, HALF - shift)
    a, b, c = [pltpu.roll(x, back, 1) for x in blocks]
    inside = lanes < HALF - shift
    return jnp.where(inside, a, b), jnp.where(inside, b, c)


def fold8(value):
    return jnp.sum(value.reshape(-1, 8, HALF), axis=0)


def prepare_kernel(measured, cols, rows, permuted):
    for j in range(measured.shape[0]):
        moved = dot(jnp.concatenate(split3(measured[j]), 1), cols[...])
        permuted[j] = dot(rows[...], jnp.concatenate(split3(moved), 0))


def place_of():
    return lax.rem(lax.axis_index("row"), 2), lax.rem(lax.axis_index("col"), 2)


def run_all(copies):
    for copy in copies:
        copy.start()
    for copy in copies:
        copy.wait()


def pack_kernel(starts, own, even, odd, cross, same, offsets, sems):
    row_odd, core = place_of()
    lanes = lane_index(8)
    value = jnp.zeros((8, HALF), F32)
    for j in range(starts.shape[1]):
        for d in range(2):
            value = jnp.where(lanes == 2 * j + d, (starts[d, j] + 1).astype(F32), value)
    for p in range(2):
        offsets[p, :, :HALF] = value
        offsets[p, :, HALF:] = value
    top = pl.ds(pl.multiple_of(HALF * row_odd, HALF), HALF)
    bottom = pl.ds(pl.multiple_of(HALF * (1 - row_odd), HALF), HALF)
    near = pl.ds(pl.multiple_of(HALF * core, HALF), HALF)
    far = pl.ds(pl.multiple_of(HALF * (1 - core), HALF), HALF)
    moves = [
        (own.at[:, top, :], odd.at[:, :HALF, :]),
        (own.at[:, bottom, :], even.at[:, :HALF, :]),
        (own.at[:, :, near], cross.at[:, :SIZE, :]),
        (own.at[:, :, far], same.at[:, :SIZE, :]),
        (offsets, odd.at[:, HALF:, :]),
        (offsets, even.at[:, HALF:, :]),
        (offsets.at[:, :, :HALF], cross.at[:, SIZE:, :]),
        (offsets.at[:, :, :HALF], same.at[:, SIZE:, :]),
    ]
    run_all([pltpu.make_async_copy(x, y, sems.at[n]) for n, (x, y) in enumerate(moves)])


def sides():
    row_odd, core = place_of()
    even_rows = pl.ds(pl.multiple_of(3 * HALF * (1 - row_odd), HALF), HALF)
    odd_rows = pl.ds(pl.multiple_of(3 * HALF * row_odd, HALF), HALF)
    return even_rows, odd_rows, 3 * core, 3 - 3 * core


def transform_kernel(
    starts, own, odd_strip, even_strip, cross, same, cross_corner, same_corner, probe_in, matrices, measured,
    keep, send, around, center, even, odd, cross_out, same_out, steps,
    tile, probe, mats, offsets, totals, sums, accum, power, sems, *slots,
):
    step = pl.program_id(0)
    modes = probe.shape[0]
    lanes = lane_index(CHUNK)
    width = measured.shape[0]
    per_slot = len(slots) // width
    slots = [slots[n * per_slot : (n + 1) * per_slot] for n in range(width)]

    @pl.when(step == 0)
    def _():
        even_rows, odd_rows, cross_block, same_block = sides()
        middle = pl.ds(HALF, SIZE)
        moves = [(probe_in, probe), (matrices, mats)]
        for block, strip, corner in ((cross_block, cross, cross_corner), (same_block, same, same_corner)):
            moves.append((strip.at[:, :SIZE, :], tile.at[:, block, middle, :]))
            moves.append((corner.at[1, :, :HALF, :], tile.at[:, block, even_rows, :]))
            moves.append((corner.at[0, :, :HALF, :], tile.at[:, block, odd_rows, :]))
        for b in range(2):
            span = pl.ds(b * HALF, HALF)
            moves.append((own.at[:, :, span], tile.at[:, 1 + b, middle, :]))
            moves.append((even_strip.at[:, :HALF, span], tile.at[:, 1 + b, even_rows, :]))
            moves.append((odd_strip.at[:, :HALF, span], tile.at[:, 1 + b, odd_rows, :]))
        strips = [x.at[0] for x in (odd_strip, even_strip, cross, same)]
        strips += [x.at[n, 0] for x in (cross_corner, same_corner) for n in range(2)]
        for n, strip in enumerate(strips):
            moves.append((strip.at[pl.ds(strip.shape[0] - 8, 8), pl.ds(0, HALF)], offsets.at[n]))
        copies = [pltpu.make_async_copy(x, y, sems.at[n]) for n, (x, y) in enumerate(moves)]
        for copy in copies:
            copy.start()
        tile[:, 4] = jnp.zeros((2, 2 * SIZE, HALF), F32)
        totals[...] = jnp.zeros_like(totals)
        sums[...] = jnp.zeros_like(sums)
        accum[...] = jnp.zeros_like(accum)
        for slot in slots:
            slot[4][:, :, 0:8, :] = jnp.zeros((2, 2, 8, HALF), F32)
            slot[4][:, :, 264:272, :] = jnp.zeros((2, 2, 8, HALF), F32)
        for copy in copies:
            copy.wait()
        for i in range(0, SIZE, CHUNK):
            part = pl.ds(i, CHUNK)
            power[part] = probe_power(probe, part)
        for n in range(8):
            around[pl.ds(n, 1), :] = offsets[n, :1, :].astype(jnp.int32)

    def right(odd, transposed):
        high, low = mats[odd, transposed, 0], mats[odd, transposed, 1]
        return jnp.concatenate([high, high, low], 0)

    def left(odd, transposed):
        high, low = mats[odd, transposed, 0], mats[odd, transposed, 1]
        return jnp.concatenate([high, low, high], 1)

    def position(n):
        col = starts[1, width * step + n]
        return starts[0, width * step + n], col // HALF, lax.rem(col, HALF)

    def enter(n):
        xs, patch = slots[n][0], slots[n][4]
        row, base, shift = position(n)
        for i in range(0, SIZE, CHUNK):
            part = pl.ds(i, CHUNK)
            where = pl.ds(row + i, CHUNK)
            obj = []
            for p in range(2):
                blocks = [tile[p, base + b, where, :] for b in range(3)]
                obj.append(gather_lanes(blocks, shift, lanes))
                for b in range(2):
                    patch[p, b, pl.ds(8 + i, CHUNK), :] = obj[p][b]
            for m in range(modes):
                wave = []
                for b in range(2):
                    span = slice(b * HALF, (b + 1) * HALF)
                    pr, pi = probe[m, 0, part, span], probe[m, 1, part, span]
                    wave.append((pr * obj[0][b] - pi * obj[1][b], pr * obj[1][b] + pi * obj[0][b]))
                for odd in range(2):
                    for p in range(2):
                        high, low = split2(wave[0][p] - wave[1][p] if odd else wave[0][p] + wave[1][p])
                        at = pl.ds(m * SIZE + i, CHUNK)
                        xs[odd, at, p * HALF : (p + 1) * HALF] = high
                        xs[odd, at, SIZE + p * HALF : SIZE + (p + 1) * HALF] = low
                        xs[odd, at, 2 * SIZE + p * HALF : 2 * SIZE + (p + 1) * HALF] = high

    def lanes_forward(n):
        xs, ys = slots[n][0], slots[n][2]
        for odd in range(2):
            ys[odd] = dot(xs[odd], right(odd, 0))

    def rows_split(n):
        zs, ys = slots[n][1], slots[n][2]
        for m in range(modes):
            for odd in range(2):
                lane_span = slice(odd * HALF, (odd + 1) * HALF)
                for i in range(0, HALF, CHUNK):
                    top = ys[odd, pl.ds(m * SIZE + i, CHUNK), :]
                    bottom = ys[odd, pl.ds(m * SIZE + HALF + i, CHUNK), :]
                    for odd_row in range(2):
                        high, low = split2(top - bottom if odd_row else top + bottom)
                        for p in range(2):
                            span = slice(p * HALF, (p + 1) * HALF)
                            at = p * HALF + i
                            zs[m, odd_row, pl.ds(at, CHUNK), lane_span] = high[:, span]
                            zs[m, odd_row, pl.ds(SIZE + at, CHUNK), lane_span] = high[:, span]
                            zs[m, odd_row, pl.ds(2 * SIZE + at, CHUNK), lane_span] = low[:, span]

    def rows_forward(n):
        zs, fs = slots[n][1], slots[n][3]
        for odd_row in range(2):
            for m in range(modes):
                fs[m, odd_row] = dot(left(odd_row, 1), zs[m, odd_row])

    def scale(n):
        zs, fs = slots[n][1], slots[n][3]
        error = jnp.zeros((8, HALF), F32)
        energy = jnp.zeros((8, HALF), F32)
        for odd_row in range(2):
            for i in range(0, HALF, CHUNK):
                parts = [[fs[m, odd_row, pl.ds(p * HALF + i, CHUNK), :] for p in range(2)] for m in range(modes)]
                intensity = parts[0][0] ** 2 + parts[0][1] ** 2 + (parts[1][0] ** 2 + parts[1][1] ** 2)
                intensity = jnp.maximum(intensity, intensity_floor)
                inverse = lax.rsqrt(intensity)
                modulus = intensity * inverse
                amplitude = measured[n, pl.ds(odd_row * HALF + i, CHUNK), :]
                factor = 1.0 - amplitude * inverse
                misfit = (modulus - amplitude) ** 2
                strength = amplitude**2
                error = error + fold8(misfit[:, :HALF]) + fold8(misfit[:, HALF:])
                energy = energy + fold8(strength[:, :HALF]) + fold8(strength[:, HALF:])
                for m in range(modes):
                    for p in range(2):
                        high, low = split2(parts[m][p] * factor)
                        at = p * HALF + i
                        zs[m, odd_row, pl.ds(at, CHUNK), :] = high
                        zs[m, odd_row, pl.ds(SIZE + at, CHUNK), :] = high
                        zs[m, odd_row, pl.ds(2 * SIZE + at, CHUNK), :] = low
        sums[0] += error
        sums[1] += energy

    def rows_back(n):
        zs, fs = slots[n][1], slots[n][3]
        for odd_row in range(2):
            for m in range(modes):
                fs[m, odd_row] = dot(left(odd_row, 0), zs[m, odd_row])

    def rows_join(n):
        xs, fs = slots[n][0], slots[n][3]
        for m in range(modes):
            for i in range(0, HALF, CHUNK):
                for p in range(2):
                    a, b = [fs[m, odd_row, pl.ds(p * HALF + i, CHUNK), :] for odd_row in range(2)]
                    for bottom in range(2):
                        high, low = split2(a - b if bottom else a + b)
                        at = pl.ds(m * SIZE + bottom * HALF + i, CHUNK)
                        for odd in range(2):
                            span = slice(odd * HALF, (odd + 1) * HALF)
                            xs[odd, at, p * HALF : (p + 1) * HALF] = high[:, span]
                            xs[odd, at, SIZE + p * HALF : SIZE + (p + 1) * HALF] = low[:, span]
                            xs[odd, at, 2 * SIZE + p * HALF : 2 * SIZE + (p + 1) * HALF] = high[:, span]

    def lanes_back(n):
        xs, ys = slots[n][0], slots[n][2]
        for odd in range(2):
            ys[odd] = dot(xs[odd], right(odd, 1))

    def leave(n):
        ys, patch = slots[n][2], slots[n][4]
        row, base, shift = position(n)
        first, last = lanes == 0, lanes == HALF - 1
        sums_of = [jnp.zeros((8, HALF), F32) for _ in range(4)]
        for i in range(0, SIZE, CHUNK):
            part = pl.ds(i, CHUNK)
            where = pl.ds(row + i, CHUNK)
            obj = [[patch[p, b, pl.ds(8 + i, CHUNK), :] for b in range(2)] for p in range(2)]
            grads = [[0.0, 0.0], [0.0, 0.0]]
            for b in range(2):
                re, im = obj[0][b], obj[1][b]
                span = slice(b * HALF, (b + 1) * HALF)
                for m in range(modes):
                    at = pl.ds(m * SIZE + i, CHUNK)
                    evens = [ys[0, at, p * HALF : (p + 1) * HALF] for p in range(2)]
                    odds = [ys[1, at, p * HALF : (p + 1) * HALF] for p in range(2)]
                    br, bi = [x - y if b else x + y for x, y in zip(evens, odds)]
                    pr, pi = probe[m, 0, part, span], probe[m, 1, part, span]
                    grads[0][b] = grads[0][b] + (pr * br + pi * bi)
                    grads[1][b] = grads[1][b] + (pr * bi - pi * br)
                    totals[b, 2 * m, part, :] += re * br + im * bi
                    totals[b, 2 * m + 1, part, :] += re * bi - im * br
                totals[b, 4, part, :] += re**2 + im**2
            for p in range(2):
                moved = spread(grads[p][0], grads[p][1], shift, lanes)
                for b in range(3):
                    accum[p, base + b, where, :] += moved[b]
            columns = []
            for p in range(2):
                before = [pltpu.roll(x, 1, 1) for x in obj[p]]
                after = [pltpu.roll(x, HALF - 1, 1) for x in obj[p]]
                columns.append(
                    (
                        jnp.where(last, after[1], after[0]) - jnp.where(first, 0.0, before[0]),
                        jnp.where(last, 0.0, after[1]) - jnp.where(first, before[0], before[1]),
                    )
                )
            for b in range(2):
                strength = power[part, b * HALF : (b + 1) * HALF]
                rows = [patch[p, b, pl.ds(9 + i, CHUNK), :] - patch[p, b, pl.ds(7 + i, CHUNK), :] for p in range(2)]
                for d, slope in enumerate((rows, [columns[0][b], columns[1][b]])):
                    sums_of[2 * d] = sums_of[2 * d] + fold8(grads[0][b] * slope[0] + grads[1][b] * slope[1])
                    sums_of[2 * d + 1] = sums_of[2 * d + 1] + fold8(strength * (slope[0] ** 2 + slope[1] ** 2))
        for d in range(2):
            numerator = 0.5 * jnp.sum(sums_of[2 * d], keepdims=True)
            denominator = 0.25 * jnp.sum(sums_of[2 * d + 1], keepdims=True) + small_value
            at = pl.ds(2 * (width * step + n) + d, 1)
            steps[at, :] = jnp.broadcast_to(-numerator / denominator, (1, HALF))

    stages = [enter, lanes_forward, rows_split, rows_forward, scale, rows_back, rows_join, lanes_back, leave]
    for at in range(len(stages) + width - 1):
        for n in range(width):
            if 0 <= at - n < len(stages):
                stages[at - n](n)

    @pl.when(step == pl.num_programs(0) - 1)
    def _():
        core = place_of()[1]
        scalar = jnp.where(lax.broadcasted_iota(jnp.int32, (1, 8, HALF), 2) == 0, jnp.sum(sums[0]), jnp.sum(sums[1]))
        for out, block in ((keep, core), (send, 1 - core)):
            for c in range(5):
                out[:, 16 * c : 16 * c + 16, :] = totals[block, c].reshape(16, 16, HALF)
            out[:, 80:88, :] = jnp.broadcast_to(scalar, (16, 8, HALF))
        even_rows, odd_rows, cross_block, same_block = sides()
        for p in range(2):
            for b in range(2):
                span = slice(b * HALF, (b + 1) * HALF)
                center[p, :, span] = accum[p, 1 + b, 128:384]
                even[p, :, span] = accum[p, 1 + b, even_rows]
                odd[p, :, span] = accum[p, 1 + b, odd_rows]
            cross_out[p] = accum[p, cross_block]
            same_out[p] = accum[p, same_block]


def probe_power(probe, part):
    return (probe[0, 0, part] ** 2 + probe[0, 1, part] ** 2) + (probe[1, 0, part] ** 2 + probe[1, 1, part] ** 2)


def light_kernel(starts, around, probe, light, power, accum):
    accum[...] = jnp.zeros_like(accum)
    for i in range(0, SIZE, CHUNK):
        part = pl.ds(i, CHUNK)
        total = probe_power(probe, part)
        power[0, part] = total[:, :HALF]
        power[1, part] = total[:, HALF:]
    lanes = lane_index(CHUNK)
    row_odd, core = place_of()
    even, cross = 1 - 2 * row_odd, 2 * core - 1
    neighbours = [(-even, None), (even, None), (None, cross), (None, -cross)]
    neighbours += [(-even, cross), (even, cross), (-even, -cross), (even, -cross)]

    def add(row, col, down, right):
        rows, source_row, row = (SIZE, 0, row + HALF) if down is None else (
            HALF, pl.multiple_of(jnp.where(down < 0, HALF, 0), HALF), row + jnp.where(down < 0, 0, 3 * HALF)
        )
        if right is None:
            col = col + HALF
        else:
            source = jnp.where(right < 0, 1, 0)
            col = col + jnp.where(right < 0, 0, 3 * HALF)
        base, shift = col // HALF, lax.rem(col, HALF)
        for i in range(0, rows, CHUNK):
            part = pl.ds(source_row + i, CHUNK)
            where = pl.ds(row + i, CHUNK)
            if right is None:
                moved = spread(power[0, part], power[1, part], shift, lanes)
            else:
                rolled = pltpu.roll(power[source, part], shift, 1)
                moved = jnp.where(lanes < shift, 0.0, rolled), jnp.where(lanes < shift, rolled, 0.0)
            for b, value in enumerate(moved):
                accum[base + b, where, :] += value

    count = starts.shape[1]
    for j in range(count):
        add(starts[0, j], starts[1, j], None, None)
    for n, (down, right) in enumerate(neighbours):
        for j in range(count):
            row, col = around[n, 2 * j] - 1, around[n, 2 * j + 1] - 1
            near = row >= 0
            if down is not None:
                near = near & jnp.where(down < 0, row > HALF, row < HALF)
            if right is not None:
                near = near & jnp.where(right < 0, col > HALF, col < HALF)

            @pl.when(near)
            def _(row=row, col=col, down=down, right=right):
                add(row, col, down, right)

    light[:, :HALF] = accum[2, 256:512]
    light[:, HALF:] = accum[3, 256:512]


def sum_kernel(chunk, total):
    total[...] = jnp.sum(chunk[...], axis=0)


def quotient_kernel(own, first, second, third, spread_out, ratio, held):
    z = 2 * lax.div(lax.axis_index("row"), 4) + lax.rem(lax.div(lax.axis_index("col"), 2), 2)
    for distance, part in enumerate((own, first, second, third)):
        held[lax.rem(z + 4 - distance, 4)] = part[...]
    total = (held[0] + held[1]) + (held[2] + held[3])
    for c in range(4):
        quotient = total[16 * c : 16 * c + 16] / total[64:80]
        spread_out[:, 16 * c : 16 * c + 16, :] = jnp.broadcast_to(quotient[None], (16, 16, HALF))
    ratio[...] = jnp.broadcast_to(total[80:81, 0:1] / total[80:81, 1:2], (8, HALF))


def fold_kernel(even, odd, cross, same, even_out, odd_out):
    even_rows, odd_rows, _, _ = sides()
    swapped = place_of()[1] == 1
    for p in range(2):
        for strip, rows, out in ((even, even_rows, even_out), (odd, odd_rows, odd_out)):
            a, b = cross[p, rows], same[p, rows]
            out[p, :, :HALF] = strip[p, :, :HALF] + jnp.where(swapped, b, a)
            out[p, :, HALF:] = strip[p, :, HALF:] + jnp.where(swapped, a, b)


def update_kernel(center, even, odd, cross, same, light, out, total):
    for p in range(2):
        total[p] = center[p]
    row_odd, core = place_of()
    even_half = pl.ds(pl.multiple_of(HALF * (1 - row_odd), HALF), HALF)
    odd_half = pl.ds(pl.multiple_of(HALF * row_odd, HALF), HALF)
    for p in range(2):
        total[p, even_half, :] += even[p]
        total[p, odd_half, :] += odd[p]
    swapped = core == 1
    for i in range(0, SIZE, CHUNK):
        part = pl.ds(i, CHUNK)
        scale = 1.0 / (light[part] + object_damping)
        for p in range(2):
            a, b = cross[p, pl.ds(HALF + i, CHUNK)], same[p, pl.ds(HALF + i, CHUNK)]
            out[p, part, :HALF] = (total[p, part, :HALF] + jnp.where(swapped, b, a)) * scale[:, :HALF]
            out[p, part, HALF:] = (total[p, part, HALF:] + jnp.where(swapped, a, b)) * scale[:, HALF:]


def assemble_kernel(mine, other, out):
    core = place_of()[1]

    def write(source, block):
        for c in range(4):
            out[c, :, block * HALF : (block + 1) * HALF] = source[:, 16 * c : 16 * c + 16, :].reshape(SIZE, HALF)

    @pl.when(core == 0)
    def _():
        write(mine, 0)
        write(other, 1)

    @pl.when(core == 1)
    def _():
        write(mine, 1)
        write(other, 0)


def whole(*shape):
    return pl.BlockSpec(shape, lambda *_: (0,) * len(shape))


ANY = pl.BlockSpec(memory_space=pl.ANY)


def shaped(shapes):
    return [jax.ShapeDtypeStruct(s, F32) for s in shapes]


def params():
    return pltpu.CompilerParams(vmem_limit_bytes=VMEM_LIMIT)


def cost(flops, size):
    return pl.CostEstimate(flops=flops, bytes_accessed=size, transcendentals=0)


def simple(kernel, scalars, arrays, shapes, scratch, flops, size):
    single = not isinstance(shapes, list)
    outs = [shapes] if single else shapes
    call = pl.pallas_call(
        kernel,
        out_shape=shaped(outs)[0] if single else shaped(outs),
        grid_spec=pltpu.PrefetchScalarGridSpec(
            num_scalar_prefetch=len(scalars),
            grid=(),
            in_specs=[whole(*x.shape) for x in arrays],
            out_specs=whole(*shapes) if single else [whole(*s) for s in outs],
            scratch_shapes=[pltpu.VMEM(s, F32) for s in scratch],
        ),
        compiler_params=params(),
        cost_estimate=cost(flops, size),
    )
    return call(*scalars, *arrays)


def pack(starts, own):
    rows, columns = (2, HALF + 8, SIZE), (2, SIZE + 8, HALF)
    return pl.pallas_call(
        pack_kernel,
        out_shape=shaped([rows, rows, columns, columns]),
        grid_spec=pltpu.PrefetchScalarGridSpec(
            num_scalar_prefetch=1,
            grid=(),
            in_specs=[pl.BlockSpec(memory_space=pltpu.HBM)],
            out_specs=[ANY] * 4,
            scratch_shapes=[pltpu.VMEM((2, 8, SIZE), F32), pltpu.SemaphoreType.DMA((8,))],
        ),
        compiler_params=params(),
        cost_estimate=cost(1 << 10, 2 << 20),
    )(starts, own)


def prepare(measured):
    cols, rows = permutation()
    arrays = [measured, jnp.asarray(cols), jnp.asarray(rows)]
    return simple(prepare_kernel, [], arrays, measured.shape, [], 1 << 30, 3 << 20)


def stepped(width, *shape):
    return pl.BlockSpec((width, *shape), lambda i, *_: (i,) + (0,) * len(shape))


def transforms(starts, own, halo, probe, measured):
    mats = jnp.asarray(constants())
    arrays = [own, *halo, probe, mats]
    count = measured.shape[0]
    width = WIDTH
    halves = (16, 88, HALF)
    rows, columns = (2, HALF, SIZE), (2, 2 * SIZE, HALF)
    shapes = [(2, SIZE, SIZE), rows, rows, columns, columns, (2 * count, HALF)]
    slot = [
        pltpu.VMEM((2, 2 * SIZE, 3 * SIZE), BF),
        pltpu.VMEM((2, 2, 3 * SIZE, SIZE), BF),
        pltpu.VMEM((2, 2 * SIZE, SIZE), F32),
        pltpu.VMEM((2, 2, SIZE, SIZE), F32),
        pltpu.VMEM((2, 2, SIZE + 16, HALF), F32),
    ]
    return pl.pallas_call(
        transform_kernel,
        out_shape=shaped([halves, halves]) + [jax.ShapeDtypeStruct((8, HALF), jnp.int32)] + shaped(shapes),
        grid_spec=pltpu.PrefetchScalarGridSpec(
            num_scalar_prefetch=1,
            grid=(count // width,),
            in_specs=[ANY] * len(arrays) + [stepped(width, SIZE, SIZE)],
            out_specs=[whole(*x) for x in [halves, halves, (8, HALF), *shapes]],
            scratch_shapes=[
                pltpu.VMEM((2, 5, 2 * SIZE, HALF), F32),
                pltpu.VMEM(probe.shape, F32),
                pltpu.VMEM(mats.shape, BF),
                pltpu.VMEM((8, 8, HALF), F32),
                pltpu.VMEM((2, 5, SIZE, HALF), F32),
                pltpu.VMEM((2, 8, HALF), F32),
                pltpu.VMEM((2, 5, 2 * SIZE, HALF), F32),
                pltpu.VMEM((SIZE, SIZE), F32),
                pltpu.SemaphoreType.DMA((24,)),
            ]
            + slot * width,
        ),
        compiler_params=params(),
        cost_estimate=cost(13 << 30, 12 << 20),
    )(starts, *arrays, measured)


def illuminate(starts, around, probe):
    scratch = [(2, SIZE, HALF), (7, 3 * SIZE, HALF)]
    return simple(light_kernel, [starts, around], [probe], (SIZE, SIZE), scratch, 2 << 30, 4 << 20)


def update(arrays):
    shape = arrays[0].shape
    return simple(update_kernel, [], arrays, shape, [shape], 1 << 20, 3 << 20)


def assemble(mine, other):
    return simple(assemble_kernel, [], [mine, other], (4, SIZE, SIZE), [], 1 << 20, 2 << 20)


def pairs_from(first, count):
    pairs = []
    for i in range(first, count - 1, 2):
        pairs += [(i, i + 1), (i + 1, i)]
    return pairs


def swap_rows(value, first):
    return lax.ppermute(value, "row", pairs_from(first, lax.axis_size("row")))


def swap_columns(value, first):
    return lax.ppermute(value, "col", pairs_from(first, lax.axis_size("col")))


def along_z(value, distance):
    pairs = []
    for row in range(lax.axis_size("row")):
        for col in range(lax.axis_size("col")):
            z = (2 * (row // 4) + col // 2 % 2 + distance) % 4
            target = (4 * (z // 2) + row % 4) * 16 + col // 4 * 4 + 2 * (z % 2) + col % 2
            pairs.append((row * 16 + col, target))
    return lax.ppermute(value, AXES, pairs)


def planes():
    groups = {}
    for row in range(lax.axis_size("row")):
        for col in range(lax.axis_size("col")):
            groups.setdefault((row // 4, col % 4), []).append(row * 16 + col)
    return list(groups.values())


def half_lanes(value, first):
    return jnp.where(first, value[..., :HALF], value[..., HALF:])


def local(object_tile, probe, amplitudes, offsets):
    starts = offsets[0, 0].T
    measured = amplitudes[0, 0]
    core = lax.rem(lax.axis_index("col"), 2)
    groups = planes()

    with jax.named_scope("object_halo"):
        even, odd, cross, same = pack(starts, object_tile)
        cross = swap_columns(cross, 1)
        odd = swap_rows(odd, 1)
        even = swap_rows(even, 0)
        same = swap_columns(same, 0)
    permuted = prepare(measured)
    with jax.named_scope("object_corners"):
        cross, odd, even, same, permuted = lax.optimization_barrier((cross, odd, even, same, permuted))
        rows = jnp.stack([odd, even])
        cross_corner = swap_columns(half_lanes(rows, core == 0), 1)
        same_corner = swap_columns(half_lanes(rows, core == 1), 0)

    halo = [odd, even, cross, same, cross_corner, same_corner]
    keep, send, around, *parts = transforms(starts, object_tile, halo, probe, permuted)

    center, even, odd, cross, same, steps = parts
    with jax.named_scope("gradient_columns"):
        cross = swap_columns(cross, 1)
        same = swap_columns(same, 0)

    with jax.named_scope("probe_reduce"):
        chunk, around = lax.optimization_barrier((keep + swap_columns(send, 0), around))
        chunk = lax.all_to_all(chunk, AXES, 0, 0, axis_index_groups=groups, tiled=True)

    with jax.named_scope("gradient_rows"):
        light = illuminate(starts, around, probe)
        even, odd = simple(fold_kernel, [], [even, odd, cross, same], [even.shape] * 2, [], 1 << 20, 1 << 20)
        chunk, light, odd, even = lax.optimization_barrier((chunk, light, odd, even))
        odd = swap_rows(odd, 1)
        even = swap_rows(even, 0)

    with jax.named_scope("probe_sum"):
        total = simple(sum_kernel, [], [chunk], (88, HALF), [], 1 << 20, 1 << 20)
        parts = [total] + [along_z(total, d) for d in (1, 2, 3)]
        shapes = [(16, 64, HALF), (8, HALF)]
        spread_out, ratio = simple(quotient_kernel, [], parts, shapes, [(4, 88, HALF)], 1 << 20, 2 << 20)
        spread_out, odd, even = lax.optimization_barrier((spread_out, odd, even))
        object_update = update([center, even, odd, cross, same, light])

    with jax.named_scope("probe_gather"):
        gathered = lax.all_to_all(spread_out, AXES, 0, 0, axis_index_groups=groups, tiled=True)
        gathered, object_update = lax.optimization_barrier((gathered, object_update))
        probe_update = assemble(gathered, swap_columns(gathered, 0)).reshape(probe.shape)

    relative_error = ratio[0, :1]
    position_step = steps[:, 0].reshape(1, 1, -1, 2)
    return (object_update, probe_update, position_step, relative_error)


def solution(mesh):
    in_specs = (
        P(None, "row", "col"),
        P(),
        P("row", "col", None, None, None),
        P("row", "col", None, None),
    )
    out_specs = (P(None, "row", "col"), P(), P("row", "col", None, None), P())
    return jax.shard_map(local, mesh=mesh, in_specs=in_specs, out_specs=out_specs, check_vma=False)
```

```python
import jax
import jax.numpy as jnp
import ml_dtypes
import numpy as np
from jax import lax
from jax.experimental import pallas as pl
from jax.experimental.pallas import tpu as pltpu
from jax.sharding import PartitionSpec as P

intensity_floor = 0.1
object_damping = 1.0
small_value = 1e-06

SIZE = 256
HALF = 128
CHUNK = 32
WIDTH = 2
BF = jnp.bfloat16
F32 = jnp.float32
AXES = ("row", "col")
VMEM_LIMIT = 32 * 2**20


def transform_matrices():
    n = np.arange(HALF)[:, None]
    q = np.arange(HALF)[None, :]
    out = []
    for odd in (0, 1):
        angle = -2.0 * np.pi * ((n * (2 * q + odd)) % SIZE) / SIZE
        re, im = np.cos(angle) / 16.0, np.sin(angle) / 16.0
        out.append(np.block([[re, im], [-im, re]]))
    return out


def split_np(matrix):
    high = matrix.astype(ml_dtypes.bfloat16)
    low = (matrix - high.astype(np.float64)).astype(ml_dtypes.bfloat16)
    return high, low


def constants():
    return np.stack([np.stack([np.stack(split_np(x)) for x in (m, m.T)]) for m in transform_matrices()])


def permutation():
    order = np.concatenate([np.arange(0, SIZE, 2), np.arange(1, SIZE, 2)])
    onehot = np.zeros((SIZE, SIZE), np.float32)
    onehot[order, np.arange(SIZE)] = 1.0
    columns = np.concatenate([onehot] * 3, 0).astype(ml_dtypes.bfloat16)
    rows = np.concatenate([onehot.T] * 3, 1).astype(ml_dtypes.bfloat16)
    return columns, rows


def split2(value):
    high = value.astype(BF)
    return high, (value - high.astype(F32)).astype(BF)


def split3(value):
    high = value.astype(BF)
    rest = value - high.astype(F32)
    middle = rest.astype(BF)
    return high, middle, (rest - middle.astype(F32)).astype(BF)


def dot(a, b):
    return jnp.dot(a, b, preferred_element_type=F32)


def lane_index(rows):
    return lax.broadcasted_iota(jnp.int32, (rows, HALF), 1)


def spread(first, second, shift, lanes):
    a = pltpu.roll(first, shift, 1)
    b = pltpu.roll(second, shift, 1)
    wrapped = lanes < shift
    return jnp.where(wrapped, 0.0, a), jnp.where(wrapped, a, b), jnp.where(wrapped, b, 0.0)


def gather_lanes(blocks, shift, lanes):
    back = jnp.where(shift == 0, 0, HALF - shift)
    a, b, c = [pltpu.roll(x, back, 1) for x in blocks]
    inside = lanes < HALF - shift
    return jnp.where(inside, a, b), jnp.where(inside, b, c)


def fold8(value):
    return jnp.sum(value.reshape(-1, 8, HALF), axis=0)


def prepare_kernel(measured, cols, rows, permuted):
    for j in range(measured.shape[0]):
        moved = dot(jnp.concatenate(split3(measured[j]), 1), cols[...])
        permuted[j] = dot(rows[...], jnp.concatenate(split3(moved), 0))


def place_of():
    return lax.rem(lax.axis_index("row"), 2), lax.rem(lax.axis_index("col"), 2)


def run_all(copies):
    for copy in copies:
        copy.start()
    for copy in copies:
        copy.wait()


def pack_kernel(starts, own, even, odd, cross, same, offsets, sems):
    row_odd, core = place_of()
    lanes = lane_index(8)
    value = jnp.zeros((8, HALF), F32)
    for j in range(starts.shape[1]):
        for d in range(2):
            value = jnp.where(lanes == 2 * j + d, (starts[d, j] + 1).astype(F32), value)
    for p in range(2):
        offsets[p, :, :HALF] = value
        offsets[p, :, HALF:] = value
    top = pl.ds(pl.multiple_of(HALF * row_odd, HALF), HALF)
    bottom = pl.ds(pl.multiple_of(HALF * (1 - row_odd), HALF), HALF)
    near = pl.ds(pl.multiple_of(HALF * core, HALF), HALF)
    far = pl.ds(pl.multiple_of(HALF * (1 - core), HALF), HALF)
    moves = [
        (own.at[:, top, :], odd.at[:, :HALF, :]),
        (own.at[:, bottom, :], even.at[:, :HALF, :]),
        (own.at[:, :, near], cross.at[:, :SIZE, :]),
        (own.at[:, :, far], same.at[:, :SIZE, :]),
        (offsets, odd.at[:, HALF:, :]),
        (offsets, even.at[:, HALF:, :]),
        (offsets.at[:, :, :HALF], cross.at[:, SIZE:, :]),
        (offsets.at[:, :, :HALF], same.at[:, SIZE:, :]),
    ]
    run_all([pltpu.make_async_copy(x, y, sems.at[n]) for n, (x, y) in enumerate(moves)])


def sides():
    row_odd, core = place_of()
    even_rows = pl.ds(pl.multiple_of(3 * HALF * (1 - row_odd), HALF), HALF)
    odd_rows = pl.ds(pl.multiple_of(3 * HALF * row_odd, HALF), HALF)
    return even_rows, odd_rows, 3 * core, 3 - 3 * core


def transform_kernel(
    starts, own, odd_strip, even_strip, cross, same, cross_corner, same_corner, probe_in, matrices, measured,
    keep, send, around, center, even, odd, cross_out, same_out, steps,
    tile, probe, mats, offsets, totals, sums, accum, power, sems, *slots,
):
    step = pl.program_id(0)
    modes = probe.shape[0]
    lanes = lane_index(CHUNK)
    width = measured.shape[0]
    per_slot = len(slots) // width
    slots = [slots[n * per_slot : (n + 1) * per_slot] for n in range(width)]

    @pl.when(step == 0)
    def _():
        even_rows, odd_rows, cross_block, same_block = sides()
        middle = pl.ds(HALF, SIZE)
        moves = [(probe_in, probe), (matrices, mats)]
        for block, strip, corner in ((cross_block, cross, cross_corner), (same_block, same, same_corner)):
            moves.append((strip.at[:, :SIZE, :], tile.at[:, block, middle, :]))
            moves.append((corner.at[1, :, :HALF, :], tile.at[:, block, even_rows, :]))
            moves.append((corner.at[0, :, :HALF, :], tile.at[:, block, odd_rows, :]))
        for b in range(2):
            span = pl.ds(b * HALF, HALF)
            moves.append((own.at[:, :, span], tile.at[:, 1 + b, middle, :]))
            moves.append((even_strip.at[:, :HALF, span], tile.at[:, 1 + b, even_rows, :]))
            moves.append((odd_strip.at[:, :HALF, span], tile.at[:, 1 + b, odd_rows, :]))
        strips = [x.at[0] for x in (odd_strip, even_strip, cross, same)]
        strips += [x.at[n, 0] for x in (cross_corner, same_corner) for n in range(2)]
        for n, strip in enumerate(strips):
            moves.append((strip.at[pl.ds(strip.shape[0] - 8, 8), pl.ds(0, HALF)], offsets.at[n]))
        copies = [pltpu.make_async_copy(x, y, sems.at[n]) for n, (x, y) in enumerate(moves)]
        for copy in copies:
            copy.start()
        tile[:, 4] = jnp.zeros((2, 2 * SIZE, HALF), F32)
        totals[...] = jnp.zeros_like(totals)
        sums[...] = jnp.zeros_like(sums)
        accum[...] = jnp.zeros_like(accum)
        for slot in slots:
            slot[4][:, :, 0:8, :] = jnp.zeros((2, 2, 8, HALF), F32)
            slot[4][:, :, 264:272, :] = jnp.zeros((2, 2, 8, HALF), F32)
        for copy in copies:
            copy.wait()
        for i in range(0, SIZE, CHUNK):
            part = pl.ds(i, CHUNK)
            power[part] = probe_power(probe, part)
        for n in range(8):
            around[pl.ds(n, 1), :] = offsets[n, :1, :].astype(jnp.int32)

    def right(odd, transposed):
        high, low = mats[odd, transposed, 0], mats[odd, transposed, 1]
        return jnp.concatenate([high, high, low], 0)

    def left(odd, transposed):
        high, low = mats[odd, transposed, 0], mats[odd, transposed, 1]
        return jnp.concatenate([high, low, high], 1)

    def position(n):
        col = starts[1, width * step + n]
        return starts[0, width * step + n], col // HALF, lax.rem(col, HALF)

    def enter(n):
        xs, patch = slots[n][0], slots[n][4]
        row, base, shift = position(n)
        for i in range(0, SIZE, CHUNK):
            part = pl.ds(i, CHUNK)
            where = pl.ds(row + i, CHUNK)
            obj = []
            for p in range(2):
                blocks = [tile[p, base + b, where, :] for b in range(3)]
                obj.append(gather_lanes(blocks, shift, lanes))
                for b in range(2):
                    patch[p, b, pl.ds(8 + i, CHUNK), :] = obj[p][b]
            for m in range(modes):
                wave = []
                for b in range(2):
                    span = slice(b * HALF, (b + 1) * HALF)
                    pr, pi = probe[m, 0, part, span], probe[m, 1, part, span]
                    wave.append((pr * obj[0][b] - pi * obj[1][b], pr * obj[1][b] + pi * obj[0][b]))
                for odd in range(2):
                    for p in range(2):
                        high, low = split2(wave[0][p] - wave[1][p] if odd else wave[0][p] + wave[1][p])
                        at = pl.ds(m * SIZE + i, CHUNK)
                        xs[odd, at, p * HALF : (p + 1) * HALF] = high
                        xs[odd, at, SIZE + p * HALF : SIZE + (p + 1) * HALF] = low
                        xs[odd, at, 2 * SIZE + p * HALF : 2 * SIZE + (p + 1) * HALF] = high

    def lanes_forward(n):
        xs, ys = slots[n][0], slots[n][2]
        for odd in range(2):
            ys[odd] = dot(xs[odd], right(odd, 0))

    def rows_split(n):
        zs, ys = slots[n][1], slots[n][2]
        for m in range(modes):
            for odd in range(2):
                lane_span = slice(odd * HALF, (odd + 1) * HALF)
                for i in range(0, HALF, CHUNK):
                    top = ys[odd, pl.ds(m * SIZE + i, CHUNK), :]
                    bottom = ys[odd, pl.ds(m * SIZE + HALF + i, CHUNK), :]
                    for odd_row in range(2):
                        high, low = split2(top - bottom if odd_row else top + bottom)
                        for p in range(2):
                            span = slice(p * HALF, (p + 1) * HALF)
                            at = p * HALF + i
                            zs[m, odd_row, pl.ds(at, CHUNK), lane_span] = high[:, span]
                            zs[m, odd_row, pl.ds(SIZE + at, CHUNK), lane_span] = high[:, span]
                            zs[m, odd_row, pl.ds(2 * SIZE + at, CHUNK), lane_span] = low[:, span]

    def rows_forward(n):
        zs, fs = slots[n][1], slots[n][3]
        for odd_row in range(2):
            for m in range(modes):
                fs[m, odd_row] = dot(left(odd_row, 1), zs[m, odd_row])

    def scale(n):
        zs, fs = slots[n][1], slots[n][3]
        error = jnp.zeros((8, HALF), F32)
        energy = jnp.zeros((8, HALF), F32)
        for odd_row in range(2):
            for i in range(0, HALF, CHUNK):
                parts = [[fs[m, odd_row, pl.ds(p * HALF + i, CHUNK), :] for p in range(2)] for m in range(modes)]
                intensity = parts[0][0] ** 2 + parts[0][1] ** 2 + (parts[1][0] ** 2 + parts[1][1] ** 2)
                intensity = jnp.maximum(intensity, intensity_floor)
                inverse = lax.rsqrt(intensity)
                modulus = intensity * inverse
                amplitude = measured[n, pl.ds(odd_row * HALF + i, CHUNK), :]
                factor = 1.0 - amplitude * inverse
                misfit = (modulus - amplitude) ** 2
                strength = amplitude**2
                error = error + fold8(misfit[:, :HALF]) + fold8(misfit[:, HALF:])
                energy = energy + fold8(strength[:, :HALF]) + fold8(strength[:, HALF:])
                for m in range(modes):
                    for p in range(2):
                        high, low = split2(parts[m][p] * factor)
                        at = p * HALF + i
                        zs[m, odd_row, pl.ds(at, CHUNK), :] = high
                        zs[m, odd_row, pl.ds(SIZE + at, CHUNK), :] = high
                        zs[m, odd_row, pl.ds(2 * SIZE + at, CHUNK), :] = low
        sums[0] += error
        sums[1] += energy

    def rows_back(n):
        zs, fs = slots[n][1], slots[n][3]
        for odd_row in range(2):
            for m in range(modes):
                fs[m, odd_row] = dot(left(odd_row, 0), zs[m, odd_row])

    def rows_join(n):
        xs, fs = slots[n][0], slots[n][3]
        for m in range(modes):
            for i in range(0, HALF, CHUNK):
                for p in range(2):
                    a, b = [fs[m, odd_row, pl.ds(p * HALF + i, CHUNK), :] for odd_row in range(2)]
                    for bottom in range(2):
                        high, low = split2(a - b if bottom else a + b)
                        at = pl.ds(m * SIZE + bottom * HALF + i, CHUNK)
                        for odd in range(2):
                            span = slice(odd * HALF, (odd + 1) * HALF)
                            xs[odd, at, p * HALF : (p + 1) * HALF] = high[:, span]
                            xs[odd, at, SIZE + p * HALF : SIZE + (p + 1) * HALF] = low[:, span]
                            xs[odd, at, 2 * SIZE + p * HALF : 2 * SIZE + (p + 1) * HALF] = high[:, span]

    def lanes_back(n):
        xs, ys = slots[n][0], slots[n][2]
        for odd in range(2):
            ys[odd] = dot(xs[odd], right(odd, 1))

    def leave(n):
        ys, patch = slots[n][2], slots[n][4]
        row, base, shift = position(n)
        first, last = lanes == 0, lanes == HALF - 1
        sums_of = [jnp.zeros((8, HALF), F32) for _ in range(4)]
        for i in range(0, SIZE, CHUNK):
            part = pl.ds(i, CHUNK)
            where = pl.ds(row + i, CHUNK)
            obj = [[patch[p, b, pl.ds(8 + i, CHUNK), :] for b in range(2)] for p in range(2)]
            grads = [[0.0, 0.0], [0.0, 0.0]]
            for b in range(2):
                re, im = obj[0][b], obj[1][b]
                span = slice(b * HALF, (b + 1) * HALF)
                for m in range(modes):
                    at = pl.ds(m * SIZE + i, CHUNK)
                    evens = [ys[0, at, p * HALF : (p + 1) * HALF] for p in range(2)]
                    odds = [ys[1, at, p * HALF : (p + 1) * HALF] for p in range(2)]
                    br, bi = [x - y if b else x + y for x, y in zip(evens, odds)]
                    pr, pi = probe[m, 0, part, span], probe[m, 1, part, span]
                    grads[0][b] = grads[0][b] + (pr * br + pi * bi)
                    grads[1][b] = grads[1][b] + (pr * bi - pi * br)
                    totals[b, 2 * m, part, :] += re * br + im * bi
                    totals[b, 2 * m + 1, part, :] += re * bi - im * br
                totals[b, 4, part, :] += re**2 + im**2
            for p in range(2):
                moved = spread(grads[p][0], grads[p][1], shift, lanes)
                for b in range(3):
                    accum[p, base + b, where, :] += moved[b]
            columns = []
            for p in range(2):
                before = [pltpu.roll(x, 1, 1) for x in obj[p]]
                after = [pltpu.roll(x, HALF - 1, 1) for x in obj[p]]
                columns.append(
                    (
                        jnp.where(last, after[1], after[0]) - jnp.where(first, 0.0, before[0]),
                        jnp.where(last, 0.0, after[1]) - jnp.where(first, before[0], before[1]),
                    )
                )
            for b in range(2):
                strength = power[part, b * HALF : (b + 1) * HALF]
                rows = [patch[p, b, pl.ds(9 + i, CHUNK), :] - patch[p, b, pl.ds(7 + i, CHUNK), :] for p in range(2)]
                for d, slope in enumerate((rows, [columns[0][b], columns[1][b]])):
                    sums_of[2 * d] = sums_of[2 * d] + fold8(grads[0][b] * slope[0] + grads[1][b] * slope[1])
                    sums_of[2 * d + 1] = sums_of[2 * d + 1] + fold8(strength * (slope[0] ** 2 + slope[1] ** 2))
        for d in range(2):
            numerator = 0.5 * jnp.sum(sums_of[2 * d], keepdims=True)
            denominator = 0.25 * jnp.sum(sums_of[2 * d + 1], keepdims=True) + small_value
            at = pl.ds(2 * (width * step + n) + d, 1)
            steps[at, :] = jnp.broadcast_to(-numerator / denominator, (1, HALF))

    stages = [enter, lanes_forward, rows_split, rows_forward, scale, rows_back, rows_join, lanes_back, leave]
    for at in range(len(stages) + width - 1):
        for n in range(width):
            if 0 <= at - n < len(stages):
                stages[at - n](n)

    @pl.when(step == pl.num_programs(0) - 1)
    def _():
        core = place_of()[1]
        scalar = jnp.where(lax.broadcasted_iota(jnp.int32, (1, 8, HALF), 2) == 0, jnp.sum(sums[0]), jnp.sum(sums[1]))
        for out, block in ((keep, core), (send, 1 - core)):
            for c in range(5):
                out[:, 16 * c : 16 * c + 16, :] = totals[block, c].reshape(16, 16, HALF)
            out[:, 80:88, :] = jnp.broadcast_to(scalar, (16, 8, HALF))
        even_rows, odd_rows, cross_block, same_block = sides()
        for p in range(2):
            for b in range(2):
                span = slice(b * HALF, (b + 1) * HALF)
                center[p, :, span] = accum[p, 1 + b, 128:384]
                even[p, :, span] = accum[p, 1 + b, even_rows]
                odd[p, :, span] = accum[p, 1 + b, odd_rows]
            cross_out[p] = accum[p, cross_block]
            same_out[p] = accum[p, same_block]


def probe_power(probe, part):
    return (probe[0, 0, part] ** 2 + probe[0, 1, part] ** 2) + (probe[1, 0, part] ** 2 + probe[1, 1, part] ** 2)


def light_kernel(starts, around, probe, light, power, accum):
    accum[...] = jnp.zeros_like(accum)
    for i in range(0, SIZE, CHUNK):
        part = pl.ds(i, CHUNK)
        total = probe_power(probe, part)
        power[0, part] = total[:, :HALF]
        power[1, part] = total[:, HALF:]
    lanes = lane_index(CHUNK)
    row_odd, core = place_of()
    even, cross = 1 - 2 * row_odd, 2 * core - 1
    neighbours = [(-even, None), (even, None), (None, cross), (None, -cross)]
    neighbours += [(-even, cross), (even, cross), (-even, -cross), (even, -cross)]

    def add(row, col, down, right):
        rows, source_row, row = (SIZE, 0, row + HALF) if down is None else (
            HALF, pl.multiple_of(jnp.where(down < 0, HALF, 0), HALF), row + jnp.where(down < 0, 0, 3 * HALF)
        )
        if right is None:
            col = col + HALF
        else:
            source = jnp.where(right < 0, 1, 0)
            col = col + jnp.where(right < 0, 0, 3 * HALF)
        base, shift = col // HALF, lax.rem(col, HALF)
        for i in range(0, rows, CHUNK):
            part = pl.ds(source_row + i, CHUNK)
            where = pl.ds(row + i, CHUNK)
            if right is None:
                moved = spread(power[0, part], power[1, part], shift, lanes)
            else:
                rolled = pltpu.roll(power[source, part], shift, 1)
                moved = jnp.where(lanes < shift, 0.0, rolled), jnp.where(lanes < shift, rolled, 0.0)
            for b, value in enumerate(moved):
                accum[base + b, where, :] += value

    count = starts.shape[1]
    for j in range(count):
        add(starts[0, j], starts[1, j], None, None)
    for n, (down, right) in enumerate(neighbours):
        for j in range(count):
            row, col = around[n, 2 * j] - 1, around[n, 2 * j + 1] - 1
            near = row >= 0
            if down is not None:
                near = near & jnp.where(down < 0, row > HALF, row < HALF)
            if right is not None:
                near = near & jnp.where(right < 0, col > HALF, col < HALF)

            @pl.when(near)
            def _(row=row, col=col, down=down, right=right):
                add(row, col, down, right)

    light[:, :HALF] = accum[2, 256:512]
    light[:, HALF:] = accum[3, 256:512]


def sum_kernel(chunk, total):
    total[...] = jnp.sum(chunk[...], axis=0)


def quotient_kernel(own, first, second, third, spread_out, ratio, held):
    z = 2 * lax.div(lax.axis_index("row"), 4) + lax.rem(lax.div(lax.axis_index("col"), 2), 2)
    for distance, part in enumerate((own, first, second, third)):
        held[lax.rem(z + 4 - distance, 4)] = part[...]
    total = (held[0] + held[1]) + (held[2] + held[3])
    for c in range(4):
        quotient = total[16 * c : 16 * c + 16] / total[64:80]
        spread_out[:, 16 * c : 16 * c + 16, :] = jnp.broadcast_to(quotient[None], (16, 16, HALF))
    ratio[...] = jnp.broadcast_to(total[80:81, 0:1] / total[80:81, 1:2], (8, HALF))


def fold_kernel(even, odd, cross, same, even_out, odd_out):
    even_rows, odd_rows, _, _ = sides()
    swapped = place_of()[1] == 1
    for p in range(2):
        for strip, rows, out in ((even, even_rows, even_out), (odd, odd_rows, odd_out)):
            a, b = cross[p, rows], same[p, rows]
            out[p, :, :HALF] = strip[p, :, :HALF] + jnp.where(swapped, b, a)
            out[p, :, HALF:] = strip[p, :, HALF:] + jnp.where(swapped, a, b)


def update_kernel(center, even, odd, cross, same, light, out, total):
    for p in range(2):
        total[p] = center[p]
    row_odd, core = place_of()
    even_half = pl.ds(pl.multiple_of(HALF * (1 - row_odd), HALF), HALF)
    odd_half = pl.ds(pl.multiple_of(HALF * row_odd, HALF), HALF)
    for p in range(2):
        total[p, even_half, :] += even[p]
        total[p, odd_half, :] += odd[p]
    swapped = core == 1
    for i in range(0, SIZE, CHUNK):
        part = pl.ds(i, CHUNK)
        scale = 1.0 / (light[part] + object_damping)
        for p in range(2):
            a, b = cross[p, pl.ds(HALF + i, CHUNK)], same[p, pl.ds(HALF + i, CHUNK)]
            out[p, part, :HALF] = (total[p, part, :HALF] + jnp.where(swapped, b, a)) * scale[:, :HALF]
            out[p, part, HALF:] = (total[p, part, HALF:] + jnp.where(swapped, a, b)) * scale[:, HALF:]


def assemble_kernel(mine, other, out):
    core = place_of()[1]

    def write(source, block):
        for c in range(4):
            out[c, :, block * HALF : (block + 1) * HALF] = source[:, 16 * c : 16 * c + 16, :].reshape(SIZE, HALF)

    @pl.when(core == 0)
    def _():
        write(mine, 0)
        write(other, 1)

    @pl.when(core == 1)
    def _():
        write(mine, 1)
        write(other, 0)


def whole(*shape):
    return pl.BlockSpec(shape, lambda *_: (0,) * len(shape))


ANY = pl.BlockSpec(memory_space=pl.ANY)


def shaped(shapes):
    return [jax.ShapeDtypeStruct(s, F32) for s in shapes]


def params(limit=VMEM_LIMIT):
    return pltpu.CompilerParams(vmem_limit_bytes=limit)


def cost(flops, size):
    return pl.CostEstimate(flops=flops, bytes_accessed=size, transcendentals=0)


def simple(kernel, scalars, arrays, shapes, scratch, flops, size):
    single = not isinstance(shapes, list)
    outs = [shapes] if single else shapes
    call = pl.pallas_call(
        kernel,
        out_shape=shaped(outs)[0] if single else shaped(outs),
        grid_spec=pltpu.PrefetchScalarGridSpec(
            num_scalar_prefetch=len(scalars),
            grid=(),
            in_specs=[whole(*x.shape) for x in arrays],
            out_specs=whole(*shapes) if single else [whole(*s) for s in outs],
            scratch_shapes=[pltpu.VMEM(s, F32) for s in scratch],
        ),
        compiler_params=params(),
        cost_estimate=cost(flops, size),
    )
    return call(*scalars, *arrays)


def pack(starts, own):
    rows, columns = (2, HALF + 8, SIZE), (2, SIZE + 8, HALF)
    return pl.pallas_call(
        pack_kernel,
        out_shape=shaped([rows, rows, columns, columns]),
        grid_spec=pltpu.PrefetchScalarGridSpec(
            num_scalar_prefetch=1,
            grid=(),
            in_specs=[pl.BlockSpec(memory_space=pltpu.HBM)],
            out_specs=[ANY] * 4,
            scratch_shapes=[pltpu.VMEM((2, 8, SIZE), F32), pltpu.SemaphoreType.DMA((8,))],
        ),
        compiler_params=params(60 * 2**20),
        cost_estimate=cost(1 << 10, 2 << 20),
    )(starts, own)


def prepare(measured):
    cols, rows = permutation()
    arrays = [measured, jnp.asarray(cols), jnp.asarray(rows)]
    return simple(prepare_kernel, [], arrays, measured.shape, [], 1 << 30, 3 << 20)


def stepped(width, *shape):
    return pl.BlockSpec((width, *shape), lambda i, *_: (i,) + (0,) * len(shape))


def transforms(starts, own, halo, probe, measured):
    mats = jnp.asarray(constants())
    arrays = [own, *halo, probe, mats]
    count = measured.shape[0]
    width = WIDTH
    halves = (16, 88, HALF)
    rows, columns = (2, HALF, SIZE), (2, 2 * SIZE, HALF)
    shapes = [(2, SIZE, SIZE), rows, rows, columns, columns, (2 * count, HALF)]
    slot = [
        pltpu.VMEM((2, 2 * SIZE, 3 * SIZE), BF),
        pltpu.VMEM((2, 2, 3 * SIZE, SIZE), BF),
        pltpu.VMEM((2, 2 * SIZE, SIZE), F32),
        pltpu.VMEM((2, 2, SIZE, SIZE), F32),
        pltpu.VMEM((2, 2, SIZE + 16, HALF), F32),
    ]
    return pl.pallas_call(
        transform_kernel,
        out_shape=shaped([halves, halves]) + [jax.ShapeDtypeStruct((8, HALF), jnp.int32)] + shaped(shapes),
        grid_spec=pltpu.PrefetchScalarGridSpec(
            num_scalar_prefetch=1,
            grid=(count // width,),
            in_specs=[ANY] * len(arrays) + [stepped(width, SIZE, SIZE)],
            out_specs=[whole(*x) for x in [halves, halves, (8, HALF), *shapes]],
            scratch_shapes=[
                pltpu.VMEM((2, 5, 2 * SIZE, HALF), F32),
                pltpu.VMEM(probe.shape, F32),
                pltpu.VMEM(mats.shape, BF),
                pltpu.VMEM((8, 8, HALF), F32),
                pltpu.VMEM((2, 5, SIZE, HALF), F32),
                pltpu.VMEM((2, 8, HALF), F32),
                pltpu.VMEM((2, 5, 2 * SIZE, HALF), F32),
                pltpu.VMEM((SIZE, SIZE), F32),
                pltpu.SemaphoreType.DMA((24,)),
            ]
            + slot * width,
        ),
        compiler_params=params(),
        cost_estimate=cost(13 << 30, 12 << 20),
    )(starts, *arrays, measured)


def illuminate(starts, around, probe):
    scratch = [(2, SIZE, HALF), (7, 3 * SIZE, HALF)]
    return simple(light_kernel, [starts, around], [probe], (SIZE, SIZE), scratch, 2 << 30, 4 << 20)


def update(arrays):
    shape = arrays[0].shape
    return simple(update_kernel, [], arrays, shape, [shape], 1 << 20, 3 << 20)


def assemble(mine, other):
    return simple(assemble_kernel, [], [mine, other], (4, SIZE, SIZE), [], 1 << 20, 2 << 20)


def pairs_from(first, count):
    pairs = []
    for i in range(first, count - 1, 2):
        pairs += [(i, i + 1), (i + 1, i)]
    return pairs


def swap_rows(value, first):
    return lax.ppermute(value, "row", pairs_from(first, lax.axis_size("row")))


def swap_columns(value, first):
    return lax.ppermute(value, "col", pairs_from(first, lax.axis_size("col")))


def along_z(value, distance):
    pairs = []
    for row in range(lax.axis_size("row")):
        for col in range(lax.axis_size("col")):
            z = (2 * (row // 4) + col // 2 % 2 + distance) % 4
            target = (4 * (z // 2) + row % 4) * 16 + col // 4 * 4 + 2 * (z % 2) + col % 2
            pairs.append((row * 16 + col, target))
    return lax.ppermute(value, AXES, pairs)


def planes():
    groups = {}
    for row in range(lax.axis_size("row")):
        for col in range(lax.axis_size("col")):
            groups.setdefault((row // 4, col % 4), []).append(row * 16 + col)
    return list(groups.values())


def half_lanes(value, first):
    return jnp.where(first, value[..., :HALF], value[..., HALF:])


def local(object_tile, probe, amplitudes, offsets):
    starts = offsets[0, 0].T
    measured = amplitudes[0, 0]
    core = lax.rem(lax.axis_index("col"), 2)
    groups = planes()

    with jax.named_scope("object_halo"):
        even, odd, cross, same = pack(starts, object_tile)
        odd = swap_rows(odd, 1)
        even = swap_rows(even, 0)
        cross = swap_columns(cross, 1)
        same = swap_columns(same, 0)
    permuted = prepare(measured)
    with jax.named_scope("object_corners"):
        odd, even, cross, same, permuted = lax.optimization_barrier((odd, even, cross, same, permuted))
        rows = jnp.stack([odd, even])
        cross_corner = swap_columns(half_lanes(rows, core == 0), 1)
        same_corner = swap_columns(half_lanes(rows, core == 1), 0)

    halo = [odd, even, cross, same, cross_corner, same_corner]
    keep, send, around, *parts = transforms(starts, object_tile, halo, probe, permuted)

    center, even, odd, cross, same, steps = parts
    with jax.named_scope("gradient_columns"):
        cross = swap_columns(cross, 1)
        same = swap_columns(same, 0)

    with jax.named_scope("probe_reduce"):
        chunk, around = lax.optimization_barrier((keep + swap_columns(send, 0), around))
        chunk = lax.all_to_all(chunk, AXES, 0, 0, axis_index_groups=groups, tiled=True)

    with jax.named_scope("gradient_rows"):
        light = illuminate(starts, around, probe)
        even, odd = simple(fold_kernel, [], [even, odd, cross, same], [even.shape] * 2, [], 1 << 20, 1 << 20)
        chunk, light, odd, even = lax.optimization_barrier((chunk, light, odd, even))
        odd = swap_rows(odd, 1)
        even = swap_rows(even, 0)

    with jax.named_scope("probe_sum"):
        total = simple(sum_kernel, [], [chunk], (88, HALF), [], 1 << 20, 1 << 20)
        parts = [total] + [along_z(total, d) for d in (1, 2, 3)]
        shapes = [(16, 64, HALF), (8, HALF)]
        spread_out, ratio = simple(quotient_kernel, [], parts, shapes, [(4, 88, HALF)], 1 << 20, 2 << 20)

    with jax.named_scope("probe_gather"):
        gathered = lax.all_to_all(spread_out, AXES, 0, 0, axis_index_groups=groups, tiled=True)
        relative_error = ratio[0, :1]
        position_step = steps[:, 0].reshape(1, 1, -1, 2)
        tied = (gathered, odd, even, relative_error, position_step)
        gathered, odd, even, relative_error, position_step = lax.optimization_barrier(tied)
        probe_update = assemble(gathered, swap_columns(gathered, 0)).reshape(probe.shape)

    object_update = update([center, even, odd, cross, same, light])
    return (object_update, probe_update, position_step, relative_error)


def solution(mesh):
    in_specs = (
        P(None, "row", "col"),
        P(),
        P("row", "col", None, None, None),
        P("row", "col", None, None),
    )
    out_specs = (P(None, "row", "col"), P(), P("row", "col", None, None), P())
    return jax.shard_map(local, mesh=mesh, in_specs=in_specs, out_specs=out_specs, check_vma=False)
```

```python
import jax
import jax.numpy as jnp
import ml_dtypes
import numpy as np
from jax import lax
from jax.experimental import pallas as pl
from jax.experimental.pallas import tpu as pltpu
from jax.sharding import PartitionSpec as P

intensity_floor = 0.1
object_damping = 1.0
small_value = 1e-06

SIZE = 256
HALF = 128
CHUNK = 32
WIDTH = 2
BF = jnp.bfloat16
F32 = jnp.float32
AXES = ("row", "col")
VMEM_LIMIT = 32 * 2**20


def transform_matrices():
    n = np.arange(HALF)[:, None]
    q = np.arange(HALF)[None, :]
    out = []
    for odd in (0, 1):
        angle = -2.0 * np.pi * ((n * (2 * q + odd)) % SIZE) / SIZE
        re, im = np.cos(angle) / 16.0, np.sin(angle) / 16.0
        out.append(np.block([[re, im], [-im, re]]))
    return out


def split_np(matrix):
    high = matrix.astype(ml_dtypes.bfloat16)
    low = (matrix - high.astype(np.float64)).astype(ml_dtypes.bfloat16)
    return high, low


def constants():
    return np.stack([np.stack([np.stack(split_np(x)) for x in (m, m.T)]) for m in transform_matrices()])


def permutation():
    order = np.concatenate([np.arange(0, SIZE, 2), np.arange(1, SIZE, 2)])
    onehot = np.zeros((SIZE, SIZE), np.float32)
    onehot[order, np.arange(SIZE)] = 1.0
    columns = np.concatenate([onehot] * 3, 0).astype(ml_dtypes.bfloat16)
    rows = np.concatenate([onehot.T] * 3, 1).astype(ml_dtypes.bfloat16)
    return columns, rows


def split2(value):
    high = value.astype(BF)
    return high, (value - high.astype(F32)).astype(BF)


def split3(value):
    high = value.astype(BF)
    rest = value - high.astype(F32)
    middle = rest.astype(BF)
    return high, middle, (rest - middle.astype(F32)).astype(BF)


def dot(a, b):
    return jnp.dot(a, b, preferred_element_type=F32)


def lane_index(rows):
    return lax.broadcasted_iota(jnp.int32, (rows, HALF), 1)


def spread(first, second, shift, lanes):
    a = pltpu.roll(first, shift, 1)
    b = pltpu.roll(second, shift, 1)
    wrapped = lanes < shift
    return jnp.where(wrapped, 0.0, a), jnp.where(wrapped, a, b), jnp.where(wrapped, b, 0.0)


def gather_lanes(blocks, shift, lanes):
    back = jnp.where(shift == 0, 0, HALF - shift)
    a, b, c = [pltpu.roll(x, back, 1) for x in blocks]
    inside = lanes < HALF - shift
    return jnp.where(inside, a, b), jnp.where(inside, b, c)


def fold8(value):
    return jnp.sum(value.reshape(-1, 8, HALF), axis=0)


def prepare_kernel(measured, cols, rows, permuted):
    for j in range(measured.shape[0]):
        moved = dot(jnp.concatenate(split3(measured[j]), 1), cols[...])
        permuted[j] = dot(rows[...], jnp.concatenate(split3(moved), 0))


def place_of():
    return lax.rem(lax.axis_index("row"), 2), lax.rem(lax.axis_index("col"), 2)


def run_all(copies):
    for copy in copies:
        copy.start()
    for copy in copies:
        copy.wait()


def pack_kernel(starts, own, even, odd, cross, same, offsets, sems):
    row_odd, core = place_of()
    lanes = lane_index(8)
    value = jnp.zeros((8, HALF), F32)
    for j in range(starts.shape[1]):
        for d in range(2):
            value = jnp.where(lanes == 2 * j + d, (starts[d, j] + 1).astype(F32), value)
    for p in range(2):
        offsets[p, :, :HALF] = value
        offsets[p, :, HALF:] = value
    top = pl.ds(pl.multiple_of(HALF * row_odd, HALF), HALF)
    bottom = pl.ds(pl.multiple_of(HALF * (1 - row_odd), HALF), HALF)
    near = pl.ds(pl.multiple_of(HALF * core, HALF), HALF)
    far = pl.ds(pl.multiple_of(HALF * (1 - core), HALF), HALF)
    moves = [
        (own.at[:, top, :], odd.at[:, :HALF, :]),
        (own.at[:, bottom, :], even.at[:, :HALF, :]),
        (own.at[:, :, near], cross.at[:, :SIZE, :]),
        (own.at[:, :, far], same.at[:, :SIZE, :]),
        (offsets, odd.at[:, HALF:, :]),
        (offsets, even.at[:, HALF:, :]),
        (offsets.at[:, :, :HALF], cross.at[:, SIZE:, :]),
        (offsets.at[:, :, :HALF], same.at[:, SIZE:, :]),
    ]
    run_all([pltpu.make_async_copy(x, y, sems.at[n]) for n, (x, y) in enumerate(moves)])


def sides():
    row_odd, core = place_of()
    even_rows = pl.ds(pl.multiple_of(3 * HALF * (1 - row_odd), HALF), HALF)
    odd_rows = pl.ds(pl.multiple_of(3 * HALF * row_odd, HALF), HALF)
    return even_rows, odd_rows, 3 * core, 3 - 3 * core


def transform_kernel(
    starts, own, odd_strip, even_strip, cross, same, cross_corner, same_corner, probe_in, matrices, measured,
    keep, send, around, center, even, odd, cross_out, same_out, steps,
    tile, probe, mats, offsets, totals, sums, accum, power, sems, *slots,
):
    step = pl.program_id(0)
    modes = probe.shape[0]
    lanes = lane_index(CHUNK)
    width = measured.shape[0]
    per_slot = len(slots) // width
    slots = [slots[n * per_slot : (n + 1) * per_slot] for n in range(width)]

    @pl.when(step == 0)
    def _():
        even_rows, odd_rows, cross_block, same_block = sides()
        middle = pl.ds(HALF, SIZE)
        moves = [(probe_in, probe), (matrices, mats)]
        for block, strip, corner in ((cross_block, cross, cross_corner), (same_block, same, same_corner)):
            moves.append((strip.at[:, :SIZE, :], tile.at[:, block, middle, :]))
            moves.append((corner.at[1, :, :HALF, :], tile.at[:, block, even_rows, :]))
            moves.append((corner.at[0, :, :HALF, :], tile.at[:, block, odd_rows, :]))
        for b in range(2):
            span = pl.ds(b * HALF, HALF)
            moves.append((own.at[:, :, span], tile.at[:, 1 + b, middle, :]))
            moves.append((even_strip.at[:, :HALF, span], tile.at[:, 1 + b, even_rows, :]))
            moves.append((odd_strip.at[:, :HALF, span], tile.at[:, 1 + b, odd_rows, :]))
        strips = [x.at[0] for x in (odd_strip, even_strip, cross, same)]
        strips += [x.at[n, 0] for x in (cross_corner, same_corner) for n in range(2)]
        for n, strip in enumerate(strips):
            moves.append((strip.at[pl.ds(strip.shape[0] - 8, 8), pl.ds(0, HALF)], offsets.at[n]))
        copies = [pltpu.make_async_copy(x, y, sems.at[n]) for n, (x, y) in enumerate(moves)]
        for copy in copies:
            copy.start()
        tile[:, 4] = jnp.zeros((2, 2 * SIZE, HALF), F32)
        totals[...] = jnp.zeros_like(totals)
        sums[...] = jnp.zeros_like(sums)
        accum[...] = jnp.zeros_like(accum)
        for slot in slots:
            slot[4][:, :, 0:8, :] = jnp.zeros((2, 2, 8, HALF), F32)
            slot[4][:, :, 264:272, :] = jnp.zeros((2, 2, 8, HALF), F32)
        for copy in copies:
            copy.wait()
        for i in range(0, SIZE, CHUNK):
            part = pl.ds(i, CHUNK)
            power[part] = probe_power(probe, part)
        for n in range(8):
            around[pl.ds(n, 1), :] = offsets[n, :1, :].astype(jnp.int32)

    def right(odd, transposed):
        high, low = mats[odd, transposed, 0], mats[odd, transposed, 1]
        return jnp.concatenate([high, high, low], 0)

    def left(odd, transposed):
        high, low = mats[odd, transposed, 0], mats[odd, transposed, 1]
        return jnp.concatenate([high, low, high], 1)

    def position(n):
        col = starts[1, width * step + n]
        return starts[0, width * step + n], col // HALF, lax.rem(col, HALF)

    def enter(n):
        xs, patch = slots[n][0], slots[n][4]
        row, base, shift = position(n)
        for i in range(0, SIZE, CHUNK):
            part = pl.ds(i, CHUNK)
            where = pl.ds(row + i, CHUNK)
            obj = []
            for p in range(2):
                blocks = [tile[p, base + b, where, :] for b in range(3)]
                obj.append(gather_lanes(blocks, shift, lanes))
                for b in range(2):
                    patch[p, b, pl.ds(8 + i, CHUNK), :] = obj[p][b]
            for m in range(modes):
                wave = []
                for b in range(2):
                    span = slice(b * HALF, (b + 1) * HALF)
                    pr, pi = probe[m, 0, part, span], probe[m, 1, part, span]
                    wave.append((pr * obj[0][b] - pi * obj[1][b], pr * obj[1][b] + pi * obj[0][b]))
                for odd in range(2):
                    for p in range(2):
                        high, low = split2(wave[0][p] - wave[1][p] if odd else wave[0][p] + wave[1][p])
                        at = pl.ds(m * SIZE + i, CHUNK)
                        xs[odd, at, p * HALF : (p + 1) * HALF] = high
                        xs[odd, at, SIZE + p * HALF : SIZE + (p + 1) * HALF] = low
                        xs[odd, at, 2 * SIZE + p * HALF : 2 * SIZE + (p + 1) * HALF] = high

    def lanes_forward(n):
        xs, ys = slots[n][0], slots[n][2]
        for odd in range(2):
            ys[odd] = dot(xs[odd], right(odd, 0))

    def rows_split(n):
        zs, ys = slots[n][1], slots[n][2]
        for m in range(modes):
            for odd in range(2):
                lane_span = slice(odd * HALF, (odd + 1) * HALF)
                for i in range(0, HALF, CHUNK):
                    top = ys[odd, pl.ds(m * SIZE + i, CHUNK), :]
                    bottom = ys[odd, pl.ds(m * SIZE + HALF + i, CHUNK), :]
                    for odd_row in range(2):
                        high, low = split2(top - bottom if odd_row else top + bottom)
                        for p in range(2):
                            span = slice(p * HALF, (p + 1) * HALF)
                            at = p * HALF + i
                            zs[m, odd_row, pl.ds(at, CHUNK), lane_span] = high[:, span]
                            zs[m, odd_row, pl.ds(SIZE + at, CHUNK), lane_span] = high[:, span]
                            zs[m, odd_row, pl.ds(2 * SIZE + at, CHUNK), lane_span] = low[:, span]

    def rows_forward(n):
        zs, fs = slots[n][1], slots[n][3]
        for odd_row in range(2):
            for m in range(modes):
                fs[m, odd_row] = dot(left(odd_row, 1), zs[m, odd_row])

    def scale(n):
        zs, fs = slots[n][1], slots[n][3]
        error = jnp.zeros((8, HALF), F32)
        energy = jnp.zeros((8, HALF), F32)
        for odd_row in range(2):
            for i in range(0, HALF, CHUNK):
                parts = [[fs[m, odd_row, pl.ds(p * HALF + i, CHUNK), :] for p in range(2)] for m in range(modes)]
                intensity = parts[0][0] ** 2 + parts[0][1] ** 2 + (parts[1][0] ** 2 + parts[1][1] ** 2)
                intensity = jnp.maximum(intensity, intensity_floor)
                inverse = lax.rsqrt(intensity)
                modulus = intensity * inverse
                amplitude = measured[n, pl.ds(odd_row * HALF + i, CHUNK), :]
                factor = 1.0 - amplitude * inverse
                misfit = (modulus - amplitude) ** 2
                strength = amplitude**2
                error = error + fold8(misfit[:, :HALF]) + fold8(misfit[:, HALF:])
                energy = energy + fold8(strength[:, :HALF]) + fold8(strength[:, HALF:])
                for m in range(modes):
                    for p in range(2):
                        high, low = split2(parts[m][p] * factor)
                        at = p * HALF + i
                        zs[m, odd_row, pl.ds(at, CHUNK), :] = high
                        zs[m, odd_row, pl.ds(SIZE + at, CHUNK), :] = high
                        zs[m, odd_row, pl.ds(2 * SIZE + at, CHUNK), :] = low
        sums[0] += error
        sums[1] += energy

    def rows_back(n):
        zs, fs = slots[n][1], slots[n][3]
        for odd_row in range(2):
            for m in range(modes):
                fs[m, odd_row] = dot(left(odd_row, 0), zs[m, odd_row])

    def rows_join(n):
        xs, fs = slots[n][0], slots[n][3]
        for m in range(modes):
            for i in range(0, HALF, CHUNK):
                for p in range(2):
                    a, b = [fs[m, odd_row, pl.ds(p * HALF + i, CHUNK), :] for odd_row in range(2)]
                    for bottom in range(2):
                        high, low = split2(a - b if bottom else a + b)
                        at = pl.ds(m * SIZE + bottom * HALF + i, CHUNK)
                        for odd in range(2):
                            span = slice(odd * HALF, (odd + 1) * HALF)
                            xs[odd, at, p * HALF : (p + 1) * HALF] = high[:, span]
                            xs[odd, at, SIZE + p * HALF : SIZE + (p + 1) * HALF] = low[:, span]
                            xs[odd, at, 2 * SIZE + p * HALF : 2 * SIZE + (p + 1) * HALF] = high[:, span]

    def lanes_back(n):
        xs, ys = slots[n][0], slots[n][2]
        for odd in range(2):
            ys[odd] = dot(xs[odd], right(odd, 1))

    def leave(n):
        ys, patch = slots[n][2], slots[n][4]
        row, base, shift = position(n)
        first, last = lanes == 0, lanes == HALF - 1
        sums_of = [jnp.zeros((8, HALF), F32) for _ in range(4)]
        for i in range(0, SIZE, CHUNK):
            part = pl.ds(i, CHUNK)
            where = pl.ds(row + i, CHUNK)
            obj = [[patch[p, b, pl.ds(8 + i, CHUNK), :] for b in range(2)] for p in range(2)]
            grads = [[0.0, 0.0], [0.0, 0.0]]
            for b in range(2):
                re, im = obj[0][b], obj[1][b]
                span = slice(b * HALF, (b + 1) * HALF)
                for m in range(modes):
                    at = pl.ds(m * SIZE + i, CHUNK)
                    evens = [ys[0, at, p * HALF : (p + 1) * HALF] for p in range(2)]
                    odds = [ys[1, at, p * HALF : (p + 1) * HALF] for p in range(2)]
                    br, bi = [x - y if b else x + y for x, y in zip(evens, odds)]
                    pr, pi = probe[m, 0, part, span], probe[m, 1, part, span]
                    grads[0][b] = grads[0][b] + (pr * br + pi * bi)
                    grads[1][b] = grads[1][b] + (pr * bi - pi * br)
                    totals[b, 2 * m, part, :] += re * br + im * bi
                    totals[b, 2 * m + 1, part, :] += re * bi - im * br
                totals[b, 4, part, :] += re**2 + im**2
            for p in range(2):
                moved = spread(grads[p][0], grads[p][1], shift, lanes)
                for b in range(3):
                    accum[p, base + b, where, :] += moved[b]
            columns = []
            for p in range(2):
                before = [pltpu.roll(x, 1, 1) for x in obj[p]]
                after = [pltpu.roll(x, HALF - 1, 1) for x in obj[p]]
                columns.append(
                    (
                        jnp.where(last, after[1], after[0]) - jnp.where(first, 0.0, before[0]),
                        jnp.where(last, 0.0, after[1]) - jnp.where(first, before[0], before[1]),
                    )
                )
            for b in range(2):
                strength = power[part, b * HALF : (b + 1) * HALF]
                rows = [patch[p, b, pl.ds(9 + i, CHUNK), :] - patch[p, b, pl.ds(7 + i, CHUNK), :] for p in range(2)]
                for d, slope in enumerate((rows, [columns[0][b], columns[1][b]])):
                    sums_of[2 * d] = sums_of[2 * d] + fold8(grads[0][b] * slope[0] + grads[1][b] * slope[1])
                    sums_of[2 * d + 1] = sums_of[2 * d + 1] + fold8(strength * (slope[0] ** 2 + slope[1] ** 2))
        for d in range(2):
            numerator = 0.5 * jnp.sum(sums_of[2 * d], keepdims=True)
            denominator = 0.25 * jnp.sum(sums_of[2 * d + 1], keepdims=True) + small_value
            at = pl.ds(2 * (width * step + n) + d, 1)
            steps[at, :] = jnp.broadcast_to(-numerator / denominator, (1, HALF))

    stages = [enter, lanes_forward, rows_split, rows_forward, scale, rows_back, rows_join, lanes_back, leave]
    for at in range(len(stages) + width - 1):
        for n in range(width):
            if 0 <= at - n < len(stages):
                stages[at - n](n)

    @pl.when(step == pl.num_programs(0) - 1)
    def _():
        core = place_of()[1]
        scalar = jnp.where(lax.broadcasted_iota(jnp.int32, (1, 8, HALF), 2) == 0, jnp.sum(sums[0]), jnp.sum(sums[1]))
        for out, block in ((keep, core), (send, 1 - core)):
            for c in range(5):
                out[:, 16 * c : 16 * c + 16, :] = totals[block, c].reshape(16, 16, HALF)
            out[:, 80:88, :] = jnp.broadcast_to(scalar, (16, 8, HALF))
        even_rows, odd_rows, cross_block, same_block = sides()
        for p in range(2):
            for b in range(2):
                span = slice(b * HALF, (b + 1) * HALF)
                center[p, :, span] = accum[p, 1 + b, 128:384]
                even[p, :, span] = accum[p, 1 + b, even_rows]
                odd[p, :, span] = accum[p, 1 + b, odd_rows]
            cross_out[p] = accum[p, cross_block]
            same_out[p] = accum[p, same_block]


def probe_power(probe, part):
    return (probe[0, 0, part] ** 2 + probe[0, 1, part] ** 2) + (probe[1, 0, part] ** 2 + probe[1, 1, part] ** 2)


def light_kernel(starts, around, probe, light, power, accum):
    accum[...] = jnp.zeros_like(accum)
    for i in range(0, SIZE, CHUNK):
        part = pl.ds(i, CHUNK)
        total = probe_power(probe, part)
        power[0, part] = total[:, :HALF]
        power[1, part] = total[:, HALF:]
    lanes = lane_index(CHUNK)
    row_odd, core = place_of()
    even, cross = 1 - 2 * row_odd, 2 * core - 1
    neighbours = [(-even, None), (even, None), (None, cross), (None, -cross)]
    neighbours += [(-even, cross), (even, cross), (-even, -cross), (even, -cross)]

    def add(row, col, down, right):
        rows, source_row, row = (SIZE, 0, row + HALF) if down is None else (
            HALF, pl.multiple_of(jnp.where(down < 0, HALF, 0), HALF), row + jnp.where(down < 0, 0, 3 * HALF)
        )
        if right is None:
            col = col + HALF
        else:
            source = jnp.where(right < 0, 1, 0)
            col = col + jnp.where(right < 0, 0, 3 * HALF)
        base, shift = col // HALF, lax.rem(col, HALF)
        for i in range(0, rows, CHUNK):
            part = pl.ds(source_row + i, CHUNK)
            where = pl.ds(row + i, CHUNK)
            if right is None:
                moved = spread(power[0, part], power[1, part], shift, lanes)
            else:
                rolled = pltpu.roll(power[source, part], shift, 1)
                moved = jnp.where(lanes < shift, 0.0, rolled), jnp.where(lanes < shift, rolled, 0.0)
            for b, value in enumerate(moved):
                accum[base + b, where, :] += value

    count = starts.shape[1]
    for j in range(count):
        add(starts[0, j], starts[1, j], None, None)
    for n, (down, right) in enumerate(neighbours):
        for j in range(count):
            row, col = around[n, 2 * j] - 1, around[n, 2 * j + 1] - 1
            near = row >= 0
            if down is not None:
                near = near & jnp.where(down < 0, row > HALF, row < HALF)
            if right is not None:
                near = near & jnp.where(right < 0, col > HALF, col < HALF)

            @pl.when(near)
            def _(row=row, col=col, down=down, right=right):
                add(row, col, down, right)

    light[:, :HALF] = accum[2, 256:512]
    light[:, HALF:] = accum[3, 256:512]


def sum_kernel(chunk, total):
    total[...] = jnp.sum(chunk[...], axis=0)


def quotient_kernel(own, first, second, third, spread_out, ratio, held):
    z = 2 * lax.div(lax.axis_index("row"), 4) + lax.rem(lax.div(lax.axis_index("col"), 2), 2)
    for distance, part in enumerate((own, first, second, third)):
        held[lax.rem(z + 4 - distance, 4)] = part[...]
    total = (held[0] + held[1]) + (held[2] + held[3])
    for c in range(4):
        quotient = total[16 * c : 16 * c + 16] / total[64:80]
        spread_out[:, 16 * c : 16 * c + 16, :] = jnp.broadcast_to(quotient[None], (16, 16, HALF))
    ratio[...] = jnp.broadcast_to(total[80:81, 0:1] / total[80:81, 1:2], (8, HALF))


def fold_kernel(even, odd, cross, same, even_out, odd_out):
    even_rows, odd_rows, _, _ = sides()
    swapped = place_of()[1] == 1
    for p in range(2):
        for strip, rows, out in ((even, even_rows, even_out), (odd, odd_rows, odd_out)):
            a, b = cross[p, rows], same[p, rows]
            out[p, :, :HALF] = strip[p, :, :HALF] + jnp.where(swapped, b, a)
            out[p, :, HALF:] = strip[p, :, HALF:] + jnp.where(swapped, a, b)


def update_kernel(center, even, odd, cross, same, light, out, total):
    for p in range(2):
        total[p] = center[p]
    row_odd, core = place_of()
    even_half = pl.ds(pl.multiple_of(HALF * (1 - row_odd), HALF), HALF)
    odd_half = pl.ds(pl.multiple_of(HALF * row_odd, HALF), HALF)
    for p in range(2):
        total[p, even_half, :] += even[p]
        total[p, odd_half, :] += odd[p]
    swapped = core == 1
    for i in range(0, SIZE, CHUNK):
        part = pl.ds(i, CHUNK)
        scale = 1.0 / (light[part] + object_damping)
        for p in range(2):
            a, b = cross[p, pl.ds(HALF + i, CHUNK)], same[p, pl.ds(HALF + i, CHUNK)]
            out[p, part, :HALF] = (total[p, part, :HALF] + jnp.where(swapped, b, a)) * scale[:, :HALF]
            out[p, part, HALF:] = (total[p, part, HALF:] + jnp.where(swapped, a, b)) * scale[:, HALF:]


def assemble_kernel(mine, other, out):
    core = place_of()[1]

    def write(source, block):
        for c in range(4):
            out[c, :, block * HALF : (block + 1) * HALF] = source[:, 16 * c : 16 * c + 16, :].reshape(SIZE, HALF)

    @pl.when(core == 0)
    def _():
        write(mine, 0)
        write(other, 1)

    @pl.when(core == 1)
    def _():
        write(mine, 1)
        write(other, 0)


def whole(*shape):
    return pl.BlockSpec(shape, lambda *_: (0,) * len(shape))


ANY = pl.BlockSpec(memory_space=pl.ANY)


def shaped(shapes):
    return [jax.ShapeDtypeStruct(s, F32) for s in shapes]


def params():
    return pltpu.CompilerParams(vmem_limit_bytes=VMEM_LIMIT)


def cost(flops, size):
    return pl.CostEstimate(flops=flops, bytes_accessed=size, transcendentals=0)


def simple(kernel, scalars, arrays, shapes, scratch, flops, size):
    single = not isinstance(shapes, list)
    outs = [shapes] if single else shapes
    call = pl.pallas_call(
        kernel,
        out_shape=shaped(outs)[0] if single else shaped(outs),
        grid_spec=pltpu.PrefetchScalarGridSpec(
            num_scalar_prefetch=len(scalars),
            grid=(),
            in_specs=[whole(*x.shape) for x in arrays],
            out_specs=whole(*shapes) if single else [whole(*s) for s in outs],
            scratch_shapes=[pltpu.VMEM(s, F32) for s in scratch],
        ),
        compiler_params=params(),
        cost_estimate=cost(flops, size),
    )
    return call(*scalars, *arrays)


def pack(starts, own):
    rows, columns = (2, HALF + 8, SIZE), (2, SIZE + 8, HALF)
    return pl.pallas_call(
        pack_kernel,
        out_shape=shaped([rows, rows, columns, columns]),
        grid_spec=pltpu.PrefetchScalarGridSpec(
            num_scalar_prefetch=1,
            grid=(),
            in_specs=[pl.BlockSpec(memory_space=pltpu.HBM)],
            out_specs=[ANY] * 4,
            scratch_shapes=[pltpu.VMEM((2, 8, SIZE), F32), pltpu.SemaphoreType.DMA((8,))],
        ),
        compiler_params=params(),
        cost_estimate=cost(1 << 10, 2 << 20),
    )(starts, own)


def prepare(measured):
    cols, rows = permutation()
    arrays = [measured, jnp.asarray(cols), jnp.asarray(rows)]
    return simple(prepare_kernel, [], arrays, measured.shape, [], 1 << 30, 3 << 20)


def stepped(width, *shape):
    return pl.BlockSpec((width, *shape), lambda i, *_: (i,) + (0,) * len(shape))


def transforms(starts, own, halo, probe, measured):
    mats = jnp.asarray(constants())
    arrays = [own, *halo, probe, mats]
    count = measured.shape[0]
    width = WIDTH
    halves = (16, 88, HALF)
    rows, columns = (2, HALF, SIZE), (2, 2 * SIZE, HALF)
    shapes = [(2, SIZE, SIZE), rows, rows, columns, columns, (2 * count, HALF)]
    slot = [
        pltpu.VMEM((2, 2 * SIZE, 3 * SIZE), BF),
        pltpu.VMEM((2, 2, 3 * SIZE, SIZE), BF),
        pltpu.VMEM((2, 2 * SIZE, SIZE), F32),
        pltpu.VMEM((2, 2, SIZE, SIZE), F32),
        pltpu.VMEM((2, 2, SIZE + 16, HALF), F32),
    ]
    return pl.pallas_call(
        transform_kernel,
        out_shape=shaped([halves, halves]) + [jax.ShapeDtypeStruct((8, HALF), jnp.int32)] + shaped(shapes),
        grid_spec=pltpu.PrefetchScalarGridSpec(
            num_scalar_prefetch=1,
            grid=(count // width,),
            in_specs=[ANY] * len(arrays) + [stepped(width, SIZE, SIZE)],
            out_specs=[whole(*x) for x in [halves, halves, (8, HALF), *shapes]],
            scratch_shapes=[
                pltpu.VMEM((2, 5, 2 * SIZE, HALF), F32),
                pltpu.VMEM(probe.shape, F32),
                pltpu.VMEM(mats.shape, BF),
                pltpu.VMEM((8, 8, HALF), F32),
                pltpu.VMEM((2, 5, SIZE, HALF), F32),
                pltpu.VMEM((2, 8, HALF), F32),
                pltpu.VMEM((2, 5, 2 * SIZE, HALF), F32),
                pltpu.VMEM((SIZE, SIZE), F32),
                pltpu.SemaphoreType.DMA((24,)),
            ]
            + slot * width,
        ),
        compiler_params=params(),
        cost_estimate=cost(13 << 30, 12 << 20),
    )(starts, *arrays, measured)


def illuminate(starts, around, probe):
    scratch = [(2, SIZE, HALF), (7, 3 * SIZE, HALF)]
    return simple(light_kernel, [starts, around], [probe], (SIZE, SIZE), scratch, 2 << 30, 4 << 20)


def update(arrays):
    shape = arrays[0].shape
    return simple(update_kernel, [], arrays, shape, [shape], 16 << 30, 3 << 20)


def assemble(mine, other):
    return simple(assemble_kernel, [], [mine, other], (4, SIZE, SIZE), [], 1 << 20, 2 << 20)


def pairs_from(first, count):
    pairs = []
    for i in range(first, count - 1, 2):
        pairs += [(i, i + 1), (i + 1, i)]
    return pairs


def swap_rows(value, first):
    return lax.ppermute(value, "row", pairs_from(first, lax.axis_size("row")))


def swap_columns(value, first):
    return lax.ppermute(value, "col", pairs_from(first, lax.axis_size("col")))


def along_z(value, distance):
    pairs = []
    for row in range(lax.axis_size("row")):
        for col in range(lax.axis_size("col")):
            z = (2 * (row // 4) + col // 2 % 2 + distance) % 4
            target = (4 * (z // 2) + row % 4) * 16 + col // 4 * 4 + 2 * (z % 2) + col % 2
            pairs.append((row * 16 + col, target))
    return lax.ppermute(value, AXES, pairs)


def planes():
    groups = {}
    for row in range(lax.axis_size("row")):
        for col in range(lax.axis_size("col")):
            groups.setdefault((row // 4, col % 4), []).append(row * 16 + col)
    return list(groups.values())


def half_lanes(value, first):
    return jnp.where(first, value[..., :HALF], value[..., HALF:])


def local(object_tile, probe, amplitudes, offsets):
    starts = offsets[0, 0].T
    measured = amplitudes[0, 0]
    core = lax.rem(lax.axis_index("col"), 2)
    groups = planes()

    with jax.named_scope("object_halo"):
        even, odd, cross, same = pack(starts, object_tile)
        odd = swap_rows(odd, 1)
        even = swap_rows(even, 0)
        cross = swap_columns(cross, 1)
        same = swap_columns(same, 0)
    permuted = prepare(measured)
    with jax.named_scope("object_corners"):
        odd, even, cross, same, permuted = lax.optimization_barrier((odd, even, cross, same, permuted))
        rows = jnp.stack([odd, even])
        cross_corner = swap_columns(half_lanes(rows, core == 0), 1)
        same_corner = swap_columns(half_lanes(rows, core == 1), 0)

    halo = [odd, even, cross, same, cross_corner, same_corner]
    keep, send, around, *parts = transforms(starts, object_tile, halo, probe, permuted)

    center, even, odd, cross, same, steps = parts
    with jax.named_scope("gradient_columns"):
        cross = swap_columns(cross, 1)
        same = swap_columns(same, 0)

    with jax.named_scope("probe_reduce"):
        chunk, around = lax.optimization_barrier((keep + swap_columns(send, 0), around))
        chunk = lax.all_to_all(chunk, AXES, 0, 0, axis_index_groups=groups, tiled=True)

    with jax.named_scope("gradient_rows"):
        light = illuminate(starts, around, probe)
        even, odd = simple(fold_kernel, [], [even, odd, cross, same], [even.shape] * 2, [], 1 << 20, 1 << 20)
        chunk, light, odd, even = lax.optimization_barrier((chunk, light, odd, even))
        odd = swap_rows(odd, 1)
        even = swap_rows(even, 0)

    with jax.named_scope("probe_sum"):
        total = simple(sum_kernel, [], [chunk], (88, HALF), [], 1 << 20, 1 << 20)
        parts = [total] + [along_z(total, d) for d in (1, 2, 3)]
        shapes = [(16, 64, HALF), (8, HALF)]
        spread_out, ratio = simple(quotient_kernel, [], parts, shapes, [(4, 88, HALF)], 1 << 20, 2 << 20)

    with jax.named_scope("probe_gather"):
        gathered = lax.all_to_all(spread_out, AXES, 0, 0, axis_index_groups=groups, tiled=True)
        object_update = update([center, even, odd, cross, same, light])
        relative_error = ratio[0, :1]
        position_step = steps[:, 0].reshape(1, 1, -1, 2)
        tied = (gathered, object_update, relative_error, position_step)
        gathered, object_update, relative_error, position_step = lax.optimization_barrier(tied)
        probe_update = assemble(gathered, swap_columns(gathered, 0)).reshape(probe.shape)

    return (object_update, probe_update, position_step, relative_error)


def solution(mesh):
    in_specs = (
        P(None, "row", "col"),
        P(),
        P("row", "col", None, None, None),
        P("row", "col", None, None),
    )
    out_specs = (P(None, "row", "col"), P(), P("row", "col", None, None), P())
    return jax.shard_map(local, mesh=mesh, in_specs=in_specs, out_specs=out_specs, check_vma=False)
```

```python
import jax
import jax.numpy as jnp
import ml_dtypes
import numpy as np
from jax import lax
from jax.experimental import pallas as pl
from jax.experimental.pallas import tpu as pltpu
from jax.sharding import PartitionSpec as P

intensity_floor = 0.1
object_damping = 1.0
small_value = 1e-06

SIZE = 256
HALF = 128
CHUNK = 32
WIDTH = 2
BF = jnp.bfloat16
F32 = jnp.float32
AXES = ("row", "col")
VMEM_LIMIT = 32 * 2**20


def transform_matrices():
    n = np.arange(HALF)[:, None]
    q = np.arange(HALF)[None, :]
    out = []
    for odd in (0, 1):
        angle = -2.0 * np.pi * ((n * (2 * q + odd)) % SIZE) / SIZE
        re, im = np.cos(angle) / 16.0, np.sin(angle) / 16.0
        out.append(np.block([[re, im], [-im, re]]))
    return out


def split_np(matrix):
    high = matrix.astype(ml_dtypes.bfloat16)
    low = (matrix - high.astype(np.float64)).astype(ml_dtypes.bfloat16)
    return high, low


def constants():
    return np.stack([np.stack([np.stack(split_np(x)) for x in (m, m.T)]) for m in transform_matrices()])


def permutation():
    order = np.concatenate([np.arange(0, SIZE, 2), np.arange(1, SIZE, 2)])
    onehot = np.zeros((SIZE, SIZE), np.float32)
    onehot[order, np.arange(SIZE)] = 1.0
    columns = np.concatenate([onehot] * 3, 0).astype(ml_dtypes.bfloat16)
    rows = np.concatenate([onehot.T] * 3, 1).astype(ml_dtypes.bfloat16)
    return columns, rows


def split2(value):
    high = value.astype(BF)
    return high, (value - high.astype(F32)).astype(BF)


def split3(value):
    high = value.astype(BF)
    rest = value - high.astype(F32)
    middle = rest.astype(BF)
    return high, middle, (rest - middle.astype(F32)).astype(BF)


def dot(a, b):
    return jnp.dot(a, b, preferred_element_type=F32)


def lane_index(rows):
    return lax.broadcasted_iota(jnp.int32, (rows, HALF), 1)


def spread(first, second, shift, lanes):
    a = pltpu.roll(first, shift, 1)
    b = pltpu.roll(second, shift, 1)
    wrapped = lanes < shift
    return jnp.where(wrapped, 0.0, a), jnp.where(wrapped, a, b), jnp.where(wrapped, b, 0.0)


def gather_lanes(blocks, shift, lanes):
    back = jnp.where(shift == 0, 0, HALF - shift)
    a, b, c = [pltpu.roll(x, back, 1) for x in blocks]
    inside = lanes < HALF - shift
    return jnp.where(inside, a, b), jnp.where(inside, b, c)


def fold8(value):
    return jnp.sum(value.reshape(-1, 8, HALF), axis=0)


def prepare_kernel(measured, cols, rows, permuted):
    for j in range(measured.shape[0]):
        moved = dot(jnp.concatenate(split3(measured[j]), 1), cols[...])
        permuted[j] = dot(rows[...], jnp.concatenate(split3(moved), 0))


def place_of():
    return lax.rem(lax.axis_index("row"), 2), lax.rem(lax.axis_index("col"), 2)


def run_all(copies):
    for copy in copies:
        copy.start()
    for copy in copies:
        copy.wait()


def pack_kernel(starts, own, even, odd, cross, same, offsets, sems):
    row_odd, core = place_of()
    lanes = lane_index(8)
    value = jnp.zeros((8, HALF), F32)
    for j in range(starts.shape[1]):
        for d in range(2):
            value = jnp.where(lanes == 2 * j + d, (starts[d, j] + 1).astype(F32), value)
    for p in range(2):
        offsets[p, :, :HALF] = value
        offsets[p, :, HALF:] = value
    top = pl.ds(pl.multiple_of(HALF * row_odd, HALF), HALF)
    bottom = pl.ds(pl.multiple_of(HALF * (1 - row_odd), HALF), HALF)
    near = pl.ds(pl.multiple_of(HALF * core, HALF), HALF)
    far = pl.ds(pl.multiple_of(HALF * (1 - core), HALF), HALF)
    moves = [
        (own.at[:, top, :], odd.at[:, :HALF, :]),
        (own.at[:, bottom, :], even.at[:, :HALF, :]),
        (own.at[:, :, near], cross.at[:, :SIZE, :]),
        (own.at[:, :, far], same.at[:, :SIZE, :]),
        (offsets, odd.at[:, HALF:, :]),
        (offsets, even.at[:, HALF:, :]),
        (offsets.at[:, :, :HALF], cross.at[:, SIZE : SIZE + 8, :]),
        (offsets.at[:, :, :HALF], same.at[:, SIZE:, :]),
    ]
    run_all([pltpu.make_async_copy(x, y, sems.at[n]) for n, (x, y) in enumerate(moves)])


def sides():
    row_odd, core = place_of()
    even_rows = pl.ds(pl.multiple_of(3 * HALF * (1 - row_odd), HALF), HALF)
    odd_rows = pl.ds(pl.multiple_of(3 * HALF * row_odd, HALF), HALF)
    return even_rows, odd_rows, 3 * core, 3 - 3 * core


def transform_kernel(
    starts, own, odd_strip, even_strip, cross, same, cross_corner, same_corner, probe_in, matrices, measured,
    keep, send, around, center, even, odd, cross_out, same_out, steps,
    tile, probe, mats, offsets, totals, sums, accum, power, sems, *slots,
):
    step = pl.program_id(0)
    modes = probe.shape[0]
    lanes = lane_index(CHUNK)
    width = measured.shape[0]
    per_slot = len(slots) // width
    slots = [slots[n * per_slot : (n + 1) * per_slot] for n in range(width)]

    @pl.when(step == 0)
    def _():
        even_rows, odd_rows, cross_block, same_block = sides()
        middle = pl.ds(HALF, SIZE)
        moves = [(probe_in, probe), (matrices, mats)]
        for block, strip, corner in ((cross_block, cross, cross_corner), (same_block, same, same_corner)):
            moves.append((strip.at[:, :SIZE, :], tile.at[:, block, middle, :]))
            moves.append((corner.at[1, :, :HALF, :], tile.at[:, block, even_rows, :]))
            moves.append((corner.at[0, :, :HALF, :], tile.at[:, block, odd_rows, :]))
        for b in range(2):
            span = pl.ds(b * HALF, HALF)
            moves.append((own.at[:, :, span], tile.at[:, 1 + b, middle, :]))
            moves.append((even_strip.at[:, :HALF, span], tile.at[:, 1 + b, even_rows, :]))
            moves.append((odd_strip.at[:, :HALF, span], tile.at[:, 1 + b, odd_rows, :]))
        strips = [(odd_strip.at[0], HALF), (even_strip.at[0], HALF), (cross.at[0], SIZE), (same.at[0], SIZE)]
        strips += [(x.at[n, 0], HALF) for x in (cross_corner, same_corner) for n in range(2)]
        for n, (strip, at) in enumerate(strips):
            moves.append((strip.at[pl.ds(at, 8), pl.ds(0, HALF)], offsets.at[n]))
        copies = [pltpu.make_async_copy(x, y, sems.at[n]) for n, (x, y) in enumerate(moves)]
        for copy in copies:
            copy.start()
        tile[:, 4] = jnp.zeros((2, 2 * SIZE, HALF), F32)
        totals[...] = jnp.zeros_like(totals)
        sums[...] = jnp.zeros_like(sums)
        accum[...] = jnp.zeros_like(accum)
        for slot in slots:
            slot[4][:, :, 0:8, :] = jnp.zeros((2, 2, 8, HALF), F32)
            slot[4][:, :, 264:272, :] = jnp.zeros((2, 2, 8, HALF), F32)
        for copy in copies:
            copy.wait()
        for i in range(0, SIZE, CHUNK):
            part = pl.ds(i, CHUNK)
            power[part] = probe_power(probe, part)
        for n in range(8):
            around[pl.ds(n, 1), :] = offsets[n, :1, :].astype(jnp.int32)

    def right(odd, transposed):
        high, low = mats[odd, transposed, 0], mats[odd, transposed, 1]
        return jnp.concatenate([high, high, low], 0)

    def left(odd, transposed):
        high, low = mats[odd, transposed, 0], mats[odd, transposed, 1]
        return jnp.concatenate([high, low, high], 1)

    def position(n):
        col = starts[1, width * step + n]
        return starts[0, width * step + n], col // HALF, lax.rem(col, HALF)

    def enter(n):
        xs, patch = slots[n][0], slots[n][4]
        row, base, shift = position(n)
        for i in range(0, SIZE, CHUNK):
            part = pl.ds(i, CHUNK)
            where = pl.ds(row + i, CHUNK)
            obj = []
            for p in range(2):
                blocks = [tile[p, base + b, where, :] for b in range(3)]
                obj.append(gather_lanes(blocks, shift, lanes))
                for b in range(2):
                    patch[p, b, pl.ds(8 + i, CHUNK), :] = obj[p][b]
            for m in range(modes):
                wave = []
                for b in range(2):
                    span = slice(b * HALF, (b + 1) * HALF)
                    pr, pi = probe[m, 0, part, span], probe[m, 1, part, span]
                    wave.append((pr * obj[0][b] - pi * obj[1][b], pr * obj[1][b] + pi * obj[0][b]))
                for odd in range(2):
                    for p in range(2):
                        high, low = split2(wave[0][p] - wave[1][p] if odd else wave[0][p] + wave[1][p])
                        at = pl.ds(m * SIZE + i, CHUNK)
                        xs[odd, at, p * HALF : (p + 1) * HALF] = high
                        xs[odd, at, SIZE + p * HALF : SIZE + (p + 1) * HALF] = low
                        xs[odd, at, 2 * SIZE + p * HALF : 2 * SIZE + (p + 1) * HALF] = high

    def lanes_forward(n):
        xs, ys = slots[n][0], slots[n][2]
        for odd in range(2):
            ys[odd] = dot(xs[odd], right(odd, 0))

    def rows_split(n):
        zs, ys = slots[n][1], slots[n][2]
        for m in range(modes):
            for odd in range(2):
                lane_span = slice(odd * HALF, (odd + 1) * HALF)
                for i in range(0, HALF, CHUNK):
                    top = ys[odd, pl.ds(m * SIZE + i, CHUNK), :]
                    bottom = ys[odd, pl.ds(m * SIZE + HALF + i, CHUNK), :]
                    for odd_row in range(2):
                        high, low = split2(top - bottom if odd_row else top + bottom)
                        for p in range(2):
                            span = slice(p * HALF, (p + 1) * HALF)
                            at = p * HALF + i
                            zs[m, odd_row, pl.ds(at, CHUNK), lane_span] = high[:, span]
                            zs[m, odd_row, pl.ds(SIZE + at, CHUNK), lane_span] = high[:, span]
                            zs[m, odd_row, pl.ds(2 * SIZE + at, CHUNK), lane_span] = low[:, span]

    def rows_forward(n):
        zs, fs = slots[n][1], slots[n][3]
        for odd_row in range(2):
            for m in range(modes):
                fs[m, odd_row] = dot(left(odd_row, 1), zs[m, odd_row])

    def scale(n):
        zs, fs = slots[n][1], slots[n][3]
        error = jnp.zeros((8, HALF), F32)
        energy = jnp.zeros((8, HALF), F32)
        for odd_row in range(2):
            for i in range(0, HALF, CHUNK):
                parts = [[fs[m, odd_row, pl.ds(p * HALF + i, CHUNK), :] for p in range(2)] for m in range(modes)]
                intensity = parts[0][0] ** 2 + parts[0][1] ** 2 + (parts[1][0] ** 2 + parts[1][1] ** 2)
                intensity = jnp.maximum(intensity, intensity_floor)
                inverse = lax.rsqrt(intensity)
                modulus = intensity * inverse
                amplitude = measured[n, pl.ds(odd_row * HALF + i, CHUNK), :]
                factor = 1.0 - amplitude * inverse
                misfit = (modulus - amplitude) ** 2
                strength = amplitude**2
                error = error + fold8(misfit[:, :HALF]) + fold8(misfit[:, HALF:])
                energy = energy + fold8(strength[:, :HALF]) + fold8(strength[:, HALF:])
                for m in range(modes):
                    for p in range(2):
                        high, low = split2(parts[m][p] * factor)
                        at = p * HALF + i
                        zs[m, odd_row, pl.ds(at, CHUNK), :] = high
                        zs[m, odd_row, pl.ds(SIZE + at, CHUNK), :] = high
                        zs[m, odd_row, pl.ds(2 * SIZE + at, CHUNK), :] = low
        sums[0] += error
        sums[1] += energy

    def rows_back(n):
        zs, fs = slots[n][1], slots[n][3]
        for odd_row in range(2):
            for m in range(modes):
                fs[m, odd_row] = dot(left(odd_row, 0), zs[m, odd_row])

    def rows_join(n):
        xs, fs = slots[n][0], slots[n][3]
        for m in range(modes):
            for i in range(0, HALF, CHUNK):
                for p in range(2):
                    a, b = [fs[m, odd_row, pl.ds(p * HALF + i, CHUNK), :] for odd_row in range(2)]
                    for bottom in range(2):
                        high, low = split2(a - b if bottom else a + b)
                        at = pl.ds(m * SIZE + bottom * HALF + i, CHUNK)
                        for odd in range(2):
                            span = slice(odd * HALF, (odd + 1) * HALF)
                            xs[odd, at, p * HALF : (p + 1) * HALF] = high[:, span]
                            xs[odd, at, SIZE + p * HALF : SIZE + (p + 1) * HALF] = low[:, span]
                            xs[odd, at, 2 * SIZE + p * HALF : 2 * SIZE + (p + 1) * HALF] = high[:, span]

    def lanes_back(n):
        xs, ys = slots[n][0], slots[n][2]
        for odd in range(2):
            ys[odd] = dot(xs[odd], right(odd, 1))

    def leave(n):
        ys, patch = slots[n][2], slots[n][4]
        row, base, shift = position(n)
        first, last = lanes == 0, lanes == HALF - 1
        sums_of = [jnp.zeros((8, HALF), F32) for _ in range(4)]
        for i in range(0, SIZE, CHUNK):
            part = pl.ds(i, CHUNK)
            where = pl.ds(row + i, CHUNK)
            obj = [[patch[p, b, pl.ds(8 + i, CHUNK), :] for b in range(2)] for p in range(2)]
            grads = [[0.0, 0.0], [0.0, 0.0]]
            for b in range(2):
                re, im = obj[0][b], obj[1][b]
                span = slice(b * HALF, (b + 1) * HALF)
                for m in range(modes):
                    at = pl.ds(m * SIZE + i, CHUNK)
                    evens = [ys[0, at, p * HALF : (p + 1) * HALF] for p in range(2)]
                    odds = [ys[1, at, p * HALF : (p + 1) * HALF] for p in range(2)]
                    br, bi = [x - y if b else x + y for x, y in zip(evens, odds)]
                    pr, pi = probe[m, 0, part, span], probe[m, 1, part, span]
                    grads[0][b] = grads[0][b] + (pr * br + pi * bi)
                    grads[1][b] = grads[1][b] + (pr * bi - pi * br)
                    totals[b, 2 * m, part, :] += re * br + im * bi
                    totals[b, 2 * m + 1, part, :] += re * bi - im * br
                totals[b, 4, part, :] += re**2 + im**2
            for p in range(2):
                moved = spread(grads[p][0], grads[p][1], shift, lanes)
                for b in range(3):
                    accum[p, base + b, where, :] += moved[b]
            columns = []
            for p in range(2):
                before = [pltpu.roll(x, 1, 1) for x in obj[p]]
                after = [pltpu.roll(x, HALF - 1, 1) for x in obj[p]]
                columns.append(
                    (
                        jnp.where(last, after[1], after[0]) - jnp.where(first, 0.0, before[0]),
                        jnp.where(last, 0.0, after[1]) - jnp.where(first, before[0], before[1]),
                    )
                )
            for b in range(2):
                strength = power[part, b * HALF : (b + 1) * HALF]
                rows = [patch[p, b, pl.ds(9 + i, CHUNK), :] - patch[p, b, pl.ds(7 + i, CHUNK), :] for p in range(2)]
                for d, slope in enumerate((rows, [columns[0][b], columns[1][b]])):
                    sums_of[2 * d] = sums_of[2 * d] + fold8(grads[0][b] * slope[0] + grads[1][b] * slope[1])
                    sums_of[2 * d + 1] = sums_of[2 * d + 1] + fold8(strength * (slope[0] ** 2 + slope[1] ** 2))
        for d in range(2):
            numerator = 0.5 * jnp.sum(sums_of[2 * d], keepdims=True)
            denominator = 0.25 * jnp.sum(sums_of[2 * d + 1], keepdims=True) + small_value
            at = pl.ds(2 * (width * step + n) + d, 1)
            steps[at, :] = jnp.broadcast_to(-numerator / denominator, (1, HALF))

    stages = [enter, lanes_forward, rows_split, rows_forward, scale, rows_back, rows_join, lanes_back, leave]
    for at in range(len(stages) + width - 1):
        for n in range(width):
            if 0 <= at - n < len(stages):
                stages[at - n](n)

    @pl.when(step == pl.num_programs(0) - 1)
    def _():
        core = place_of()[1]
        scalar = jnp.where(lax.broadcasted_iota(jnp.int32, (1, 8, HALF), 2) == 0, jnp.sum(sums[0]), jnp.sum(sums[1]))
        for out, block in ((keep, core), (send, 1 - core)):
            for c in range(5):
                out[:, 16 * c : 16 * c + 16, :] = totals[block, c].reshape(16, 16, HALF)
            out[:, 80:88, :] = jnp.broadcast_to(scalar, (16, 8, HALF))
        even_rows, odd_rows, cross_block, same_block = sides()
        for p in range(2):
            for b in range(2):
                span = slice(b * HALF, (b + 1) * HALF)
                center[p, :, span] = accum[p, 1 + b, 128:384]
                even[p, :, span] = accum[p, 1 + b, even_rows]
                odd[p, :, span] = accum[p, 1 + b, odd_rows]
            cross_out[p] = accum[p, cross_block]
            same_out[p] = accum[p, same_block]


def probe_power(probe, part):
    return (probe[0, 0, part] ** 2 + probe[0, 1, part] ** 2) + (probe[1, 0, part] ** 2 + probe[1, 1, part] ** 2)


def light_kernel(starts, around, probe, light, power, accum):
    accum[...] = jnp.zeros_like(accum)
    for i in range(0, SIZE, CHUNK):
        part = pl.ds(i, CHUNK)
        total = probe_power(probe, part)
        power[0, part] = total[:, :HALF]
        power[1, part] = total[:, HALF:]
    lanes = lane_index(CHUNK)
    row_odd, core = place_of()
    even, cross = 1 - 2 * row_odd, 2 * core - 1
    neighbours = [(-even, None), (even, None), (None, cross), (None, -cross)]
    neighbours += [(-even, cross), (even, cross), (-even, -cross), (even, -cross)]

    def add(row, col, down, right):
        rows, source_row, row = (SIZE, 0, row + HALF) if down is None else (
            HALF, pl.multiple_of(jnp.where(down < 0, HALF, 0), HALF), row + jnp.where(down < 0, 0, 3 * HALF)
        )
        if right is None:
            col = col + HALF
        else:
            source = jnp.where(right < 0, 1, 0)
            col = col + jnp.where(right < 0, 0, 3 * HALF)
        base, shift = col // HALF, lax.rem(col, HALF)
        for i in range(0, rows, CHUNK):
            part = pl.ds(source_row + i, CHUNK)
            where = pl.ds(row + i, CHUNK)
            if right is None:
                moved = spread(power[0, part], power[1, part], shift, lanes)
            else:
                rolled = pltpu.roll(power[source, part], shift, 1)
                moved = jnp.where(lanes < shift, 0.0, rolled), jnp.where(lanes < shift, rolled, 0.0)
            for b, value in enumerate(moved):
                accum[base + b, where, :] += value

    count = starts.shape[1]
    for j in range(count):
        add(starts[0, j], starts[1, j], None, None)
    for n, (down, right) in enumerate(neighbours):
        for j in range(count):
            row, col = around[n, 2 * j] - 1, around[n, 2 * j + 1] - 1
            near = row >= 0
            if down is not None:
                near = near & jnp.where(down < 0, row > HALF, row < HALF)
            if right is not None:
                near = near & jnp.where(right < 0, col > HALF, col < HALF)

            @pl.when(near)
            def _(row=row, col=col, down=down, right=right):
                add(row, col, down, right)

    light[:, :HALF] = accum[2, 256:512]
    light[:, HALF:] = accum[3, 256:512]


def sum_kernel(chunk, total):
    total[...] = jnp.sum(chunk[...], axis=0)


def quotient_kernel(own, first, second, third, spread_out, ratio, held):
    z = 2 * lax.div(lax.axis_index("row"), 4) + lax.rem(lax.div(lax.axis_index("col"), 2), 2)
    for distance, part in enumerate((own, first, second, third)):
        held[lax.rem(z + 4 - distance, 4)] = part[...]
    total = (held[0] + held[1]) + (held[2] + held[3])
    for c in range(4):
        quotient = total[16 * c : 16 * c + 16] / total[64:80]
        spread_out[:, 16 * c : 16 * c + 16, :] = jnp.broadcast_to(quotient[None], (16, 16, HALF))
    ratio[...] = jnp.broadcast_to(total[80:81, 0:1] / total[80:81, 1:2], (8, HALF))


def fold_kernel(even, odd, cross, same, even_out, odd_out):
    even_rows, odd_rows, _, _ = sides()
    swapped = place_of()[1] == 1
    for p in range(2):
        for strip, rows, out in ((even, even_rows, even_out), (odd, odd_rows, odd_out)):
            a, b = cross[p, rows], same[p, rows]
            out[p, :, :HALF] = strip[p, :, :HALF] + jnp.where(swapped, b, a)
            out[p, :, HALF:] = strip[p, :, HALF:] + jnp.where(swapped, a, b)


def update_kernel(center, even, odd, cross, same, light, out, total):
    for p in range(2):
        total[p] = center[p]
    row_odd, core = place_of()
    even_half = pl.ds(pl.multiple_of(HALF * (1 - row_odd), HALF), HALF)
    odd_half = pl.ds(pl.multiple_of(HALF * row_odd, HALF), HALF)
    for p in range(2):
        total[p, even_half, :] += even[p]
        total[p, odd_half, :] += odd[p]
    swapped = core == 1
    for i in range(0, SIZE, CHUNK):
        part = pl.ds(i, CHUNK)
        scale = 1.0 / (light[part] + object_damping)
        for p in range(2):
            a, b = cross[p, pl.ds(HALF + i, CHUNK)], same[p, pl.ds(HALF + i, CHUNK)]
            out[p, part, :HALF] = (total[p, part, :HALF] + jnp.where(swapped, b, a)) * scale[:, :HALF]
            out[p, part, HALF:] = (total[p, part, HALF:] + jnp.where(swapped, a, b)) * scale[:, HALF:]


def assemble_kernel(mine, other, out):
    core = place_of()[1]

    def write(source, block):
        for c in range(4):
            out[c, :, block * HALF : (block + 1) * HALF] = source[:, 16 * c : 16 * c + 16, :].reshape(SIZE, HALF)

    @pl.when(core == 0)
    def _():
        write(mine, 0)
        write(other, 1)

    @pl.when(core == 1)
    def _():
        write(mine, 1)
        write(other, 0)


def whole(*shape):
    return pl.BlockSpec(shape, lambda *_: (0,) * len(shape))


ANY = pl.BlockSpec(memory_space=pl.ANY)


def shaped(shapes):
    return [jax.ShapeDtypeStruct(s, F32) for s in shapes]


def params():
    return pltpu.CompilerParams(vmem_limit_bytes=VMEM_LIMIT)


def cost(flops, size):
    return pl.CostEstimate(flops=flops, bytes_accessed=size, transcendentals=0)


def simple(kernel, scalars, arrays, shapes, scratch, flops, size):
    single = not isinstance(shapes, list)
    outs = [shapes] if single else shapes
    call = pl.pallas_call(
        kernel,
        out_shape=shaped(outs)[0] if single else shaped(outs),
        grid_spec=pltpu.PrefetchScalarGridSpec(
            num_scalar_prefetch=len(scalars),
            grid=(),
            in_specs=[whole(*x.shape) for x in arrays],
            out_specs=whole(*shapes) if single else [whole(*s) for s in outs],
            scratch_shapes=[pltpu.VMEM(s, F32) for s in scratch],
        ),
        compiler_params=params(),
        cost_estimate=cost(flops, size),
    )
    return call(*scalars, *arrays)


def pack(starts, own):
    rows, crossing, columns = (2, HALF + 8, SIZE), (2, SIZE + 24, HALF), (2, SIZE + 8, HALF)
    return pl.pallas_call(
        pack_kernel,
        out_shape=shaped([rows, rows, crossing, columns]),
        grid_spec=pltpu.PrefetchScalarGridSpec(
            num_scalar_prefetch=1,
            grid=(),
            in_specs=[pl.BlockSpec(memory_space=pltpu.HBM)],
            out_specs=[ANY] * 4,
            scratch_shapes=[pltpu.VMEM((2, 8, SIZE), F32), pltpu.SemaphoreType.DMA((8,))],
        ),
        compiler_params=params(),
        cost_estimate=cost(1 << 10, 2 << 20),
    )(starts, own)


def prepare(measured):
    cols, rows = permutation()
    arrays = [measured, jnp.asarray(cols), jnp.asarray(rows)]
    return simple(prepare_kernel, [], arrays, measured.shape, [], 1 << 30, 3 << 20)


def stepped(width, *shape):
    return pl.BlockSpec((width, *shape), lambda i, *_: (i,) + (0,) * len(shape))


def transforms(starts, own, halo, probe, measured):
    mats = jnp.asarray(constants())
    arrays = [own, *halo, probe, mats]
    count = measured.shape[0]
    width = WIDTH
    halves = (16, 88, HALF)
    rows, columns = (2, HALF, SIZE), (2, 2 * SIZE, HALF)
    shapes = [(2, SIZE, SIZE), rows, rows, columns, columns, (2 * count, HALF)]
    slot = [
        pltpu.VMEM((2, 2 * SIZE, 3 * SIZE), BF),
        pltpu.VMEM((2, 2, 3 * SIZE, SIZE), BF),
        pltpu.VMEM((2, 2 * SIZE, SIZE), F32),
        pltpu.VMEM((2, 2, SIZE, SIZE), F32),
        pltpu.VMEM((2, 2, SIZE + 16, HALF), F32),
    ]
    return pl.pallas_call(
        transform_kernel,
        out_shape=shaped([halves, halves]) + [jax.ShapeDtypeStruct((8, HALF), jnp.int32)] + shaped(shapes),
        grid_spec=pltpu.PrefetchScalarGridSpec(
            num_scalar_prefetch=1,
            grid=(count // width,),
            in_specs=[ANY] * len(arrays) + [stepped(width, SIZE, SIZE)],
            out_specs=[whole(*x) for x in [halves, halves, (8, HALF), *shapes]],
            scratch_shapes=[
                pltpu.VMEM((2, 5, 2 * SIZE, HALF), F32),
                pltpu.VMEM(probe.shape, F32),
                pltpu.VMEM(mats.shape, BF),
                pltpu.VMEM((8, 8, HALF), F32),
                pltpu.VMEM((2, 5, SIZE, HALF), F32),
                pltpu.VMEM((2, 8, HALF), F32),
                pltpu.VMEM((2, 5, 2 * SIZE, HALF), F32),
                pltpu.VMEM((SIZE, SIZE), F32),
                pltpu.SemaphoreType.DMA((24,)),
            ]
            + slot * width,
        ),
        compiler_params=params(),
        cost_estimate=cost(13 << 30, 12 << 20),
    )(starts, *arrays, measured)


def illuminate(starts, around, probe):
    scratch = [(2, SIZE, HALF), (7, 3 * SIZE, HALF)]
    return simple(light_kernel, [starts, around], [probe], (SIZE, SIZE), scratch, 2 << 30, 4 << 20)


def update(arrays):
    shape = arrays[0].shape
    return simple(update_kernel, [], arrays, shape, [shape], 1 << 20, 3 << 20)


def assemble(mine, other):
    return simple(assemble_kernel, [], [mine, other], (4, SIZE, SIZE), [], 1 << 20, 2 << 20)


def pairs_from(first, count):
    pairs = []
    for i in range(first, count - 1, 2):
        pairs += [(i, i + 1), (i + 1, i)]
    return pairs


def swap_rows(value, first):
    return lax.ppermute(value, "row", pairs_from(first, lax.axis_size("row")))


def swap_columns(value, first):
    return lax.ppermute(value, "col", pairs_from(first, lax.axis_size("col")))


def along_z(value, distance):
    pairs = []
    for row in range(lax.axis_size("row")):
        for col in range(lax.axis_size("col")):
            z = (2 * (row // 4) + col // 2 % 2 + distance) % 4
            target = (4 * (z // 2) + row % 4) * 16 + col // 4 * 4 + 2 * (z % 2) + col % 2
            pairs.append((row * 16 + col, target))
    return lax.ppermute(value, AXES, pairs)


def planes():
    groups = {}
    for row in range(lax.axis_size("row")):
        for col in range(lax.axis_size("col")):
            groups.setdefault((row // 4, col % 4), []).append(row * 16 + col)
    return list(groups.values())


def half_lanes(value, first):
    return jnp.where(first, value[..., :HALF], value[..., HALF:])


def local(object_tile, probe, amplitudes, offsets):
    starts = offsets[0, 0].T
    measured = amplitudes[0, 0]
    core = lax.rem(lax.axis_index("col"), 2)
    groups = planes()

    with jax.named_scope("object_halo"):
        even, odd, cross, same = pack(starts, object_tile)
        odd = swap_rows(odd, 1)
        even = swap_rows(even, 0)
        cross = swap_columns(cross, 1)
        same = swap_columns(same, 0)
    permuted = prepare(measured)
    with jax.named_scope("object_corners"):
        odd, even, cross, same, permuted = lax.optimization_barrier((odd, even, cross, same, permuted))
        rows = jnp.stack([odd, even])
        cross_corner = swap_columns(half_lanes(rows, core == 0), 1)
        same_corner = swap_columns(half_lanes(rows, core == 1), 0)

    halo = [odd, even, cross, same, cross_corner, same_corner]
    keep, send, around, *parts = transforms(starts, object_tile, halo, probe, permuted)

    center, even, odd, cross, same, steps = parts
    with jax.named_scope("gradient_columns"):
        cross = swap_columns(cross, 1)
        same = swap_columns(same, 0)

    with jax.named_scope("probe_reduce"):
        chunk, around = lax.optimization_barrier((keep + swap_columns(send, 0), around))
        chunk = lax.all_to_all(chunk, AXES, 0, 0, axis_index_groups=groups, tiled=True)

    with jax.named_scope("gradient_rows"):
        light = illuminate(starts, around, probe)
        even, odd = simple(fold_kernel, [], [even, odd, cross, same], [even.shape] * 2, [], 1 << 20, 1 << 20)
        chunk, light, odd, even = lax.optimization_barrier((chunk, light, odd, even))

    with jax.named_scope("probe_sum"):
        total = simple(sum_kernel, [], [chunk], (88, HALF), [], 1 << 20, 1 << 20)
        parts = [total] + [along_z(total, d) for d in (1, 2, 3)]
        shapes = [(16, 64, HALF), (8, HALF)]
        spread_out, ratio = simple(quotient_kernel, [], parts, shapes, [(4, 88, HALF)], 1 << 20, 2 << 20)
        spread_out, odd, even = lax.optimization_barrier((spread_out, odd, even))
        odd = swap_rows(odd, 1)
        even = swap_rows(even, 0)

    with jax.named_scope("probe_gather"):
        gathered = lax.all_to_all(spread_out, AXES, 0, 0, axis_index_groups=groups, tiled=True)
        object_update = update([center, even, odd, cross, same, light])
        relative_error = ratio[0, :1]
        position_step = steps[:, 0].reshape(1, 1, -1, 2)
        tied = (gathered, object_update, relative_error, position_step)
        gathered, object_update, relative_error, position_step = lax.optimization_barrier(tied)
        probe_update = assemble(gathered, swap_columns(gathered, 0)).reshape(probe.shape)

    return (object_update, probe_update, position_step, relative_error)


def solution(mesh):
    in_specs = (
        P(None, "row", "col"),
        P(),
        P("row", "col", None, None, None),
        P("row", "col", None, None),
    )
    out_specs = (P(None, "row", "col"), P(), P("row", "col", None, None), P())
    return jax.shard_map(local, mesh=mesh, in_specs=in_specs, out_specs=out_specs, check_vma=False)
```

```python
import jax
import jax.numpy as jnp
import ml_dtypes
import numpy as np
from jax import lax
from jax.experimental import pallas as pl
from jax.experimental.pallas import tpu as pltpu
from jax.sharding import PartitionSpec as P

intensity_floor = 0.1
object_damping = 1.0
small_value = 1e-06

SIZE = 256
HALF = 128
CHUNK = 32
WIDTH = 2
BF = jnp.bfloat16
F32 = jnp.float32
AXES = ("row", "col")
VMEM_LIMIT = 32 * 2**20


def transform_matrices():
    n = np.arange(HALF)[:, None]
    q = np.arange(HALF)[None, :]
    out = []
    for odd in (0, 1):
        angle = -2.0 * np.pi * ((n * (2 * q + odd)) % SIZE) / SIZE
        re, im = np.cos(angle) / 16.0, np.sin(angle) / 16.0
        out.append(np.block([[re, im], [-im, re]]))
    return out


def split_np(matrix):
    high = matrix.astype(ml_dtypes.bfloat16)
    low = (matrix - high.astype(np.float64)).astype(ml_dtypes.bfloat16)
    return high, low


def constants():
    return np.stack([np.stack([np.stack(split_np(x)) for x in (m, m.T)]) for m in transform_matrices()])


def permutation():
    order = np.concatenate([np.arange(0, SIZE, 2), np.arange(1, SIZE, 2)])
    onehot = np.zeros((SIZE, SIZE), np.float32)
    onehot[order, np.arange(SIZE)] = 1.0
    columns = np.concatenate([onehot] * 3, 0).astype(ml_dtypes.bfloat16)
    rows = np.concatenate([onehot.T] * 3, 1).astype(ml_dtypes.bfloat16)
    return columns, rows


def split2(value):
    high = value.astype(BF)
    return high, (value - high.astype(F32)).astype(BF)


def split3(value):
    high = value.astype(BF)
    rest = value - high.astype(F32)
    middle = rest.astype(BF)
    return high, middle, (rest - middle.astype(F32)).astype(BF)


def dot(a, b):
    return jnp.dot(a, b, preferred_element_type=F32)


def lane_index(rows):
    return lax.broadcasted_iota(jnp.int32, (rows, HALF), 1)


def spread(first, second, shift, lanes):
    a = pltpu.roll(first, shift, 1)
    b = pltpu.roll(second, shift, 1)
    wrapped = lanes < shift
    return jnp.where(wrapped, 0.0, a), jnp.where(wrapped, a, b), jnp.where(wrapped, b, 0.0)


def gather_lanes(blocks, shift, lanes):
    back = jnp.where(shift == 0, 0, HALF - shift)
    a, b, c = [pltpu.roll(x, back, 1) for x in blocks]
    inside = lanes < HALF - shift
    return jnp.where(inside, a, b), jnp.where(inside, b, c)


def fold8(value):
    return jnp.sum(value.reshape(-1, 8, HALF), axis=0)


def prepare_kernel(measured, cols, rows, permuted):
    for j in range(measured.shape[0]):
        moved = dot(jnp.concatenate(split3(measured[j]), 1), cols[...])
        permuted[j] = dot(rows[...], jnp.concatenate(split3(moved), 0))


def place_of():
    return lax.rem(lax.axis_index("row"), 2), lax.rem(lax.axis_index("col"), 2)


def run_all(copies):
    for copy in copies:
        copy.start()
    for copy in copies:
        copy.wait()


def pack_kernel(starts, own, even, odd, cross, same, offsets, sems):
    row_odd, core = place_of()
    lanes = lane_index(8)
    value = jnp.zeros((8, HALF), F32)
    for j in range(starts.shape[1]):
        for d in range(2):
            value = jnp.where(lanes == 2 * j + d, (starts[d, j] + 1).astype(F32), value)
    for p in range(2):
        offsets[p, :, :HALF] = value
        offsets[p, :, HALF:] = value
    top = pl.ds(pl.multiple_of(HALF * row_odd, HALF), HALF)
    bottom = pl.ds(pl.multiple_of(HALF * (1 - row_odd), HALF), HALF)
    near = pl.ds(pl.multiple_of(HALF * core, HALF), HALF)
    far = pl.ds(pl.multiple_of(HALF * (1 - core), HALF), HALF)
    moves = [
        (own.at[:, top, :], odd.at[:, :HALF, :]),
        (own.at[:, bottom, :], even.at[:, :HALF, :]),
        (own.at[:, :, near], cross.at[:, :SIZE, :]),
        (own.at[:, :, far], same.at[:, :SIZE, :]),
        (offsets, odd.at[:, HALF:, :]),
        (offsets, even.at[:, HALF:, :]),
        (offsets.at[:, :, :HALF], cross.at[:, SIZE : SIZE + 8, :]),
        (offsets.at[:, :, :HALF], same.at[:, SIZE:, :]),
    ]
    run_all([pltpu.make_async_copy(x, y, sems.at[n]) for n, (x, y) in enumerate(moves)])


def sides():
    row_odd, core = place_of()
    even_rows = pl.ds(pl.multiple_of(3 * HALF * (1 - row_odd), HALF), HALF)
    odd_rows = pl.ds(pl.multiple_of(3 * HALF * row_odd, HALF), HALF)
    return even_rows, odd_rows, 3 * core, 3 - 3 * core


def transform_kernel(
    starts, own, odd_strip, even_strip, cross, same, cross_corner, same_corner, probe_in, matrices, measured,
    keep, send, around, center, even, odd, cross_out, same_out, steps,
    tile, probe, mats, offsets, totals, sums, accum, power, sems, *slots,
):
    step = pl.program_id(0)
    modes = probe.shape[0]
    lanes = lane_index(CHUNK)
    width = measured.shape[0]
    per_slot = len(slots) // width
    slots = [slots[n * per_slot : (n + 1) * per_slot] for n in range(width)]

    @pl.when(step == 0)
    def _():
        even_rows, odd_rows, cross_block, same_block = sides()
        middle = pl.ds(HALF, SIZE)
        moves = [(probe_in, probe), (matrices, mats)]
        for block, strip, corner in ((cross_block, cross, cross_corner), (same_block, same, same_corner)):
            moves.append((strip.at[:, :SIZE, :], tile.at[:, block, middle, :]))
            moves.append((corner.at[1, :, :HALF, :], tile.at[:, block, even_rows, :]))
            moves.append((corner.at[0, :, :HALF, :], tile.at[:, block, odd_rows, :]))
        for b in range(2):
            span = pl.ds(b * HALF, HALF)
            moves.append((own.at[:, :, span], tile.at[:, 1 + b, middle, :]))
            moves.append((even_strip.at[:, :HALF, span], tile.at[:, 1 + b, even_rows, :]))
            moves.append((odd_strip.at[:, :HALF, span], tile.at[:, 1 + b, odd_rows, :]))
        strips = [(odd_strip.at[0], HALF), (even_strip.at[0], HALF), (cross.at[0], SIZE), (same.at[0], SIZE)]
        strips += [(x.at[n, 0], HALF) for x in (cross_corner, same_corner) for n in range(2)]
        for n, (strip, at) in enumerate(strips):
            moves.append((strip.at[pl.ds(at, 8), pl.ds(0, HALF)], offsets.at[n]))
        copies = [pltpu.make_async_copy(x, y, sems.at[n]) for n, (x, y) in enumerate(moves)]
        for copy in copies:
            copy.start()
        tile[:, 4] = jnp.zeros((2, 2 * SIZE, HALF), F32)
        totals[...] = jnp.zeros_like(totals)
        sums[...] = jnp.zeros_like(sums)
        accum[...] = jnp.zeros_like(accum)
        for slot in slots:
            slot[4][:, :, 0:8, :] = jnp.zeros((2, 2, 8, HALF), F32)
            slot[4][:, :, 264:272, :] = jnp.zeros((2, 2, 8, HALF), F32)
        for copy in copies:
            copy.wait()
        for i in range(0, SIZE, CHUNK):
            part = pl.ds(i, CHUNK)
            power[part] = probe_power(probe, part)
        for n in range(8):
            around[pl.ds(n, 1), :] = offsets[n, :1, :].astype(jnp.int32)

    def right(odd, transposed):
        high, low = mats[odd, transposed, 0], mats[odd, transposed, 1]
        return jnp.concatenate([high, high, low], 0)

    def left(odd, transposed):
        high, low = mats[odd, transposed, 0], mats[odd, transposed, 1]
        return jnp.concatenate([high, low, high], 1)

    def position(n):
        col = starts[1, width * step + n]
        return starts[0, width * step + n], col // HALF, lax.rem(col, HALF)

    def enter(n):
        xs, patch = slots[n][0], slots[n][4]
        row, base, shift = position(n)
        for i in range(0, SIZE, CHUNK):
            part = pl.ds(i, CHUNK)
            where = pl.ds(row + i, CHUNK)
            obj = []
            for p in range(2):
                blocks = [tile[p, base + b, where, :] for b in range(3)]
                obj.append(gather_lanes(blocks, shift, lanes))
                for b in range(2):
                    patch[p, b, pl.ds(8 + i, CHUNK), :] = obj[p][b]
            for m in range(modes):
                wave = []
                for b in range(2):
                    span = slice(b * HALF, (b + 1) * HALF)
                    pr, pi = probe[m, 0, part, span], probe[m, 1, part, span]
                    wave.append((pr * obj[0][b] - pi * obj[1][b], pr * obj[1][b] + pi * obj[0][b]))
                for odd in range(2):
                    for p in range(2):
                        high, low = split2(wave[0][p] - wave[1][p] if odd else wave[0][p] + wave[1][p])
                        at = pl.ds(m * SIZE + i, CHUNK)
                        xs[odd, at, p * HALF : (p + 1) * HALF] = high
                        xs[odd, at, SIZE + p * HALF : SIZE + (p + 1) * HALF] = low
                        xs[odd, at, 2 * SIZE + p * HALF : 2 * SIZE + (p + 1) * HALF] = high

    def lanes_forward(n):
        xs, ys = slots[n][0], slots[n][2]
        for odd in range(2):
            ys[odd] = dot(xs[odd], right(odd, 0))

    def rows_split(n):
        zs, ys = slots[n][1], slots[n][2]
        for m in range(modes):
            for odd in range(2):
                lane_span = slice(odd * HALF, (odd + 1) * HALF)
                for i in range(0, HALF, CHUNK):
                    top = ys[odd, pl.ds(m * SIZE + i, CHUNK), :]
                    bottom = ys[odd, pl.ds(m * SIZE + HALF + i, CHUNK), :]
                    for odd_row in range(2):
                        high, low = split2(top - bottom if odd_row else top + bottom)
                        for p in range(2):
                            span = slice(p * HALF, (p + 1) * HALF)
                            at = p * HALF + i
                            zs[m, odd_row, pl.ds(at, CHUNK), lane_span] = high[:, span]
                            zs[m, odd_row, pl.ds(SIZE + at, CHUNK), lane_span] = high[:, span]
                            zs[m, odd_row, pl.ds(2 * SIZE + at, CHUNK), lane_span] = low[:, span]

    def rows_forward(n):
        zs, fs = slots[n][1], slots[n][3]
        for odd_row in range(2):
            for m in range(modes):
                fs[m, odd_row] = dot(left(odd_row, 1), zs[m, odd_row])

    def scale(n):
        zs, fs = slots[n][1], slots[n][3]
        error = jnp.zeros((8, HALF), F32)
        energy = jnp.zeros((8, HALF), F32)
        for odd_row in range(2):
            for i in range(0, HALF, CHUNK):
                parts = [[fs[m, odd_row, pl.ds(p * HALF + i, CHUNK), :] for p in range(2)] for m in range(modes)]
                intensity = parts[0][0] ** 2 + parts[0][1] ** 2 + (parts[1][0] ** 2 + parts[1][1] ** 2)
                intensity = jnp.maximum(intensity, intensity_floor)
                inverse = lax.rsqrt(intensity)
                modulus = intensity * inverse
                amplitude = measured[n, pl.ds(odd_row * HALF + i, CHUNK), :]
                factor = 1.0 - amplitude * inverse
                misfit = (modulus - amplitude) ** 2
                strength = amplitude**2
                error = error + fold8(misfit[:, :HALF]) + fold8(misfit[:, HALF:])
                energy = energy + fold8(strength[:, :HALF]) + fold8(strength[:, HALF:])
                for m in range(modes):
                    for p in range(2):
                        high, low = split2(parts[m][p] * factor)
                        at = p * HALF + i
                        zs[m, odd_row, pl.ds(at, CHUNK), :] = high
                        zs[m, odd_row, pl.ds(SIZE + at, CHUNK), :] = high
                        zs[m, odd_row, pl.ds(2 * SIZE + at, CHUNK), :] = low
        sums[0] += error
        sums[1] += energy

    def rows_back(n):
        zs, fs = slots[n][1], slots[n][3]
        for odd_row in range(2):
            for m in range(modes):
                fs[m, odd_row] = dot(left(odd_row, 0), zs[m, odd_row])

    def rows_join(n):
        xs, fs = slots[n][0], slots[n][3]
        for m in range(modes):
            for i in range(0, HALF, CHUNK):
                for p in range(2):
                    a, b = [fs[m, odd_row, pl.ds(p * HALF + i, CHUNK), :] for odd_row in range(2)]
                    for bottom in range(2):
                        high, low = split2(a - b if bottom else a + b)
                        at = pl.ds(m * SIZE + bottom * HALF + i, CHUNK)
                        for odd in range(2):
                            span = slice(odd * HALF, (odd + 1) * HALF)
                            xs[odd, at, p * HALF : (p + 1) * HALF] = high[:, span]
                            xs[odd, at, SIZE + p * HALF : SIZE + (p + 1) * HALF] = low[:, span]
                            xs[odd, at, 2 * SIZE + p * HALF : 2 * SIZE + (p + 1) * HALF] = high[:, span]

    def lanes_back(n):
        xs, ys = slots[n][0], slots[n][2]
        for odd in range(2):
            ys[odd] = dot(xs[odd], right(odd, 1))

    def leave(n):
        ys, patch = slots[n][2], slots[n][4]
        row, base, shift = position(n)
        first, last = lanes == 0, lanes == HALF - 1
        sums_of = [jnp.zeros((8, HALF), F32) for _ in range(4)]
        for i in range(0, SIZE, CHUNK):
            part = pl.ds(i, CHUNK)
            where = pl.ds(row + i, CHUNK)
            obj = [[patch[p, b, pl.ds(8 + i, CHUNK), :] for b in range(2)] for p in range(2)]
            grads = [[0.0, 0.0], [0.0, 0.0]]
            for b in range(2):
                re, im = obj[0][b], obj[1][b]
                span = slice(b * HALF, (b + 1) * HALF)
                for m in range(modes):
                    at = pl.ds(m * SIZE + i, CHUNK)
                    evens = [ys[0, at, p * HALF : (p + 1) * HALF] for p in range(2)]
                    odds = [ys[1, at, p * HALF : (p + 1) * HALF] for p in range(2)]
                    br, bi = [x - y if b else x + y for x, y in zip(evens, odds)]
                    pr, pi = probe[m, 0, part, span], probe[m, 1, part, span]
                    grads[0][b] = grads[0][b] + (pr * br + pi * bi)
                    grads[1][b] = grads[1][b] + (pr * bi - pi * br)
                    totals[b, 2 * m, part, :] += re * br + im * bi
                    totals[b, 2 * m + 1, part, :] += re * bi - im * br
                totals[b, 4, part, :] += re**2 + im**2
            for p in range(2):
                moved = spread(grads[p][0], grads[p][1], shift, lanes)
                for b in range(3):
                    accum[p, base + b, where, :] += moved[b]
            columns = []
            for p in range(2):
                before = [pltpu.roll(x, 1, 1) for x in obj[p]]
                after = [pltpu.roll(x, HALF - 1, 1) for x in obj[p]]
                columns.append(
                    (
                        jnp.where(last, after[1], after[0]) - jnp.where(first, 0.0, before[0]),
                        jnp.where(last, 0.0, after[1]) - jnp.where(first, before[0], before[1]),
                    )
                )
            for b in range(2):
                strength = power[part, b * HALF : (b + 1) * HALF]
                rows = [patch[p, b, pl.ds(9 + i, CHUNK), :] - patch[p, b, pl.ds(7 + i, CHUNK), :] for p in range(2)]
                for d, slope in enumerate((rows, [columns[0][b], columns[1][b]])):
                    sums_of[2 * d] = sums_of[2 * d] + fold8(grads[0][b] * slope[0] + grads[1][b] * slope[1])
                    sums_of[2 * d + 1] = sums_of[2 * d + 1] + fold8(strength * (slope[0] ** 2 + slope[1] ** 2))
        for d in range(2):
            numerator = 0.5 * jnp.sum(sums_of[2 * d], keepdims=True)
            denominator = 0.25 * jnp.sum(sums_of[2 * d + 1], keepdims=True) + small_value
            at = pl.ds(2 * (width * step + n) + d, 1)
            steps[at, :] = jnp.broadcast_to(-numerator / denominator, (1, HALF))

    stages = [enter, lanes_forward, rows_split, rows_forward, scale, rows_back, rows_join, lanes_back, leave]
    for at in range(len(stages) + width - 1):
        for n in range(width):
            if 0 <= at - n < len(stages):
                stages[at - n](n)

    @pl.when(step == pl.num_programs(0) - 1)
    def _():
        core = place_of()[1]
        scalar = jnp.where(lax.broadcasted_iota(jnp.int32, (1, 8, HALF), 2) == 0, jnp.sum(sums[0]), jnp.sum(sums[1]))
        for out, block in ((keep, core), (send, 1 - core)):
            for c in range(5):
                out[:, 16 * c : 16 * c + 16, :] = totals[block, c].reshape(16, 16, HALF)
            out[:, 80:88, :] = jnp.broadcast_to(scalar, (16, 8, HALF))
        even_rows, odd_rows, cross_block, same_block = sides()
        for p in range(2):
            for b in range(2):
                span = slice(b * HALF, (b + 1) * HALF)
                center[p, :, span] = accum[p, 1 + b, 128:384]
                even[p, :, span] = accum[p, 1 + b, even_rows]
                odd[p, :, span] = accum[p, 1 + b, odd_rows]
            cross_out[p] = accum[p, cross_block]
            same_out[p] = accum[p, same_block]


def probe_power(probe, part):
    return (probe[0, 0, part] ** 2 + probe[0, 1, part] ** 2) + (probe[1, 0, part] ** 2 + probe[1, 1, part] ** 2)


def light_kernel(starts, around, probe, light, power, accum):
    accum[...] = jnp.zeros_like(accum)
    for i in range(0, SIZE, CHUNK):
        part = pl.ds(i, CHUNK)
        total = probe_power(probe, part)
        power[0, part] = total[:, :HALF]
        power[1, part] = total[:, HALF:]
    lanes = lane_index(CHUNK)
    row_odd, core = place_of()
    even, cross = 1 - 2 * row_odd, 2 * core - 1
    neighbours = [(-even, None), (even, None), (None, cross), (None, -cross)]
    neighbours += [(-even, cross), (even, cross), (-even, -cross), (even, -cross)]

    def add(row, col, down, right):
        rows, source_row, row = (SIZE, 0, row + HALF) if down is None else (
            HALF, pl.multiple_of(jnp.where(down < 0, HALF, 0), HALF), row + jnp.where(down < 0, 0, 3 * HALF)
        )
        if right is None:
            col = col + HALF
        else:
            source = jnp.where(right < 0, 1, 0)
            col = col + jnp.where(right < 0, 0, 3 * HALF)
        base, shift = col // HALF, lax.rem(col, HALF)
        for i in range(0, rows, CHUNK):
            part = pl.ds(source_row + i, CHUNK)
            where = pl.ds(row + i, CHUNK)
            if right is None:
                moved = spread(power[0, part], power[1, part], shift, lanes)
            else:
                rolled = pltpu.roll(power[source, part], shift, 1)
                moved = jnp.where(lanes < shift, 0.0, rolled), jnp.where(lanes < shift, rolled, 0.0)
            for b, value in enumerate(moved):
                accum[base + b, where, :] += value

    count = starts.shape[1]
    for j in range(count):
        add(starts[0, j], starts[1, j], None, None)
    for n, (down, right) in enumerate(neighbours):
        for j in range(count):
            row, col = around[n, 2 * j] - 1, around[n, 2 * j + 1] - 1
            near = row >= 0
            if down is not None:
                near = near & jnp.where(down < 0, row > HALF, row < HALF)
            if right is not None:
                near = near & jnp.where(right < 0, col > HALF, col < HALF)

            @pl.when(near)
            def _(row=row, col=col, down=down, right=right):
                add(row, col, down, right)

    light[:, :HALF] = accum[2, 256:512]
    light[:, HALF:] = accum[3, 256:512]


def sum_kernel(chunk, total):
    total[...] = jnp.sum(chunk[...], axis=0)


def quotient_kernel(own, first, second, third, spread_out, ratio, held):
    z = 2 * lax.div(lax.axis_index("row"), 4) + lax.rem(lax.div(lax.axis_index("col"), 2), 2)
    for distance, part in enumerate((own, first, second, third)):
        held[lax.rem(z + 4 - distance, 4)] = part[...]
    total = (held[0] + held[1]) + (held[2] + held[3])
    for c in range(4):
        quotient = total[16 * c : 16 * c + 16] / total[64:80]
        spread_out[:, 16 * c : 16 * c + 16, :] = jnp.broadcast_to(quotient[None], (16, 16, HALF))
    ratio[...] = jnp.broadcast_to(total[80:81, 0:1] / total[80:81, 1:2], (8, HALF))


def fold_kernel(even, odd, cross, same, even_out, odd_out):
    even_rows, odd_rows, _, _ = sides()
    swapped = place_of()[1] == 1
    for p in range(2):
        for strip, rows, out in ((even, even_rows, even_out), (odd, odd_rows, odd_out)):
            a, b = cross[p, rows], same[p, rows]
            out[p, :HALF, :HALF] = strip[p, :, :HALF] + jnp.where(swapped, b, a)
            out[p, :HALF, HALF:] = strip[p, :, HALF:] + jnp.where(swapped, a, b)
    odd_out[:, HALF:, :] = jnp.zeros((2, 8, SIZE), F32)


def update_kernel(center, even, odd, cross, same, light, out, total):
    for p in range(2):
        total[p] = center[p]
    row_odd, core = place_of()
    even_half = pl.ds(pl.multiple_of(HALF * (1 - row_odd), HALF), HALF)
    odd_half = pl.ds(pl.multiple_of(HALF * row_odd, HALF), HALF)
    for p in range(2):
        total[p, even_half, :] += even[p]
        total[p, odd_half, :] += odd[p, :HALF]
    swapped = core == 1
    for i in range(0, SIZE, CHUNK):
        part = pl.ds(i, CHUNK)
        scale = 1.0 / (light[part] + object_damping)
        for p in range(2):
            a, b = cross[p, pl.ds(HALF + i, CHUNK)], same[p, pl.ds(HALF + i, CHUNK)]
            out[p, part, :HALF] = (total[p, part, :HALF] + jnp.where(swapped, b, a)) * scale[:, :HALF]
            out[p, part, HALF:] = (total[p, part, HALF:] + jnp.where(swapped, a, b)) * scale[:, HALF:]


def assemble_kernel(mine, other, out):
    core = place_of()[1]

    def write(source, block):
        for c in range(4):
            out[c, :, block * HALF : (block + 1) * HALF] = source[:, 16 * c : 16 * c + 16, :].reshape(SIZE, HALF)

    @pl.when(core == 0)
    def _():
        write(mine, 0)
        write(other, 1)

    @pl.when(core == 1)
    def _():
        write(mine, 1)
        write(other, 0)


def whole(*shape):
    return pl.BlockSpec(shape, lambda *_: (0,) * len(shape))


ANY = pl.BlockSpec(memory_space=pl.ANY)


def shaped(shapes):
    return [jax.ShapeDtypeStruct(s, F32) for s in shapes]


def params():
    return pltpu.CompilerParams(vmem_limit_bytes=VMEM_LIMIT)


def cost(flops, size):
    return pl.CostEstimate(flops=flops, bytes_accessed=size, transcendentals=0)


def simple(kernel, scalars, arrays, shapes, scratch, flops, size):
    single = not isinstance(shapes, list)
    outs = [shapes] if single else shapes
    call = pl.pallas_call(
        kernel,
        out_shape=shaped(outs)[0] if single else shaped(outs),
        grid_spec=pltpu.PrefetchScalarGridSpec(
            num_scalar_prefetch=len(scalars),
            grid=(),
            in_specs=[whole(*x.shape) for x in arrays],
            out_specs=whole(*shapes) if single else [whole(*s) for s in outs],
            scratch_shapes=[pltpu.VMEM(s, F32) for s in scratch],
        ),
        compiler_params=params(),
        cost_estimate=cost(flops, size),
    )
    return call(*scalars, *arrays)


def pack(starts, own):
    rows, crossing, columns = (2, HALF + 8, SIZE), (2, SIZE + 24, HALF), (2, SIZE + 8, HALF)
    return pl.pallas_call(
        pack_kernel,
        out_shape=shaped([rows, rows, crossing, columns]),
        grid_spec=pltpu.PrefetchScalarGridSpec(
            num_scalar_prefetch=1,
            grid=(),
            in_specs=[pl.BlockSpec(memory_space=pltpu.HBM)],
            out_specs=[ANY] * 4,
            scratch_shapes=[pltpu.VMEM((2, 8, SIZE), F32), pltpu.SemaphoreType.DMA((8,))],
        ),
        compiler_params=params(),
        cost_estimate=cost(1 << 10, 2 << 20),
    )(starts, own)


def prepare(measured):
    cols, rows = permutation()
    arrays = [measured, jnp.asarray(cols), jnp.asarray(rows)]
    return simple(prepare_kernel, [], arrays, measured.shape, [], 1 << 30, 3 << 20)


def stepped(width, *shape):
    return pl.BlockSpec((width, *shape), lambda i, *_: (i,) + (0,) * len(shape))


def transforms(starts, own, halo, probe, measured):
    mats = jnp.asarray(constants())
    arrays = [own, *halo, probe, mats]
    count = measured.shape[0]
    width = WIDTH
    halves = (16, 88, HALF)
    rows, columns = (2, HALF, SIZE), (2, 2 * SIZE, HALF)
    shapes = [(2, SIZE, SIZE), rows, rows, columns, columns, (2 * count, HALF)]
    slot = [
        pltpu.VMEM((2, 2 * SIZE, 3 * SIZE), BF),
        pltpu.VMEM((2, 2, 3 * SIZE, SIZE), BF),
        pltpu.VMEM((2, 2 * SIZE, SIZE), F32),
        pltpu.VMEM((2, 2, SIZE, SIZE), F32),
        pltpu.VMEM((2, 2, SIZE + 16, HALF), F32),
    ]
    return pl.pallas_call(
        transform_kernel,
        out_shape=shaped([halves, halves]) + [jax.ShapeDtypeStruct((8, HALF), jnp.int32)] + shaped(shapes),
        grid_spec=pltpu.PrefetchScalarGridSpec(
            num_scalar_prefetch=1,
            grid=(count // width,),
            in_specs=[ANY] * len(arrays) + [stepped(width, SIZE, SIZE)],
            out_specs=[whole(*x) for x in [halves, halves, (8, HALF), *shapes]],
            scratch_shapes=[
                pltpu.VMEM((2, 5, 2 * SIZE, HALF), F32),
                pltpu.VMEM(probe.shape, F32),
                pltpu.VMEM(mats.shape, BF),
                pltpu.VMEM((8, 8, HALF), F32),
                pltpu.VMEM((2, 5, SIZE, HALF), F32),
                pltpu.VMEM((2, 8, HALF), F32),
                pltpu.VMEM((2, 5, 2 * SIZE, HALF), F32),
                pltpu.VMEM((SIZE, SIZE), F32),
                pltpu.SemaphoreType.DMA((24,)),
            ]
            + slot * width,
        ),
        compiler_params=params(),
        cost_estimate=cost(13 << 30, 12 << 20),
    )(starts, *arrays, measured)


def illuminate(starts, around, probe):
    scratch = [(2, SIZE, HALF), (7, 3 * SIZE, HALF)]
    return simple(light_kernel, [starts, around], [probe], (SIZE, SIZE), scratch, 2 << 30, 4 << 20)


def update(arrays):
    shape = arrays[0].shape
    return simple(update_kernel, [], arrays, shape, [shape], 1 << 20, 3 << 20)


def assemble(mine, other):
    return simple(assemble_kernel, [], [mine, other], (4, SIZE, SIZE), [], 1 << 20, 2 << 20)


def pairs_from(first, count):
    pairs = []
    for i in range(first, count - 1, 2):
        pairs += [(i, i + 1), (i + 1, i)]
    return pairs


def swap_rows(value, first):
    return lax.ppermute(value, "row", pairs_from(first, lax.axis_size("row")))


def swap_columns(value, first):
    return lax.ppermute(value, "col", pairs_from(first, lax.axis_size("col")))


def along_z(value, distance):
    pairs = []
    for row in range(lax.axis_size("row")):
        for col in range(lax.axis_size("col")):
            z = (2 * (row // 4) + col // 2 % 2 + distance) % 4
            target = (4 * (z // 2) + row % 4) * 16 + col // 4 * 4 + 2 * (z % 2) + col % 2
            pairs.append((row * 16 + col, target))
    return lax.ppermute(value, AXES, pairs)


def planes():
    groups = {}
    for row in range(lax.axis_size("row")):
        for col in range(lax.axis_size("col")):
            groups.setdefault((row // 4, col % 4), []).append(row * 16 + col)
    return list(groups.values())


def half_lanes(value, first):
    return jnp.where(first, value[..., :HALF], value[..., HALF:])


def local(object_tile, probe, amplitudes, offsets):
    starts = offsets[0, 0].T
    measured = amplitudes[0, 0]
    core = lax.rem(lax.axis_index("col"), 2)
    groups = planes()

    with jax.named_scope("object_halo"):
        even, odd, cross, same = pack(starts, object_tile)
        odd = swap_rows(odd, 1)
        even = swap_rows(even, 0)
        cross = swap_columns(cross, 1)
        same = swap_columns(same, 0)
    permuted = prepare(measured)
    with jax.named_scope("object_corners"):
        odd, even, cross, same, permuted = lax.optimization_barrier((odd, even, cross, same, permuted))
        rows = jnp.stack([odd, even])
        cross_corner = swap_columns(half_lanes(rows, core == 0), 1)
        same_corner = swap_columns(half_lanes(rows, core == 1), 0)

    halo = [odd, even, cross, same, cross_corner, same_corner]
    keep, send, around, *parts = transforms(starts, object_tile, halo, probe, permuted)

    center, even, odd, cross, same, steps = parts
    with jax.named_scope("gradient_columns"):
        cross = swap_columns(cross, 1)
        same = swap_columns(same, 0)

    with jax.named_scope("probe_reduce"):
        chunk, around = lax.optimization_barrier((keep + swap_columns(send, 0), around))
        chunk = lax.all_to_all(chunk, AXES, 0, 0, axis_index_groups=groups, tiled=True)

    with jax.named_scope("gradient_rows"):
        light = illuminate(starts, around, probe)
        even, odd = simple(fold_kernel, [], [even, odd, cross, same], [even.shape, (2, HALF + 8, SIZE)], [], 1 << 20, 1 << 20)
        chunk, light, odd, even = lax.optimization_barrier((chunk, light, odd, even))

    with jax.named_scope("probe_sum"):
        total = simple(sum_kernel, [], [chunk], (88, HALF), [], 1 << 20, 1 << 20)
        parts = [total] + [along_z(total, d) for d in (1, 2, 3)]
        shapes = [(16, 64, HALF), (8, HALF)]
        spread_out, ratio = simple(quotient_kernel, [], parts, shapes, [(4, 88, HALF)], 1 << 20, 2 << 20)
        spread_out, odd, even = lax.optimization_barrier((spread_out, odd, even))
        odd = swap_rows(odd, 1)
        even = swap_rows(even, 0)

    with jax.named_scope("probe_gather"):
        gathered = lax.all_to_all(spread_out, AXES, 0, 0, axis_index_groups=groups, tiled=True)
        relative_error = ratio[0, :1]
        position_step = steps[:, 0].reshape(1, 1, -1, 2)
        tied = (gathered, relative_error, position_step)
        gathered, relative_error, position_step = lax.optimization_barrier(tied)
        probe_update = assemble(gathered, swap_columns(gathered, 0)).reshape(probe.shape)

    probe_update, odd, even = lax.optimization_barrier((probe_update, odd, even))
    object_update = update([center, even, odd, cross, same, light])
    return (object_update, probe_update, position_step, relative_error)


def solution(mesh):
    in_specs = (
        P(None, "row", "col"),
        P(),
        P("row", "col", None, None, None),
        P("row", "col", None, None),
    )
    out_specs = (P(None, "row", "col"), P(), P("row", "col", None, None), P())
    return jax.shard_map(local, mesh=mesh, in_specs=in_specs, out_specs=out_specs, check_vma=False)
```

```python
import jax
import jax.numpy as jnp
import ml_dtypes
import numpy as np
from jax import lax
from jax.experimental import pallas as pl
from jax.experimental.pallas import tpu as pltpu
from jax.sharding import PartitionSpec as P

intensity_floor = 0.1
object_damping = 1.0
small_value = 1e-06

SIZE = 256
HALF = 128
CHUNK = 32
WIDTH = 2
BF = jnp.bfloat16
F32 = jnp.float32
AXES = ("row", "col")
VMEM_LIMIT = 32 * 2**20


def transform_matrices():
    n = np.arange(HALF)[:, None]
    q = np.arange(HALF)[None, :]
    out = []
    for odd in (0, 1):
        angle = -2.0 * np.pi * ((n * (2 * q + odd)) % SIZE) / SIZE
        re, im = np.cos(angle) / 16.0, np.sin(angle) / 16.0
        out.append(np.block([[re, im], [-im, re]]))
    return out


def split_np(matrix):
    high = matrix.astype(ml_dtypes.bfloat16)
    low = (matrix - high.astype(np.float64)).astype(ml_dtypes.bfloat16)
    return high, low


def constants():
    return np.stack([np.stack([np.stack(split_np(x)) for x in (m, m.T)]) for m in transform_matrices()])


def permutation():
    order = np.concatenate([np.arange(0, SIZE, 2), np.arange(1, SIZE, 2)])
    onehot = np.zeros((SIZE, SIZE), np.float32)
    onehot[order, np.arange(SIZE)] = 1.0
    columns = np.concatenate([onehot] * 3, 0).astype(ml_dtypes.bfloat16)
    rows = np.concatenate([onehot.T] * 3, 1).astype(ml_dtypes.bfloat16)
    return columns, rows


def split2(value):
    high = value.astype(BF)
    return high, (value - high.astype(F32)).astype(BF)


def split3(value):
    high = value.astype(BF)
    rest = value - high.astype(F32)
    middle = rest.astype(BF)
    return high, middle, (rest - middle.astype(F32)).astype(BF)


def dot(a, b):
    return jnp.dot(a, b, preferred_element_type=F32)


def lane_index(rows):
    return lax.broadcasted_iota(jnp.int32, (rows, HALF), 1)


def spread(first, second, shift, lanes):
    a = pltpu.roll(first, shift, 1)
    b = pltpu.roll(second, shift, 1)
    wrapped = lanes < shift
    return jnp.where(wrapped, 0.0, a), jnp.where(wrapped, a, b), jnp.where(wrapped, b, 0.0)


def gather_lanes(blocks, shift, lanes):
    back = jnp.where(shift == 0, 0, HALF - shift)
    a, b, c = [pltpu.roll(x, back, 1) for x in blocks]
    inside = lanes < HALF - shift
    return jnp.where(inside, a, b), jnp.where(inside, b, c)


def fold8(value):
    return jnp.sum(value.reshape(-1, 8, HALF), axis=0)


def prepare_kernel(measured, cols, rows, permuted):
    for j in range(measured.shape[0]):
        moved = dot(jnp.concatenate(split3(measured[j]), 1), cols[...])
        permuted[j] = dot(rows[...], jnp.concatenate(split3(moved), 0))


def place_of():
    return lax.rem(lax.axis_index("row"), 2), lax.rem(lax.axis_index("col"), 2)


def run_all(copies):
    for copy in copies:
        copy.start()
    for copy in copies:
        copy.wait()


def pack_kernel(starts, own, even, odd, cross, same, offsets, sems):
    row_odd, core = place_of()
    lanes = lane_index(8)
    value = jnp.zeros((8, HALF), F32)
    for j in range(starts.shape[1]):
        for d in range(2):
            value = jnp.where(lanes == 2 * j + d, (starts[d, j] + 1).astype(F32), value)
    for p in range(2):
        offsets[p, :, :HALF] = value
        offsets[p, :, HALF:] = value
    top = pl.ds(pl.multiple_of(HALF * row_odd, HALF), HALF)
    bottom = pl.ds(pl.multiple_of(HALF * (1 - row_odd), HALF), HALF)
    near = pl.ds(pl.multiple_of(HALF * core, HALF), HALF)
    far = pl.ds(pl.multiple_of(HALF * (1 - core), HALF), HALF)
    moves = [
        (own.at[:, top, :], odd.at[:, :HALF, :]),
        (own.at[:, bottom, :], even.at[:, :HALF, :]),
        (own.at[:, :, near], cross.at[:, :SIZE, :]),
        (own.at[:, :, far], same.at[:, :SIZE, :]),
        (offsets, odd.at[:, HALF:, :]),
        (offsets, even.at[:, HALF:, :]),
        (offsets.at[:, :, :HALF], cross.at[:, SIZE : SIZE + 8, :]),
        (offsets.at[:, :, :HALF], same.at[:, SIZE:, :]),
    ]
    run_all([pltpu.make_async_copy(x, y, sems.at[n]) for n, (x, y) in enumerate(moves)])


def sides():
    row_odd, core = place_of()
    even_rows = pl.ds(pl.multiple_of(3 * HALF * (1 - row_odd), HALF), HALF)
    odd_rows = pl.ds(pl.multiple_of(3 * HALF * row_odd, HALF), HALF)
    return even_rows, odd_rows, 3 * core, 3 - 3 * core


def transform_kernel(
    starts, own, odd_strip, even_strip, cross, same, cross_corner, same_corner, probe_in, matrices, measured,
    keep, send, around, center, even, odd, cross_out, same_out, steps,
    tile, probe, mats, offsets, totals, sums, accum, power, sems, *slots,
):
    step = pl.program_id(0)
    modes = probe.shape[0]
    lanes = lane_index(CHUNK)
    width = measured.shape[0]
    per_slot = len(slots) // width
    slots = [slots[n * per_slot : (n + 1) * per_slot] for n in range(width)]

    @pl.when(step == 0)
    def _():
        even_rows, odd_rows, cross_block, same_block = sides()
        middle = pl.ds(HALF, SIZE)
        moves = [(probe_in, probe), (matrices, mats)]
        for block, strip, corner in ((cross_block, cross, cross_corner), (same_block, same, same_corner)):
            moves.append((strip.at[:, :SIZE, :], tile.at[:, block, middle, :]))
            moves.append((corner.at[1, :, :HALF, :], tile.at[:, block, even_rows, :]))
            moves.append((corner.at[0, :, :HALF, :], tile.at[:, block, odd_rows, :]))
        for b in range(2):
            span = pl.ds(b * HALF, HALF)
            moves.append((own.at[:, :, span], tile.at[:, 1 + b, middle, :]))
            moves.append((even_strip.at[:, :HALF, span], tile.at[:, 1 + b, even_rows, :]))
            moves.append((odd_strip.at[:, :HALF, span], tile.at[:, 1 + b, odd_rows, :]))
        strips = [(odd_strip.at[0], HALF), (even_strip.at[0], HALF), (cross.at[0], SIZE), (same.at[0], SIZE)]
        strips += [(x.at[n, 0], HALF) for x in (cross_corner, same_corner) for n in range(2)]
        for n, (strip, at) in enumerate(strips):
            moves.append((strip.at[pl.ds(at, 8), pl.ds(0, HALF)], offsets.at[n]))
        copies = [pltpu.make_async_copy(x, y, sems.at[n]) for n, (x, y) in enumerate(moves)]
        for copy in copies:
            copy.start()
        tile[:, 4] = jnp.zeros((2, 2 * SIZE, HALF), F32)
        totals[...] = jnp.zeros_like(totals)
        sums[...] = jnp.zeros_like(sums)
        accum[...] = jnp.zeros_like(accum)
        for slot in slots:
            slot[4][:, :, 0:8, :] = jnp.zeros((2, 2, 8, HALF), F32)
            slot[4][:, :, 264:272, :] = jnp.zeros((2, 2, 8, HALF), F32)
        for copy in copies:
            copy.wait()
        for i in range(0, SIZE, CHUNK):
            part = pl.ds(i, CHUNK)
            power[part] = probe_power(probe, part)
        for n in range(8):
            around[pl.ds(n, 1), :] = offsets[n, :1, :].astype(jnp.int32)

    def right(odd, transposed):
        high, low = mats[odd, transposed, 0], mats[odd, transposed, 1]
        return jnp.concatenate([high, high, low], 0)

    def left(odd, transposed):
        high, low = mats[odd, transposed, 0], mats[odd, transposed, 1]
        return jnp.concatenate([high, low, high], 1)

    def position(n):
        col = starts[1, width * step + n]
        return starts[0, width * step + n], col // HALF, lax.rem(col, HALF)

    def enter(n):
        xs, patch = slots[n][0], slots[n][4]
        row, base, shift = position(n)
        for i in range(0, SIZE, CHUNK):
            part = pl.ds(i, CHUNK)
            where = pl.ds(row + i, CHUNK)
            obj = []
            for p in range(2):
                blocks = [tile[p, base + b, where, :] for b in range(3)]
                obj.append(gather_lanes(blocks, shift, lanes))
                for b in range(2):
                    patch[p, b, pl.ds(8 + i, CHUNK), :] = obj[p][b]
            for m in range(modes):
                wave = []
                for b in range(2):
                    span = slice(b * HALF, (b + 1) * HALF)
                    pr, pi = probe[m, 0, part, span], probe[m, 1, part, span]
                    wave.append((pr * obj[0][b] - pi * obj[1][b], pr * obj[1][b] + pi * obj[0][b]))
                for odd in range(2):
                    for p in range(2):
                        high, low = split2(wave[0][p] - wave[1][p] if odd else wave[0][p] + wave[1][p])
                        at = pl.ds(m * SIZE + i, CHUNK)
                        xs[odd, at, p * HALF : (p + 1) * HALF] = high
                        xs[odd, at, SIZE + p * HALF : SIZE + (p + 1) * HALF] = low
                        xs[odd, at, 2 * SIZE + p * HALF : 2 * SIZE + (p + 1) * HALF] = high

    def lanes_forward(n):
        xs, ys = slots[n][0], slots[n][2]
        for odd in range(2):
            ys[odd] = dot(xs[odd], right(odd, 0))

    def rows_split(n):
        zs, ys = slots[n][1], slots[n][2]
        for m in range(modes):
            for odd in range(2):
                lane_span = slice(odd * HALF, (odd + 1) * HALF)
                for i in range(0, HALF, CHUNK):
                    top = ys[odd, pl.ds(m * SIZE + i, CHUNK), :]
                    bottom = ys[odd, pl.ds(m * SIZE + HALF + i, CHUNK), :]
                    for odd_row in range(2):
                        high, low = split2(top - bottom if odd_row else top + bottom)
                        for p in range(2):
                            span = slice(p * HALF, (p + 1) * HALF)
                            at = p * HALF + i
                            zs[m, odd_row, pl.ds(at, CHUNK), lane_span] = high[:, span]
                            zs[m, odd_row, pl.ds(SIZE + at, CHUNK), lane_span] = high[:, span]
                            zs[m, odd_row, pl.ds(2 * SIZE + at, CHUNK), lane_span] = low[:, span]

    def rows_forward(n):
        zs, fs = slots[n][1], slots[n][3]
        for odd_row in range(2):
            for m in range(modes):
                fs[m, odd_row] = dot(left(odd_row, 1), zs[m, odd_row])

    def scale(n):
        zs, fs = slots[n][1], slots[n][3]
        error = jnp.zeros((8, HALF), F32)
        energy = jnp.zeros((8, HALF), F32)
        for odd_row in range(2):
            for i in range(0, HALF, CHUNK):
                parts = [[fs[m, odd_row, pl.ds(p * HALF + i, CHUNK), :] for p in range(2)] for m in range(modes)]
                intensity = parts[0][0] ** 2 + parts[0][1] ** 2 + (parts[1][0] ** 2 + parts[1][1] ** 2)
                intensity = jnp.maximum(intensity, intensity_floor)
                inverse = lax.rsqrt(intensity)
                modulus = intensity * inverse
                amplitude = measured[n, pl.ds(odd_row * HALF + i, CHUNK), :]
                factor = 1.0 - amplitude * inverse
                misfit = (modulus - amplitude) ** 2
                strength = amplitude**2
                error = error + fold8(misfit[:, :HALF]) + fold8(misfit[:, HALF:])
                energy = energy + fold8(strength[:, :HALF]) + fold8(strength[:, HALF:])
                for m in range(modes):
                    for p in range(2):
                        high, low = split2(parts[m][p] * factor)
                        at = p * HALF + i
                        zs[m, odd_row, pl.ds(at, CHUNK), :] = high
                        zs[m, odd_row, pl.ds(SIZE + at, CHUNK), :] = high
                        zs[m, odd_row, pl.ds(2 * SIZE + at, CHUNK), :] = low
        sums[0] += error
        sums[1] += energy

    def rows_back(n):
        zs, fs = slots[n][1], slots[n][3]
        for odd_row in range(2):
            for m in range(modes):
                fs[m, odd_row] = dot(left(odd_row, 0), zs[m, odd_row])

    def rows_join(n):
        xs, fs = slots[n][0], slots[n][3]
        for m in range(modes):
            for i in range(0, HALF, CHUNK):
                for p in range(2):
                    a, b = [fs[m, odd_row, pl.ds(p * HALF + i, CHUNK), :] for odd_row in range(2)]
                    for bottom in range(2):
                        high, low = split2(a - b if bottom else a + b)
                        at = pl.ds(m * SIZE + bottom * HALF + i, CHUNK)
                        for odd in range(2):
                            span = slice(odd * HALF, (odd + 1) * HALF)
                            xs[odd, at, p * HALF : (p + 1) * HALF] = high[:, span]
                            xs[odd, at, SIZE + p * HALF : SIZE + (p + 1) * HALF] = low[:, span]
                            xs[odd, at, 2 * SIZE + p * HALF : 2 * SIZE + (p + 1) * HALF] = high[:, span]

    def lanes_back(n):
        xs, ys = slots[n][0], slots[n][2]
        for odd in range(2):
            ys[odd] = dot(xs[odd], right(odd, 1))

    def leave(n):
        ys, patch = slots[n][2], slots[n][4]
        row, base, shift = position(n)
        first, last = lanes == 0, lanes == HALF - 1
        sums_of = [jnp.zeros((8, HALF), F32) for _ in range(4)]
        for i in range(0, SIZE, CHUNK):
            part = pl.ds(i, CHUNK)
            where = pl.ds(row + i, CHUNK)
            obj = [[patch[p, b, pl.ds(8 + i, CHUNK), :] for b in range(2)] for p in range(2)]
            grads = [[0.0, 0.0], [0.0, 0.0]]
            for b in range(2):
                re, im = obj[0][b], obj[1][b]
                span = slice(b * HALF, (b + 1) * HALF)
                for m in range(modes):
                    at = pl.ds(m * SIZE + i, CHUNK)
                    evens = [ys[0, at, p * HALF : (p + 1) * HALF] for p in range(2)]
                    odds = [ys[1, at, p * HALF : (p + 1) * HALF] for p in range(2)]
                    br, bi = [x - y if b else x + y for x, y in zip(evens, odds)]
                    pr, pi = probe[m, 0, part, span], probe[m, 1, part, span]
                    grads[0][b] = grads[0][b] + (pr * br + pi * bi)
                    grads[1][b] = grads[1][b] + (pr * bi - pi * br)
                    totals[b, 2 * m, part, :] += re * br + im * bi
                    totals[b, 2 * m + 1, part, :] += re * bi - im * br
                totals[b, 4, part, :] += re**2 + im**2
            for p in range(2):
                moved = spread(grads[p][0], grads[p][1], shift, lanes)
                for b in range(3):
                    accum[p, base + b, where, :] += moved[b]
            columns = []
            for p in range(2):
                before = [pltpu.roll(x, 1, 1) for x in obj[p]]
                after = [pltpu.roll(x, HALF - 1, 1) for x in obj[p]]
                columns.append(
                    (
                        jnp.where(last, after[1], after[0]) - jnp.where(first, 0.0, before[0]),
                        jnp.where(last, 0.0, after[1]) - jnp.where(first, before[0], before[1]),
                    )
                )
            for b in range(2):
                strength = power[part, b * HALF : (b + 1) * HALF]
                rows = [patch[p, b, pl.ds(9 + i, CHUNK), :] - patch[p, b, pl.ds(7 + i, CHUNK), :] for p in range(2)]
                for d, slope in enumerate((rows, [columns[0][b], columns[1][b]])):
                    sums_of[2 * d] = sums_of[2 * d] + fold8(grads[0][b] * slope[0] + grads[1][b] * slope[1])
                    sums_of[2 * d + 1] = sums_of[2 * d + 1] + fold8(strength * (slope[0] ** 2 + slope[1] ** 2))
        for d in range(2):
            numerator = 0.5 * jnp.sum(sums_of[2 * d], keepdims=True)
            denominator = 0.25 * jnp.sum(sums_of[2 * d + 1], keepdims=True) + small_value
            at = pl.ds(2 * (width * step + n) + d, 1)
            steps[at, :] = jnp.broadcast_to(-numerator / denominator, (1, HALF))

    stages = [enter, lanes_forward, rows_split, rows_forward, scale, rows_back, rows_join, lanes_back, leave]
    for at in range(len(stages) + width - 1):
        for n in range(width):
            if 0 <= at - n < len(stages):
                stages[at - n](n)

    @pl.when(step == pl.num_programs(0) - 1)
    def _():
        core = place_of()[1]
        scalar = jnp.where(lax.broadcasted_iota(jnp.int32, (1, 8, HALF), 2) == 0, jnp.sum(sums[0]), jnp.sum(sums[1]))
        for out, block in ((keep, core), (send, 1 - core)):
            for c in range(5):
                out[:, 16 * c : 16 * c + 16, :] = totals[block, c].reshape(16, 16, HALF)
            out[:, 80:88, :] = jnp.broadcast_to(scalar, (16, 8, HALF))
        even_rows, odd_rows, cross_block, same_block = sides()
        for p in range(2):
            for b in range(2):
                span = slice(b * HALF, (b + 1) * HALF)
                center[p, :, span] = accum[p, 1 + b, 128:384]
                even[p, :, span] = accum[p, 1 + b, even_rows]
                odd[p, :, span] = accum[p, 1 + b, odd_rows]
            cross_out[p] = accum[p, cross_block]
            same_out[p] = accum[p, same_block]


def probe_power(probe, part):
    return (probe[0, 0, part] ** 2 + probe[0, 1, part] ** 2) + (probe[1, 0, part] ** 2 + probe[1, 1, part] ** 2)


def light_kernel(starts, around, probe, light, power, accum):
    accum[...] = jnp.zeros_like(accum)
    for i in range(0, SIZE, CHUNK):
        part = pl.ds(i, CHUNK)
        total = probe_power(probe, part)
        power[0, part] = total[:, :HALF]
        power[1, part] = total[:, HALF:]
    lanes = lane_index(CHUNK)
    row_odd, core = place_of()
    even, cross = 1 - 2 * row_odd, 2 * core - 1
    neighbours = [(-even, None), (even, None), (None, cross), (None, -cross)]
    neighbours += [(-even, cross), (even, cross), (-even, -cross), (even, -cross)]

    def add(row, col, down, right):
        rows, source_row, row = (SIZE, 0, row + HALF) if down is None else (
            HALF, pl.multiple_of(jnp.where(down < 0, HALF, 0), HALF), row + jnp.where(down < 0, 0, 3 * HALF)
        )
        if right is None:
            col = col + HALF
        else:
            source = jnp.where(right < 0, 1, 0)
            col = col + jnp.where(right < 0, 0, 3 * HALF)
        base, shift = col // HALF, lax.rem(col, HALF)
        for i in range(0, rows, CHUNK):
            part = pl.ds(source_row + i, CHUNK)
            where = pl.ds(row + i, CHUNK)
            if right is None:
                moved = spread(power[0, part], power[1, part], shift, lanes)
            else:
                rolled = pltpu.roll(power[source, part], shift, 1)
                moved = jnp.where(lanes < shift, 0.0, rolled), jnp.where(lanes < shift, rolled, 0.0)
            for b, value in enumerate(moved):
                accum[base + b, where, :] += value

    count = starts.shape[1]
    for j in range(count):
        add(starts[0, j], starts[1, j], None, None)
    for n, (down, right) in enumerate(neighbours):
        for j in range(count):
            row, col = around[n, 2 * j] - 1, around[n, 2 * j + 1] - 1
            near = row >= 0
            if down is not None:
                near = near & jnp.where(down < 0, row > HALF, row < HALF)
            if right is not None:
                near = near & jnp.where(right < 0, col > HALF, col < HALF)

            @pl.when(near)
            def _(row=row, col=col, down=down, right=right):
                add(row, col, down, right)

    light[:, :HALF] = accum[2, 256:512]
    light[:, HALF:] = accum[3, 256:512]


def sum_kernel(chunk, total):
    total[...] = jnp.sum(chunk[...], axis=0)


def quotient_kernel(own, first, second, third, spread_out, ratio, held):
    z = 2 * lax.div(lax.axis_index("row"), 4) + lax.rem(lax.div(lax.axis_index("col"), 2), 2)
    for distance, part in enumerate((own, first, second, third)):
        held[lax.rem(z + 4 - distance, 4)] = part[...]
    total = (held[0] + held[1]) + (held[2] + held[3])
    for c in range(4):
        quotient = total[16 * c : 16 * c + 16] / total[64:80]
        spread_out[:, 16 * c : 16 * c + 16, :] = jnp.broadcast_to(quotient[None], (16, 16, HALF))
    ratio[...] = jnp.broadcast_to(total[80:81, 0:1] / total[80:81, 1:2], (8, HALF))


def fold_kernel(even, odd, cross, same, even_out, odd_out):
    even_rows, odd_rows, _, _ = sides()
    swapped = place_of()[1] == 1
    for p in range(2):
        for strip, rows, out in ((even, even_rows, even_out), (odd, odd_rows, odd_out)):
            a, b = cross[p, rows], same[p, rows]
            out[p, :HALF, :HALF] = strip[p, :, :HALF] + jnp.where(swapped, b, a)
            out[p, :HALF, HALF:] = strip[p, :, HALF:] + jnp.where(swapped, a, b)
    odd_out[:, HALF:, :] = jnp.zeros((2, 8, SIZE), F32)


def update_kernel(center, even, odd, cross, same, light, out, total):
    for p in range(2):
        total[p] = center[p]
    row_odd, core = place_of()
    even_half = pl.ds(pl.multiple_of(HALF * (1 - row_odd), HALF), HALF)
    odd_half = pl.ds(pl.multiple_of(HALF * row_odd, HALF), HALF)
    for p in range(2):
        total[p, even_half, :] += even[p]
        total[p, odd_half, :] += odd[p, :HALF]
    swapped = core == 1
    for i in range(0, SIZE, CHUNK):
        part = pl.ds(i, CHUNK)
        scale = 1.0 / (light[part] + object_damping)
        for p in range(2):
            a, b = cross[p, pl.ds(HALF + i, CHUNK)], same[p, pl.ds(HALF + i, CHUNK)]
            out[p, part, :HALF] = (total[p, part, :HALF] + jnp.where(swapped, b, a)) * scale[:, :HALF]
            out[p, part, HALF:] = (total[p, part, HALF:] + jnp.where(swapped, a, b)) * scale[:, HALF:]


def assemble_kernel(mine, other, out):
    core = place_of()[1]

    def write(source, block):
        for c in range(4):
            out[c, :, block * HALF : (block + 1) * HALF] = source[:, 16 * c : 16 * c + 16, :].reshape(SIZE, HALF)

    @pl.when(core == 0)
    def _():
        write(mine, 0)
        write(other, 1)

    @pl.when(core == 1)
    def _():
        write(mine, 1)
        write(other, 0)


def whole(*shape):
    return pl.BlockSpec(shape, lambda *_: (0,) * len(shape))


ANY = pl.BlockSpec(memory_space=pl.ANY)


def shaped(shapes):
    return [jax.ShapeDtypeStruct(s, F32) for s in shapes]


def params():
    return pltpu.CompilerParams(vmem_limit_bytes=VMEM_LIMIT)


def cost(flops, size):
    return pl.CostEstimate(flops=flops, bytes_accessed=size, transcendentals=0)


def simple(kernel, scalars, arrays, shapes, scratch, flops, size):
    single = not isinstance(shapes, list)
    outs = [shapes] if single else shapes
    call = pl.pallas_call(
        kernel,
        out_shape=shaped(outs)[0] if single else shaped(outs),
        grid_spec=pltpu.PrefetchScalarGridSpec(
            num_scalar_prefetch=len(scalars),
            grid=(),
            in_specs=[whole(*x.shape) for x in arrays],
            out_specs=whole(*shapes) if single else [whole(*s) for s in outs],
            scratch_shapes=[pltpu.VMEM(s, F32) for s in scratch],
        ),
        compiler_params=params(),
        cost_estimate=cost(flops, size),
    )
    return call(*scalars, *arrays)


def pack(starts, own):
    rows, crossing, columns = (2, HALF + 8, SIZE), (2, SIZE + 24, HALF), (2, SIZE + 8, HALF)
    return pl.pallas_call(
        pack_kernel,
        out_shape=shaped([rows, rows, crossing, columns]),
        grid_spec=pltpu.PrefetchScalarGridSpec(
            num_scalar_prefetch=1,
            grid=(),
            in_specs=[pl.BlockSpec(memory_space=pltpu.HBM)],
            out_specs=[ANY] * 4,
            scratch_shapes=[pltpu.VMEM((2, 8, SIZE), F32), pltpu.SemaphoreType.DMA((8,))],
        ),
        compiler_params=params(),
        cost_estimate=cost(1 << 10, 2 << 20),
    )(starts, own)


def prepare(measured):
    cols, rows = permutation()
    arrays = [measured, jnp.asarray(cols), jnp.asarray(rows)]
    return simple(prepare_kernel, [], arrays, measured.shape, [], 1 << 30, 3 << 20)


def stepped(width, *shape):
    return pl.BlockSpec((width, *shape), lambda i, *_: (i,) + (0,) * len(shape))


def transforms(starts, own, halo, probe, measured):
    mats = jnp.asarray(constants())
    arrays = [own, *halo, probe, mats]
    count = measured.shape[0]
    width = WIDTH
    halves = (16, 88, HALF)
    rows, columns = (2, HALF, SIZE), (2, 2 * SIZE, HALF)
    shapes = [(2, SIZE, SIZE), rows, rows, columns, columns, (2 * count, HALF)]
    slot = [
        pltpu.VMEM((2, 2 * SIZE, 3 * SIZE), BF),
        pltpu.VMEM((2, 2, 3 * SIZE, SIZE), BF),
        pltpu.VMEM((2, 2 * SIZE, SIZE), F32),
        pltpu.VMEM((2, 2, SIZE, SIZE), F32),
        pltpu.VMEM((2, 2, SIZE + 16, HALF), F32),
    ]
    return pl.pallas_call(
        transform_kernel,
        out_shape=shaped([halves, halves]) + [jax.ShapeDtypeStruct((8, HALF), jnp.int32)] + shaped(shapes),
        grid_spec=pltpu.PrefetchScalarGridSpec(
            num_scalar_prefetch=1,
            grid=(count // width,),
            in_specs=[ANY] * len(arrays) + [stepped(width, SIZE, SIZE)],
            out_specs=[whole(*x) for x in [halves, halves, (8, HALF), *shapes]],
            scratch_shapes=[
                pltpu.VMEM((2, 5, 2 * SIZE, HALF), F32),
                pltpu.VMEM(probe.shape, F32),
                pltpu.VMEM(mats.shape, BF),
                pltpu.VMEM((8, 8, HALF), F32),
                pltpu.VMEM((2, 5, SIZE, HALF), F32),
                pltpu.VMEM((2, 8, HALF), F32),
                pltpu.VMEM((2, 5, 2 * SIZE, HALF), F32),
                pltpu.VMEM((SIZE, SIZE), F32),
                pltpu.SemaphoreType.DMA((24,)),
            ]
            + slot * width,
        ),
        compiler_params=params(),
        cost_estimate=cost(13 << 30, 12 << 20),
    )(starts, *arrays, measured)


def illuminate(starts, around, probe):
    scratch = [(2, SIZE, HALF), (7, 3 * SIZE, HALF)]
    return simple(light_kernel, [starts, around], [probe], (SIZE, SIZE), scratch, 2 << 30, 4 << 20)


def update(arrays):
    shape = arrays[0].shape
    return simple(update_kernel, [], arrays, shape, [shape], 1 << 20, 3 << 20)


def assemble(mine, other):
    return simple(assemble_kernel, [], [mine, other], (4, SIZE, SIZE), [], 1 << 20, 2 << 20)


def pairs_from(first, count):
    pairs = []
    for i in range(first, count - 1, 2):
        pairs += [(i, i + 1), (i + 1, i)]
    return pairs


def swap_rows(value, first):
    return lax.ppermute(value, "row", pairs_from(first, lax.axis_size("row")))


def swap_columns(value, first):
    return lax.ppermute(value, "col", pairs_from(first, lax.axis_size("col")))


def along_z(value, distance):
    pairs = []
    for row in range(lax.axis_size("row")):
        for col in range(lax.axis_size("col")):
            z = (2 * (row // 4) + col // 2 % 2 + distance) % 4
            target = (4 * (z // 2) + row % 4) * 16 + col // 4 * 4 + 2 * (z % 2) + col % 2
            pairs.append((row * 16 + col, target))
    return lax.ppermute(value, AXES, pairs)


def planes():
    groups = {}
    for row in range(lax.axis_size("row")):
        for col in range(lax.axis_size("col")):
            groups.setdefault((row // 4, col % 4), []).append(row * 16 + col)
    return list(groups.values())


def half_lanes(value, first):
    return jnp.where(first, value[..., :HALF], value[..., HALF:])


def local(object_tile, probe, amplitudes, offsets):
    starts = offsets[0, 0].T
    measured = amplitudes[0, 0]
    core = lax.rem(lax.axis_index("col"), 2)
    groups = planes()

    with jax.named_scope("object_halo"):
        even, odd, cross, same = pack(starts, object_tile)
        odd = swap_rows(odd, 1)
        even = swap_rows(even, 0)
        cross = swap_columns(cross, 1)
        same = swap_columns(same, 0)
    permuted = prepare(measured)
    with jax.named_scope("object_corners"):
        odd, even, cross, same, permuted = lax.optimization_barrier((odd, even, cross, same, permuted))
        rows = jnp.stack([odd, even])
        cross_corner = swap_columns(half_lanes(rows, core == 0), 1)
        same_corner = swap_columns(half_lanes(rows, core == 1), 0)

    halo = [odd, even, cross, same, cross_corner, same_corner]
    keep, send, around, *parts = transforms(starts, object_tile, halo, probe, permuted)

    center, even, odd, cross, same, steps = parts
    with jax.named_scope("gradient_columns"):
        cross = swap_columns(cross, 1)
        same = swap_columns(same, 0)

    with jax.named_scope("probe_reduce"):
        chunk, around = lax.optimization_barrier((keep + swap_columns(send, 0), around))
        chunk = lax.all_to_all(chunk, AXES, 0, 0, axis_index_groups=groups, tiled=True)

    with jax.named_scope("gradient_rows"):
        light = illuminate(starts, around, probe)
        even, odd = simple(fold_kernel, [], [even, odd, cross, same], [even.shape, (2, HALF + 8, SIZE)], [], 1 << 20, 1 << 20)
        chunk, light, odd, even = lax.optimization_barrier((chunk, light, odd, even))

    with jax.named_scope("probe_sum"):
        total = simple(sum_kernel, [], [chunk], (88, HALF), [], 1 << 20, 1 << 20)
        parts = [total] + [along_z(total, d) for d in (1, 2, 3)]
        shapes = [(16, 64, HALF), (8, HALF)]
        spread_out, ratio = simple(quotient_kernel, [], parts, shapes, [(4, 88, HALF)], 1 << 20, 2 << 20)
        spread_out, odd, even = lax.optimization_barrier((spread_out, odd, even))
        odd = swap_rows(odd, 1)
        even = swap_rows(even, 0)

    with jax.named_scope("probe_gather"):
        gathered = lax.all_to_all(spread_out, AXES, 0, 0, axis_index_groups=groups, tiled=True)
        object_update = update([center, even, odd, cross, same, light])
        relative_error = ratio[0, :1]
        position_step = steps[:, 0].reshape(1, 1, -1, 2)
        tied = (gathered, object_update, relative_error, position_step)
        gathered, object_update, relative_error, position_step = lax.optimization_barrier(tied)
        probe_update = assemble(gathered, swap_columns(gathered, 0)).reshape(probe.shape)

    return (object_update, probe_update, position_step, relative_error)


def solution(mesh):
    in_specs = (
        P(None, "row", "col"),
        P(),
        P("row", "col", None, None, None),
        P("row", "col", None, None),
    )
    out_specs = (P(None, "row", "col"), P(), P("row", "col", None, None), P())
    return jax.shard_map(local, mesh=mesh, in_specs=in_specs, out_specs=out_specs, check_vma=False)
```

```python
import jax
import jax.numpy as jnp
import ml_dtypes
import numpy as np
from jax import lax
from jax.experimental import pallas as pl
from jax.experimental.pallas import tpu as pltpu
from jax.sharding import PartitionSpec as P

intensity_floor = 0.1
object_damping = 1.0
small_value = 1e-06

SIZE = 256
HALF = 128
CHUNK = 32
WIDTH = 4
BF = jnp.bfloat16
F32 = jnp.float32
AXES = ("row", "col")
VMEM_LIMIT = 32 * 2**20


def transform_matrices():
    n = np.arange(HALF)[:, None]
    q = np.arange(HALF)[None, :]
    out = []
    for odd in (0, 1):
        angle = -2.0 * np.pi * ((n * (2 * q + odd)) % SIZE) / SIZE
        re, im = np.cos(angle) / 16.0, np.sin(angle) / 16.0
        out.append(np.block([[re, im], [-im, re]]))
    return out


def split_np(matrix):
    high = matrix.astype(ml_dtypes.bfloat16)
    low = (matrix - high.astype(np.float64)).astype(ml_dtypes.bfloat16)
    return high, low


def constants():
    return np.stack([np.stack([np.stack(split_np(x)) for x in (m, m.T)]) for m in transform_matrices()])


def permutation():
    order = np.concatenate([np.arange(0, SIZE, 2), np.arange(1, SIZE, 2)])
    onehot = np.zeros((SIZE, SIZE), np.float32)
    onehot[order, np.arange(SIZE)] = 1.0
    columns = np.concatenate([onehot] * 3, 0).astype(ml_dtypes.bfloat16)
    rows = np.concatenate([onehot.T] * 3, 1).astype(ml_dtypes.bfloat16)
    return columns, rows


def split2(value):
    high = value.astype(BF)
    return high, (value - high.astype(F32)).astype(BF)


def split3(value):
    high = value.astype(BF)
    rest = value - high.astype(F32)
    middle = rest.astype(BF)
    return high, middle, (rest - middle.astype(F32)).astype(BF)


def dot(a, b):
    return jnp.dot(a, b, preferred_element_type=F32)


def lane_index(rows):
    return lax.broadcasted_iota(jnp.int32, (rows, HALF), 1)


def spread(first, second, shift, lanes):
    a = pltpu.roll(first, shift, 1)
    b = pltpu.roll(second, shift, 1)
    wrapped = lanes < shift
    return jnp.where(wrapped, 0.0, a), jnp.where(wrapped, a, b), jnp.where(wrapped, b, 0.0)


def gather_lanes(blocks, shift, lanes):
    back = jnp.where(shift == 0, 0, HALF - shift)
    a, b, c = [pltpu.roll(x, back, 1) for x in blocks]
    inside = lanes < HALF - shift
    return jnp.where(inside, a, b), jnp.where(inside, b, c)


def fold8(value):
    return jnp.sum(value.reshape(-1, 8, HALF), axis=0)


def prepare_kernel(measured, cols, rows, permuted):
    for j in range(measured.shape[0]):
        moved = dot(jnp.concatenate(split3(measured[j]), 1), cols[...])
        permuted[j] = dot(rows[...], jnp.concatenate(split3(moved), 0))


def place_of():
    return lax.rem(lax.axis_index("row"), 2), lax.rem(lax.axis_index("col"), 2)


def run_all(copies):
    for copy in copies:
        copy.start()
    for copy in copies:
        copy.wait()


def pack_kernel(starts, own, even, odd, cross, same, offsets, sems):
    row_odd, core = place_of()
    lanes = lane_index(8)
    value = jnp.zeros((8, HALF), F32)
    for j in range(starts.shape[1]):
        for d in range(2):
            value = jnp.where(lanes == 2 * j + d, (starts[d, j] + 1).astype(F32), value)
    for p in range(2):
        offsets[p, :, :HALF] = value
        offsets[p, :, HALF:] = value
    top = pl.ds(pl.multiple_of(HALF * row_odd, HALF), HALF)
    bottom = pl.ds(pl.multiple_of(HALF * (1 - row_odd), HALF), HALF)
    near = pl.ds(pl.multiple_of(HALF * core, HALF), HALF)
    far = pl.ds(pl.multiple_of(HALF * (1 - core), HALF), HALF)
    moves = [
        (own.at[:, top, :], odd.at[:, :HALF, :]),
        (own.at[:, bottom, :], even.at[:, :HALF, :]),
        (own.at[:, :, near], cross.at[:, :SIZE, :]),
        (own.at[:, :, far], same.at[:, :SIZE, :]),
        (offsets, odd.at[:, HALF:, :]),
        (offsets, even.at[:, HALF:, :]),
        (offsets.at[:, :, :HALF], cross.at[:, SIZE : SIZE + 8, :]),
        (offsets.at[:, :, :HALF], same.at[:, SIZE:, :]),
    ]
    run_all([pltpu.make_async_copy(x, y, sems.at[n]) for n, (x, y) in enumerate(moves)])


def sides():
    row_odd, core = place_of()
    even_rows = pl.ds(pl.multiple_of(3 * HALF * (1 - row_odd), HALF), HALF)
    odd_rows = pl.ds(pl.multiple_of(3 * HALF * row_odd, HALF), HALF)
    return even_rows, odd_rows, 3 * core, 3 - 3 * core


def transform_kernel(
    starts, own, odd_strip, even_strip, cross, same, cross_corner, same_corner, probe_in, matrices, measured,
    keep, send, around, center, even, odd, cross_out, same_out, steps,
    tile, probe, mats, offsets, totals, sums, accum, power, sems, *slots,
):
    step = pl.program_id(0)
    modes = probe.shape[0]
    lanes = lane_index(CHUNK)
    width = measured.shape[0]
    per_slot = len(slots) // width
    slots = [slots[n * per_slot : (n + 1) * per_slot] for n in range(width)]

    @pl.when(step == 0)
    def _():
        even_rows, odd_rows, cross_block, same_block = sides()
        middle = pl.ds(HALF, SIZE)
        moves = [(probe_in, probe), (matrices, mats)]
        for block, strip, corner in ((cross_block, cross, cross_corner), (same_block, same, same_corner)):
            moves.append((strip.at[:, :SIZE, :], tile.at[:, block, middle, :]))
            moves.append((corner.at[1, :, :HALF, :], tile.at[:, block, even_rows, :]))
            moves.append((corner.at[0, :, :HALF, :], tile.at[:, block, odd_rows, :]))
        for b in range(2):
            span = pl.ds(b * HALF, HALF)
            moves.append((own.at[:, :, span], tile.at[:, 1 + b, middle, :]))
            moves.append((even_strip.at[:, :HALF, span], tile.at[:, 1 + b, even_rows, :]))
            moves.append((odd_strip.at[:, :HALF, span], tile.at[:, 1 + b, odd_rows, :]))
        strips = [(odd_strip.at[0], HALF), (even_strip.at[0], HALF), (cross.at[0], SIZE), (same.at[0], SIZE)]
        strips += [(x.at[n, 0], HALF) for x in (cross_corner, same_corner) for n in range(2)]
        for n, (strip, at) in enumerate(strips):
            moves.append((strip.at[pl.ds(at, 8), pl.ds(0, HALF)], offsets.at[n]))
        copies = [pltpu.make_async_copy(x, y, sems.at[n]) for n, (x, y) in enumerate(moves)]
        for copy in copies:
            copy.start()
        tile[:, 4] = jnp.zeros((2, 2 * SIZE, HALF), F32)
        totals[...] = jnp.zeros_like(totals)
        sums[...] = jnp.zeros_like(sums)
        accum[...] = jnp.zeros_like(accum)
        for slot in slots:
            slot[4][:, :, 0:8, :] = jnp.zeros((2, 2, 8, HALF), F32)
            slot[4][:, :, 264:272, :] = jnp.zeros((2, 2, 8, HALF), F32)
        for copy in copies:
            copy.wait()
        for i in range(0, SIZE, CHUNK):
            part = pl.ds(i, CHUNK)
            power[part] = probe_power(probe, part)
        for n in range(8):
            around[pl.ds(n, 1), :] = offsets[n, :1, :].astype(jnp.int32)

    def right(odd, transposed):
        high, low = mats[odd, transposed, 0], mats[odd, transposed, 1]
        return jnp.concatenate([high, high, low], 0)

    def left(odd, transposed):
        high, low = mats[odd, transposed, 0], mats[odd, transposed, 1]
        return jnp.concatenate([high, low, high], 1)

    def position(n):
        col = starts[1, width * step + n]
        return starts[0, width * step + n], col // HALF, lax.rem(col, HALF)

    def enter(n):
        xs, patch = slots[n][0], slots[n][4]
        row, base, shift = position(n)
        for i in range(0, SIZE, CHUNK):
            part = pl.ds(i, CHUNK)
            where = pl.ds(row + i, CHUNK)
            obj = []
            for p in range(2):
                blocks = [tile[p, base + b, where, :] for b in range(3)]
                obj.append(gather_lanes(blocks, shift, lanes))
                for b in range(2):
                    patch[p, b, pl.ds(8 + i, CHUNK), :] = obj[p][b]
            for m in range(modes):
                wave = []
                for b in range(2):
                    span = slice(b * HALF, (b + 1) * HALF)
                    pr, pi = probe[m, 0, part, span], probe[m, 1, part, span]
                    wave.append((pr * obj[0][b] - pi * obj[1][b], pr * obj[1][b] + pi * obj[0][b]))
                for odd in range(2):
                    for p in range(2):
                        high, low = split2(wave[0][p] - wave[1][p] if odd else wave[0][p] + wave[1][p])
                        at = pl.ds(m * SIZE + i, CHUNK)
                        xs[odd, at, p * HALF : (p + 1) * HALF] = high
                        xs[odd, at, SIZE + p * HALF : SIZE + (p + 1) * HALF] = low
                        xs[odd, at, 2 * SIZE + p * HALF : 2 * SIZE + (p + 1) * HALF] = high

    def lanes_forward(n):
        xs, ys = slots[n][0], slots[n][2]
        for odd in range(2):
            ys[odd] = dot(xs[odd], right(odd, 0))

    def rows_split(n):
        zs, ys = slots[n][1], slots[n][2]
        for m in range(modes):
            for odd in range(2):
                lane_span = slice(odd * HALF, (odd + 1) * HALF)
                for i in range(0, HALF, CHUNK):
                    top = ys[odd, pl.ds(m * SIZE + i, CHUNK), :]
                    bottom = ys[odd, pl.ds(m * SIZE + HALF + i, CHUNK), :]
                    for odd_row in range(2):
                        high, low = split2(top - bottom if odd_row else top + bottom)
                        for p in range(2):
                            span = slice(p * HALF, (p + 1) * HALF)
                            at = p * HALF + i
                            zs[m, odd_row, pl.ds(at, CHUNK), lane_span] = high[:, span]
                            zs[m, odd_row, pl.ds(SIZE + at, CHUNK), lane_span] = high[:, span]
                            zs[m, odd_row, pl.ds(2 * SIZE + at, CHUNK), lane_span] = low[:, span]

    def rows_forward(n):
        zs, fs = slots[n][1], slots[n][3]
        for odd_row in range(2):
            for m in range(modes):
                fs[m, odd_row] = dot(left(odd_row, 1), zs[m, odd_row])

    def scale(n):
        zs, fs = slots[n][1], slots[n][3]
        error = jnp.zeros((8, HALF), F32)
        energy = jnp.zeros((8, HALF), F32)
        for odd_row in range(2):
            for i in range(0, HALF, CHUNK):
                parts = [[fs[m, odd_row, pl.ds(p * HALF + i, CHUNK), :] for p in range(2)] for m in range(modes)]
                intensity = parts[0][0] ** 2 + parts[0][1] ** 2 + (parts[1][0] ** 2 + parts[1][1] ** 2)
                intensity = jnp.maximum(intensity, intensity_floor)
                inverse = lax.rsqrt(intensity)
                modulus = intensity * inverse
                amplitude = measured[n, pl.ds(odd_row * HALF + i, CHUNK), :]
                factor = 1.0 - amplitude * inverse
                misfit = (modulus - amplitude) ** 2
                strength = amplitude**2
                error = error + fold8(misfit[:, :HALF]) + fold8(misfit[:, HALF:])
                energy = energy + fold8(strength[:, :HALF]) + fold8(strength[:, HALF:])
                for m in range(modes):
                    for p in range(2):
                        high, low = split2(parts[m][p] * factor)
                        at = p * HALF + i
                        zs[m, odd_row, pl.ds(at, CHUNK), :] = high
                        zs[m, odd_row, pl.ds(SIZE + at, CHUNK), :] = high
                        zs[m, odd_row, pl.ds(2 * SIZE + at, CHUNK), :] = low
        sums[0] += error
        sums[1] += energy

    def rows_back(n):
        zs, fs = slots[n][1], slots[n][3]
        for odd_row in range(2):
            for m in range(modes):
                fs[m, odd_row] = dot(left(odd_row, 0), zs[m, odd_row])

    def rows_join(n):
        xs, fs = slots[n][0], slots[n][3]
        for m in range(modes):
            for i in range(0, HALF, CHUNK):
                for p in range(2):
                    a, b = [fs[m, odd_row, pl.ds(p * HALF + i, CHUNK), :] for odd_row in range(2)]
                    for bottom in range(2):
                        high, low = split2(a - b if bottom else a + b)
                        at = pl.ds(m * SIZE + bottom * HALF + i, CHUNK)
                        for odd in range(2):
                            span = slice(odd * HALF, (odd + 1) * HALF)
                            xs[odd, at, p * HALF : (p + 1) * HALF] = high[:, span]
                            xs[odd, at, SIZE + p * HALF : SIZE + (p + 1) * HALF] = low[:, span]
                            xs[odd, at, 2 * SIZE + p * HALF : 2 * SIZE + (p + 1) * HALF] = high[:, span]

    def lanes_back(n):
        xs, ys = slots[n][0], slots[n][2]
        for odd in range(2):
            ys[odd] = dot(xs[odd], right(odd, 1))

    def leave(n):
        ys, patch = slots[n][2], slots[n][4]
        row, base, shift = position(n)
        first, last = lanes == 0, lanes == HALF - 1
        sums_of = [jnp.zeros((8, HALF), F32) for _ in range(4)]
        for i in range(0, SIZE, CHUNK):
            part = pl.ds(i, CHUNK)
            where = pl.ds(row + i, CHUNK)
            obj = [[patch[p, b, pl.ds(8 + i, CHUNK), :] for b in range(2)] for p in range(2)]
            grads = [[0.0, 0.0], [0.0, 0.0]]
            for b in range(2):
                re, im = obj[0][b], obj[1][b]
                span = slice(b * HALF, (b + 1) * HALF)
                for m in range(modes):
                    at = pl.ds(m * SIZE + i, CHUNK)
                    evens = [ys[0, at, p * HALF : (p + 1) * HALF] for p in range(2)]
                    odds = [ys[1, at, p * HALF : (p + 1) * HALF] for p in range(2)]
                    br, bi = [x - y if b else x + y for x, y in zip(evens, odds)]
                    pr, pi = probe[m, 0, part, span], probe[m, 1, part, span]
                    grads[0][b] = grads[0][b] + (pr * br + pi * bi)
                    grads[1][b] = grads[1][b] + (pr * bi - pi * br)
                    totals[b, 2 * m, part, :] += re * br + im * bi
                    totals[b, 2 * m + 1, part, :] += re * bi - im * br
                totals[b, 4, part, :] += re**2 + im**2
            for p in range(2):
                moved = spread(grads[p][0], grads[p][1], shift, lanes)
                for b in range(3):
                    accum[p, base + b, where, :] += moved[b]
            columns = []
            for p in range(2):
                before = [pltpu.roll(x, 1, 1) for x in obj[p]]
                after = [pltpu.roll(x, HALF - 1, 1) for x in obj[p]]
                columns.append(
                    (
                        jnp.where(last, after[1], after[0]) - jnp.where(first, 0.0, before[0]),
                        jnp.where(last, 0.0, after[1]) - jnp.where(first, before[0], before[1]),
                    )
                )
            for b in range(2):
                strength = power[part, b * HALF : (b + 1) * HALF]
                rows = [patch[p, b, pl.ds(9 + i, CHUNK), :] - patch[p, b, pl.ds(7 + i, CHUNK), :] for p in range(2)]
                for d, slope in enumerate((rows, [columns[0][b], columns[1][b]])):
                    sums_of[2 * d] = sums_of[2 * d] + fold8(grads[0][b] * slope[0] + grads[1][b] * slope[1])
                    sums_of[2 * d + 1] = sums_of[2 * d + 1] + fold8(strength * (slope[0] ** 2 + slope[1] ** 2))
        for d in range(2):
            numerator = 0.5 * jnp.sum(sums_of[2 * d], keepdims=True)
            denominator = 0.25 * jnp.sum(sums_of[2 * d + 1], keepdims=True) + small_value
            at = pl.ds(2 * (width * step + n) + d, 1)
            steps[at, :] = jnp.broadcast_to(-numerator / denominator, (1, HALF))

    stages = [enter, lanes_forward, rows_split, rows_forward, scale, rows_back, rows_join, lanes_back, leave]
    for at in range(len(stages) + width - 1):
        for n in range(width):
            if 0 <= at - n < len(stages):
                stages[at - n](n)

    @pl.when(step == pl.num_programs(0) - 1)
    def _():
        core = place_of()[1]
        scalar = jnp.where(lax.broadcasted_iota(jnp.int32, (1, 8, HALF), 2) == 0, jnp.sum(sums[0]), jnp.sum(sums[1]))
        for out, block in ((keep, core), (send, 1 - core)):
            for c in range(5):
                out[:, 16 * c : 16 * c + 16, :] = totals[block, c].reshape(16, 16, HALF)
            out[:, 80:88, :] = jnp.broadcast_to(scalar, (16, 8, HALF))
        even_rows, odd_rows, cross_block, same_block = sides()
        for p in range(2):
            for b in range(2):
                span = slice(b * HALF, (b + 1) * HALF)
                center[p, :, span] = accum[p, 1 + b, 128:384]
                even[p, :, span] = accum[p, 1 + b, even_rows]
                odd[p, :, span] = accum[p, 1 + b, odd_rows]
            cross_out[p] = accum[p, cross_block]
            same_out[p] = accum[p, same_block]


def probe_power(probe, part):
    return (probe[0, 0, part] ** 2 + probe[0, 1, part] ** 2) + (probe[1, 0, part] ** 2 + probe[1, 1, part] ** 2)


def light_kernel(starts, around, probe, light, power, accum):
    accum[...] = jnp.zeros_like(accum)
    for i in range(0, SIZE, CHUNK):
        part = pl.ds(i, CHUNK)
        total = probe_power(probe, part)
        power[0, part] = total[:, :HALF]
        power[1, part] = total[:, HALF:]
    lanes = lane_index(CHUNK)
    row_odd, core = place_of()
    even, cross = 1 - 2 * row_odd, 2 * core - 1
    neighbours = [(-even, None), (even, None), (None, cross), (None, -cross)]
    neighbours += [(-even, cross), (even, cross), (-even, -cross), (even, -cross)]

    def add(row, col, down, right):
        rows, source_row, row = (SIZE, 0, row + HALF) if down is None else (
            HALF, pl.multiple_of(jnp.where(down < 0, HALF, 0), HALF), row + jnp.where(down < 0, 0, 3 * HALF)
        )
        if right is None:
            col = col + HALF
        else:
            source = jnp.where(right < 0, 1, 0)
            col = col + jnp.where(right < 0, 0, 3 * HALF)
        base, shift = col // HALF, lax.rem(col, HALF)
        for i in range(0, rows, CHUNK):
            part = pl.ds(source_row + i, CHUNK)
            where = pl.ds(row + i, CHUNK)
            if right is None:
                moved = spread(power[0, part], power[1, part], shift, lanes)
            else:
                rolled = pltpu.roll(power[source, part], shift, 1)
                moved = jnp.where(lanes < shift, 0.0, rolled), jnp.where(lanes < shift, rolled, 0.0)
            for b, value in enumerate(moved):
                accum[base + b, where, :] += value

    count = starts.shape[1]
    for j in range(count):
        add(starts[0, j], starts[1, j], None, None)
    for n, (down, right) in enumerate(neighbours):
        for j in range(count):
            row, col = around[n, 2 * j] - 1, around[n, 2 * j + 1] - 1
            near = row >= 0
            if down is not None:
                near = near & jnp.where(down < 0, row > HALF, row < HALF)
            if right is not None:
                near = near & jnp.where(right < 0, col > HALF, col < HALF)

            @pl.when(near)
            def _(row=row, col=col, down=down, right=right):
                add(row, col, down, right)

    light[:, :HALF] = accum[2, 256:512]
    light[:, HALF:] = accum[3, 256:512]


def sum_kernel(chunk, total):
    total[...] = jnp.sum(chunk[...], axis=0)


def quotient_kernel(own, first, second, third, spread_out, ratio, held):
    z = 2 * lax.div(lax.axis_index("row"), 4) + lax.rem(lax.div(lax.axis_index("col"), 2), 2)
    for distance, part in enumerate((own, first, second, third)):
        held[lax.rem(z + 4 - distance, 4)] = part[...]
    total = (held[0] + held[1]) + (held[2] + held[3])
    for c in range(4):
        quotient = total[16 * c : 16 * c + 16] / total[64:80]
        spread_out[:, 16 * c : 16 * c + 16, :] = jnp.broadcast_to(quotient[None], (16, 16, HALF))
    ratio[...] = jnp.broadcast_to(total[80:81, 0:1] / total[80:81, 1:2], (8, HALF))


def fold_kernel(even, odd, cross, same, even_out, odd_out):
    even_rows, odd_rows, _, _ = sides()
    swapped = place_of()[1] == 1
    for p in range(2):
        for strip, rows, out in ((even, even_rows, even_out), (odd, odd_rows, odd_out)):
            a, b = cross[p, rows], same[p, rows]
            out[p, :, :HALF] = strip[p, :, :HALF] + jnp.where(swapped, b, a)
            out[p, :, HALF:] = strip[p, :, HALF:] + jnp.where(swapped, a, b)


def update_kernel(center, even, odd, cross, same, light, out, total):
    for p in range(2):
        total[p] = center[p]
    row_odd, core = place_of()
    even_half = pl.ds(pl.multiple_of(HALF * (1 - row_odd), HALF), HALF)
    odd_half = pl.ds(pl.multiple_of(HALF * row_odd, HALF), HALF)
    for p in range(2):
        total[p, even_half, :] += even[p]
        total[p, odd_half, :] += odd[p]
    swapped = core == 1
    for i in range(0, SIZE, CHUNK):
        part = pl.ds(i, CHUNK)
        scale = 1.0 / (light[part] + object_damping)
        for p in range(2):
            a, b = cross[p, pl.ds(HALF + i, CHUNK)], same[p, pl.ds(HALF + i, CHUNK)]
            out[p, part, :HALF] = (total[p, part, :HALF] + jnp.where(swapped, b, a)) * scale[:, :HALF]
            out[p, part, HALF:] = (total[p, part, HALF:] + jnp.where(swapped, a, b)) * scale[:, HALF:]


def assemble_kernel(mine, other, out):
    core = place_of()[1]

    def write(source, block):
        for c in range(4):
            out[c, :, block * HALF : (block + 1) * HALF] = source[:, 16 * c : 16 * c + 16, :].reshape(SIZE, HALF)

    @pl.when(core == 0)
    def _():
        write(mine, 0)
        write(other, 1)

    @pl.when(core == 1)
    def _():
        write(mine, 1)
        write(other, 0)


def whole(*shape):
    return pl.BlockSpec(shape, lambda *_: (0,) * len(shape))


ANY = pl.BlockSpec(memory_space=pl.ANY)


def shaped(shapes):
    return [jax.ShapeDtypeStruct(s, F32) for s in shapes]


def params():
    return pltpu.CompilerParams(vmem_limit_bytes=VMEM_LIMIT)


def cost(flops, size):
    return pl.CostEstimate(flops=flops, bytes_accessed=size, transcendentals=0)


def simple(kernel, scalars, arrays, shapes, scratch, flops, size):
    single = not isinstance(shapes, list)
    outs = [shapes] if single else shapes
    call = pl.pallas_call(
        kernel,
        out_shape=shaped(outs)[0] if single else shaped(outs),
        grid_spec=pltpu.PrefetchScalarGridSpec(
            num_scalar_prefetch=len(scalars),
            grid=(),
            in_specs=[whole(*x.shape) for x in arrays],
            out_specs=whole(*shapes) if single else [whole(*s) for s in outs],
            scratch_shapes=[pltpu.VMEM(s, F32) for s in scratch],
        ),
        compiler_params=params(),
        cost_estimate=cost(flops, size),
    )
    return call(*scalars, *arrays)


def pack(starts, own):
    rows, crossing, columns = (2, HALF + 8, SIZE), (2, SIZE + 24, HALF), (2, SIZE + 8, HALF)
    return pl.pallas_call(
        pack_kernel,
        out_shape=shaped([rows, rows, crossing, columns]),
        grid_spec=pltpu.PrefetchScalarGridSpec(
            num_scalar_prefetch=1,
            grid=(),
            in_specs=[pl.BlockSpec(memory_space=pltpu.HBM)],
            out_specs=[ANY] * 4,
            scratch_shapes=[pltpu.VMEM((2, 8, SIZE), F32), pltpu.SemaphoreType.DMA((8,))],
        ),
        compiler_params=params(),
        cost_estimate=cost(1 << 10, 2 << 20),
    )(starts, own)


def prepare(measured):
    cols, rows = permutation()
    arrays = [measured, jnp.asarray(cols), jnp.asarray(rows)]
    return simple(prepare_kernel, [], arrays, measured.shape, [], 1 << 30, 3 << 20)


def stepped(width, *shape):
    return pl.BlockSpec((width, *shape), lambda i, *_: (i,) + (0,) * len(shape))


def transforms(starts, own, halo, probe, measured):
    mats = jnp.asarray(constants())
    arrays = [own, *halo, probe, mats]
    count = measured.shape[0]
    width = WIDTH
    halves = (16, 88, HALF)
    rows, columns = (2, HALF, SIZE), (2, 2 * SIZE, HALF)
    shapes = [(2, SIZE, SIZE), rows, rows, columns, columns, (2 * count, HALF)]
    slot = [
        pltpu.VMEM((2, 2 * SIZE, 3 * SIZE), BF),
        pltpu.VMEM((2, 2, 3 * SIZE, SIZE), BF),
        pltpu.VMEM((2, 2 * SIZE, SIZE), F32),
        pltpu.VMEM((2, 2, SIZE, SIZE), F32),
        pltpu.VMEM((2, 2, SIZE + 16, HALF), F32),
    ]
    return pl.pallas_call(
        transform_kernel,
        out_shape=shaped([halves, halves]) + [jax.ShapeDtypeStruct((8, HALF), jnp.int32)] + shaped(shapes),
        grid_spec=pltpu.PrefetchScalarGridSpec(
            num_scalar_prefetch=1,
            grid=(count // width,),
            in_specs=[ANY] * len(arrays) + [stepped(width, SIZE, SIZE)],
            out_specs=[whole(*x) for x in [halves, halves, (8, HALF), *shapes]],
            scratch_shapes=[
                pltpu.VMEM((2, 5, 2 * SIZE, HALF), F32),
                pltpu.VMEM(probe.shape, F32),
                pltpu.VMEM(mats.shape, BF),
                pltpu.VMEM((8, 8, HALF), F32),
                pltpu.VMEM((2, 5, SIZE, HALF), F32),
                pltpu.VMEM((2, 8, HALF), F32),
                pltpu.VMEM((2, 5, 2 * SIZE, HALF), F32),
                pltpu.VMEM((SIZE, SIZE), F32),
                pltpu.SemaphoreType.DMA((24,)),
            ]
            + slot * width,
        ),
        compiler_params=pltpu.CompilerParams(vmem_limit_bytes=42 * 2**20),
        cost_estimate=cost(13 << 30, 12 << 20),
    )(starts, *arrays, measured)


def illuminate(starts, around, probe):
    scratch = [(2, SIZE, HALF), (7, 3 * SIZE, HALF)]
    return simple(light_kernel, [starts, around], [probe], (SIZE, SIZE), scratch, 2 << 30, 4 << 20)


def update(arrays):
    shape = arrays[0].shape
    return simple(update_kernel, [], arrays, shape, [shape], 1 << 20, 3 << 20)


def assemble(mine, other):
    return simple(assemble_kernel, [], [mine, other], (4, SIZE, SIZE), [], 1 << 20, 2 << 20)


def pairs_from(first, count):
    pairs = []
    for i in range(first, count - 1, 2):
        pairs += [(i, i + 1), (i + 1, i)]
    return pairs


def swap_rows(value, first):
    return lax.ppermute(value, "row", pairs_from(first, lax.axis_size("row")))


def swap_columns(value, first):
    return lax.ppermute(value, "col", pairs_from(first, lax.axis_size("col")))


def along_z(value, distance):
    pairs = []
    for row in range(lax.axis_size("row")):
        for col in range(lax.axis_size("col")):
            z = (2 * (row // 4) + col // 2 % 2 + distance) % 4
            target = (4 * (z // 2) + row % 4) * 16 + col // 4 * 4 + 2 * (z % 2) + col % 2
            pairs.append((row * 16 + col, target))
    return lax.ppermute(value, AXES, pairs)


def planes():
    groups = {}
    for row in range(lax.axis_size("row")):
        for col in range(lax.axis_size("col")):
            groups.setdefault((row // 4, col % 4), []).append(row * 16 + col)
    return list(groups.values())


def half_lanes(value, first):
    return jnp.where(first, value[..., :HALF], value[..., HALF:])


def local(object_tile, probe, amplitudes, offsets):
    starts = offsets[0, 0].T
    measured = amplitudes[0, 0]
    core = lax.rem(lax.axis_index("col"), 2)
    groups = planes()

    with jax.named_scope("object_halo"):
        even, odd, cross, same = pack(starts, object_tile)
        odd = swap_rows(odd, 1)
        even = swap_rows(even, 0)
        cross = swap_columns(cross, 1)
        same = swap_columns(same, 0)
    permuted = prepare(measured)
    with jax.named_scope("object_corners"):
        odd, even, cross, same, permuted = lax.optimization_barrier((odd, even, cross, same, permuted))
        rows = jnp.stack([odd, even])
        cross_corner = swap_columns(half_lanes(rows, core == 0), 1)
        same_corner = swap_columns(half_lanes(rows, core == 1), 0)

    halo = [odd, even, cross, same, cross_corner, same_corner]
    keep, send, around, *parts = transforms(starts, object_tile, halo, probe, permuted)

    center, even, odd, cross, same, steps = parts
    with jax.named_scope("gradient_columns"):
        cross = swap_columns(cross, 1)
        same = swap_columns(same, 0)

    with jax.named_scope("probe_reduce"):
        chunk, around = lax.optimization_barrier((keep + swap_columns(send, 0), around))
        chunk = lax.all_to_all(chunk, AXES, 0, 0, axis_index_groups=groups, tiled=True)

    with jax.named_scope("gradient_rows"):
        light = illuminate(starts, around, probe)
        even, odd = simple(fold_kernel, [], [even, odd, cross, same], [even.shape] * 2, [], 1 << 20, 1 << 20)
        chunk, light, odd, even = lax.optimization_barrier((chunk, light, odd, even))

    with jax.named_scope("probe_sum"):
        total = simple(sum_kernel, [], [chunk], (88, HALF), [], 1 << 20, 1 << 20)
        parts = [total] + [along_z(total, d) for d in (1, 2, 3)]
        shapes = [(16, 64, HALF), (8, HALF)]
        spread_out, ratio = simple(quotient_kernel, [], parts, shapes, [(4, 88, HALF)], 1 << 20, 2 << 20)
        spread_out, odd, even = lax.optimization_barrier((spread_out, odd, even))
        odd = swap_rows(odd, 1)
        even = swap_rows(even, 0)

    with jax.named_scope("probe_gather"):
        gathered = lax.all_to_all(spread_out, AXES, 0, 0, axis_index_groups=groups, tiled=True)
        object_update = update([center, even, odd, cross, same, light])
        relative_error = ratio[0, :1]
        position_step = steps[:, 0].reshape(1, 1, -1, 2)
        tied = (gathered, object_update, relative_error, position_step)
        gathered, object_update, relative_error, position_step = lax.optimization_barrier(tied)
        probe_update = assemble(gathered, swap_columns(gathered, 0)).reshape(probe.shape)

    return (object_update, probe_update, position_step, relative_error)


def solution(mesh):
    in_specs = (
        P(None, "row", "col"),
        P(),
        P("row", "col", None, None, None),
        P("row", "col", None, None),
    )
    out_specs = (P(None, "row", "col"), P(), P("row", "col", None, None), P())
    return jax.shard_map(local, mesh=mesh, in_specs=in_specs, out_specs=out_specs, check_vma=False)
```
